32 devices in a mesh: head: 4 (over x, core), blk: 8 (over z, y).
Axes of the slice: x: 2, y: 2, z: 4, core: 2. Of those that a mesh axis runs over, the one named last changes fastest.
Arguments:
- block_input: bfloat16 [8, 512, 2048], P('blk', 'head'), may hold values from -6 to 6
- out_cotangent: bfloat16 [8, 512, 2048], P('blk', 'head'), may hold values from -6 to 6
- start_flags: int32 [8, 512], P('blk'), may hold values from 0 to 1, as said below
- in_weight: float32 [2048, 8240], P(('head', 'blk'))
- out_weight: float32 [4096, 2048], P(('head', 'blk'))
- gate_up_weight: float32 [2048, 8192], P(('head', 'blk')), may hold values from -0.125 to 0.125
- down_weight: float32 [4096, 2048], P(('head', 'blk')), may hold values from -0.09375 to 0.09375
- first_gain: float32 [2048], replicated, may hold values from 0.5 to 1.5
- second_gain: float32 [2048], replicated, may hold values from 0.5 to 1.5
- conv_weight: float32 [4, 3584], replicated, may hold values from -0.5 to 0.5
- conv_bias: float32 [3584], replicated, may hold values from -0.3 to 0.3
- step_bias: float32 [48], replicated, may hold values from -1 to 1
- decay_log: float32 [48], replicated, may hold values from -9.5 to -3
- skip_gain: float32 [48], replicated, may hold values from 0.5 to 1.5
Outputs:
- block_output: bfloat16 [8, 512, 2048], P('blk', 'head')
- grad_input: bfloat16 [8, 512, 2048], P('blk', 'head')
- grad_in_weight: float32 [2048, 8240], P(('head', 'blk'))
- grad_out_weight: float32 [4096, 2048], P(('head', 'blk'))
- grad_gate_up_weight: float32 [2048, 8192], P(('head', 'blk'))
- grad_down_weight: float32 [4096, 2048], P(('head', 'blk'))
- grad_first_gain: float32 [2048], replicated
- grad_second_gain: float32 [2048], replicated
- grad_conv_weight: float32 [4, 3584], replicated
- grad_conv_bias: float32 [3584], replicated
- grad_step_bias: float32 [48], replicated
- grad_decay_log: float32 [48], replicated
- grad_skip_gain: float32 [48], replicated
The draws below stay inside these ranges and needn't reach their ends.
Inputs may be any that keep to these rules, and one draw needn't show every extreme that they name: `start_flags`: token 0 starts a sequence; besides it, one start lies within 1024 tokens of each k * 8192 for 1 <= k < 4096/8192, and a few more lie in the last eighth of the tokens.
All inputs are finite; a program needn't handle non-finite values.
Results may differ from the reference program's by a relative error of at most 0.017.
Values may be sent and summed in bfloat16 or wider, within the bound.
No kernel may reach another device: no remote copies, remote signals or barrier semaphores. Data moves between devices by JAX's collectives and lax.ppermute only.
A program may use at most 576 MiB of HBM per device.

```python
import jax
import jax.numpy as jnp
from jax import lax

D = 2048
QH = 8
KVH = 2
HD = 128
MH = 48
MP = 64
NS = 256
FF = 4096
KW = 4
SEQ_LEN = 8192
SPAN = 512
SPANS = 8
TOKENS = 4096
WIN = 8240
MIXW = 4096
CONVCH = 3584
N_HEAD = 4


def draw_start_flags(key, part):
    key = jax.random.fold_in(key, 7)
    key_jitter, key_extra = jax.random.split(key, 2)
    positions = jnp.arange(TOKENS, dtype=jnp.int32)
    starts_count = max(TOKENS // SEQ_LEN, 1)
    jitter_reach = SEQ_LEN // 8
    jitter = jax.random.randint(key_jitter, (starts_count,), -jitter_reach, jitter_reach + 1)
    nominal = jnp.arange(starts_count, dtype=jnp.int32) * SEQ_LEN
    placed = jnp.where(nominal > 0, nominal + jitter, 0)
    flags = jnp.any(positions[:, None] == placed[None, :], axis=1)
    tail_begin = TOKENS - min(SEQ_LEN, TOKENS) // 8
    extra = jax.random.randint(key_extra, (TOKENS,), 0, 16) == 0
    flags = flags | (positions == 0) | extra & (positions >= tail_begin)
    return flags.astype(jnp.int32).reshape(SPANS, SPAN)


def draw_in_weight(key, part):
    key = jax.random.fold_in(key, 11)
    noise = jax.random.normal(key, (D, WIN), jnp.float32)
    column = jnp.arange(WIN, dtype=jnp.int32)
    mixer_end = QH * HD + 2 * KVH * HD + 2 * MH * MP
    scales = jnp.where(column < mixer_end, 1.0, 0.5)
    return noise * scales[None, :] * D ** (-0.5)


def draw_out_weight(key, part):
    key = jax.random.fold_in(key, 13)
    noise = jax.random.normal(key, (MIXW, D), jnp.float32)
    row_line = jnp.arange(MIXW, dtype=jnp.int32)
    scales = jnp.where(row_line < QH * HD, 0.25, (MH * MP) ** (-0.5))
    return noise * scales[:, None]


def steps_of(own_key, shape, cuts, least, largest):
    loudness, own = 1.0, jax.random.fold_in(own_key, 6)
    for dim, shards_of in cuts:
        draws = jnp.exp(jax.random.uniform(jax.random.fold_in(own, dim), (shards_of,), jnp.float32, least / len(cuts), largest / len(cuts)))
        loudness = loudness * jnp.repeat(draws, shape[dim] // shards_of).reshape([-1 if axis == dim else 1 for axis in range(len(shape))])
    return loudness


def normal_values(rng, shape, deviation, reach, cuts=(), kind=jnp.bfloat16):
    factor_of = steps_of(rng, shape, cuts, -0.22, 0.18) if cuts else 1.0
    drawn = jax.random.normal(rng, shape, jnp.float32) * deviation * factor_of
    return jnp.minimum(jnp.maximum(drawn, -reach), reach).astype(kind)


def setup_inputs(seed: int = 0) -> dict:
    keys = jax.random.split(jax.random.key(seed), 15)
    return {
        "block_input": normal_values(keys[0], (SPANS, SPAN, D), 1.0, 6.0, ((0, 8), (1, 4))),
        "out_cotangent": normal_values(keys[1], (SPANS, SPAN, D), 1.0, 6.0, ((0, 8), (1, 4))),
        "start_flags": draw_start_flags(jax.random.fold_in(keys[14], 71), 0),
        "in_weight": draw_in_weight(jax.random.fold_in(keys[14], 71), 0),
        "out_weight": draw_out_weight(jax.random.fold_in(keys[14], 71), 0),
        "gate_up_weight": normal_values(keys[5], (D, 2 * FF), D ** -0.5, 0.125, ((0, 32),), jnp.float32),
        "down_weight": normal_values(keys[6], (FF, D), FF ** -0.5, 0.09375, ((0, 32),), jnp.float32),
        "first_gain": jnp.clip(1.0 + 0.1 * jax.random.normal(keys[7], (D,), jnp.float32), 0.5, 1.5),
        "second_gain": jnp.clip(1.0 + 0.1 * jax.random.normal(keys[8], (D,), jnp.float32), 0.5, 1.5),
        "conv_weight": jnp.clip(jax.random.uniform(keys[9], (KW, CONVCH), jnp.float32, -0.5, 0.5), -0.5, 0.5),
        "conv_bias": jnp.clip(jax.random.uniform(keys[10], (CONVCH,), jnp.float32, -0.3, 0.3), -0.3, 0.3),
        "step_bias": jnp.clip(jax.random.uniform(keys[11], (MH,), jnp.float32, -1.0, 1.0), -1.0, 1.0),
        "decay_log": jnp.clip(jax.random.uniform(keys[12], (MH,), jnp.float32, -9.5, -3.0), -9.5, -3.0),
        "skip_gain": jnp.clip(jax.random.uniform(keys[13], (MH,), jnp.float32, 0.5, 1.5), 0.5, 1.5),
    }


precise = lax.Precision.HIGHEST
epsilon = 1e-05
rope_base = 100000000000.0
masked_score = -1e+30

@jax.custom_vjp
def low(v):
    return lax.optimization_barrier(v.astype(jnp.bfloat16)).astype(jnp.float32)

@jax.custom_vjp
def low_back(v):
    return v

def low_keep(v):
    return (low(v), None)

def low_pass(kept, grad):
    return (grad,)

def back_keep(v):
    return (v, None)

def back_low(kept, grad):
    return (low(grad),)
low.defvjp(low_keep, low_pass)
low_back.defvjp(back_keep, back_low)

def product(left_side, right_side):
    return jnp.dot(left_side, right_side, precision=precise)

def rms_norm(values_in, gain_vector):
    return values_in * lax.rsqrt(lax.optimization_barrier(jnp.mean(values_in * values_in, axis=-1, keepdims=True)) + epsilon) * gain_vector

def rotate(values_in, positions):
    half_width = values_in.shape[-1] // 2
    frequencies = rope_base ** (-jnp.arange(half_width, dtype=jnp.float32) * 2.0 / values_in.shape[-1])
    angles = positions[:, None] * frequencies[None, :]
    cosine = jnp.cos(angles)[:, None, :]
    sine_part = jnp.sin(angles)[:, None, :]
    first_half = values_in[..., :half_width]
    second_half = values_in[..., half_width:]
    return jnp.concatenate([first_half * cosine - second_half * sine_part, second_half * cosine + first_half * sine_part], axis=-1)

def causal_conv(values_in, conv_taps, conv_shift, keep_masks):
    result = conv_shift + conv_taps[0] * values_in
    for lag_index in range(1, KW):
        padding = [(lag_index, 0)] + [(0, 0)] * (values_in.ndim - 1)
        delayed = jnp.pad(values_in, padding)[:TOKENS]
        keep_line = keep_masks[lag_index].reshape((TOKENS,) + (1,) * (values_in.ndim - 1))
        result = result + conv_taps[lag_index] * keep_line * delayed
    return result

def reference(block_input, out_cotangent, start_flags, in_weight, out_weight, gate_up_weight, down_weight, first_gain, second_gain, conv_weight, conv_bias, step_bias, decay_log, skip_gain):
    flag_ints = start_flags.reshape(TOKENS).astype(jnp.int32)
    flag_line = flag_ints.astype(jnp.float32)
    positions = jnp.arange(TOKENS, dtype=jnp.int32)
    float_positions = positions.astype(jnp.float32)
    starts_at = lax.cummax(jnp.where(flag_ints > 0, positions, jnp.zeros_like(positions)), axis=0)
    keep_masks = [jnp.ones((TOKENS,), jnp.float32)]
    for lag_index in range(1, KW):
        delayed = jnp.pad(flag_line, (lag_index - 1, 0))[:TOKENS]
        keep_masks.append(keep_masks[-1] * (1.0 - delayed))
    groups = QH // N_HEAD
    spread_kv = N_HEAD // KVH
    mamba_group = MH // N_HEAD
    query_width = QH * HD
    kv_width = KVH * HD
    mamba_width = MH * MP
    score_scale = HD ** (-0.5)

    def whole_layer(tokens, w_in, w_out, w_gate_up, w_down, gain_one, gain_two, taps_all, shift_all, step_shift, decay_rate, skip_all):
        normed = low(rms_norm(tokens, gain_one))
        mixed_in = low_back(product(normed, low(w_in)))
        base_z = query_width + 2 * kv_width
        base_x = base_z + mamba_width
        base_b = base_x + mamba_width
        base_dt = base_b + 2 * NS
        query = mixed_in[:, :query_width].reshape(TOKENS, QH, HD)
        key_heads = mixed_in[:, query_width:query_width + kv_width].reshape(TOKENS, KVH, HD)
        value_heads = mixed_in[:, query_width + kv_width:base_z].reshape(TOKENS, KVH, HD)
        query = low_back(low(rotate(query, float_positions)))
        key_groups = low_back(jnp.repeat(low(rotate(key_heads, float_positions)), spread_kv, axis=1))
        value_groups = low_back(jnp.repeat(low(value_heads), spread_kv, axis=1))
        gate_z = low_back(low(mixed_in[:, base_z:base_x]))
        inner_x = low_back(low(mixed_in[:, base_x:base_b]))
        b_groups = low_back(jnp.repeat(low(mixed_in[:, base_b:base_b + NS])[:, None, :], N_HEAD, axis=1))
        c_groups = low_back(jnp.repeat(low(mixed_in[:, base_b + NS:base_dt])[:, None, :], N_HEAD, axis=1))
        step_raw = low_back(low(mixed_in[:, base_dt:]))

        def attend(pieces):
            block_query, first_visible, block_id = pieces
            query_pos = block_id * SPAN + jnp.arange(SPAN, dtype=jnp.int32)
            scores = jnp.einsum('tgqd,sgd->gqts', block_query, key_groups, precision=precise) * score_scale
            visible = (positions[None, :] <= query_pos[:, None]) & (positions[None, :] >= first_visible[:, None])
            scores = jnp.where(visible, scores, masked_score)
            probabilities = jax.nn.softmax(scores, axis=-1)
            return jnp.einsum('gqts,sgd->tgqd', probabilities, value_groups, precision=precise)
        attended = lax.map(jax.checkpoint(attend), (query.reshape(SPANS, SPAN, N_HEAD, groups, HD), starts_at.reshape(SPANS, SPAN), jnp.arange(SPANS, dtype=jnp.int32)))
        attended = attended.reshape(TOKENS, query_width)
        x_act = jax.nn.silu(causal_conv(inner_x, taps_all[:, :mamba_width], shift_all[:mamba_width], keep_masks))
        b_act = jax.nn.silu(causal_conv(b_groups, taps_all[:, mamba_width:mamba_width + NS], shift_all[mamba_width:mamba_width + NS], keep_masks))
        c_act = jax.nn.silu(causal_conv(c_groups, taps_all[:, mamba_width + NS:], shift_all[mamba_width + NS:], keep_masks))
        step_size = jax.nn.softplus(step_raw + step_shift)
        log_decay = -step_size * jnp.exp(decay_rate)
        skip_table = skip_all.reshape(N_HEAD, mamba_group)

        def mamba_span(chain_state, pieces):
            inner_act, into_act, outof_act, step_act, decay_act, gate_act, flags_span = pieces
            cumulative = jnp.cumsum(decay_act, axis=0)
            segment = jnp.cumsum(flags_span)
            index_line = jnp.arange(SPAN, dtype=jnp.int32)
            related = (segment[:, None] == segment[None, :]) & (index_line[:, None] >= index_line[None, :])
            related = related[:, :, None, None]
            spread = cumulative[:, None] - cumulative[None, :]
            decays = jnp.where(related, jnp.exp(jnp.where(related, spread, 0.0)), 0.0)
            scores = jnp.einsum('tgn,sgn->tsg', outof_act, into_act, precision=precise)
            weights = decays * scores[..., None] * step_act[None]
            within = jnp.einsum('tsgm,sgmp->tgmp', weights, inner_act, precision=precise)
            fresh = (segment == 0).astype(jnp.float32)
            entering = jnp.exp(cumulative) * fresh[:, None, None]
            carried = entering[..., None] * jnp.einsum('gmpn,tgn->tgmp', chain_state, outof_act, precision=precise)
            output = (within + carried + skip_table[None, :, :, None] * inner_act) * jax.nn.silu(gate_act)
            ending = jnp.where((segment == segment[-1])[:, None, None], jnp.exp(cumulative[-1][None] - cumulative), 0.0)
            local_state = jnp.einsum('sgm,sgmp,sgn->gmpn', ending * step_act, inner_act, into_act, precision=precise)
            span_factor = jnp.exp(cumulative[-1]) * fresh[-1]
            return (span_factor[..., None, None] * chain_state + local_state, output)
        pieces = (x_act.reshape(SPANS, SPAN, N_HEAD, mamba_group, MP), b_act.reshape(SPANS, SPAN, N_HEAD, NS), c_act.reshape(SPANS, SPAN, N_HEAD, NS), step_size.reshape(SPANS, SPAN, N_HEAD, mamba_group), log_decay.reshape(SPANS, SPAN, N_HEAD, mamba_group), gate_z.reshape(SPANS, SPAN, N_HEAD, mamba_group, MP), flag_line.reshape(SPANS, SPAN))
        initial_state = jnp.zeros((N_HEAD, mamba_group, MP, NS), jnp.float32)
        mamba_out = lax.scan(jax.checkpoint(mamba_span), initial_state, pieces)[1].reshape(TOKENS, mamba_width)
        mixer = jnp.concatenate([low_back(low(attended)), low_back(low(mamba_out))], axis=1)
        hidden_one = tokens + low_back(product(mixer, low(w_out)))
        gate_up = low_back(product(low(rms_norm(hidden_one, gain_two)), low(w_gate_up)))
        activated = low(jax.nn.silu(gate_up[:, :FF]) * gate_up[:, FF:])
        return hidden_one + product(activated, low(w_down))
    tokens = block_input.reshape(TOKENS, D).astype(jnp.float32)
    result, pullback = jax.vjp(whole_layer, tokens, in_weight, out_weight, gate_up_weight, down_weight, first_gain, second_gain, conv_weight, conv_bias, step_bias, decay_log, skip_gain)
    grads = pullback(out_cotangent.reshape(TOKENS, D).astype(jnp.float32))
    return (result.astype(jnp.bfloat16).reshape(SPANS, SPAN, D), grads[0].astype(jnp.bfloat16).reshape(SPANS, SPAN, D), grads[1], grads[2], grads[3], grads[4], grads[5], grads[6], grads[7], grads[8], grads[9], grads[10], grads[11])
```

```python
from functools import partial

import jax
import jax.numpy as jnp
from jax import lax
from jax.sharding import PartitionSpec as P

QH = 8
KVH = 2
HD = 128
MH = 48
MP = 64
NS = 256
FF = 4096
KW = 4


precise = lax.Precision.HIGHEST
epsilon = 1e-05
rope_base = 100000000000.0
masked_score = -1e30


def passed_along(shard, axis, by):
    peers = lax.axis_size(axis)
    pairs = [(i, i + by) for i in range(peers) if 0 <= i + by < peers]
    return lax.ppermute(shard, axis, pairs)


def prefix(shard, axis, combine, identity):
    peers, mine = (lax.axis_size(axis), lax.axis_index(axis))
    everything = jax.tree.map(
        lambda part, kind: lax.all_gather(part.astype(kind), axis),
        shard,
        (jnp.bfloat16, jnp.bfloat16, jnp.bfloat16),
    )
    start = jax.tree.map(
        lambda part, zero: jnp.broadcast_to(jnp.asarray(zero, part.dtype), part.shape),
        shard,
        identity,
    )

    def step(k, before):
        reached = k < mine
        new = combine(
            before, jax.tree.map(lambda part, own: part[k].astype(own.dtype), everything, shard)
        )
        return jax.tree.map(lambda a, b: jnp.where(reached, a, b), new, before)

    return lax.fori_loop(0, peers, step, start)


def carried_in(shard, axis, join, neutral):
    count = lax.axis_size(axis)
    place = lax.axis_index(axis)
    ahead = count - 1 - place
    gathered = jax.tree.map(
        lambda a, kind: lax.all_gather(a.astype(kind), axis),
        shard,
        jax.tree.map(lambda a: jnp.bfloat16 if a.dtype == jnp.float32 else a.dtype, shard),
    )
    state = jax.tree.map(lambda a, e: jnp.zeros_like(a) + jnp.asarray(e, a.dtype), shard, neutral)

    def one(step, state):
        source = count - 1 - step
        return join(
            state,
            jax.tree.map(
                lambda a, own: lax.dynamic_index_in_dim(a, source, 0, False).astype(own.dtype),
                gathered,
                shard,
            ),
        )

    return lax.fori_loop(0, ahead, one, state)


def ring_of(axis):
    peers = lax.axis_size(axis)
    if peers != 8:
        return list(range(peers))
    return [0, 2, 4, 6, 7, 5, 3, 1]


def gather_blocks(shard):
    return lax.all_gather(
        shard, "blk", axis=0, tiled=True, axis_index_groups=[ring_of("blk")]
    )


def scatter_blocks(partial_sums):
    return lax.psum_scatter(
        partial_sums,
        "blk",
        scatter_dimension=0,
        tiled=True,
        axis_index_groups=[ring_of("blk")],
    )


def from_head(shard, distance):
    peers = lax.axis_size("head")
    return lax.ppermute(shard, "head", [(i, i ^ distance) for i in range(peers)])


def by_distance(parts):
    mine = lax.axis_index("head")
    stacked = jnp.stack(parts)
    return [
        lax.dynamic_index_in_dim(stacked, jnp.bitwise_xor(mine, j), 0, False)
        for j in range(len(parts))
    ]


def gather_heads(shard):
    across = from_head(shard, 2)
    beside = from_head(jnp.stack([shard, across]), 1)
    return by_distance([shard, beside[0], across, beside[1]])


def scatter_heads(chunks):
    mine = lax.axis_index("head")

    def chunk(distance):
        return lax.dynamic_index_in_dim(chunks, jnp.bitwise_xor(mine, distance), 0, False)

    got = from_head(jnp.stack([chunk(1), chunk(3)]), 1)
    near = chunk(0) + got[0]
    far = (chunk(2) + got[1]).astype(jnp.bfloat16)
    return near + from_head(far, 2).astype(jnp.float32)


def ring_features(values_in):
    heads, ring = lax.axis_size("head"), ring_of("blk")
    rows, width = values_in.shape
    cut = values_in.reshape(rows, heads, len(ring), width // (heads * len(ring)))
    return jnp.concatenate([cut[:, :, k, :].reshape(rows, -1) for k in ring], axis=1)


def plain_features(values_in):
    heads, ring = lax.axis_size("head"), ring_of("blk")
    rows, width = values_in.shape
    cut = values_in.reshape(rows, len(ring), heads, width // (heads * len(ring)))
    places = [ring.index(k) for k in range(len(ring))]
    return jnp.concatenate(
        [cut[:, places[k], j, :] for j in range(heads) for k in range(len(ring))], axis=1
    )


def mixer_place():
    heads, ring = lax.axis_size("head"), ring_of("blk")
    peers = heads * len(ring)
    rows = (QH * HD + MH * MP) // peers
    query_blocks, mamba_blocks = QH * HD // rows // heads, MH * MP // rows // heads
    pairs = []
    for r in range(peers):
        if r < query_blocks * heads:
            group, slot = divmod(r, query_blocks)
        else:
            group, slot = divmod(r - query_blocks * heads, mamba_blocks)
            slot += query_blocks
        pairs.append((r, group * len(ring) + ring[slot]))
    return pairs


def column_cuts():
    query_end = QH * HD
    z_begin = query_end + 2 * KVH * HD
    x_begin = z_begin + MH * MP
    b_begin = x_begin + MH * MP
    dt_begin = b_begin + 2 * NS
    heads = lax.axis_size("head")
    cuts = []
    for j in range(heads):
        kind, kv_head = j % 2, j // 2
        kv_begin = query_end + kind * KVH * HD + kv_head * HD
        cuts.append(
            [
                (j * QH * HD // heads, QH * HD // heads),
                (kv_begin, HD),
                (z_begin + j * MH * MP // heads, MH * MP // heads),
                (x_begin + j * MH * MP // heads, MH * MP // heads),
                (b_begin + j * 2 * NS // heads, 2 * NS // heads),
                (dt_begin + j * MH // heads, MH // heads),
            ]
        )
    return cuts


step_pad = 128


def pack_in(weight):
    groups = []
    for cuts in column_cuts():
        pieces = [weight[:, begin : begin + size] for begin, size in cuts]
        pad = jnp.zeros((weight.shape[0], step_pad - cuts[-1][1]), weight.dtype)
        groups.append(jnp.concatenate(pieces + [pad], axis=1))
    return jnp.stack(groups)


def unpack_in(groups):
    pieces = []
    for j, cuts in enumerate(column_cuts()):
        at = 0
        for begin, size in cuts:
            pieces.append((begin, groups[j][:, at : at + size]))
            at += size
    pieces.sort(key=lambda item: item[0])
    return jnp.concatenate([piece for _, piece in pieces], axis=1)


def pack_ffn(weight):
    heads, ring = lax.axis_size("head"), ring_of("blk")
    unit = FF // (heads * len(ring))
    cut = weight.reshape(weight.shape[0], 2, heads, len(ring), unit)
    return jnp.stack(
        [
            jnp.concatenate([cut[:, half, j, k] for half in range(2) for k in ring], axis=1)
            for j in range(heads)
        ]
    )


def unpack_ffn(groups):
    heads, ring = lax.axis_size("head"), ring_of("blk")
    rows = groups.shape[1]
    cut = groups.reshape(heads, rows, 2, len(ring), FF // (heads * len(ring)))
    return jnp.concatenate(
        [
            cut[j, :, half, ring.index(k)]
            for half in range(2)
            for j in range(heads)
            for k in range(len(ring))
        ],
        axis=1,
    )


def swap_groups(groups):
    return lax.all_to_all(groups, "head", split_axis=0, concat_axis=0, tiled=True)


def outer_grad(left_side, grad_side):
    return lax.dot_general(
        left_side, grad_side, (((0,), (0,)), ((), ())), preferred_element_type=jnp.float32
    )


def times_transposed(grad_side, weight):
    return lax.dot_general(
        grad_side, weight, (((1,), (1,)), ((), ())), preferred_element_type=jnp.float32
    )


def rotate(values_in, positions, direction):
    half_width = values_in.shape[-1] // 2
    frequencies = rope_base ** (
        -jnp.arange(half_width, dtype=jnp.float32) * 2.0 / values_in.shape[-1]
    )
    angles = positions.astype(jnp.float32)[:, None] * frequencies[None, :]
    cosine = jnp.cos(angles)[:, None, :]
    sine_part = direction * jnp.sin(angles)[:, None, :]
    first_half = values_in[..., :half_width]
    second_half = values_in[..., half_width:]
    return jnp.concatenate(
        [
            first_half * cosine - second_half * sine_part,
            second_half * cosine + first_half * sine_part,
        ],
        axis=-1,
    )


def norm_back(values_in, inverse, gain_vector, grad_side):
    scaled = grad_side * gain_vector
    mean_term = jnp.mean(scaled * values_in, axis=-1, keepdims=True)
    return inverse * scaled - values_in * inverse**3 * mean_term


def combine_states(earlier, later):
    return (
        later[1][:, None, None] * earlier[0] + later[0],
        earlier[1] * later[1],
        jnp.maximum(earlier[2], later[2]),
    )


def combine_grads(earlier, later):
    return (later[0] * earlier[0], later[1] + later[0][:, None, None] * earlier[1])


def mamba_prepare(extended, conv_taps, conv_shift, step_raw, step_shift, decay_rate, keep_masks):
    length = step_raw.shape[0]
    lag_total = conv_taps.shape[0]
    result = conv_shift + conv_taps[0] * extended[lag_total - 1 :]
    for lag_index in range(1, lag_total):
        begin = lag_total - 1 - lag_index
        result = (
            result
            + conv_taps[lag_index]
            * keep_masks[lag_index][:, None]
            * extended[begin : begin + length]
        )
    active = jax.nn.silu(result)
    inner_width = active.shape[1] - 2 * NS
    inner_act = active[:, :inner_width].reshape(length, inner_width // MP, MP)
    into_act = active[:, inner_width : inner_width + NS]
    outof_act = active[:, inner_width + NS :]
    step_size = jax.nn.softplus(step_raw + step_shift)
    cumulative = jnp.cumsum(-step_size * jnp.exp(decay_rate), axis=0)
    return (inner_act, into_act, outof_act, step_size, cumulative)


def mamba_state(inner_act, into_act, step_size, cumulative, segment):
    ending = jnp.where(
        (segment == segment[-1])[:, None], jnp.exp(cumulative[-1][None, :] - cumulative), 0.0
    )
    local_state = jnp.einsum(
        "sm,smp,sn->mpn", ending * step_size, inner_act, into_act, precision=precise
    )
    span_factor = jnp.exp(cumulative[-1]) * (segment[-1] == 0).astype(jnp.float32)
    return (local_state, span_factor)


def mamba_output(
    inner_act, into_act, outof_act, step_size, cumulative, gate_act, skip_local, state_in, segment
):
    length = step_size.shape[0]
    index_line = jnp.arange(length, dtype=jnp.int32)
    related = (segment[:, None] == segment[None, :]) & (index_line[:, None] >= index_line[None, :])
    scores = jnp.dot(outof_act, into_act.T, precision=precise)

    def one_head(head_items):
        cum_head, step_head, inner_head = head_items
        spread = cum_head[:, None] - cum_head[None, :]
        decays = jnp.where(related, jnp.exp(jnp.where(related, spread, 0.0)), 0.0)
        weights = decays * scores * step_head[None, :]
        return jnp.dot(weights, inner_head, precision=precise)

    within = lax.map(
        jax.checkpoint(one_head), (cumulative.T, step_size.T, jnp.transpose(inner_act, (1, 0, 2)))
    )
    within = jnp.transpose(within, (1, 0, 2))
    entering = jnp.exp(cumulative) * (segment == 0).astype(jnp.float32)[:, None]
    carried = entering[:, :, None] * jnp.einsum(
        "mpn,tn->tmp", state_in, outof_act, precision=precise
    )
    return (within + carried + skip_local[None, :, None] * inner_act) * jax.nn.silu(gate_act)


def per_device(
    block_input,
    out_cotangent,
    start_flags,
    in_weight,
    out_weight,
    gate_up_weight,
    down_weight,
    first_gain,
    second_gain,
    conv_weight,
    conv_bias,
    step_bias,
    decay_log,
    skip_gain,
):
    head_count = lax.axis_size("head")
    blocks = lax.axis_size("blk")
    head_index = lax.axis_index("head")
    block_index = lax.axis_index("blk")
    tokens = block_input[0].astype(jnp.float32)
    row_count = tokens.shape[0]
    span_rows = row_count * head_count
    query_group = QH // head_count
    mamba_group = MH // head_count
    mamba_width = MH * MP
    group_query = query_group * HD
    group_inner = mamba_group * MP
    score_scale = HD ** (-0.5)
    out_pairs = mixer_place()
    weights_in = gather_blocks(
        swap_groups(pack_in(in_weight.astype(jnp.bfloat16))).reshape(
            head_count * in_weight.shape[0], -1
        )
    )
    weights_out = gather_blocks(
        lax.ppermute(out_weight.astype(jnp.bfloat16), ("head", "blk"), out_pairs)
    )
    weights_ffn = gather_blocks(
        swap_groups(pack_ffn(gate_up_weight.astype(jnp.bfloat16))).reshape(
            head_count * gate_up_weight.shape[0], -1
        )
    )
    weights_down = gather_blocks(down_weight.astype(jnp.bfloat16))
    positions = block_index * span_rows + jnp.arange(span_rows, dtype=jnp.int32)
    span_tokens = jnp.concatenate(gather_heads(block_input[0]), axis=0).astype(jnp.float32)
    span_inverse = lax.rsqrt(jnp.mean(span_tokens * span_tokens, axis=-1, keepdims=True) + epsilon)
    normed_one = ring_features((span_tokens * span_inverse * first_gain).astype(jnp.bfloat16))
    projected = jnp.dot(normed_one, weights_in, preferred_element_type=jnp.float32)
    inverse_one = lax.rsqrt(jnp.mean(tokens * tokens, axis=-1, keepdims=True) + epsilon)
    cut_kv = group_query
    cut_z = cut_kv + HD
    cut_x = cut_z + group_inner
    cut_b = cut_x + group_inner
    cut_dt = cut_b + 2 * NS // head_count
    even = head_index % 2 == 0
    query_local = rotate(
        projected[:, :group_query].reshape(span_rows, query_group, HD), positions, 1.0
    ).astype(jnp.bfloat16)
    query_float = query_local.astype(jnp.float32)
    kv_plain = projected[:, cut_kv:cut_z]
    kv_mine = jnp.where(
        even, rotate(kv_plain.reshape(span_rows, 1, HD), positions, 1.0)[:, 0], kv_plain
    ).astype(jnp.bfloat16)
    kv_beside = from_head(kv_mine, 1)
    kv_local = jnp.where(
        even,
        jnp.concatenate([kv_mine, kv_beside], axis=1),
        jnp.concatenate([kv_beside, kv_mine], axis=1),
    )
    gate_act = (
        projected[:, cut_z:cut_x]
        .astype(jnp.bfloat16)
        .astype(jnp.float32)
        .reshape(span_rows, mamba_group, MP)
    )
    conv_local = jnp.concatenate(
        [projected[:, cut_x:cut_b].astype(jnp.bfloat16)]
        + gather_heads(projected[:, cut_b:cut_dt].astype(jnp.bfloat16)),
        axis=1,
    )
    step_local = (
        projected[:, cut_dt : cut_dt + mamba_group].astype(jnp.bfloat16).astype(jnp.float32)
    )
    flags_local = start_flags[0]
    rim_rows, rim_flags = passed_along(
        (
            conv_local[span_rows - (KW - 1) :],
            flags_local[span_rows - (KW - 2) :].astype(jnp.bfloat16),
        ),
        "blk",
        1,
    )
    flag_ext = jnp.concatenate([rim_flags.astype(jnp.float32), flags_local.astype(jnp.float32)])
    keep_masks = [jnp.ones((span_rows,), jnp.float32)]
    for lag_index in range(1, KW):
        begin = KW - 1 - lag_index
        keep_masks.append(keep_masks[-1] * (1.0 - flag_ext[begin : begin + span_rows]))
    extended = jnp.concatenate([rim_rows, conv_local], axis=0).astype(jnp.float32)
    conv_taps = jnp.concatenate(
        [
            lax.dynamic_slice_in_dim(conv_weight, head_index * group_inner, group_inner, 1),
            conv_weight[:, mamba_width:],
        ],
        axis=1,
    )
    conv_shift = jnp.concatenate(
        [
            lax.dynamic_slice_in_dim(conv_bias, head_index * group_inner, group_inner, 0),
            conv_bias[mamba_width:],
        ]
    )
    step_shift = lax.dynamic_slice_in_dim(step_bias, head_index * mamba_group, mamba_group, 0)
    decay_rate = lax.dynamic_slice_in_dim(decay_log, head_index * mamba_group, mamba_group, 0)
    skip_local = lax.dynamic_slice_in_dim(skip_gain, head_index * mamba_group, mamba_group, 0)
    prepared, prepare_back = jax.vjp(
        partial(mamba_prepare, keep_masks=keep_masks),
        extended,
        conv_taps,
        conv_shift,
        step_local,
        step_shift,
        decay_rate,
    )
    inner_act, into_act, outof_act, step_size, cumulative = prepared
    segment = jnp.cumsum(flags_local)
    state_pair, state_back = jax.vjp(
        partial(mamba_state, segment=segment), inner_act, into_act, step_size, cumulative
    )
    local_state, span_factor = state_pair
    query_pos = block_index * span_rows + jnp.arange(span_rows, dtype=jnp.int32)
    last_start = jnp.max(jnp.where(flags_local > 0, query_pos, -1)).astype(jnp.float32)
    identity = (jnp.zeros_like(local_state), jnp.ones_like(span_factor), jnp.float32(-1.0))
    state_in, factor_in, start_in = prefix(
        (local_state, span_factor, last_start), "blk", combine_states, identity
    )
    mamba_out, output_back = jax.vjp(
        partial(mamba_output, segment=segment),
        inner_act,
        into_act,
        outof_act,
        step_size,
        cumulative,
        gate_act,
        skip_local,
        state_in,
    )
    local_start = lax.cummax(jnp.where(flags_local > 0, query_pos, -1), axis=0)
    first_visible = jnp.maximum(local_start, start_in.astype(jnp.int32))
    earliest_visible = jnp.min(first_visible)
    last_query = block_index * span_rows + span_rows - 1

    def visible_mask(key_start, key_total):
        key_pos = key_start + jnp.arange(key_total, dtype=jnp.int32)
        return (key_pos[None, :] <= query_pos[:, None]) & (
            key_pos[None, :] >= first_visible[:, None]
        )

    def attend_block(carried_state, key_block, key_start):
        running_top, running_total, summed = carried_state
        scores = (
            jnp.einsum(
                "tqd,sd->tqs", query_local, key_block[:, :HD], preferred_element_type=jnp.float32
            )
            * score_scale
        )
        visible = visible_mask(key_start, key_block.shape[0])[:, None, :]
        scores = jnp.where(visible, scores, masked_score)
        new_top = jnp.maximum(running_top, jnp.max(scores, axis=-1))
        probabilities = jnp.where(visible, jnp.exp(scores - new_top[..., None]), 0.0)
        rescale = jnp.exp(running_top - new_top)
        running_total = running_total * rescale + jnp.sum(probabilities, axis=-1)
        summed = summed * rescale[..., None] + jnp.einsum(
            "tqs,sd->tqd", probabilities, key_block[:, HD:].astype(jnp.float32), precision=precise
        )
        return (new_top, running_total, summed)

    def make_piece(block_fn):

        def one_block(carried_state, key_block, key_start):
            needed = (key_start <= last_query) & (key_start + key_block.shape[0] > earliest_visible)
            return lax.cond(
                needed,
                lambda unchanged: block_fn(unchanged, key_block, key_start),
                lambda unchanged: unchanged,
                carried_state,
            )

        def piece_fn(carried_state, shard_piece, first_row):
            piece_rows = shard_piece.shape[0]
            stacked = shard_piece.reshape(piece_rows // span_rows, span_rows, shard_piece.shape[1])
            begins = span_rows * jnp.arange(piece_rows // span_rows, dtype=jnp.int32)

            def scan_step(inner_state, pair_items):
                return (one_block(inner_state, pair_items[0], pair_items[1]), None)

            return lax.scan(scan_step, carried_state, (stacked, begins))[0]

        return piece_fn

    initial = (
        jnp.full((span_rows, query_group), masked_score, jnp.float32),
        jnp.zeros((span_rows, query_group), jnp.float32),
        jnp.zeros((span_rows, query_group, HD), jnp.float32),
    )
    running_top, running_total, summed = make_piece(attend_block)(
        initial, lax.all_gather(kv_local, "blk", axis=0, tiled=True), jnp.int32(0)
    )
    attended = summed / running_total[..., None]
    log_total = running_top + jnp.log(running_total)
    mixer_heads = jnp.concatenate(
        [
            attended.reshape(span_rows, group_query).astype(jnp.bfloat16),
            mamba_out.reshape(span_rows, group_inner).astype(jnp.bfloat16),
        ],
        axis=1,
    )
    mixed = jnp.dot(mixer_heads, weights_out, preferred_element_type=jnp.float32)
    hidden_one = tokens + scatter_heads(mixed.reshape(head_count, row_count, -1))
    inverse_two = lax.rsqrt(jnp.mean(hidden_one * hidden_one, axis=-1, keepdims=True) + epsilon)
    normed_two = jnp.concatenate(
        gather_heads(ring_features((hidden_one * inverse_two * second_gain).astype(jnp.bfloat16))),
        axis=0,
    )
    gate_up = jnp.dot(normed_two, weights_ffn, preferred_element_type=jnp.float32)
    group_units = FF // head_count
    gate_part = gate_up[:, :group_units]
    up_part = gate_up[:, group_units:]
    activated = (jax.nn.silu(gate_part) * up_part).astype(jnp.bfloat16)
    downed = jnp.dot(activated, weights_down, preferred_element_type=jnp.float32)
    block_output = hidden_one + scatter_heads(downed.reshape(head_count, row_count, -1))
    cotangent = out_cotangent[0]
    span_cotangent = jnp.concatenate(gather_heads(cotangent), axis=0)
    grad_down = scatter_blocks(outer_grad(activated, span_cotangent).astype(jnp.bfloat16)).astype(
        jnp.float32
    )
    grad_activated = times_transposed(span_cotangent, weights_down)
    sigmoid_gate = jax.nn.sigmoid(gate_part)
    grad_gate_up = jnp.concatenate(
        [
            grad_activated * up_part * sigmoid_gate * (1.0 + gate_part * (1.0 - sigmoid_gate)),
            grad_activated * jax.nn.silu(gate_part),
        ],
        axis=1,
    ).astype(jnp.bfloat16)
    grad_ffn = scatter_blocks(outer_grad(normed_two, grad_gate_up).astype(jnp.bfloat16))
    grad_ffn = unpack_ffn(swap_groups(grad_ffn.reshape(head_count, -1, 2 * group_units))).astype(
        jnp.float32
    )
    grad_normed_two = plain_features(
        scatter_heads(
            times_transposed(grad_gate_up, weights_ffn).reshape(head_count, row_count, -1)
        )
    )
    grad_hidden = cotangent.astype(jnp.float32) + norm_back(
        hidden_one, inverse_two, second_gain, grad_normed_two
    )
    grad_second = jnp.sum(grad_normed_two * hidden_one * inverse_two, axis=0)
    span_grad_hidden = jnp.concatenate(gather_heads(grad_hidden.astype(jnp.bfloat16)), axis=0)
    grad_mix_weight = lax.ppermute(
        scatter_blocks(outer_grad(mixer_heads, span_grad_hidden).astype(jnp.bfloat16)),
        ("head", "blk"),
        [(there, here) for here, there in out_pairs],
    ).astype(jnp.float32)
    grad_heads = times_transposed(span_grad_hidden, weights_out).astype(jnp.bfloat16)
    grad_attended = grad_heads[:, :group_query].reshape(span_rows, query_group, HD)
    grad_attended_float = grad_attended.astype(jnp.float32)
    grad_mamba = grad_heads[:, group_query:].astype(jnp.float32).reshape(span_rows, mamba_group, MP)
    row_delta = jnp.sum(grad_attended_float * attended, axis=-1)

    def grad_block(pair_items, key_block, key_start):
        grad_query, grad_keys_all = pair_items
        keys_float = key_block[:, :HD].astype(jnp.float32)
        scores = (
            jnp.einsum(
                "tqd,sd->tqs", query_local, key_block[:, :HD], preferred_element_type=jnp.float32
            )
            * score_scale
        )
        visible = visible_mask(key_start, key_block.shape[0])[:, None, :]
        probabilities = jnp.where(
            visible, jnp.exp(jnp.where(visible, scores, 0.0) - log_total[..., None]), 0.0
        )
        grad_probs = jnp.einsum(
            "tqd,sd->tqs", grad_attended, key_block[:, HD:], preferred_element_type=jnp.float32
        )
        grad_scores = probabilities * (grad_probs - row_delta[..., None])
        grad_query = grad_query + score_scale * jnp.einsum(
            "tqs,sd->tqd", grad_scores, keys_float, precision=precise
        )
        grad_key = score_scale * jnp.einsum(
            "tqs,tqd->sd", grad_scores, query_float, precision=precise
        )
        grad_value = jnp.einsum(
            "tqs,tqd->sd", probabilities, grad_attended_float, precision=precise
        )
        current = lax.dynamic_slice_in_dim(grad_keys_all, key_start, key_block.shape[0], 0)
        grad_keys_all = lax.dynamic_update_slice_in_dim(
            grad_keys_all, current + jnp.concatenate([grad_key, grad_value], axis=1), key_start, 0
        )
        return (grad_query, grad_keys_all)

    initial_back = (
        jnp.zeros((span_rows, query_group, HD), jnp.float32),
        jnp.zeros((blocks * span_rows, 2 * HD), jnp.float32),
    )
    grad_query_all, grad_keys_all = make_piece(grad_block)(
        initial_back, lax.all_gather(kv_local, "blk", axis=0, tiled=True), jnp.int32(0)
    )
    grad_keys_own = lax.psum_scatter(
        grad_keys_all.astype(jnp.bfloat16), "blk", scatter_dimension=0, tiled=True
    )
    out_grads = output_back(grad_mamba)
    (
        grad_inner_b,
        grad_into_b,
        grad_outof,
        grad_step_b,
        grad_cum_b,
        grad_gate,
        grad_skip,
        grad_state_in,
    ) = out_grads
    suffix = carried_in(
        (span_factor, grad_state_in),
        "blk",
        combine_grads,
        (jnp.ones_like(span_factor), jnp.zeros_like(grad_state_in)),
    )
    later_grad = suffix[1]
    grad_factor = jnp.sum(later_grad * state_in, axis=(1, 2))
    grad_inner_a, grad_into_a, grad_step_a, grad_cum_a = state_back((later_grad, grad_factor))
    prep_grads = prepare_back(
        (
            grad_inner_a + grad_inner_b,
            grad_into_a + grad_into_b,
            grad_outof,
            grad_step_a + grad_step_b,
            grad_cum_a + grad_cum_b,
        )
    )
    grad_extended, grad_taps, grad_shift, grad_raw, grad_step_shift, grad_rate = prep_grads
    rim_back = passed_along(grad_extended[: KW - 1], "blk", -1)
    conv_grad = grad_extended[KW - 1 :] + jnp.pad(rim_back, ((span_rows - (KW - 1), 0), (0, 0)))
    keys_mine = jnp.where(even, grad_keys_own[:, :HD], grad_keys_own[:, HD:])
    keys_other = jnp.where(even, grad_keys_own[:, HD:], grad_keys_own[:, :HD])
    grad_kv = keys_mine.astype(jnp.float32) + from_head(keys_other, 1).astype(jnp.float32)
    grad_kv = jnp.where(
        even, rotate(grad_kv.reshape(span_rows, 1, HD), positions, -1.0)[:, 0], grad_kv
    )
    grad_query_seq = rotate(
        grad_query_all.astype(jnp.bfloat16).astype(jnp.float32), positions, -1.0
    ).reshape(span_rows, group_query)
    grad_bc = conv_grad[:, group_inner:].astype(jnp.bfloat16).astype(jnp.float32)
    grad_bc = scatter_heads(
        jnp.stack(jnp.split(grad_bc, head_count, axis=1))
    )
    grad_projected = jnp.concatenate(
        [
            grad_query_seq,
            grad_kv,
            grad_gate.reshape(span_rows, group_inner),
            conv_grad[:, :group_inner],
            grad_bc,
            grad_raw,
            jnp.zeros((span_rows, step_pad - mamba_group), jnp.float32),
        ],
        axis=1,
    ).astype(jnp.bfloat16)
    grad_proj_weight = scatter_blocks(outer_grad(normed_one, grad_projected).astype(jnp.bfloat16))
    grad_proj_weight = unpack_in(
        swap_groups(grad_proj_weight.reshape(head_count, -1, grad_projected.shape[1]))
    ).astype(jnp.float32)
    grad_normed_one = plain_features(
        scatter_heads(
            times_transposed(grad_projected, weights_in).reshape(head_count, row_count, -1)
        )
    )
    grad_input = (grad_hidden + norm_back(tokens, inverse_one, first_gain, grad_normed_one)).astype(
        jnp.bfloat16
    )
    grad_first = jnp.sum(grad_normed_one * tokens * inverse_one, axis=0)
    grad_conv_weight = jnp.concatenate(
        [
            lax.dynamic_update_slice_in_dim(
                jnp.zeros((KW, mamba_width), jnp.float32),
                grad_taps[:, :group_inner],
                head_index * group_inner,
                1,
            ),
            grad_taps[:, group_inner:],
        ],
        axis=1,
    )
    grad_conv_bias = jnp.concatenate(
        [
            lax.dynamic_update_slice_in_dim(
                jnp.zeros((mamba_width,), jnp.float32),
                grad_shift[:group_inner],
                head_index * group_inner,
                0,
            ),
            grad_shift[group_inner:],
        ]
    )
    grad_step_bias = lax.dynamic_update_slice_in_dim(
        jnp.zeros((MH,), jnp.float32), grad_step_shift, head_index * mamba_group, 0
    )
    grad_decay = lax.dynamic_update_slice_in_dim(
        jnp.zeros((MH,), jnp.float32), grad_rate, head_index * mamba_group, 0
    )
    grad_skip_full = lax.dynamic_update_slice_in_dim(
        jnp.zeros((MH,), jnp.float32), grad_skip, head_index * mamba_group, 0
    )
    summed_small = lax.psum(
        (
            grad_first,
            grad_second,
            grad_conv_weight,
            grad_conv_bias,
            grad_step_bias,
            grad_decay,
            grad_skip_full,
        ),
        ("head", "blk"),
    )
    return (
        block_output.astype(jnp.bfloat16)[None],
        grad_input[None],
        grad_proj_weight,
        grad_mix_weight,
        grad_ffn,
        grad_down,
        summed_small[0],
        summed_small[1],
        summed_small[2],
        summed_small[3],
        summed_small[4],
        summed_small[5],
        summed_small[6],
    )


def solution(mesh):
    placed = (
        P("blk", "head", None),
        P("blk", "head", None),
        P("blk", None),
        P(("head", "blk"), None),
        P(("head", "blk"), None),
        P(("head", "blk"), None),
        P(("head", "blk"), None),
        P(),
        P(),
        P(),
        P(),
        P(),
        P(),
        P(),
    )
    return jax.shard_map(
        per_device,
        mesh=mesh,
        in_specs=placed,
        out_specs=(
            P("blk", "head", None),
            P("blk", "head", None),
            P(("head", "blk"), None),
            P(("head", "blk"), None),
            P(("head", "blk"), None),
            P(("head", "blk"), None),
            P(),
            P(),
            P(),
            P(),
            P(),
            P(),
            P(),
        ),
        check_vma=False,
    )
```

```python
import math
from functools import partial

import jax
import jax.numpy as jnp
from jax import lax
from jax.experimental import pallas as pl
from jax.experimental.pallas import tpu as pltpu
from jax.sharding import PartitionSpec as P

QH = 8
KVH = 2
HD = 128
MH = 48
MP = 64
NS = 256
FF = 4096
KW = 4


epsilon = 1e-05
rope_base = 100000000000.0
masked_score = -1e30


def passed_along(shard, axis, by):
    peers = lax.axis_size(axis)
    pairs = [(i, i + by) for i in range(peers) if 0 <= i + by < peers]
    return lax.ppermute(shard, axis, pairs)


def ring_of(axis):
    peers = lax.axis_size(axis)
    if peers != 8:
        return list(range(peers))
    return [0, 2, 4, 6, 7, 5, 3, 1]


def gather_blocks(shard):
    return lax.all_gather(
        shard, "blk", axis=0, tiled=True, axis_index_groups=[ring_of("blk")]
    )


def scatter_blocks(partial_sums):
    return lax.psum_scatter(
        partial_sums,
        "blk",
        scatter_dimension=0,
        tiled=True,
        axis_index_groups=[ring_of("blk")],
    )


def from_head(shard, distance):
    peers = lax.axis_size("head")
    return lax.ppermute(shard, "head", [(i, i ^ distance) for i in range(peers)])


def by_distance(parts):
    mine = lax.axis_index("head")
    stacked = jnp.stack(parts)
    return [
        lax.dynamic_index_in_dim(stacked, jnp.bitwise_xor(mine, j), 0, False)
        for j in range(len(parts))
    ]


def gather_heads(shard):
    across = from_head(shard, 2)
    beside = from_head(jnp.stack([shard, across]), 1)
    return by_distance([shard, beside[0], across, beside[1]])


def scatter_heads(chunks):
    mine = lax.axis_index("head")

    def chunk(distance):
        return lax.dynamic_index_in_dim(chunks, jnp.bitwise_xor(mine, distance), 0, False)

    got = from_head(jnp.stack([chunk(1), chunk(3)]), 1)
    near = chunk(0) + got[0]
    far = (chunk(2) + got[1]).astype(jnp.bfloat16)
    return near + from_head(far, 2).astype(jnp.float32)


def ring_features(values_in):
    heads, ring = lax.axis_size("head"), ring_of("blk")
    rows, width = values_in.shape
    cut = values_in.reshape(rows, heads, len(ring), width // (heads * len(ring)))
    return jnp.concatenate([cut[:, :, k, :].reshape(rows, -1) for k in ring], axis=1)


def plain_features(values_in):
    heads, ring = lax.axis_size("head"), ring_of("blk")
    rows, width = values_in.shape
    cut = values_in.reshape(rows, len(ring), heads, width // (heads * len(ring)))
    places = [ring.index(k) for k in range(len(ring))]
    return jnp.concatenate(
        [cut[:, places[k], j, :] for j in range(heads) for k in range(len(ring))], axis=1
    )


def mixer_place():
    heads, ring = lax.axis_size("head"), ring_of("blk")
    peers = heads * len(ring)
    rows = (QH * HD + MH * MP) // peers
    query_blocks, mamba_blocks = QH * HD // rows // heads, MH * MP // rows // heads
    pairs = []
    for r in range(peers):
        if r < query_blocks * heads:
            group, slot = divmod(r, query_blocks)
        else:
            group, slot = divmod(r - query_blocks * heads, mamba_blocks)
            slot += query_blocks
        pairs.append((r, group * len(ring) + ring[slot]))
    return pairs


def column_cuts():
    query_end = QH * HD
    z_begin = query_end + 2 * KVH * HD
    x_begin = z_begin + MH * MP
    b_begin = x_begin + MH * MP
    dt_begin = b_begin + 2 * NS
    heads = lax.axis_size("head")
    cuts = []
    for j in range(heads):
        kind, kv_head = j % 2, j // 2
        kv_begin = query_end + kind * KVH * HD + kv_head * HD
        cuts.append(
            [
                (x_begin + j * MH * MP // heads, MH * MP // heads),
                (b_begin + j * 2 * NS // heads, 2 * NS // heads),
                (dt_begin + j * MH // heads, MH // heads),
                (0, MH // heads - step_pad),
                (j * QH * HD // heads, QH * HD // heads),
                (kv_begin, HD),
                (z_begin + j * MH * MP // heads, MH * MP // heads),
            ]
        )
    return cuts


step_pad = 128


def pack_in(weight):
    groups = []
    for cuts in column_cuts():
        pieces = [
            weight[:, begin : begin + size]
            if size > 0
            else jnp.zeros((weight.shape[0], -size), weight.dtype)
            for begin, size in cuts
        ]
        groups.append(jnp.concatenate(pieces, axis=1))
    return jnp.stack(groups)


def unpack_in(groups):
    pieces = []
    for j, cuts in enumerate(column_cuts()):
        at = 0
        for begin, size in cuts:
            if size > 0:
                pieces.append((begin, groups[j][:, at : at + size]))
            at += abs(size)
    pieces.sort(key=lambda item: item[0])
    return jnp.concatenate([piece for _, piece in pieces], axis=1)


def pack_ffn(weight):
    heads, ring = lax.axis_size("head"), ring_of("blk")
    unit = FF // (heads * len(ring))
    cut = weight.reshape(weight.shape[0], 2, heads, len(ring), unit)
    return jnp.stack(
        [
            jnp.concatenate([cut[:, half, j, k] for half in range(2) for k in ring], axis=1)
            for j in range(heads)
        ]
    )


def unpack_ffn(groups):
    heads, ring = lax.axis_size("head"), ring_of("blk")
    rows = groups.shape[1]
    cut = groups.reshape(heads, rows, 2, len(ring), FF // (heads * len(ring)))
    return jnp.concatenate(
        [
            cut[j, :, half, ring.index(k)]
            for half in range(2)
            for j in range(heads)
            for k in range(len(ring))
        ],
        axis=1,
    )


def swap_groups(groups):
    return lax.all_to_all(groups, "head", split_axis=0, concat_axis=0, tiled=True)


def outer_grad(left_side, grad_side):
    return lax.dot_general(
        left_side, grad_side, (((0,), (0,)), ((), ())), preferred_element_type=jnp.float32
    )


def times_transposed(grad_side, weight):
    return lax.dot_general(
        grad_side, weight, (((1,), (1,)), ((), ())), preferred_element_type=jnp.float32
    )


def rotate(values_in, positions, direction):
    half_width = values_in.shape[-1] // 2
    frequencies = rope_base ** (
        -jnp.arange(half_width, dtype=jnp.float32) * 2.0 / values_in.shape[-1]
    )
    angles = positions.astype(jnp.float32)[:, None] * frequencies[None, :]
    cosine = jnp.cos(angles)[:, None, :]
    sine_part = direction * jnp.sin(angles)[:, None, :]
    first_half = values_in[..., :half_width]
    second_half = values_in[..., half_width:]
    return jnp.concatenate(
        [
            first_half * cosine - second_half * sine_part,
            second_half * cosine + first_half * sine_part,
        ],
        axis=-1,
    )


def norm_back(values_in, inverse, gain_vector, grad_side):
    scaled = grad_side * gain_vector
    mean_term = jnp.mean(scaled * values_in, axis=-1, keepdims=True)
    return inverse * scaled - values_in * inverse**3 * mean_term


chunk = 128
lanes = 128
low = jnp.bfloat16
exact = lax.Precision.HIGHEST


def dot_nn(a, b, precision=None):
    return lax.dot_general(
        a, b, (((1,), (0,)), ((), ())), precision=precision, preferred_element_type=jnp.float32
    )


def dot_nt(a, b):
    return lax.dot_general(a, b, (((1,), (1,)), ((), ())), preferred_element_type=jnp.float32)


def dot_tn(a, b):
    return lax.dot_general(a, b, (((0,), (0,)), ((), ())), preferred_element_type=jnp.float32)


def iota(shape, dim):
    return lax.broadcasted_iota(jnp.int32, shape, dim)


def spread(per_head, pair):
    rows = per_head.shape[0]
    first = per_head[:, 2 * pair : 2 * pair + 1]
    second = per_head[:, 2 * pair + 1 : 2 * pair + 2]
    return jnp.where(iota((rows, lanes), 1) < MP, first, second)


def head_sums(products, pair):
    mine = 2 * pair + (iota((lanes, lanes), 0) >= MP).astype(jnp.int32)
    ones = (mine == iota((lanes, lanes), 1)).astype(jnp.float32)
    return dot_nn(products, ones, exact)


def chunk_terms(decay, segment, segment_before):
    lower = iota((chunk, chunk), 0) >= iota((chunk, chunk), 1)
    cumulative = dot_nn(lower.astype(jnp.float32), decay, exact)
    total = cumulative[chunk - 1 :, :]
    segment_end = segment[chunk - 1 :, :]
    related = lower & (segment == segment.T)
    entering = jnp.where(segment == segment_before, jnp.exp(cumulative), 0.0)
    ending = jnp.where(segment == segment_end, jnp.exp(total - cumulative), 0.0)
    whole = jnp.where(segment_end == segment_before, jnp.exp(total), 0.0)
    return cumulative, cumulative.T, related, entering, ending, whole, total, segment_end


def decays_of(cumulative, transposed, related, head):
    apart = cumulative[:, head : head + 1] - transposed[head : head + 1, :]
    return jnp.exp(jnp.where(related, apart, masked_score))


def row_factor(whole, pair, width):
    first = whole[:, 2 * pair : 2 * pair + 1]
    second = whole[:, 2 * pair + 1 : 2 * pair + 2]
    return jnp.where(iota((lanes, width), 0) < MP, first, second)


def chunk_rows(index):
    return pl.ds(pl.multiple_of(index * chunk, chunk), chunk)


def ssd_local(x_ref, b_ref, c_ref, step_ref, decay_ref, seg_ref, y_ref, state_ref, enter_ref, fac_ref):
    pairs = x_ref.shape[1] // lanes
    state_ref[...] = jnp.zeros_like(state_ref)

    def body(index, carry):
        segment_before, base = carry
        rows = chunk_rows(index)
        segment = seg_ref[rows, :]
        cumulative, transposed, related, entering, ending, whole, total, segment_end = chunk_terms(
            decay_ref[rows, :], segment, segment_before
        )
        enter_ref[rows, :] = jnp.where(segment == 0.0, jnp.exp(base + cumulative), 0.0)
        into = b_ref[rows, :].astype(low)
        outof = c_ref[rows, :].astype(low)
        step = step_ref[rows, :]
        scores = dot_nt(outof, into)
        left = iota((chunk, lanes), 1) < MP
        for pair in range(pairs):
            cols = slice(pair * lanes, (pair + 1) * lanes)
            taken = x_ref[rows, cols] * spread(step, pair)
            taken_low = taken.astype(low)
            parts = []
            for head in (2 * pair, 2 * pair + 1):
                weights = decays_of(cumulative, transposed, related, head) * scores
                parts.append(dot_nn(weights.astype(low), taken_low))
            state = state_ref[cols, :]
            y_ref[rows, cols] = jnp.where(left, parts[0], parts[1]) + spread(
                entering, pair
            ) * dot_nt(outof, state.astype(low))
            kept = (taken * spread(ending, pair)).astype(low)
            state_ref[cols, :] = row_factor(whole, pair, state.shape[1]) * state + dot_tn(
                kept, into
            )
        return segment_end, base + total

    start = jnp.zeros((1, lanes), jnp.float32)
    segment_end, base = lax.fori_loop(0, x_ref.shape[0] // chunk, body, (start, start))
    fac_ref[...] = jnp.broadcast_to(
        jnp.where(segment_end == 0.0, jnp.exp(base), 0.0), fac_ref.shape
    )


def ssd_finish(y_ref, enter_ref, c_ref, state_ref, x_ref, z_ref, skip_ref, ssd_ref, out_ref):
    pairs = x_ref.shape[1] // lanes

    def body(index, carry):
        rows = chunk_rows(index)
        outof = c_ref[rows, :].astype(low)
        entering = enter_ref[rows, :]
        for pair in range(pairs):
            cols = slice(pair * lanes, (pair + 1) * lanes)
            ssd = y_ref[rows, cols] + spread(entering, pair) * dot_nt(outof, state_ref[cols, :])
            ssd_ref[rows, cols] = ssd
            gate = z_ref[rows, cols].astype(jnp.float32)
            total = ssd + skip_ref[:, cols] * x_ref[rows, cols]
            out_ref[rows, cols] = (total * gate / (1.0 + jnp.exp(-gate))).astype(low)
        return carry

    lax.fori_loop(0, x_ref.shape[0] // chunk, body, 0)


def ssd_gate_back(
    grad_ref, z_ref, ssd_ref, x_ref, skip_ref, enter_ref, c_ref, dy_ref, dz_ref, dstate_ref, dskip_ref
):
    pairs = x_ref.shape[1] // lanes
    dstate_ref[...] = jnp.zeros_like(dstate_ref)
    dskip_ref[...] = jnp.zeros_like(dskip_ref)

    def body(index, carry):
        rows = chunk_rows(index)
        outof = c_ref[rows, :].astype(low)
        entering = enter_ref[rows, :]
        for pair in range(pairs):
            cols = slice(pair * lanes, (pair + 1) * lanes)
            gate = z_ref[rows, cols].astype(jnp.float32)
            sigmoid = 1.0 / (1.0 + jnp.exp(-gate))
            grad = grad_ref[rows, cols].astype(jnp.float32)
            x = x_ref[rows, cols]
            total = ssd_ref[rows, cols] + skip_ref[:, cols] * x
            dz_ref[rows, cols] = (
                grad * total * sigmoid * (1.0 + gate * (1.0 - sigmoid))
            ).astype(low)
            dy = grad * gate * sigmoid
            dy_ref[rows, cols] = dy
            dskip_ref[:, cols] += jnp.broadcast_to(
                jnp.sum(dy * x, axis=0, keepdims=True), (dskip_ref.shape[0], lanes)
            )
            dstate_ref[cols, :] += dot_tn((dy * spread(entering, pair)).astype(low), outof)
        return carry

    lax.fori_loop(0, x_ref.shape[0] // chunk, body, 0)


def ssd_back(
    x_ref, b_ref, c_ref, step_ref, decay_ref, seg_ref, dy_ref, ssd_ref, skip_ref, state_ref, later_ref,
    dx_ref, db_ref, dc_ref, dstep_ref, ddecay_ref, states, grads,
):
    pairs = x_ref.shape[1] // lanes
    chunks = x_ref.shape[0] // chunk
    zero_row = jnp.zeros((1, lanes), jnp.float32)

    def before(index):
        rows = pl.ds(pl.multiple_of(jnp.maximum(index - 1, 0) * chunk, chunk), chunk)
        return jnp.where(index == 0, 0.0, seg_ref[rows, :][chunk - 1 :, :])

    states[0] = state_ref[...].astype(jnp.float32)

    def forward(index, carry):
        rows = chunk_rows(index)
        _, _, _, _, ending, whole, _, _ = chunk_terms(
            decay_ref[rows, :], seg_ref[rows, :], before(index)
        )
        into = b_ref[rows, :].astype(low)
        step = step_ref[rows, :]
        for pair in range(pairs):
            cols = slice(pair * lanes, (pair + 1) * lanes)
            kept = (x_ref[rows, cols] * spread(step, pair) * spread(ending, pair)).astype(low)
            state = states[index, cols, :]
            states[index + 1, cols, :] = row_factor(
                whole, pair, state.shape[1]
            ) * state + dot_tn(kept, into)
        return carry

    lax.fori_loop(0, chunks, forward, 0)
    grads[...] = later_ref[...].astype(jnp.float32)
    last = jnp.zeros((8, lanes), jnp.float32)
    for pair in range(pairs):
        cols = slice(pair * lanes, (pair + 1) * lanes)
        product = grads[cols, :] * states[chunks, cols, :]
        along = lax.dot_general(
            jnp.ones((8, product.shape[1]), jnp.float32),
            product,
            (((1,), (1,)), ((), ())),
            precision=exact,
            preferred_element_type=jnp.float32,
        )
        last = last + head_sums(along, pair)

    def backward(at, carry):
        index = chunks - 1 - at
        rows = chunk_rows(index)
        cumulative, transposed, related, entering, ending, whole, _, _ = chunk_terms(
            decay_ref[rows, :], seg_ref[rows, :], before(index)
        )
        into = b_ref[rows, :].astype(low)
        outof = c_ref[rows, :].astype(low)
        step = step_ref[rows, :]
        scores = dot_nt(outof, into)
        left = iota((chunk, lanes), 1) < MP
        grad_scores = jnp.zeros((chunk, chunk), jnp.float32)
        grad_into = jnp.zeros((chunk, b_ref.shape[1]), jnp.float32)
        grad_outof = jnp.zeros((chunk, b_ref.shape[1]), jnp.float32)
        grad_cum = jnp.zeros((chunk, lanes), jnp.float32)
        grad_step = jnp.zeros((chunk, lanes), jnp.float32)
        for pair in range(pairs):
            cols = slice(pair * lanes, (pair + 1) * lanes)
            x = x_ref[rows, cols]
            step_pair = spread(step, pair)
            taken = x * step_pair
            taken_low = taken.astype(low)
            dy = dy_ref[rows, cols]
            dy_low = dy.astype(low)
            parts = []
            for half, head in enumerate((2 * pair, 2 * pair + 1)):
                decays = decays_of(cumulative, transposed, related, head)
                parts.append(dot_tn((decays * scores).astype(low), dy_low))
                own = jnp.where(left if half == 0 else ~left, dy_low, jnp.zeros_like(dy_low))
                grad_scores = grad_scores + decays * dot_nt(own, taken_low)
            later = grads[cols, :]
            later_low = later.astype(low)
            ending_pair = spread(ending, pair)
            grad_taken = jnp.where(left, parts[0], parts[1]) + ending_pair * dot_nt(
                into, later_low
            )
            grad_into = grad_into + dot_nn((taken * ending_pair).astype(low), later_low)
            dy_enter = (dy * spread(entering, pair)).astype(low)
            grad_outof = grad_outof + dot_nn(dy_enter, states[index, cols, :].astype(low))
            grads[cols, :] = row_factor(whole, pair, later.shape[1]) * later + dot_tn(
                dy_enter, outof
            )
            grad_cum = grad_cum + head_sums(dy * ssd_ref[rows, cols] - taken * grad_taken, pair)
            grad_step = grad_step + head_sums(x * grad_taken, pair)
            dx_ref[rows, cols] = step_pair * grad_taken + skip_ref[:, cols] * dy
        grad_scores_low = grad_scores.astype(low)
        db_ref[rows, :] = grad_into + dot_tn(grad_scores_low, outof)
        dc_ref[rows, :] = grad_outof + dot_nn(grad_scores_low, into)
        dstep_ref[rows, :] = grad_step
        upper = (iota((chunk, chunk), 0) <= iota((chunk, chunk), 1)).astype(jnp.float32)
        ddecay_ref[rows, :] = dot_nn(upper, grad_cum, exact) + carry
        return carry + jnp.sum(grad_cum, axis=0, keepdims=True)

    lax.fori_loop(0, chunks, backward, last[:1, :] + zero_row)


def attend(place_ref, q_ref, first_ref, k_ref, v_ref, out_ref, lse_ref, top, total, summed):
    away = pl.program_id(0)
    mine, earliest, latest = place_ref[0], place_ref[1], place_ref[2]
    span = q_ref.shape[0]
    heads = q_ref.shape[1] // HD
    key_start = (mine - away) * span

    @pl.when(away == 0)
    def _():
        top[...] = jnp.full_like(top, masked_score)
        total[...] = jnp.zeros_like(total)
        summed[...] = jnp.zeros_like(summed)

    def one(masked):
        keys = k_ref[0]
        values = v_ref[0]
        if masked:
            key_pos = key_start + iota((span, span), 1)
            query_pos = mine * span + iota((span, span), 0)
            visible = (key_pos <= query_pos) & (key_pos >= first_ref[:, :1])
        for head in range(heads):
            cols = slice(head * HD, (head + 1) * HD)
            scores = dot_nt(q_ref[:, cols], keys) * HD**-0.5
            if masked:
                scores = jnp.where(visible, scores, masked_score)
            old_top = top[head][:, :1]
            new_top = jnp.maximum(old_top, jnp.max(scores, axis=1, keepdims=True))
            weights = jnp.exp(scores - new_top)
            scale = jnp.exp(old_top - new_top)
            total[head] = total[head] * scale + jnp.sum(weights, axis=1, keepdims=True)
            top[head] = jnp.broadcast_to(new_top, (span, lanes))
            summed[head] = summed[head] * scale + dot_nn(weights.astype(low), values)

    needed = (away <= mine) & (key_start + span > earliest)
    plain = (away > 0) & (key_start >= latest)
    pl.when(needed & plain)(lambda: one(False))
    pl.when(needed & jnp.logical_not(plain))(lambda: one(True))

    @pl.when(away == pl.num_programs(0) - 1)
    def _():
        for head in range(heads):
            cols = slice(head * HD, (head + 1) * HD)
            out_ref[:, cols] = summed[head] / total[head]
            lse_ref[head] = top[head] + jnp.log(total[head])


def attend_back(
    place_ref, q_ref, first_ref, k_ref, v_ref, grad_ref, out_ref, lse_ref, dq_ref, dk_ref, dv_ref
):
    away = pl.program_id(0)
    mine, earliest, latest = place_ref[0], place_ref[1], place_ref[2]
    span = q_ref.shape[0]
    heads = q_ref.shape[1] // HD
    key_start = (mine - away) * span

    @pl.when(away == 0)
    def _():
        dq_ref[...] = jnp.zeros_like(dq_ref)

    def one(masked):
        keys = k_ref[0]
        values = v_ref[0]
        if masked:
            key_pos = key_start + iota((span, span), 1)
            query_pos = mine * span + iota((span, span), 0)
            visible = (key_pos <= query_pos) & (key_pos >= first_ref[:, :1])
        grad_keys = jnp.zeros(keys.shape, jnp.float32)
        grad_values = jnp.zeros(keys.shape, jnp.float32)
        for head in range(heads):
            cols = slice(head * HD, (head + 1) * HD)
            query = q_ref[:, cols]
            grad = grad_ref[:, cols]
            delta = jnp.sum(
                grad.astype(jnp.float32) * out_ref[:, cols], axis=1, keepdims=True
            )
            scores = dot_nt(query, keys) * HD**-0.5
            if masked:
                scores = jnp.where(visible, scores, masked_score)
            weights = jnp.exp(scores - lse_ref[head][:, :1])
            changes = weights * (dot_nt(grad, values) - delta)
            weights_low = weights.astype(low)
            changes_low = (changes * HD**-0.5).astype(low)
            grad_values = grad_values + dot_tn(weights_low, grad)
            grad_keys = grad_keys + dot_tn(changes_low, query)
            dq_ref[:, cols] += dot_nn(changes_low, keys)
        dk_ref[0] = grad_keys.astype(low)
        dv_ref[0] = grad_values.astype(low)

    needed = (away <= mine) & (key_start + span > earliest)
    plain = (away > 0) & (key_start >= latest)
    pl.when(needed & plain)(lambda: one(False))
    pl.when(needed & jnp.logical_not(plain))(lambda: one(True))

    @pl.when(jnp.logical_not(needed))
    def _():
        dk_ref[...] = jnp.zeros_like(dk_ref)
        dv_ref[...] = jnp.zeros_like(dv_ref)


def shaped(shape, kind):
    return jax.ShapeDtypeStruct(shape, kind)


def whole_call(kernel, outputs, scratch, flops, *operands):
    sizes = sum(math.prod(a.shape) * a.dtype.itemsize for a in (*operands, *outputs))
    return pl.pallas_call(
        kernel,
        out_shape=outputs,
        in_specs=[pl.BlockSpec(memory_space=pltpu.VMEM)] * len(operands),
        out_specs=[pl.BlockSpec(memory_space=pltpu.VMEM)] * len(outputs),
        scratch_shapes=scratch,
        compiler_params=pltpu.CompilerParams(vmem_limit_bytes=kernel_memory),
        cost_estimate=pl.CostEstimate(flops=flops, bytes_accessed=sizes, transcendentals=0),
    )(*operands)


kernel_memory = 44 * 1024 * 1024


def attention(place, query, first_visible, keys, values):
    away, span = keys.shape[0], query.shape[0]
    heads = query.shape[1] // HD
    same = lambda d, place: (0, 0)
    block = lambda d, place: (d, 0, 0)
    return pl.pallas_call(
        attend,
        grid_spec=pltpu.PrefetchScalarGridSpec(
            num_scalar_prefetch=1,
            grid=(away,),
            in_specs=[
                pl.BlockSpec(query.shape, same),
                pl.BlockSpec(first_visible.shape, same),
                pl.BlockSpec((1, span, HD), block),
                pl.BlockSpec((1, span, HD), block),
            ],
            out_specs=[
                pl.BlockSpec(query.shape, same),
                pl.BlockSpec((heads, span, lanes), lambda d, place: (0, 0, 0)),
            ],
            scratch_shapes=[
                pltpu.VMEM((heads, span, lanes), jnp.float32),
                pltpu.VMEM((heads, span, lanes), jnp.float32),
                pltpu.VMEM((heads, span, HD), jnp.float32),
            ],
        ),
        out_shape=[
            shaped(query.shape, jnp.float32),
            shaped((heads, span, lanes), jnp.float32),
        ],
        compiler_params=pltpu.CompilerParams(vmem_limit_bytes=kernel_memory),
        cost_estimate=pl.CostEstimate(
            flops=20 * 10**9, bytes_accessed=4 * 10**6, transcendentals=0
        ),
    )(place, query, first_visible, keys, values)


def attention_back(place, query, first_visible, keys, values, grad, out, lse):
    away, span = keys.shape[0], query.shape[0]
    same = lambda d, place: (0, 0)
    block = lambda d, place: (d, 0, 0)
    return pl.pallas_call(
        attend_back,
        grid_spec=pltpu.PrefetchScalarGridSpec(
            num_scalar_prefetch=1,
            grid=(away,),
            in_specs=[
                pl.BlockSpec(query.shape, same),
                pl.BlockSpec(first_visible.shape, same),
                pl.BlockSpec((1, span, HD), block),
                pl.BlockSpec((1, span, HD), block),
                pl.BlockSpec(query.shape, same),
                pl.BlockSpec(query.shape, same),
                pl.BlockSpec(lse.shape, lambda d, place: (0, 0, 0)),
            ],
            out_specs=[
                pl.BlockSpec(query.shape, same),
                pl.BlockSpec((1, span, HD), block),
                pl.BlockSpec((1, span, HD), block),
            ],
        ),
        out_shape=[
            shaped(query.shape, jnp.float32),
            shaped(keys.shape, low),
            shaped(keys.shape, low),
        ],
        compiler_params=pltpu.CompilerParams(vmem_limit_bytes=kernel_memory),
        cost_estimate=pl.CostEstimate(
            flops=30 * 10**9, bytes_accessed=4 * 10**6, transcendentals=0
        ),
    )(place, query, first_visible, keys, values, grad, out, lse)


def conv_act(extended, conv_taps, conv_shift, keep_masks):
    length = keep_masks[0].shape[0]
    result = conv_shift + conv_taps[0] * extended[KW - 1 :]
    for lag_index in range(1, KW):
        begin = KW - 1 - lag_index
        result = (
            result
            + conv_taps[lag_index]
            * keep_masks[lag_index][:, None]
            * extended[begin : begin + length]
        )
    return jax.nn.silu(result)


def step_and_decay(step_raw, step_shift, decay_rate):
    step_size = jax.nn.softplus(step_raw + step_shift)
    return step_size, -step_size * jnp.exp(decay_rate)


def in_lanes(per_head):
    return jnp.pad(per_head, ((0, 0), (0, lanes - per_head.shape[1])))


def chained(local, factor, backwards):
    blocks = lax.axis_size("blk")
    share = local.shape[0] // blocks
    per_row = jnp.repeat(factor, MP).reshape(blocks, 1, share)
    rough = per_row.astype(low)
    rest = (per_row - rough.astype(jnp.float32)).astype(low)
    extra = jnp.pad(
        jnp.concatenate([rough, rest], axis=1), ((0, 0), (0, 14), (0, local.shape[1] - share))
    )
    sent = jnp.concatenate([local.reshape(blocks, share, -1).astype(low), extra], axis=1)
    got = lax.all_to_all(sent, "blk", split_axis=0, concat_axis=0, tiled=True)
    parts = got[:, :share].astype(jnp.float32)
    factors = (
        got[:, share, :share].astype(jnp.float32) + got[:, share + 1, :share].astype(jnp.float32)
    )[:, :, None]
    state = jnp.zeros_like(parts[0])
    states = [None] * blocks
    for k in range(blocks - 1, -1, -1) if backwards else range(blocks):
        states[k] = state.astype(low)
        state = factors[k] * state + parts[k]
    back = lax.all_to_all(jnp.stack(states), "blk", split_axis=0, concat_axis=0, tiled=True)
    return back.reshape(local.shape)


def summed_over(values_in, axis):
    peers = lax.axis_size(axis)
    by = 1
    while by < peers:
        values_in = values_in + lax.ppermute(values_in, axis, [(i, i ^ by) for i in range(peers)])
        by *= 2
    return values_in


def per_device(
    block_input,
    out_cotangent,
    start_flags,
    in_weight,
    out_weight,
    gate_up_weight,
    down_weight,
    first_gain,
    second_gain,
    conv_weight,
    conv_bias,
    step_bias,
    decay_log,
    skip_gain,
):
    head_count = lax.axis_size("head")
    blocks = lax.axis_size("blk")
    head_index = lax.axis_index("head")
    block_index = lax.axis_index("blk")
    tokens = block_input[0].astype(jnp.float32)
    row_count = tokens.shape[0]
    span_rows = row_count * head_count
    query_group = QH // head_count
    mamba_group = MH // head_count
    mamba_width = MH * MP
    group_query = query_group * HD
    group_inner = mamba_group * MP
    even = head_index % 2 == 0
    out_pairs = mixer_place()

    flags_all = lax.all_gather(start_flags[0], "blk", axis=0, tiled=True)
    packed_in = swap_groups(pack_in(in_weight.astype(low))).reshape(
        head_count * in_weight.shape[0], -1
    )
    conv_columns = group_inner + 2 * NS // head_count + step_pad
    weights_conv = gather_blocks(packed_in[:, :conv_columns])
    weights_rest = gather_blocks(packed_in[:, conv_columns:])
    weights_out = gather_blocks(
        lax.ppermute(out_weight.astype(low), ("head", "blk"), out_pairs)
    )
    weights_ffn = gather_blocks(
        swap_groups(pack_ffn(gate_up_weight.astype(low))).reshape(
            head_count * gate_up_weight.shape[0], -1
        )
    )
    weights_down = gather_blocks(down_weight.astype(low))
    cotangent = out_cotangent[0]
    span_tokens = jnp.concatenate(gather_heads(block_input[0]), axis=0).astype(jnp.float32)
    span_cotangent = jnp.concatenate(gather_heads(cotangent), axis=0)

    positions = block_index * span_rows + jnp.arange(span_rows, dtype=jnp.int32)
    all_positions = jnp.arange(blocks * span_rows, dtype=jnp.int32)
    starts_all = lax.cummax(jnp.where(flags_all > 0, all_positions, 0), axis=0)
    first_visible = lax.dynamic_slice_in_dim(starts_all, block_index * span_rows, span_rows, 0)
    flags_before = jnp.concatenate([jnp.zeros((KW - 2,), jnp.int32), flags_all])
    flag_ext = lax.dynamic_slice_in_dim(
        flags_before, block_index * span_rows, span_rows + KW - 2, 0
    ).astype(jnp.float32)
    segment = jnp.broadcast_to(
        jnp.cumsum(start_flags[0]).astype(jnp.float32)[:, None], (span_rows, lanes)
    )
    place = jnp.stack([block_index, jnp.min(first_visible), jnp.max(first_visible)])
    first_wide = jnp.broadcast_to(first_visible[:, None], (span_rows, lanes))
    keep_masks = [jnp.ones((span_rows,), jnp.float32)]
    for lag_index in range(1, KW):
        begin = KW - 1 - lag_index
        keep_masks.append(keep_masks[-1] * (1.0 - flag_ext[begin : begin + span_rows]))
    conv_taps = jnp.concatenate(
        [
            lax.dynamic_slice_in_dim(conv_weight, head_index * group_inner, group_inner, 1),
            conv_weight[:, mamba_width:],
        ],
        axis=1,
    )
    conv_shift = jnp.concatenate(
        [
            lax.dynamic_slice_in_dim(conv_bias, head_index * group_inner, group_inner, 0),
            conv_bias[mamba_width:],
        ]
    )
    step_shift = lax.dynamic_slice_in_dim(step_bias, head_index * mamba_group, mamba_group, 0)
    decay_rate = lax.dynamic_slice_in_dim(decay_log, head_index * mamba_group, mamba_group, 0)
    skip_local = lax.dynamic_slice_in_dim(skip_gain, head_index * mamba_group, mamba_group, 0)
    skip_wide = jnp.repeat(skip_local, MP)[None, :]

    span_inverse = lax.rsqrt(jnp.mean(span_tokens * span_tokens, axis=-1, keepdims=True) + epsilon)
    normed_one = ring_features((span_tokens * span_inverse * first_gain).astype(low))
    inverse_one = lax.rsqrt(jnp.mean(tokens * tokens, axis=-1, keepdims=True) + epsilon)

    projected = jnp.dot(normed_one, weights_conv, preferred_element_type=jnp.float32)
    cut_b = group_inner
    cut_dt = cut_b + 2 * NS // head_count
    conv_local = jnp.concatenate(
        [projected[:, :cut_b].astype(low)]
        + gather_heads(projected[:, cut_b:cut_dt].astype(low)),
        axis=1,
    )
    step_local = projected[:, cut_dt : cut_dt + mamba_group].astype(low).astype(jnp.float32)
    rim_rows = passed_along(conv_local[span_rows - (KW - 1) :], "blk", 1)
    extended = jnp.concatenate([rim_rows, conv_local], axis=0).astype(jnp.float32)
    active, conv_back = jax.vjp(
        partial(conv_act, keep_masks=keep_masks), extended, conv_taps, conv_shift
    )
    (step_size, log_decay), step_back = jax.vjp(
        step_and_decay, step_local, step_shift, decay_rate
    )
    inner_act = active[:, :group_inner]
    into_act = active[:, group_inner : group_inner + NS]
    outof_act = active[:, group_inner + NS :]
    step_wide = in_lanes(step_size)
    decay_wide = in_lanes(log_decay)
    tall = shaped((span_rows, group_inner), jnp.float32)
    narrow = shaped((span_rows, lanes), jnp.float32)
    state_shape = (group_inner, NS)
    within, local_state, entering, factor = whole_call(
        ssd_local,
        [tall, shaped(state_shape, jnp.float32), narrow, shaped((8, lanes), jnp.float32)],
        [],
        6 * 10**9,
        inner_act,
        into_act,
        outof_act,
        step_wide,
        decay_wide,
        segment,
    )
    span_factor = factor[0, :mamba_group]
    state_in = chained(local_state, span_factor, False)

    cut_kv = group_query
    cut_z = cut_kv + HD
    projected_rest = jnp.dot(normed_one, weights_rest, preferred_element_type=jnp.float32)
    query_local = (
        rotate(
            projected_rest[:, :group_query].reshape(span_rows, query_group, HD), positions, 1.0
        )
        .astype(low)
        .reshape(span_rows, group_query)
    )
    kv_plain = projected_rest[:, cut_kv:cut_z]
    kv_mine = jnp.where(
        even, rotate(kv_plain.reshape(span_rows, 1, HD), positions, 1.0)[:, 0], kv_plain
    ).astype(low)
    gate_act = projected_rest[:, cut_z:].astype(low)
    kv_blocks = jnp.stack([kv_mine] + [passed_along(kv_mine, "blk", d) for d in range(1, blocks)])
    kv_beside = from_head(kv_blocks, 1)
    keys = jnp.where(even, kv_blocks, kv_beside)
    values = jnp.where(even, kv_beside, kv_blocks)
    attended, lse = attention(place, query_local, first_wide, keys, values)

    ssd, mamba_out = whole_call(
        ssd_finish,
        [tall, shaped((span_rows, group_inner), low)],
        [],
        2 * 10**9,
        within,
        entering,
        outof_act,
        state_in,
        inner_act,
        gate_act,
        skip_wide,
    )
    mixer_heads = jnp.concatenate([attended.astype(low), mamba_out], axis=1)
    mixed = jnp.dot(mixer_heads, weights_out, preferred_element_type=jnp.float32)
    hidden_one = tokens + scatter_heads(mixed.reshape(head_count, row_count, -1))
    inverse_two = lax.rsqrt(jnp.mean(hidden_one * hidden_one, axis=-1, keepdims=True) + epsilon)
    normed_two = jnp.concatenate(
        gather_heads(ring_features((hidden_one * inverse_two * second_gain).astype(low))),
        axis=0,
    )
    gate_up = jnp.dot(normed_two, weights_ffn, preferred_element_type=jnp.float32)
    group_units = FF // head_count
    gate_part = gate_up[:, :group_units]
    up_part = gate_up[:, group_units:]
    activated = (jax.nn.silu(gate_part) * up_part).astype(low)
    downed = jnp.dot(activated, weights_down, preferred_element_type=jnp.float32)
    block_output = hidden_one + scatter_heads(downed.reshape(head_count, row_count, -1))
    grad_down = scatter_blocks(outer_grad(activated, span_cotangent).astype(low)).astype(
        jnp.float32
    )
    grad_activated = times_transposed(span_cotangent, weights_down)
    sigmoid_gate = jax.nn.sigmoid(gate_part)
    grad_gate_up = jnp.concatenate(
        [
            grad_activated * up_part * sigmoid_gate * (1.0 + gate_part * (1.0 - sigmoid_gate)),
            grad_activated * jax.nn.silu(gate_part),
        ],
        axis=1,
    ).astype(low)
    grad_ffn = scatter_blocks(outer_grad(normed_two, grad_gate_up).astype(low))
    grad_ffn = unpack_ffn(swap_groups(grad_ffn.reshape(head_count, -1, 2 * group_units))).astype(
        jnp.float32
    )
    grad_normed_two = plain_features(
        scatter_heads(
            times_transposed(grad_gate_up, weights_ffn).reshape(head_count, row_count, -1)
        )
    )
    grad_hidden = cotangent.astype(jnp.float32) + norm_back(
        hidden_one, inverse_two, second_gain, grad_normed_two
    )
    grad_second = jnp.sum(grad_normed_two * hidden_one * inverse_two, axis=0)
    span_grad_hidden = jnp.concatenate(gather_heads(grad_hidden.astype(low)), axis=0)
    grad_mix_weight = lax.ppermute(
        scatter_blocks(outer_grad(mixer_heads, span_grad_hidden).astype(low)),
        ("head", "blk"),
        [(there, here) for here, there in out_pairs],
    ).astype(jnp.float32)
    grad_heads = times_transposed(span_grad_hidden, weights_out).astype(low)

    grad_ssd, grad_gate, grad_state_in, grad_skip_wide = whole_call(
        ssd_gate_back,
        [
            tall,
            shaped((span_rows, group_inner), low),
            shaped(state_shape, jnp.float32),
            shaped((8, group_inner), jnp.float32),
        ],
        [],
        2 * 10**9,
        grad_heads[:, group_query:],
        gate_act,
        ssd,
        inner_act,
        skip_wide,
        entering,
        outof_act,
    )
    grad_skip = grad_skip_wide[0].reshape(mamba_group, MP).sum(axis=1)
    later_grad = chained(grad_state_in, span_factor, True)

    grad_query, grad_keys, grad_values = attention_back(
        place,
        query_local,
        first_wide,
        keys,
        values,
        grad_heads[:, :group_query],
        attended,
        lse,
    )
    kept_kv = jnp.where(even, grad_keys, grad_values)
    given_kv = jnp.where(even, grad_values, grad_keys)
    kv_sums = (kept_kv.astype(jnp.float32) + from_head(given_kv, 1).astype(jnp.float32)).astype(
        low
    )
    grad_kv = kv_sums[0].astype(jnp.float32)
    for d in range(1, blocks):
        grad_kv = grad_kv + passed_along(kv_sums[d], "blk", -d).astype(jnp.float32)
    grad_kv = jnp.where(
        even, rotate(grad_kv.reshape(span_rows, 1, HD), positions, -1.0)[:, 0], grad_kv
    )
    grad_query_seq = rotate(
        grad_query.reshape(span_rows, query_group, HD), positions, -1.0
    ).reshape(span_rows, group_query)
    grad_rest = jnp.concatenate(
        [grad_query_seq.astype(low), grad_kv.astype(low), grad_gate], axis=1
    )
    grad_rest_weight = scatter_blocks(outer_grad(normed_one, grad_rest).astype(low))

    grad_inner, grad_into, grad_outof, grad_step, grad_decay_line = whole_call(
        ssd_back,
        [
            tall,
            shaped((span_rows, NS), jnp.float32),
            shaped((span_rows, NS), jnp.float32),
            narrow,
            narrow,
        ],
        [
            pltpu.VMEM((span_rows // chunk + 1, group_inner, NS), jnp.float32),
            pltpu.VMEM((group_inner, NS), jnp.float32),
        ],
        10 * 10**9,
        inner_act,
        into_act,
        outof_act,
        step_wide,
        decay_wide,
        segment,
        grad_ssd,
        ssd,
        skip_wide,
        state_in,
        later_grad,
    )
    grad_raw, grad_step_shift, grad_rate = step_back(
        (grad_step[:, :mamba_group], grad_decay_line[:, :mamba_group])
    )
    grad_extended, grad_taps, grad_shift = conv_back(
        jnp.concatenate([grad_inner, grad_into, grad_outof], axis=1)
    )
    rim_back = passed_along(grad_extended[: KW - 1], "blk", -1)
    conv_grad = grad_extended[KW - 1 :] + jnp.pad(rim_back, ((span_rows - (KW - 1), 0), (0, 0)))
    grad_bc = conv_grad[:, group_inner:].astype(low).astype(jnp.float32)
    grad_bc = scatter_heads(jnp.stack(jnp.split(grad_bc, head_count, axis=1)))
    grad_conv = jnp.concatenate(
        [
            conv_grad[:, :group_inner],
            grad_bc,
            grad_raw,
            jnp.zeros((span_rows, step_pad - mamba_group), jnp.float32),
        ],
        axis=1,
    ).astype(low)
    grad_conv_in = scatter_blocks(outer_grad(normed_one, grad_conv).astype(low))
    grad_proj_weight = unpack_in(
        jnp.concatenate(
            [
                swap_groups(part.reshape(head_count, in_weight.shape[0], -1))
                for part in (grad_conv_in, grad_rest_weight)
            ],
            axis=2,
        )
    ).astype(jnp.float32)
    grad_normed_one = times_transposed(grad_rest, weights_rest) + times_transposed(
        grad_conv, weights_conv
    )
    grad_normed_one = plain_features(
        scatter_heads(grad_normed_one.reshape(head_count, row_count, -1))
    )
    grad_input = (grad_hidden + norm_back(tokens, inverse_one, first_gain, grad_normed_one)).astype(
        low
    )
    grad_first = jnp.sum(grad_normed_one * tokens * inverse_one, axis=0)

    def own_part(values_in, total):
        return lax.dynamic_update_slice_in_dim(
            jnp.zeros(values_in.shape[:-1] + (total,), jnp.float32),
            values_in,
            head_index * values_in.shape[-1],
            values_in.ndim - 1,
        )

    small = [
        grad_first,
        grad_second,
        jnp.concatenate(
            [own_part(grad_taps[:, :group_inner], mamba_width), grad_taps[:, group_inner:]], axis=1
        ),
        jnp.concatenate(
            [own_part(grad_shift[:group_inner], mamba_width), grad_shift[group_inner:]]
        ),
        own_part(grad_step_shift, MH),
        own_part(grad_rate, MH),
        own_part(grad_skip, MH),
    ]
    line = jnp.concatenate([part.reshape(-1) for part in small])
    line = jnp.pad(line, (0, -line.shape[0] % 1024)).reshape(-1, 128)
    line = summed_over(summed_over(line, "head"), "blk").reshape(-1)
    summed_small = []
    at = 0
    for part in small:
        summed_small.append(line[at : at + part.size].reshape(part.shape))
        at += part.size
    return (
        block_output.astype(low)[None],
        grad_input[None],
        grad_proj_weight,
        grad_mix_weight,
        grad_ffn,
        grad_down,
        *summed_small,
    )


def solution(mesh):
    placed = (
        P("blk", "head", None),
        P("blk", "head", None),
        P("blk", None),
        P(("head", "blk"), None),
        P(("head", "blk"), None),
        P(("head", "blk"), None),
        P(("head", "blk"), None),
        P(),
        P(),
        P(),
        P(),
        P(),
        P(),
        P(),
    )
    return jax.shard_map(
        per_device,
        mesh=mesh,
        in_specs=placed,
        out_specs=(
            P("blk", "head", None),
            P("blk", "head", None),
            P(("head", "blk"), None),
            P(("head", "blk"), None),
            P(("head", "blk"), None),
            P(("head", "blk"), None),
            P(),
            P(),
            P(),
            P(),
            P(),
            P(),
            P(),
        ),
        check_vma=False,
    )
```

```python
import math
from functools import partial

import jax
import jax.numpy as jnp
from jax import lax
from jax.experimental import pallas as pl
from jax.experimental.pallas import tpu as pltpu
from jax.sharding import PartitionSpec as P

D = 2048
QH = 8
KVH = 2
HD = 128
MH = 48
MP = 64
NS = 256
FF = 4096
KW = 4


epsilon = 1e-05
rope_base = 100000000000.0
masked_score = -1e30


def after(value, *others):
    return lax.optimization_barrier((value, *others))[0]


def passed_along(shard, axis, by):
    peers = lax.axis_size(axis)
    pairs = [(i, i + by) for i in range(peers) if 0 <= i + by < peers]
    return lax.ppermute(shard, axis, pairs)


def ring_of(axis):
    peers = lax.axis_size(axis)
    if peers != 8:
        return list(range(peers))
    return [0, 2, 4, 6, 7, 5, 3, 1]


def gather_blocks(shard):
    return lax.all_gather(shard, "blk", axis=0, tiled=True, axis_index_groups=[ring_of("blk")])


def scatter_blocks(partial_sums):
    return lax.psum_scatter(
        partial_sums,
        "blk",
        scatter_dimension=0,
        tiled=True,
        axis_index_groups=[ring_of("blk")],
    )


def from_head(shard, distance):
    peers = lax.axis_size("head")
    return lax.ppermute(shard, "head", [(i, i ^ distance) for i in range(peers)])


def gather_heads(shard):
    across = from_head(shard, 2)
    return [shard, across, from_head(shard, 1), from_head(across, 1)]


def in_head_order(parts):
    mine = lax.axis_index("head")
    stacked = jnp.stack([parts[0], parts[2], parts[1], parts[3]])
    return [
        lax.dynamic_index_in_dim(stacked, jnp.bitwise_xor(mine, j), 0, False) for j in range(4)
    ]


def scatter_pairs(own, other, middle=jnp.float32):
    rows = own.shape[0] // 2
    got = from_head(other.astype(middle), 1).astype(jnp.float32)
    far = from_head((own[rows:] + got[rows:]).astype(low), 2)
    return own[:rows] + got[:rows] + far.astype(jnp.float32)


def swap_heads(pieces):
    return lax.all_to_all(pieces, "head", split_axis=0, concat_axis=0, tiled=True)


def mixer_place():
    heads, ring = lax.axis_size("head"), ring_of("blk")
    peers = heads * len(ring)
    rows = (QH * HD + MH * MP) // peers
    query_blocks, mamba_blocks = QH * HD // rows // heads, MH * MP // rows // heads
    pairs = []
    for r in range(peers):
        if r < query_blocks * heads:
            group, slot = divmod(r, query_blocks)
        else:
            group, slot = divmod(r - query_blocks * heads, mamba_blocks)
            slot += query_blocks
        pairs.append((r, group * len(ring) + ring[slot]))
    return pairs


kv_begin = QH * HD
z_begin = kv_begin + 2 * KVH * HD
x_begin = z_begin + MH * MP
b_begin = x_begin + MH * MP
dt_begin = b_begin + 2 * NS
query_columns = QH * HD // 4
inner_columns = MH * MP // 4
bc_columns = 2 * NS // 4
step_heads = MH // 4
step_at = inner_columns + bc_columns
kv_at = step_at + 128
conv_columns = kv_at + HD
rest_columns = query_columns + inner_columns


def column_parts(head):
    conv = [
        (x_begin + head * inner_columns, 0, inner_columns),
        (b_begin + head * bc_columns, inner_columns, bc_columns),
        (kv_begin + (head % 2) * KVH * HD + (head // 2) * HD, kv_at, HD),
    ]
    rest = [
        (head * query_columns, 0, query_columns),
        (z_begin + head * inner_columns, query_columns, inner_columns),
    ]
    return conv, rest


def pack_in(place_ref, weight_ref, conv_ref, rest_ref, tail_ref):
    tail_ref[...] = jnp.zeros_like(tail_ref)
    tail_ref[:, :MH] = weight_ref[:, dt_begin : dt_begin + MH]
    last = tail_ref[...]
    lane = iota(last.shape, 1)
    for head in range(4):
        for parts, ref in zip(column_parts(head), (conv_ref, rest_ref)):
            for begin, at, size in parts:
                ref[head, :, at : at + size] = weight_ref[:, begin : begin + size].astype(low)
        steps = pltpu.roll(last, lanes - step_heads * head, 1) if head else last
        conv_ref[head, :, step_at:kv_at] = jnp.where(lane < step_heads, steps, 0.0).astype(low)


def unpack_in(place_ref, conv_ref, rest_ref, out_ref):
    total = jnp.zeros((out_ref.shape[0], lanes), jnp.float32)
    lane = iota(total.shape, 1)
    for head in range(4):
        for parts, ref in zip(column_parts(head), (conv_ref, rest_ref)):
            for begin, at, size in parts:
                out_ref[:, begin : begin + size] = ref[head, :, at : at + size].astype(jnp.float32)
        steps = conv_ref[head, :, step_at:kv_at].astype(jnp.float32)
        steps = jnp.where(lane < step_heads, steps, 0.0)
        total = total + (pltpu.roll(steps, step_heads * head, 1) if head else steps)
    out_ref[:, dt_begin : dt_begin + MH] = total[:, :MH]


def ffn_moves(ring):
    unit = FF // (4 * len(ring))
    return unit, [
        (
            head,
            half * FF + (head * len(ring) + k) * unit,
            half * (FF // 4) + i * unit,
        )
        for half in range(2)
        for head in range(4)
        for i, k in enumerate(ring)
    ]


def pack_ffn(place_ref, weight_ref, out_ref, *, ring):
    unit, moves = ffn_moves(ring)
    for head, begin, at in moves:
        out_ref[head, :, at : at + unit] = weight_ref[:, begin : begin + unit].astype(low)


def unpack_ffn(place_ref, in_ref, out_ref, *, ring):
    unit, moves = ffn_moves(ring)
    for head, begin, at in moves:
        out_ref[:, begin : begin + unit] = in_ref[head, :, at : at + unit].astype(jnp.float32)


def inverse_rms(values_in):
    return lax.rsqrt(jnp.mean(values_in * values_in, axis=1, keepdims=True) + epsilon)


def feature_moves(ring):
    piece = D // 4 // len(ring)
    return piece, [
        ((e * len(ring) + k) * piece, (4 * i + e) * piece)
        for e in range(4)
        for i, k in enumerate(ring)
    ]


def whole_lanes(begin, size):
    return pl.ds(pl.multiple_of(begin, 128), size)


def norm_one(place_ref, own, across, beside, both, gain_ref, out_ref, line_ref, *, ring):
    rows = own.shape[0]
    piece, moves = feature_moves(ring)
    for distance, ref in ((0, own), (2, across), (1, beside), (3, both)):
        x = ref[...].astype(jnp.float32)
        line_ref[...] = (x * inverse_rms(x) * gain_ref[...]).astype(low)
        there = jnp.bitwise_xor(place_ref[0], distance) * rows
        there = pl.ds(pl.multiple_of(there, rows), rows)
        for source, at in moves:
            out_ref[there, at : at + piece] = line_ref[:, source : source + piece]


def norm_two(place_ref, mixed_ref, tokens_ref, gain_ref, hidden_ref, out_ref, line_ref, *, ring):
    hidden = tokens_ref[...].astype(jnp.float32) + mixed_ref[...]
    hidden_ref[...] = hidden
    line_ref[...] = (hidden * inverse_rms(hidden) * gain_ref[...]).astype(low)
    piece, moves = feature_moves(ring)
    for source, at in moves:
        out_ref[:, at : at + piece] = line_ref[:, source : source + piece]


def back_two(
    place_ref, grad_ref, hidden_ref, cotangent_ref, gain_ref, out_ref, low_ref, sum_ref, plain_ref,
    *, ring,
):
    piece, moves = feature_moves(ring)
    for source, at in moves:
        plain_ref[:, source : source + piece] = grad_ref[:, at : at + piece]
    grad = plain_ref[...]
    hidden = hidden_ref[...]
    inverse = inverse_rms(hidden)
    scaled = grad * gain_ref[...]
    total = (
        cotangent_ref[...].astype(jnp.float32)
        + inverse * scaled
        - hidden * (inverse * inverse * inverse * jnp.mean(scaled * hidden, axis=1, keepdims=True))
    )
    out_ref[...] = total
    low_ref[...] = total.astype(low)
    sum_ref[...] = jnp.broadcast_to(
        jnp.sum(grad * hidden * inverse, axis=0, keepdims=True), sum_ref.shape
    )


def back_one(
    place_ref, grad_ref, tokens_ref, hidden_ref, gain_ref, out_ref, plain_ref, *, ring
):
    piece, moves = feature_moves(ring)
    for source, at in moves:
        plain_ref[:, source : source + piece] = grad_ref[:, at : at + piece]
    grad = plain_ref[...]
    x = tokens_ref[...].astype(jnp.float32)
    inverse = inverse_rms(x)
    scaled = grad * gain_ref[...]
    out_ref[...] = (
        hidden_ref[...]
        + inverse * scaled
        - x * (inverse * inverse * inverse * jnp.mean(scaled * x, axis=1, keepdims=True))
    ).astype(low)


def turned(values_in, cosine, sine):
    return values_in * cosine + pltpu.roll(values_in, HD // 2, 1) * sine


def rope_kv(place_ref, in_ref, cosine_ref, sine_ref, out_ref):
    kv = in_ref[...]
    kv = jnp.where(place_ref[1] == 0, turned(kv, cosine_ref[...], sine_ref[...]), kv).astype(low)
    for k in range(out_ref.shape[0]):
        out_ref[k] = kv


def rope_query(place_ref, in_ref, cosine_ref, sine_ref, query_ref, gate_ref):
    cosine, sine = cosine_ref[...], sine_ref[...]
    for begin in range(0, query_columns, HD):
        query_ref[:, begin : begin + HD] = turned(
            in_ref[:, begin : begin + HD], cosine, sine
        ).astype(low)
    gate_ref[...] = in_ref[:, query_columns:].astype(low)


def query_back(place_ref, query_ref, gate_ref, cosine_ref, sine_ref, out_ref):
    cosine, sine = cosine_ref[...], -sine_ref[...]
    for begin in range(0, query_columns, HD):
        rounded = query_ref[:, begin : begin + HD].astype(low).astype(jnp.float32)
        out_ref[:, begin : begin + HD] = turned(rounded, cosine, sine).astype(low)
    out_ref[:, query_columns:] = gate_ref[...]


def join_conv(place_ref, inner_ref, own, across, beside, both, out_ref):
    out_ref[:, :inner_columns] = inner_ref[...].astype(low)
    for distance, ref in ((0, own), (2, across), (1, beside), (3, both)):
        at = inner_columns + jnp.bitwise_xor(place_ref[0], distance) * lanes
        out_ref[:, whole_lanes(at, lanes)] = ref[...]


def conv_joined(
    place_ref, inner_ref, near_ref, far_ref, step_ref, cosine_ref, sine_ref, kv_ref, out_ref
):
    out_ref[:, :inner_columns] = inner_ref[...].astype(low)
    out_ref[:, inner_columns:step_at] = (near_ref[...] + far_ref[...].astype(jnp.float32)).astype(low)
    out_ref[:, step_at:kv_at] = step_ref[...].astype(low)
    kv = kv_ref[0].astype(jnp.float32)
    for k in range(1, kv_ref.shape[0]):
        kv = kv + kv_ref[k].astype(jnp.float32)
    out_ref[:, kv_at:] = jnp.where(
        place_ref[1] == 0, turned(kv, cosine_ref[...], -sine_ref[...]), kv
    ).astype(low)


def relative_order(place_ref, first_ref, second_ref, first_out, second_out):
    for at, distance in enumerate((0, 2, 1, 3)):
        there = jnp.bitwise_xor(place_ref[0], distance) * chunk
        there = pl.ds(pl.multiple_of(there, chunk), chunk)
        rows = slice(at * chunk, (at + 1) * chunk)
        first_out[rows, :] = first_ref[there, :]
        second_out[rows, :] = second_ref[there, :]


def outer_grad(left_side, grad_side):
    return lax.dot_general(
        left_side, grad_side, (((0,), (0,)), ((), ())), preferred_element_type=jnp.float32
    )


def times_transposed(grad_side, weight):
    return lax.dot_general(
        grad_side, weight, (((1,), (1,)), ((), ())), preferred_element_type=jnp.float32
    )


chunk = 128
lanes = 128
low = jnp.bfloat16
exact = lax.Precision.HIGHEST


def dot_nn(a, b, precision=None):
    return lax.dot_general(
        a, b, (((1,), (0,)), ((), ())), precision=precision, preferred_element_type=jnp.float32
    )


def dot_nt(a, b):
    return lax.dot_general(a, b, (((1,), (1,)), ((), ())), preferred_element_type=jnp.float32)


def dot_tn(a, b):
    return lax.dot_general(a, b, (((0,), (0,)), ((), ())), preferred_element_type=jnp.float32)


def iota(shape, dim):
    return lax.broadcasted_iota(jnp.int32, shape, dim)


def spread(per_head, pair):
    rows = per_head.shape[0]
    first = per_head[:, 2 * pair : 2 * pair + 1]
    second = per_head[:, 2 * pair + 1 : 2 * pair + 2]
    return jnp.where(iota((rows, lanes), 1) < MP, first, second)


def head_sums(products, pair):
    mine = 2 * pair + (iota((lanes, lanes), 0) >= MP).astype(jnp.int32)
    ones = (mine == iota((lanes, lanes), 1)).astype(jnp.float32)
    return dot_nn(products, ones, exact)


def chunk_terms(decay, segment, segment_before):
    lower = iota((chunk, chunk), 0) >= iota((chunk, chunk), 1)
    cumulative = dot_nn(lower.astype(jnp.float32), decay, exact)
    total = cumulative[chunk - 1 :, :]
    segment_end = segment[chunk - 1 :, :]
    related = lower & (segment == segment.T)
    entering = jnp.where(segment == segment_before, jnp.exp(cumulative), 0.0)
    ending = jnp.where(segment == segment_end, jnp.exp(total - cumulative), 0.0)
    whole = jnp.where(segment_end == segment_before, jnp.exp(total), 0.0)
    return cumulative, cumulative.T, related, entering, ending, whole, total, segment_end


def decays_of(cumulative, transposed, related, head):
    apart = cumulative[:, head : head + 1] - transposed[head : head + 1, :]
    return jnp.exp(jnp.where(related, apart, masked_score))


def row_factor(whole, pair, width):
    first = whole[:, 2 * pair : 2 * pair + 1]
    second = whole[:, 2 * pair + 1 : 2 * pair + 2]
    return jnp.where(iota((lanes, width), 0) < MP, first, second)


def chunk_rows(index):
    return pl.ds(pl.multiple_of(index * chunk, chunk), chunk)


def pack_states(state_ref, factor, out_ref):
    blocks, rows, width = out_ref.shape
    share = rows - extra_rows
    row = iota((extra_rows, width), 0)
    for k in range(blocks):
        extra = jnp.zeros((extra_rows, width), jnp.float32)
        for e in range(4):
            head = k * share // MP + e
            if head * MP < state_ref.shape[0]:
                whole = factor[:, head : head + 1]
                rough = whole.astype(low).astype(jnp.float32)
                extra = jnp.where(row == e, rough, extra)
                extra = jnp.where(row == 4 + e, whole - rough, extra)
        out_ref[k, :extra_rows, :] = extra.astype(low)
        out_ref[k, extra_rows:, :] = state_ref[k * share : (k + 1) * share, :].astype(low)


extra_rows = 16


def chain(place_ref, got_ref, out_ref, backwards):
    blocks, rows, width = got_ref.shape
    share = rows - extra_rows
    row = iota((share, width), 0) + lax.rem(place_ref[4] * share, MP)
    state = jnp.zeros((share, width), jnp.float32)
    for k in range(blocks - 1, -1, -1) if backwards else range(blocks):
        out_ref[k] = state.astype(low)
        extra = got_ref[k, :extra_rows, :].astype(jnp.float32)
        factor = extra[0:1, :] + extra[4:5, :]
        for e in range(1, 4):
            factor = jnp.where(row >= e * MP, extra[e : e + 1, :] + extra[4 + e : 5 + e, :], factor)
        state = factor * state + got_ref[k, extra_rows:, :].astype(jnp.float32)


def ssd_local(
    place_ref, x_ref, b_ref, c_ref, step_ref, decay_ref, seg_ref,
    y_ref, sent_ref, enter_ref, fac_ref, state_ref,
):
    pairs = x_ref.shape[1] // lanes
    state_ref[...] = jnp.zeros_like(state_ref)

    def body(index, carry):
        segment_before, base = carry
        rows = chunk_rows(index)
        segment = seg_ref[rows, :]
        cumulative, transposed, related, entering, ending, whole, total, segment_end = chunk_terms(
            decay_ref[rows, :], segment, segment_before
        )
        enter_ref[rows, :] = jnp.where(segment == 0.0, jnp.exp(base + cumulative), 0.0)
        into = b_ref[rows, :].astype(low)
        outof = c_ref[rows, :].astype(low)
        step = step_ref[rows, :]
        scores = dot_nt(outof, into)
        left = iota((chunk, lanes), 1) < MP
        for pair in range(pairs):
            cols = slice(pair * lanes, (pair + 1) * lanes)
            taken = x_ref[rows, cols] * spread(step, pair)
            taken_low = taken.astype(low)
            parts = []
            for head in (2 * pair, 2 * pair + 1):
                weights = decays_of(cumulative, transposed, related, head) * scores
                parts.append(dot_nn(weights.astype(low), taken_low))
            state = state_ref[cols, :]
            y_ref[rows, cols] = jnp.where(left, parts[0], parts[1]) + spread(
                entering, pair
            ) * dot_nt(outof, state.astype(low))
            kept = (taken * spread(ending, pair)).astype(low)
            state_ref[cols, :] = row_factor(whole, pair, state.shape[1]) * state + dot_tn(
                kept, into
            )
        return segment_end, base + total

    start = jnp.zeros((1, lanes), jnp.float32)
    segment_end, base = lax.fori_loop(0, x_ref.shape[0] // chunk, body, (start, start))
    factor = jnp.where(segment_end == 0.0, jnp.exp(base), 0.0)
    fac_ref[...] = jnp.broadcast_to(factor, fac_ref.shape)
    pack_states(state_ref, factor, sent_ref)


def relative_rows(place_ref, index):
    distance = jnp.bitwise_xor(place_ref[0], index)
    at = (distance % 2) * 2 + distance // 2
    return pl.ds(pl.multiple_of(at * chunk, chunk), chunk)


def ssd_finish(
    place_ref, y_ref, enter_ref, c_ref, state_ref, x_ref, z_ref, skip_ref, attended_ref,
    ssd_ref, mixer_ref,
):
    pairs = x_ref.shape[1] // lanes
    width = attended_ref.shape[1]

    def body(index, carry):
        rows = chunk_rows(index)
        there = relative_rows(place_ref, index)
        outof = c_ref[rows, :].astype(low)
        entering = enter_ref[rows, :]
        mixer_ref[there, :width] = attended_ref[rows, :].astype(low)
        for pair in range(pairs):
            cols = slice(pair * lanes, (pair + 1) * lanes)
            ssd = y_ref[rows, cols] + spread(entering, pair) * dot_nt(outof, state_ref[cols, :])
            ssd_ref[rows, cols] = ssd
            gate = z_ref[rows, cols].astype(jnp.float32)
            total = ssd + skip_ref[:, cols] * x_ref[rows, cols]
            mixer_ref[there, width + pair * lanes : width + (pair + 1) * lanes] = (
                total * gate / (1.0 + jnp.exp(-gate))
            ).astype(low)
        return carry

    lax.fori_loop(0, x_ref.shape[0] // chunk, body, 0)


def ssd_gate_back(
    place_ref, grad_ref, z_ref, ssd_ref, x_ref, skip_ref, enter_ref, c_ref, fac_ref,
    dy_ref, dz_ref, sent_ref, dskip_ref, datt_ref, dstate_ref,
):
    pairs = x_ref.shape[1] // lanes
    width = datt_ref.shape[1]
    dstate_ref[...] = jnp.zeros_like(dstate_ref)
    dskip_ref[...] = jnp.zeros_like(dskip_ref)

    def body(index, carry):
        rows = chunk_rows(index)
        there = relative_rows(place_ref, index)
        outof = c_ref[rows, :].astype(low)
        entering = enter_ref[rows, :]
        datt_ref[rows, :] = grad_ref[there, :width]
        for pair in range(pairs):
            cols = slice(pair * lanes, (pair + 1) * lanes)
            gate = z_ref[rows, cols].astype(jnp.float32)
            sigmoid = 1.0 / (1.0 + jnp.exp(-gate))
            grad = grad_ref[
                there, width + pair * lanes : width + (pair + 1) * lanes
            ].astype(jnp.float32)
            x = x_ref[rows, cols]
            total = ssd_ref[rows, cols] + skip_ref[:, cols] * x
            dz_ref[rows, cols] = (
                grad * total * sigmoid * (1.0 + gate * (1.0 - sigmoid))
            ).astype(low)
            dy = grad * gate * sigmoid
            dy_ref[rows, cols] = dy
            dskip_ref[:, cols] += jnp.broadcast_to(
                jnp.sum(dy * x, axis=0, keepdims=True), (dskip_ref.shape[0], lanes)
            )
            dstate_ref[cols, :] += dot_tn((dy * spread(entering, pair)).astype(low), outof)
        return carry

    lax.fori_loop(0, x_ref.shape[0] // chunk, body, 0)
    pack_states(dstate_ref, fac_ref[:1, :], sent_ref)


def ssd_back(
    place_ref, x_ref, b_ref, c_ref, step_ref, decay_ref, seg_ref, dy_ref, ssd_ref, skip_ref, state_ref, later_ref,
    dx_ref, db_ref, dc_ref, dstep_ref, ddecay_ref, states, grads,
):
    pairs = x_ref.shape[1] // lanes
    chunks = x_ref.shape[0] // chunk
    zero_row = jnp.zeros((1, lanes), jnp.float32)

    def before(index):
        rows = pl.ds(pl.multiple_of(jnp.maximum(index - 1, 0) * chunk, chunk), chunk)
        return jnp.where(index == 0, 0.0, seg_ref[rows, :][chunk - 1 :, :])

    states[0] = state_ref[...].astype(jnp.float32)

    def forward(index, carry):
        rows = chunk_rows(index)
        _, _, _, _, ending, whole, _, _ = chunk_terms(
            decay_ref[rows, :], seg_ref[rows, :], before(index)
        )
        into = b_ref[rows, :].astype(low)
        step = step_ref[rows, :]
        for pair in range(pairs):
            cols = slice(pair * lanes, (pair + 1) * lanes)
            kept = (x_ref[rows, cols] * spread(step, pair) * spread(ending, pair)).astype(low)
            state = states[index, cols, :]
            states[index + 1, cols, :] = row_factor(
                whole, pair, state.shape[1]
            ) * state + dot_tn(kept, into)
        return carry

    lax.fori_loop(0, chunks, forward, 0)
    grads[...] = later_ref[...].astype(jnp.float32)
    last = jnp.zeros((8, lanes), jnp.float32)
    for pair in range(pairs):
        cols = slice(pair * lanes, (pair + 1) * lanes)
        product = grads[cols, :] * states[chunks, cols, :]
        along = lax.dot_general(
            jnp.ones((8, product.shape[1]), jnp.float32),
            product,
            (((1,), (1,)), ((), ())),
            precision=exact,
            preferred_element_type=jnp.float32,
        )
        last = last + head_sums(along, pair)

    def backward(at, carry):
        index = chunks - 1 - at
        rows = chunk_rows(index)
        cumulative, transposed, related, entering, ending, whole, _, _ = chunk_terms(
            decay_ref[rows, :], seg_ref[rows, :], before(index)
        )
        into = b_ref[rows, :].astype(low)
        outof = c_ref[rows, :].astype(low)
        step = step_ref[rows, :]
        scores = dot_nt(outof, into)
        left = iota((chunk, lanes), 1) < MP
        grad_scores = jnp.zeros((chunk, chunk), jnp.float32)
        grad_into = jnp.zeros((chunk, b_ref.shape[1]), jnp.float32)
        grad_outof = jnp.zeros((chunk, b_ref.shape[1]), jnp.float32)
        grad_cum = jnp.zeros((chunk, lanes), jnp.float32)
        grad_step = jnp.zeros((chunk, lanes), jnp.float32)
        for pair in range(pairs):
            cols = slice(pair * lanes, (pair + 1) * lanes)
            x = x_ref[rows, cols]
            step_pair = spread(step, pair)
            taken = x * step_pair
            taken_low = taken.astype(low)
            dy = dy_ref[rows, cols]
            dy_low = dy.astype(low)
            parts = []
            for half, head in enumerate((2 * pair, 2 * pair + 1)):
                decays = decays_of(cumulative, transposed, related, head)
                parts.append(dot_tn((decays * scores).astype(low), dy_low))
                own = jnp.where(left if half == 0 else ~left, dy_low, jnp.zeros_like(dy_low))
                grad_scores = grad_scores + decays * dot_nt(own, taken_low)
            later = grads[cols, :]
            later_low = later.astype(low)
            ending_pair = spread(ending, pair)
            grad_taken = jnp.where(left, parts[0], parts[1]) + ending_pair * dot_nt(
                into, later_low
            )
            grad_into = grad_into + dot_nn((taken * ending_pair).astype(low), later_low)
            dy_enter = (dy * spread(entering, pair)).astype(low)
            grad_outof = grad_outof + dot_nn(dy_enter, states[index, cols, :].astype(low))
            grads[cols, :] = row_factor(whole, pair, later.shape[1]) * later + dot_tn(
                dy_enter, outof
            )
            grad_cum = grad_cum + head_sums(dy * ssd_ref[rows, cols] - taken * grad_taken, pair)
            grad_step = grad_step + head_sums(x * grad_taken, pair)
            dx_ref[rows, cols] = step_pair * grad_taken + skip_ref[:, cols] * dy
        grad_scores_low = grad_scores.astype(low)
        db_ref[rows, :] = grad_into + dot_tn(grad_scores_low, outof)
        dc_ref[rows, :] = grad_outof + dot_nn(grad_scores_low, into)
        dstep_ref[rows, :] = grad_step
        upper = (iota((chunk, chunk), 0) <= iota((chunk, chunk), 1)).astype(jnp.float32)
        ddecay_ref[rows, :] = dot_nn(upper, grad_cum, exact) + carry
        return carry + jnp.sum(grad_cum, axis=0, keepdims=True)

    lax.fori_loop(0, chunks, backward, last[:1, :] + zero_row)


def needed_and_plain(place_ref, block, span):
    mine, earliest, latest = place_ref[0], place_ref[1], place_ref[2]
    needed = (block <= mine) & ((block + 1) * span > earliest)
    return needed, (block < mine) & (block * span >= latest)


def visible_keys(place_ref, first_ref, block, span):
    key_pos = block * span + iota((span, span), 1)
    query_pos = place_ref[0] * span + iota((span, span), 0)
    return (key_pos <= query_pos) & (key_pos >= first_ref[:, :1])


def attend(place_ref, q_ref, first_ref, k_ref, v_ref, out_ref, lse_ref, top, total, summed):
    block = pl.program_id(0)
    span = q_ref.shape[0]
    heads = q_ref.shape[1] // HD

    @pl.when(block == 0)
    def _():
        top[...] = jnp.full_like(top, masked_score)
        total[...] = jnp.zeros_like(total)
        summed[...] = jnp.zeros_like(summed)

    def one(masked):
        keys = k_ref[0]
        values = v_ref[0]
        if masked:
            visible = visible_keys(place_ref, first_ref, block, span)
        for head in range(heads):
            cols = slice(head * HD, (head + 1) * HD)
            scores = dot_nt(q_ref[:, cols], keys) * HD**-0.5
            if masked:
                scores = jnp.where(visible, scores, masked_score)
            old_top = top[head][:, :1]
            new_top = jnp.maximum(old_top, jnp.max(scores, axis=1, keepdims=True))
            weights = jnp.exp(scores - new_top)
            if masked:
                weights = jnp.where(visible, weights, 0.0)
            scale = jnp.exp(old_top - new_top)
            total[head] = total[head] * scale + jnp.sum(weights, axis=1, keepdims=True)
            top[head] = jnp.broadcast_to(new_top, (span, lanes))
            summed[head] = summed[head] * scale + dot_nn(weights.astype(low), values)

    needed, plain = needed_and_plain(place_ref, block, span)
    pl.when(needed & plain)(lambda: one(False))
    pl.when(needed & jnp.logical_not(plain))(lambda: one(True))

    @pl.when(block == pl.num_programs(0) - 1)
    def _():
        for head in range(heads):
            cols = slice(head * HD, (head + 1) * HD)
            out_ref[:, cols] = summed[head] / total[head]
            lse_ref[head] = top[head] + jnp.log(total[head])


def attend_back(
    place_ref, q_ref, first_ref, k_ref, v_ref, grad_ref, out_ref, lse_ref, dq_ref, dk_ref, dv_ref
):
    block = pl.program_id(0)
    span = q_ref.shape[0]
    heads = q_ref.shape[1] // HD

    @pl.when(block == 0)
    def _():
        dq_ref[...] = jnp.zeros_like(dq_ref)

    def one(masked):
        keys = k_ref[0]
        values = v_ref[0]
        if masked:
            visible = visible_keys(place_ref, first_ref, block, span)
        grad_keys = jnp.zeros(keys.shape, jnp.float32)
        grad_values = jnp.zeros(keys.shape, jnp.float32)
        for head in range(heads):
            cols = slice(head * HD, (head + 1) * HD)
            query = q_ref[:, cols]
            grad = grad_ref[:, cols]
            delta = jnp.sum(
                grad.astype(jnp.float32) * out_ref[:, cols], axis=1, keepdims=True
            )
            scores = dot_nt(query, keys) * HD**-0.5
            if masked:
                scores = jnp.where(visible, scores, masked_score)
            weights = jnp.exp(scores - lse_ref[head][:, :1])
            changes = weights * (dot_nt(grad, values) - delta)
            weights_low = weights.astype(low)
            changes_low = (changes * HD**-0.5).astype(low)
            grad_values = grad_values + dot_tn(weights_low, grad)
            grad_keys = grad_keys + dot_tn(changes_low, query)
            dq_ref[:, cols] += dot_nn(changes_low, keys)
        dk_ref[0] = grad_keys.astype(low)
        dv_ref[0] = grad_values.astype(low)

    needed, plain = needed_and_plain(place_ref, block, span)
    pl.when(needed & plain)(lambda: one(False))
    pl.when(needed & jnp.logical_not(plain))(lambda: one(True))

    @pl.when(jnp.logical_not(needed))
    def _():
        dk_ref[...] = jnp.zeros_like(dk_ref)
        dv_ref[...] = jnp.zeros_like(dv_ref)


def shaped(shape, kind):
    return jax.ShapeDtypeStruct(shape, kind)


def call(kernel, outputs, place, operands, after=(), scratch=(), flops=10**6):
    count, skipped = len(operands), len(operands) + len(after)
    sizes = sum(math.prod(a.shape) * a.dtype.itemsize for a in (*operands, *outputs))

    def body(place_ref, *refs):
        kernel(place_ref, *refs[:count], *refs[skipped:])

    return pl.pallas_call(
        body,
        out_shape=outputs,
        in_specs=[pl.BlockSpec(memory_space=pltpu.SMEM)]
        + [pl.BlockSpec(memory_space=pltpu.VMEM)] * count
        + [pl.BlockSpec(memory_space=pl.ANY)] * len(after),
        out_specs=[pl.BlockSpec(memory_space=pltpu.VMEM)] * len(outputs),
        scratch_shapes=list(scratch),
        compiler_params=pltpu.CompilerParams(vmem_limit_bytes=kernel_memory),
        cost_estimate=pl.CostEstimate(flops=flops, bytes_accessed=sizes, transcendentals=0),
    )(place, *operands, *after)


kernel_memory = 44 * 1024 * 1024


def attention(place, query, first_visible, keys, values, after):
    away, span = keys.shape[0], query.shape[0]
    heads = query.shape[1] // HD
    same = lambda d, place: (0, 0)
    block = lambda d, place: (d, 0, 0)
    def body(*refs):
        attend(*refs[:5], *refs[5 + len(after) :])

    return pl.pallas_call(
        body,
        grid_spec=pltpu.PrefetchScalarGridSpec(
            num_scalar_prefetch=1,
            grid=(away,),
            in_specs=[
                pl.BlockSpec(query.shape, same),
                pl.BlockSpec(first_visible.shape, same),
                pl.BlockSpec((1, span, HD), block),
                pl.BlockSpec((1, span, HD), block),
            ]
            + [pl.BlockSpec(memory_space=pl.ANY)] * len(after),
            out_specs=[
                pl.BlockSpec(query.shape, same),
                pl.BlockSpec((heads, span, lanes), lambda d, place: (0, 0, 0)),
            ],
            scratch_shapes=[
                pltpu.VMEM((heads, span, lanes), jnp.float32),
                pltpu.VMEM((heads, span, lanes), jnp.float32),
                pltpu.VMEM((heads, span, HD), jnp.float32),
            ],
        ),
        out_shape=[
            shaped(query.shape, jnp.float32),
            shaped((heads, span, lanes), jnp.float32),
        ],
        compiler_params=pltpu.CompilerParams(vmem_limit_bytes=kernel_memory),
        cost_estimate=pl.CostEstimate(
            flops=20 * 10**9, bytes_accessed=4 * 10**6, transcendentals=0
        ),
    )(place, query, first_visible, keys, values, *after)


def attention_back(place, query, first_visible, keys, values, grad, out, lse, after):
    away, span = keys.shape[0], query.shape[0]
    same = lambda d, place: (0, 0)
    block = lambda d, place: (d, 0, 0)
    def body(*refs):
        attend_back(*refs[:8], *refs[8 + len(after) :])

    return pl.pallas_call(
        body,
        grid_spec=pltpu.PrefetchScalarGridSpec(
            num_scalar_prefetch=1,
            grid=(away,),
            in_specs=[
                pl.BlockSpec(query.shape, same),
                pl.BlockSpec(first_visible.shape, same),
                pl.BlockSpec((1, span, HD), block),
                pl.BlockSpec((1, span, HD), block),
                pl.BlockSpec(query.shape, same),
                pl.BlockSpec(query.shape, same),
                pl.BlockSpec(lse.shape, lambda d, place: (0, 0, 0)),
            ]
            + [pl.BlockSpec(memory_space=pl.ANY)] * len(after),
            out_specs=[
                pl.BlockSpec(query.shape, same),
                pl.BlockSpec((1, span, HD), block),
                pl.BlockSpec((1, span, HD), block),
            ],
        ),
        out_shape=[
            shaped(query.shape, jnp.float32),
            shaped(keys.shape, low),
            shaped(keys.shape, low),
        ],
        compiler_params=pltpu.CompilerParams(vmem_limit_bytes=kernel_memory),
        cost_estimate=pl.CostEstimate(
            flops=30 * 10**9, bytes_accessed=4 * 10**6, transcendentals=0
        ),
    )(place, query, first_visible, keys, values, grad, out, lse, *after)


def conv_act(extended, conv_taps, conv_shift, keep_masks):
    length = keep_masks[0].shape[0]
    result = conv_shift + conv_taps[0] * extended[KW - 1 :]
    for lag_index in range(1, KW):
        begin = KW - 1 - lag_index
        result = (
            result
            + conv_taps[lag_index]
            * keep_masks[lag_index][:, None]
            * extended[begin : begin + length]
        )
    return jax.nn.silu(result)


def step_and_decay(step_raw, step_shift, decay_rate):
    step_size = jax.nn.softplus(step_raw + step_shift)
    return step_size, -step_size * jnp.exp(decay_rate)


def in_lanes(per_head):
    return jnp.pad(per_head, ((0, 0), (0, lanes - per_head.shape[1])))


def summed_over(values_in, axis):
    peers = lax.axis_size(axis)
    by = 1
    while by < peers:
        values_in = values_in + lax.ppermute(values_in, axis, [(i, i ^ by) for i in range(peers)])
        by *= 2
    return values_in


def per_device(
    block_input,
    out_cotangent,
    start_flags,
    in_weight,
    out_weight,
    gate_up_weight,
    down_weight,
    first_gain,
    second_gain,
    conv_weight,
    conv_bias,
    step_bias,
    decay_log,
    skip_gain,
):
    head_count = lax.axis_size("head")
    blocks = lax.axis_size("blk")
    head_index = lax.axis_index("head")
    block_index = lax.axis_index("blk")
    ring = ring_of("blk")
    tokens = block_input[0]
    cotangent = out_cotangent[0]
    row_count = tokens.shape[0]
    span_rows = row_count * head_count
    mamba_width = MH * MP
    even = head_index % 2 == 0
    out_pairs = mixer_place()
    place = jnp.stack(
        [head_index, head_index % 2, 0, 0, block_index, 0, 0, 0]
    ).astype(jnp.int32)

    rows_in = in_weight.shape[0]
    flags_all = summed_over(
        lax.dynamic_update_slice_in_dim(
            jnp.zeros((blocks * span_rows,), jnp.int32),
            start_flags[0],
            block_index * span_rows,
            0,
        ),
        "blk",
    )
    packed_conv, packed_rest = call(
        pack_in,
        [
            shaped((4, rows_in, conv_columns), low),
            shaped((4, rows_in, rest_columns), low),
        ],
        place,
        [in_weight],
        scratch=[pltpu.VMEM((rows_in, lanes), jnp.float32)],
    )
    conv_rows = swap_heads(packed_conv).reshape(-1, conv_columns)
    weights_conv = gather_blocks(conv_rows)
    rest_rows = swap_heads(after(packed_rest, conv_rows)).reshape(-1, rest_columns)
    weights_rest = gather_blocks(rest_rows)
    gathered_tokens = gather_heads(after(tokens, conv_rows))
    out_rows = lax.ppermute(after(out_weight.astype(low), rest_rows), ("head", "blk"), out_pairs)
    weights_out = gather_blocks(out_rows)
    rows_ffn = gate_up_weight.shape[0]
    units = FF // 4
    packed_ffn = call(
        partial(pack_ffn, ring=ring),
        [shaped((4, rows_ffn, 2 * units), low)],
        place,
        [after(gate_up_weight, rest_rows)],
    )[0]
    ffn_rows = swap_heads(packed_ffn).reshape(-1, 2 * units)
    weights_ffn = gather_blocks(after(ffn_rows, out_rows))
    weights_down = gather_blocks(after(down_weight.astype(low), ffn_rows))
    model_cotangent = jnp.concatenate(gather_heads(after(cotangent, ffn_rows)))

    positions = block_index * span_rows + jnp.arange(span_rows, dtype=jnp.int32)
    all_positions = jnp.arange(blocks * span_rows, dtype=jnp.int32)
    starts_all = lax.cummax(jnp.where(flags_all > 0, all_positions, 0), axis=0)
    first_visible = lax.dynamic_slice_in_dim(starts_all, block_index * span_rows, span_rows, 0)
    flags_before = jnp.concatenate([jnp.zeros((KW - 2,), jnp.int32), flags_all])
    flag_ext = lax.dynamic_slice_in_dim(
        flags_before, block_index * span_rows, span_rows + KW - 2, 0
    ).astype(jnp.float32)
    segment = jnp.broadcast_to(
        jnp.cumsum(start_flags[0]).astype(jnp.float32)[:, None], (span_rows, lanes)
    )
    view = jnp.stack([block_index, jnp.min(first_visible), jnp.max(first_visible)])
    first_wide = jnp.broadcast_to(first_visible[:, None], (span_rows, lanes))
    keep_masks = [jnp.ones((span_rows,), jnp.float32)]
    for lag_index in range(1, KW):
        begin = KW - 1 - lag_index
        keep_masks.append(keep_masks[-1] * (1.0 - flag_ext[begin : begin + span_rows]))
    frequencies = rope_base ** (-jnp.arange(HD // 2, dtype=jnp.float32) * 2.0 / HD)
    angles = positions.astype(jnp.float32)[:, None] * frequencies[None, :]
    cosine = jnp.cos(angles)
    sine = jnp.sin(angles)
    cosine_wide = jnp.concatenate([cosine, cosine], axis=1)
    sine_wide = jnp.concatenate([-sine, sine], axis=1)
    conv_taps = jnp.concatenate(
        [
            lax.dynamic_slice_in_dim(conv_weight, head_index * inner_columns, inner_columns, 1),
            conv_weight[:, mamba_width:],
        ],
        axis=1,
    )
    conv_shift = jnp.concatenate(
        [
            lax.dynamic_slice_in_dim(conv_bias, head_index * inner_columns, inner_columns, 0),
            conv_bias[mamba_width:],
        ]
    )
    step_shift = lax.dynamic_slice_in_dim(step_bias, head_index * step_heads, step_heads, 0)
    decay_rate = lax.dynamic_slice_in_dim(decay_log, head_index * step_heads, step_heads, 0)
    skip_local = lax.dynamic_slice_in_dim(skip_gain, head_index * step_heads, step_heads, 0)
    skip_wide = jnp.repeat(skip_local, MP)[None, :]

    normed_one = call(
        partial(norm_one, ring=ring),
        [shaped((span_rows, D), low)],
        place,
        [*gathered_tokens, first_gain[None, :]],
        scratch=[pltpu.VMEM((row_count, D), low)],
    )[0]

    projected = jnp.dot(normed_one, weights_conv, preferred_element_type=jnp.float32)
    kv_mine = call(
        rope_kv,
        [shaped((blocks, span_rows, HD), low)],
        place,
        [projected[:, kv_at:], cosine_wide, sine_wide],
    )[0]
    pair_bc = projected[:, inner_columns:step_at].astype(low)
    conv_local = call(
        join_conv,
        [shaped((span_rows, inner_columns + 2 * NS), low)],
        place,
        [projected[:, :inner_columns], *gather_heads(pair_bc)],
    )[0]
    step_local = projected[:, step_at : step_at + step_heads].astype(low).astype(jnp.float32)
    rim_rows = passed_along(conv_local[span_rows - (KW - 1) :], "blk", 1)
    extended = jnp.concatenate([rim_rows, conv_local], axis=0).astype(jnp.float32)
    active, conv_back = jax.vjp(
        partial(conv_act, keep_masks=keep_masks), extended, conv_taps, conv_shift
    )
    (step_size, log_decay), step_back = jax.vjp(
        step_and_decay, step_local, step_shift, decay_rate
    )
    inner_act = active[:, :inner_columns]
    into_act = active[:, inner_columns : inner_columns + NS]
    outof_act = active[:, inner_columns + NS :]
    step_wide = in_lanes(step_size)
    decay_wide = in_lanes(log_decay)
    tall = shaped((span_rows, inner_columns), jnp.float32)
    tall_low = shaped((span_rows, inner_columns), low)
    narrow = shaped((span_rows, lanes), jnp.float32)
    share = inner_columns // blocks
    sent = shaped((blocks, extra_rows + share, NS), low)
    state_scratch = pltpu.VMEM((inner_columns, NS), jnp.float32)

    def chained(payload, backwards, after=()):
        got = lax.all_to_all(payload, "blk", split_axis=0, concat_axis=0, tiled=True)
        states = call(
            partial(chain, backwards=backwards),
            [shaped((blocks, share, NS), low)],
            place,
            [got],
            after=after,
        )[0]
        moved = lax.all_to_all(states, "blk", split_axis=0, concat_axis=0, tiled=True)
        return moved.reshape(inner_columns, NS), states

    within, state_sent, entering, factor = call(
        ssd_local,
        [tall, sent, narrow, shaped((8, lanes), jnp.float32)],
        place,
        [inner_act, into_act, outof_act, step_wide, decay_wide, segment],
        after=[ffn_rows],
        scratch=[state_scratch],
        flops=6 * 10**9,
    )
    state_in, states_mine = chained(state_sent, False)

    normed_after = after(normed_one, states_mine)
    projected_rest = jnp.dot(normed_after, weights_rest, preferred_element_type=jnp.float32)
    query_local, gate_act = call(
        rope_query,
        [shaped((span_rows, query_columns), low), tall_low],
        place,
        [projected_rest, cosine_wide, sine_wide],
    )
    kv_blocks = lax.all_to_all(
        after(kv_mine, state_sent), "blk", split_axis=0, concat_axis=0, tiled=True
    )
    kv_beside = from_head(kv_blocks, 1)
    keys = jnp.where(even, kv_blocks, kv_beside)
    values = jnp.where(even, kv_beside, kv_blocks)
    attended, lse = attention(
        view, query_local, first_wide, keys, values, [states_mine, model_cotangent]
    )

    ssd, mixer = call(
        ssd_finish,
        [tall, shaped((span_rows, query_columns + inner_columns), low)],
        place,
        [within, entering, outof_act, state_in, inner_act, gate_act, skip_wide, attended],
        flops=2 * 10**9,
    )
    pair_rows = 2 * row_count
    mixed_other = jnp.dot(mixer[pair_rows:], weights_out, preferred_element_type=jnp.float32)
    mixed_own = jnp.dot(mixer[:pair_rows], weights_out, preferred_element_type=jnp.float32)
    mixed = scatter_pairs(mixed_own, mixed_other)
    hidden_one, normed_two = call(
        partial(norm_two, ring=ring),
        [shaped((row_count, D), jnp.float32), shaped((row_count, D), low)],
        place,
        [mixed, tokens, second_gain[None, :]],
        scratch=[pltpu.VMEM((row_count, D), low)],
    )
    model_normed = jnp.concatenate(gather_heads(normed_two))
    gate_up = jnp.dot(model_normed, weights_ffn, preferred_element_type=jnp.float32)
    gate_part, up_part = gate_up[:, :units], gate_up[:, units:]
    activated = (jax.nn.silu(gate_part) * up_part).astype(low)
    grad_activated = times_transposed(model_cotangent, weights_down)
    sigmoid_gate = jax.nn.sigmoid(gate_part)
    grad_gate_up = jnp.concatenate(
        [
            grad_activated * up_part * sigmoid_gate * (1.0 + gate_part * (1.0 - sigmoid_gate)),
            grad_activated * jax.nn.silu(gate_part),
        ],
        axis=1,
    ).astype(low)
    grad_down_low = outer_grad(activated, model_cotangent).astype(low)
    grad_down = scatter_blocks(grad_down_low)
    gate_up_late = after(grad_gate_up, grad_down_low)
    grad_norm_other = times_transposed(gate_up_late[pair_rows:], weights_ffn).astype(low)
    grad_norm_own = times_transposed(gate_up_late[:pair_rows], weights_ffn)
    grad_normed_two = scatter_pairs(grad_norm_own, grad_norm_other, low)
    grad_ffn_low = outer_grad(model_normed, after(grad_gate_up, grad_norm_own)).astype(low)
    grad_ffn = scatter_blocks(after(grad_ffn_low, grad_down))

    grad_hidden, grad_hidden_low, grad_second = call(
        partial(back_two, ring=ring),
        [
            shaped((row_count, D), jnp.float32),
            shaped((row_count, D), low),
            shaped((8, D), jnp.float32),
        ],
        place,
        [
            grad_normed_two,
            hidden_one,
            cotangent,
            second_gain[None, :],
        ],
        after=[grad_down_low, grad_ffn_low],
        scratch=[pltpu.VMEM((row_count, D), jnp.float32)],
    )
    span_grad_hidden = jnp.concatenate(gather_heads(after(grad_hidden_low, grad_down)))
    grad_heads = times_transposed(span_grad_hidden, weights_out).astype(low)
    grad_ssd, grad_gate, grad_sent, grad_skip_wide, grad_attended = call(
        ssd_gate_back,
        [
            tall,
            tall_low,
            sent,
            shaped((8, inner_columns), jnp.float32),
            shaped((span_rows, query_columns), low),
        ],
        place,
        [grad_heads, gate_act, ssd, inner_act, skip_wide, entering, outof_act, factor],
        scratch=[state_scratch],
        flops=2 * 10**9,
    )
    grad_ffn_weight = call(
        partial(unpack_ffn, ring=ring),
        [shaped(gate_up_weight.shape, jnp.float32)],
        place,
        [swap_heads(grad_ffn.reshape(4, rows_ffn, 2 * units))],
    )[0]
    activated_late = after(activated, span_grad_hidden)
    downed_other = jnp.dot(
        activated_late[pair_rows:], weights_down, preferred_element_type=jnp.float32
    )
    downed_own = jnp.dot(
        activated_late[:pair_rows], weights_down, preferred_element_type=jnp.float32
    )
    block_output = (hidden_one + scatter_pairs(downed_own, downed_other, low)).astype(low)

    grad_skip = grad_skip_wide[0].reshape(step_heads, MP).sum(axis=1)
    grad_out_low = outer_grad(mixer, span_grad_hidden).astype(low)
    grad_out_sum = scatter_blocks(after(grad_out_low, grad_ffn))
    grad_mix_weight = lax.ppermute(
        grad_out_sum, ("head", "blk"), [(there, here) for here, there in out_pairs]
    ).astype(jnp.float32)
    later_grad, _ = chained(grad_sent, True)

    grad_query, grad_keys, grad_values = attention_back(
        view,
        query_local,
        first_wide,
        keys,
        values,
        grad_attended,
        attended,
        lse,
        [grad_out_low],
    )
    kept_kv = jnp.where(even, grad_keys, grad_values)
    given_kv = jnp.where(even, grad_values, grad_keys)
    kv_sums = (kept_kv.astype(jnp.float32) + from_head(given_kv, 1).astype(jnp.float32)).astype(
        low
    )
    grad_rest = call(
        query_back,
        [shaped((span_rows, rest_columns), low)],
        place,
        [grad_query, grad_gate, cosine_wide, sine_wide],
    )[0]
    grad_rest_low = outer_grad(normed_one, grad_rest).astype(low)
    grad_rest_in = scatter_blocks(after(grad_rest_low, grad_out_sum))
    grad_kv_parts = lax.all_to_all(kv_sums, "blk", split_axis=0, concat_axis=0, tiled=True)

    grad_inner, grad_into, grad_outof, grad_step, grad_decay_line = call(
        ssd_back,
        [
            tall,
            shaped((span_rows, NS), jnp.float32),
            shaped((span_rows, NS), jnp.float32),
            narrow,
            narrow,
        ],
        place,
        [
            inner_act,
            into_act,
            outof_act,
            step_wide,
            decay_wide,
            segment,
            grad_ssd,
            ssd,
            skip_wide,
            state_in,
            later_grad,
        ],
        after=[kv_sums, grad_rest_low, block_output],
        scratch=[
            pltpu.VMEM((span_rows // chunk + 1, inner_columns, NS), jnp.float32),
            state_scratch,
        ],
        flops=10 * 10**9,
    )
    grad_raw, grad_step_shift, grad_rate = step_back(
        (grad_step[:, :step_heads], grad_decay_line[:, :step_heads])
    )
    grad_inner = after(grad_inner, grad_ffn)
    grad_extended, grad_taps, grad_shift = conv_back(
        jnp.concatenate([grad_inner, grad_into, grad_outof], axis=1)
    )
    rim_back = passed_along(grad_extended[: KW - 1], "blk", -1)
    conv_grad = grad_extended[KW - 1 :] + jnp.pad(rim_back, ((span_rows - (KW - 1), 0), (0, 0)))
    grad_bc = conv_grad[:, inner_columns:].astype(low).astype(jnp.float32)

    def tile_at(distance):
        at = jnp.bitwise_xor(head_index, distance) * lanes
        return lax.dynamic_slice_in_dim(grad_bc, at, lanes, 1)

    bc_beside = from_head(jnp.stack([tile_at(1), tile_at(3)]).astype(low), 1).astype(jnp.float32)
    bc_far = from_head((tile_at(2) + bc_beside[1]).astype(low), 2)
    bc_near = tile_at(0) + bc_beside[0]
    grad_conv = call(
        conv_joined,
        [shaped((span_rows, conv_columns), low)],
        place,
        [
            conv_grad[:, :inner_columns],
            bc_near,
            bc_far,
            in_lanes(grad_raw),
            cosine_wide,
            sine_wide,
            grad_kv_parts,
        ],
    )[0]
    grad_conv_low = outer_grad(normed_one, grad_conv).astype(low)
    grad_conv_in = scatter_blocks(after(grad_conv_low, grad_rest_in))
    grad_proj_weight = call(
        unpack_in,
        [shaped(in_weight.shape, jnp.float32)],
        place,
        [
            swap_heads(part.reshape(4, rows_in, -1))
            for part in (grad_conv_in, grad_rest_in)
        ],
    )[0]
    conv_moved, rest_moved = call(
        relative_order,
        [shaped((span_rows, conv_columns), low), shaped((span_rows, rest_columns), low)],
        place,
        [grad_conv, grad_rest],
        after=[grad_conv_low],
    )

    def back_in(part):
        return times_transposed(rest_moved[part], weights_rest) + times_transposed(
            conv_moved[part], weights_conv
        )

    grad_normed_other = back_in(slice(pair_rows, span_rows)).astype(low)
    grad_normed_own = back_in(slice(0, pair_rows))
    grad_normed_other = after(grad_normed_other, grad_out_sum)
    grad_input = call(
        partial(back_one, ring=ring),
        [shaped((row_count, D), low)],
        place,
        [
            scatter_pairs(grad_normed_own, grad_normed_other, low),
            tokens,
            grad_hidden,
            first_gain[None, :],
        ],
        scratch=[pltpu.VMEM((row_count, D), jnp.float32)],
    )[0]
    first_line = jnp.sum(
        weights_conv.astype(jnp.float32) * grad_conv_low.astype(jnp.float32), axis=1
    ) + jnp.sum(weights_rest.astype(jnp.float32) * grad_rest_low.astype(jnp.float32), axis=1)
    first_line = first_line.reshape(blocks, 4, -1)
    first_line = jnp.stack([first_line[ring.index(k)] for k in range(blocks)], axis=1).reshape(D)

    def own_part(values_in, total):
        return lax.dynamic_update_slice_in_dim(
            jnp.zeros(values_in.shape[:-1] + (total,), jnp.float32),
            values_in,
            head_index * values_in.shape[-1],
            values_in.ndim - 1,
        )

    small = [
        first_line / first_gain,
        grad_second[0],
        jnp.concatenate(
            [own_part(grad_taps[:, :inner_columns], mamba_width), grad_taps[:, inner_columns:]],
            axis=1,
        ),
        jnp.concatenate(
            [own_part(grad_shift[:inner_columns], mamba_width), grad_shift[inner_columns:]]
        ),
        own_part(grad_step_shift, MH),
        own_part(grad_rate, MH),
        own_part(grad_skip, MH),
    ]
    line = jnp.concatenate([part.reshape(-1) for part in small])
    line = jnp.pad(line, (0, -line.shape[0] % 1024)).reshape(-1, 128)
    line = summed_over(summed_over(line, "head"), "blk").reshape(-1)
    summed_small = []
    at = 0
    for part in small:
        summed_small.append(line[at : at + part.size].reshape(part.shape))
        at += part.size
    return (
        block_output[None],
        grad_input[None],
        grad_proj_weight,
        grad_mix_weight,
        grad_ffn_weight,
        grad_down.astype(jnp.float32),
        *summed_small,
    )


def own_first(chunks, mine, order=(0, 1, 2, 3)):
    return [lax.dynamic_index_in_dim(chunks, jnp.bitwise_xor(mine, d), 0, False) for d in order]


def solution(mesh):
    placed = (
        P("blk", "head", None),
        P("blk", "head", None),
        P("blk", None),
        P(("head", "blk"), None),
        P(("head", "blk"), None),
        P(("head", "blk"), None),
        P(("head", "blk"), None),
        P(),
        P(),
        P(),
        P(),
        P(),
        P(),
        P(),
    )
    return jax.shard_map(
        per_device,
        mesh=mesh,
        in_specs=placed,
        out_specs=(
            P("blk", "head", None),
            P("blk", "head", None),
            P(("head", "blk"), None),
            P(("head", "blk"), None),
            P(("head", "blk"), None),
            P(("head", "blk"), None),
            P(),
            P(),
            P(),
            P(),
            P(),
            P(),
            P(),
        ),
        check_vma=False,
    )
```

```python
import math
from functools import partial

import jax
import jax.numpy as jnp
from jax import lax
from jax.experimental import pallas as pl
from jax.experimental.pallas import tpu as pltpu
from jax.sharding import PartitionSpec as P

D = 2048
QH = 8
KVH = 2
HD = 128
MH = 48
MP = 64
NS = 256
FF = 4096
KW = 4


epsilon = 1e-05
rope_base = 100000000000.0
masked_score = -1e30


def after(value, *others):
    return lax.optimization_barrier((value, *others))[0]


def passed_along(shard, axis, by):
    peers = lax.axis_size(axis)
    pairs = [(i, i + by) for i in range(peers) if 0 <= i + by < peers]
    return lax.ppermute(shard, axis, pairs)


def ring_of(axis):
    peers = lax.axis_size(axis)
    if peers != 8:
        return list(range(peers))
    return [0, 2, 4, 6, 7, 5, 3, 1]


def gather_blocks(shard):
    return lax.all_gather(shard, "blk", axis=0, tiled=True, axis_index_groups=[ring_of("blk")])


def scatter_blocks(partial_sums):
    return lax.psum_scatter(
        partial_sums,
        "blk",
        scatter_dimension=0,
        tiled=True,
        axis_index_groups=[ring_of("blk")],
    )


def from_head(shard, distance):
    peers = lax.axis_size("head")
    return lax.ppermute(shard, "head", [(i, i ^ distance) for i in range(peers)])


def gather_heads(shard):
    across = from_head(shard, 2)
    return [shard, across, from_head(shard, 1), from_head(across, 1)]


def in_head_order(parts):
    mine = lax.axis_index("head")
    stacked = jnp.stack([parts[0], parts[2], parts[1], parts[3]])
    return [
        lax.dynamic_index_in_dim(stacked, jnp.bitwise_xor(mine, j), 0, False) for j in range(4)
    ]


def scatter_pairs(own, other, middle=jnp.float32):
    rows = own.shape[0] // 2
    got = from_head(other.astype(middle), 1).astype(jnp.float32)
    far = from_head((own[rows:] + got[rows:]).astype(low), 2)
    return own[:rows] + got[:rows] + far.astype(jnp.float32)


def swap_heads(pieces):
    return lax.all_to_all(pieces, "head", split_axis=0, concat_axis=0, tiled=True)


def mixer_place():
    heads, ring = lax.axis_size("head"), ring_of("blk")
    peers = heads * len(ring)
    rows = (QH * HD + MH * MP) // peers
    query_blocks, mamba_blocks = QH * HD // rows // heads, MH * MP // rows // heads
    pairs = []
    for r in range(peers):
        if r < query_blocks * heads:
            group, slot = divmod(r, query_blocks)
        else:
            group, slot = divmod(r - query_blocks * heads, mamba_blocks)
            slot += query_blocks
        pairs.append((r, group * len(ring) + ring[slot]))
    return pairs


kv_begin = QH * HD
z_begin = kv_begin + 2 * KVH * HD
x_begin = z_begin + MH * MP
b_begin = x_begin + MH * MP
dt_begin = b_begin + 2 * NS
query_columns = QH * HD // 4
inner_columns = MH * MP // 4
bc_columns = 2 * NS // 4
step_heads = MH // 4
step_at = inner_columns + bc_columns
kv_at = step_at + 128
conv_columns = kv_at + HD
rest_columns = query_columns + inner_columns


def column_parts(head):
    conv = [
        (x_begin + head * inner_columns, 0, inner_columns),
        (b_begin + head * bc_columns, inner_columns, bc_columns),
        (kv_begin + (head % 2) * KVH * HD + (head // 2) * HD, kv_at, HD),
    ]
    rest = [
        (head * query_columns, 0, query_columns),
        (z_begin + head * inner_columns, query_columns, inner_columns),
    ]
    return conv, rest


def pack_in(place_ref, weight_ref, conv_ref, rest_ref, tail_ref):
    tail_ref[...] = jnp.zeros_like(tail_ref)
    tail_ref[:, :MH] = weight_ref[:, dt_begin : dt_begin + MH]
    last = tail_ref[...]
    lane = iota(last.shape, 1)
    for head in range(4):
        for parts, ref in zip(column_parts(head), (conv_ref, rest_ref)):
            for begin, at, size in parts:
                ref[head, :, at : at + size] = weight_ref[:, begin : begin + size].astype(low)
        steps = pltpu.roll(last, lanes - step_heads * head, 1) if head else last
        conv_ref[head, :, step_at:kv_at] = jnp.where(lane < step_heads, steps, 0.0).astype(low)


def unpack_in(place_ref, conv_ref, rest_ref, out_ref):
    total = jnp.zeros((out_ref.shape[0], lanes), jnp.float32)
    lane = iota(total.shape, 1)
    for head in range(4):
        for parts, ref in zip(column_parts(head), (conv_ref, rest_ref)):
            for begin, at, size in parts:
                out_ref[:, begin : begin + size] = ref[head, :, at : at + size].astype(jnp.float32)
        steps = conv_ref[head, :, step_at:kv_at].astype(jnp.float32)
        steps = jnp.where(lane < step_heads, steps, 0.0)
        total = total + (pltpu.roll(steps, step_heads * head, 1) if head else steps)
    out_ref[:, dt_begin : dt_begin + MH] = total[:, :MH]


def ffn_moves(ring):
    unit = FF // (4 * len(ring))
    return unit, [
        (
            head,
            half * FF + (head * len(ring) + k) * unit,
            half * (FF // 4) + i * unit,
        )
        for half in range(2)
        for head in range(4)
        for i, k in enumerate(ring)
    ]


def pack_ffn(place_ref, weight_ref, out_ref, *, ring):
    unit, moves = ffn_moves(ring)
    for head, begin, at in moves:
        out_ref[head, :, at : at + unit] = weight_ref[:, begin : begin + unit].astype(low)


def unpack_ffn(place_ref, in_ref, out_ref, *, ring):
    unit, moves = ffn_moves(ring)
    for head, begin, at in moves:
        out_ref[:, begin : begin + unit] = in_ref[head, :, at : at + unit].astype(jnp.float32)


def inverse_rms(values_in):
    return lax.rsqrt(jnp.mean(values_in * values_in, axis=1, keepdims=True) + epsilon)


def feature_moves(ring):
    piece = D // 4 // len(ring)
    return piece, [
        ((e * len(ring) + k) * piece, (4 * i + e) * piece)
        for e in range(4)
        for i, k in enumerate(ring)
    ]


def whole_lanes(begin, size):
    return pl.ds(pl.multiple_of(begin, 128), size)


def norm_one(place_ref, own, across, beside, both, gain_ref, out_ref, line_ref, *, ring):
    rows = own.shape[0]
    piece, moves = feature_moves(ring)
    for distance, ref in ((0, own), (2, across), (1, beside), (3, both)):
        x = ref[...].astype(jnp.float32)
        line_ref[...] = (x * inverse_rms(x) * gain_ref[...]).astype(low)
        there = jnp.bitwise_xor(place_ref[0], distance) * rows
        there = pl.ds(pl.multiple_of(there, rows), rows)
        for source, at in moves:
            out_ref[there, at : at + piece] = line_ref[:, source : source + piece]


def norm_two(place_ref, mixed_ref, tokens_ref, gain_ref, hidden_ref, out_ref, line_ref, *, ring):
    hidden = tokens_ref[...].astype(jnp.float32) + mixed_ref[...]
    hidden_ref[...] = hidden
    line_ref[...] = (hidden * inverse_rms(hidden) * gain_ref[...]).astype(low)
    piece, moves = feature_moves(ring)
    for source, at in moves:
        out_ref[:, at : at + piece] = line_ref[:, source : source + piece]


def back_two(
    place_ref, grad_ref, hidden_ref, cotangent_ref, gain_ref, out_ref, low_ref, sum_ref, plain_ref,
    *, ring,
):
    piece, moves = feature_moves(ring)
    for source, at in moves:
        plain_ref[:, source : source + piece] = grad_ref[:, at : at + piece]
    grad = plain_ref[...]
    hidden = hidden_ref[...]
    inverse = inverse_rms(hidden)
    scaled = grad * gain_ref[...]
    total = (
        cotangent_ref[...].astype(jnp.float32)
        + inverse * scaled
        - hidden * (inverse * inverse * inverse * jnp.mean(scaled * hidden, axis=1, keepdims=True))
    )
    out_ref[...] = total
    low_ref[...] = total.astype(low)
    sum_ref[...] = jnp.broadcast_to(
        jnp.sum(grad * hidden * inverse, axis=0, keepdims=True), sum_ref.shape
    )


def back_one(
    place_ref, grad_ref, tokens_ref, hidden_ref, gain_ref, out_ref, plain_ref, *, ring
):
    piece, moves = feature_moves(ring)
    for source, at in moves:
        plain_ref[:, source : source + piece] = grad_ref[:, at : at + piece]
    grad = plain_ref[...]
    x = tokens_ref[...].astype(jnp.float32)
    inverse = inverse_rms(x)
    scaled = grad * gain_ref[...]
    out_ref[...] = (
        hidden_ref[...]
        + inverse * scaled
        - x * (inverse * inverse * inverse * jnp.mean(scaled * x, axis=1, keepdims=True))
    ).astype(low)


def turned(values_in, cosine, sine):
    return values_in * cosine + pltpu.roll(values_in, HD // 2, 1) * sine


def rope_kv(place_ref, in_ref, cosine_ref, sine_ref, out_ref):
    kv = in_ref[...]
    kv = jnp.where(place_ref[1] == 0, turned(kv, cosine_ref[...], sine_ref[...]), kv).astype(low)
    for k in range(out_ref.shape[0]):
        out_ref[k] = kv


def rope_query(place_ref, in_ref, cosine_ref, sine_ref, query_ref, gate_ref):
    cosine, sine = cosine_ref[...], sine_ref[...]
    for begin in range(0, query_columns, HD):
        query_ref[:, begin : begin + HD] = turned(
            in_ref[:, begin : begin + HD], cosine, sine
        ).astype(low)
    gate_ref[...] = in_ref[:, query_columns:].astype(low)


def query_back(place_ref, query_ref, gate_ref, cosine_ref, sine_ref, out_ref):
    cosine, sine = cosine_ref[...], -sine_ref[...]
    for begin in range(0, query_columns, HD):
        rounded = query_ref[:, begin : begin + HD].astype(low).astype(jnp.float32)
        out_ref[:, begin : begin + HD] = turned(rounded, cosine, sine).astype(low)
    out_ref[:, query_columns:] = gate_ref[...]


def join_conv(place_ref, inner_ref, own, across, beside, both, out_ref):
    out_ref[:, :inner_columns] = inner_ref[...].astype(low)
    for distance, ref in ((0, own), (2, across), (1, beside), (3, both)):
        at = inner_columns + jnp.bitwise_xor(place_ref[0], distance) * lanes
        out_ref[:, whole_lanes(at, lanes)] = ref[...]


def conv_joined(
    place_ref, inner_ref, near_ref, far_ref, step_ref, cosine_ref, sine_ref, kv_ref, out_ref
):
    out_ref[:, :inner_columns] = inner_ref[...].astype(low)
    out_ref[:, inner_columns:step_at] = (near_ref[...] + far_ref[...].astype(jnp.float32)).astype(low)
    out_ref[:, step_at:kv_at] = step_ref[...].astype(low)
    kv = kv_ref[0].astype(jnp.float32)
    for k in range(1, kv_ref.shape[0]):
        kv = kv + kv_ref[k].astype(jnp.float32)
    out_ref[:, kv_at:] = jnp.where(
        place_ref[1] == 0, turned(kv, cosine_ref[...], -sine_ref[...]), kv
    ).astype(low)


def relative_order(place_ref, first_ref, second_ref, first_out, second_out):
    for at, distance in enumerate((0, 2, 1, 3)):
        there = jnp.bitwise_xor(place_ref[0], distance) * chunk
        there = pl.ds(pl.multiple_of(there, chunk), chunk)
        rows = slice(at * chunk, (at + 1) * chunk)
        first_out[rows, :] = first_ref[there, :]
        second_out[rows, :] = second_ref[there, :]


def outer_grad(left_side, grad_side):
    return lax.dot_general(
        left_side, grad_side, (((0,), (0,)), ((), ())), preferred_element_type=jnp.float32
    )


def times_transposed(grad_side, weight):
    return lax.dot_general(
        grad_side, weight, (((1,), (1,)), ((), ())), preferred_element_type=jnp.float32
    )


chunk = 128
lanes = 128
low = jnp.bfloat16
exact = lax.Precision.HIGHEST


def dot_nn(a, b, precision=None):
    return lax.dot_general(
        a, b, (((1,), (0,)), ((), ())), precision=precision, preferred_element_type=jnp.float32
    )


def dot_nt(a, b):
    return lax.dot_general(a, b, (((1,), (1,)), ((), ())), preferred_element_type=jnp.float32)


def dot_tn(a, b):
    return lax.dot_general(a, b, (((0,), (0,)), ((), ())), preferred_element_type=jnp.float32)


def iota(shape, dim):
    return lax.broadcasted_iota(jnp.int32, shape, dim)


def spread(per_head, pair):
    rows = per_head.shape[0]
    first = per_head[:, 2 * pair : 2 * pair + 1]
    second = per_head[:, 2 * pair + 1 : 2 * pair + 2]
    return jnp.where(iota((rows, lanes), 1) < MP, first, second)


def head_sums(products, pair):
    mine = 2 * pair + (iota((lanes, lanes), 0) >= MP).astype(jnp.int32)
    ones = (mine == iota((lanes, lanes), 1)).astype(jnp.float32)
    return dot_nn(products, ones, exact)


def chunk_terms(decay, segment, segment_before):
    lower = iota((chunk, chunk), 0) >= iota((chunk, chunk), 1)
    cumulative = dot_nn(lower.astype(jnp.float32), decay, exact)
    total = cumulative[chunk - 1 :, :]
    segment_end = segment[chunk - 1 :, :]
    related = lower & (segment == segment.T)
    entering = jnp.where(segment == segment_before, jnp.exp(cumulative), 0.0)
    ending = jnp.where(segment == segment_end, jnp.exp(total - cumulative), 0.0)
    whole = jnp.where(segment_end == segment_before, jnp.exp(total), 0.0)
    return cumulative, cumulative.T, related, entering, ending, whole, total, segment_end


def decays_of(cumulative, transposed, related, head):
    apart = cumulative[:, head : head + 1] - transposed[head : head + 1, :]
    return jnp.exp(jnp.where(related, apart, masked_score))


def row_factor(whole, pair, width):
    first = whole[:, 2 * pair : 2 * pair + 1]
    second = whole[:, 2 * pair + 1 : 2 * pair + 2]
    return jnp.where(iota((lanes, width), 0) < MP, first, second)


def chunk_rows(index):
    return pl.ds(pl.multiple_of(index * chunk, chunk), chunk)


def pack_states(state_ref, factor, out_ref):
    blocks, rows, width = out_ref.shape
    share = rows - extra_rows
    row = iota((extra_rows, width), 0)
    for k in range(blocks):
        extra = jnp.zeros((extra_rows, width), jnp.float32)
        for e in range(4):
            head = k * share // MP + e
            if head * MP < state_ref.shape[0]:
                whole = factor[:, head : head + 1]
                rough = whole.astype(low).astype(jnp.float32)
                extra = jnp.where(row == e, rough, extra)
                extra = jnp.where(row == 4 + e, whole - rough, extra)
        out_ref[k, :extra_rows, :] = extra.astype(low)
        out_ref[k, extra_rows:, :] = state_ref[k * share : (k + 1) * share, :].astype(low)


extra_rows = 16


def chain(place_ref, got_ref, out_ref, backwards):
    blocks, rows, width = got_ref.shape
    share = rows - extra_rows
    row = iota((share, width), 0) + lax.rem(place_ref[4] * share, MP)
    state = jnp.zeros((share, width), jnp.float32)
    for k in range(blocks - 1, -1, -1) if backwards else range(blocks):
        out_ref[k] = state.astype(low)
        extra = got_ref[k, :extra_rows, :].astype(jnp.float32)
        factor = extra[0:1, :] + extra[4:5, :]
        for e in range(1, 4):
            factor = jnp.where(row >= e * MP, extra[e : e + 1, :] + extra[4 + e : 5 + e, :], factor)
        state = factor * state + got_ref[k, extra_rows:, :].astype(jnp.float32)


def ssd_local(
    place_ref, x_ref, b_ref, c_ref, step_ref, decay_ref, seg_ref,
    y_ref, sent_ref, enter_ref, fac_ref, state_ref,
):
    pairs = x_ref.shape[1] // lanes
    state_ref[...] = jnp.zeros_like(state_ref)

    def body(index, carry):
        segment_before, base = carry
        rows = chunk_rows(index)
        segment = seg_ref[rows, :]
        cumulative, transposed, related, entering, ending, whole, total, segment_end = chunk_terms(
            decay_ref[rows, :], segment, segment_before
        )
        enter_ref[rows, :] = jnp.where(segment == 0.0, jnp.exp(base + cumulative), 0.0)
        into = b_ref[rows, :].astype(low)
        outof = c_ref[rows, :].astype(low)
        step = step_ref[rows, :]
        scores = dot_nt(outof, into)
        left = iota((chunk, lanes), 1) < MP
        for pair in range(pairs):
            cols = slice(pair * lanes, (pair + 1) * lanes)
            taken = x_ref[rows, cols] * spread(step, pair)
            taken_low = taken.astype(low)
            parts = []
            for head in (2 * pair, 2 * pair + 1):
                weights = decays_of(cumulative, transposed, related, head) * scores
                parts.append(dot_nn(weights.astype(low), taken_low))
            state = state_ref[cols, :]
            y_ref[rows, cols] = jnp.where(left, parts[0], parts[1]) + spread(
                entering, pair
            ) * dot_nt(outof, state.astype(low))
            kept = (taken * spread(ending, pair)).astype(low)
            state_ref[cols, :] = row_factor(whole, pair, state.shape[1]) * state + dot_tn(
                kept, into
            )
        return segment_end, base + total

    start = jnp.zeros((1, lanes), jnp.float32)
    segment_end, base = lax.fori_loop(0, x_ref.shape[0] // chunk, body, (start, start))
    factor = jnp.where(segment_end == 0.0, jnp.exp(base), 0.0)
    fac_ref[...] = jnp.broadcast_to(factor, fac_ref.shape)
    pack_states(state_ref, factor, sent_ref)


def relative_rows(place_ref, index):
    distance = jnp.bitwise_xor(place_ref[0], index)
    at = (distance % 2) * 2 + distance // 2
    return pl.ds(pl.multiple_of(at * chunk, chunk), chunk)


def ssd_finish(
    place_ref, y_ref, enter_ref, c_ref, state_ref, x_ref, z_ref, skip_ref, attended_ref,
    ssd_ref, mixer_ref,
):
    pairs = x_ref.shape[1] // lanes
    width = attended_ref.shape[1]

    def body(index, carry):
        rows = chunk_rows(index)
        there = relative_rows(place_ref, index)
        outof = c_ref[rows, :].astype(low)
        entering = enter_ref[rows, :]
        mixer_ref[there, :width] = attended_ref[rows, :].astype(low)
        for pair in range(pairs):
            cols = slice(pair * lanes, (pair + 1) * lanes)
            ssd = y_ref[rows, cols] + spread(entering, pair) * dot_nt(outof, state_ref[cols, :])
            ssd_ref[rows, cols] = ssd
            gate = z_ref[rows, cols].astype(jnp.float32)
            total = ssd + skip_ref[:, cols] * x_ref[rows, cols]
            mixer_ref[there, width + pair * lanes : width + (pair + 1) * lanes] = (
                total * gate / (1.0 + jnp.exp(-gate))
            ).astype(low)
        return carry

    lax.fori_loop(0, x_ref.shape[0] // chunk, body, 0)


def ssd_gate_back(
    place_ref, grad_ref, z_ref, ssd_ref, x_ref, skip_ref, enter_ref, c_ref, fac_ref,
    dy_ref, dz_ref, sent_ref, dskip_ref, datt_ref, dstate_ref,
):
    pairs = x_ref.shape[1] // lanes
    width = datt_ref.shape[1]
    dstate_ref[...] = jnp.zeros_like(dstate_ref)
    dskip_ref[...] = jnp.zeros_like(dskip_ref)

    def body(index, carry):
        rows = chunk_rows(index)
        there = relative_rows(place_ref, index)
        outof = c_ref[rows, :].astype(low)
        entering = enter_ref[rows, :]
        datt_ref[rows, :] = grad_ref[there, :width]
        for pair in range(pairs):
            cols = slice(pair * lanes, (pair + 1) * lanes)
            gate = z_ref[rows, cols].astype(jnp.float32)
            sigmoid = 1.0 / (1.0 + jnp.exp(-gate))
            grad = grad_ref[
                there, width + pair * lanes : width + (pair + 1) * lanes
            ].astype(jnp.float32)
            x = x_ref[rows, cols]
            total = ssd_ref[rows, cols] + skip_ref[:, cols] * x
            dz_ref[rows, cols] = (
                grad * total * sigmoid * (1.0 + gate * (1.0 - sigmoid))
            ).astype(low)
            dy = grad * gate * sigmoid
            dy_ref[rows, cols] = dy
            dskip_ref[:, cols] += jnp.broadcast_to(
                jnp.sum(dy * x, axis=0, keepdims=True), (dskip_ref.shape[0], lanes)
            )
            dstate_ref[cols, :] += dot_tn((dy * spread(entering, pair)).astype(low), outof)
        return carry

    lax.fori_loop(0, x_ref.shape[0] // chunk, body, 0)
    pack_states(dstate_ref, fac_ref[:1, :], sent_ref)


def ssd_back(
    place_ref, x_ref, b_ref, c_ref, step_ref, decay_ref, seg_ref, dy_ref, ssd_ref, skip_ref, state_ref, later_ref,
    dx_ref, db_ref, dc_ref, dstep_ref, ddecay_ref, states, grads,
):
    pairs = x_ref.shape[1] // lanes
    chunks = x_ref.shape[0] // chunk
    zero_row = jnp.zeros((1, lanes), jnp.float32)

    def before(index):
        rows = pl.ds(pl.multiple_of(jnp.maximum(index - 1, 0) * chunk, chunk), chunk)
        return jnp.where(index == 0, 0.0, seg_ref[rows, :][chunk - 1 :, :])

    states[0] = state_ref[...].astype(jnp.float32)

    def forward(index, carry):
        rows = chunk_rows(index)
        _, _, _, _, ending, whole, _, _ = chunk_terms(
            decay_ref[rows, :], seg_ref[rows, :], before(index)
        )
        into = b_ref[rows, :].astype(low)
        step = step_ref[rows, :]
        for pair in range(pairs):
            cols = slice(pair * lanes, (pair + 1) * lanes)
            kept = (x_ref[rows, cols] * spread(step, pair) * spread(ending, pair)).astype(low)
            state = states[index, cols, :]
            states[index + 1, cols, :] = row_factor(
                whole, pair, state.shape[1]
            ) * state + dot_tn(kept, into)
        return carry

    lax.fori_loop(0, chunks, forward, 0)
    grads[...] = later_ref[...].astype(jnp.float32)
    last = jnp.zeros((8, lanes), jnp.float32)
    for pair in range(pairs):
        cols = slice(pair * lanes, (pair + 1) * lanes)
        product = grads[cols, :] * states[chunks, cols, :]
        along = lax.dot_general(
            jnp.ones((8, product.shape[1]), jnp.float32),
            product,
            (((1,), (1,)), ((), ())),
            precision=exact,
            preferred_element_type=jnp.float32,
        )
        last = last + head_sums(along, pair)

    def backward(at, carry):
        index = chunks - 1 - at
        rows = chunk_rows(index)
        cumulative, transposed, related, entering, ending, whole, _, _ = chunk_terms(
            decay_ref[rows, :], seg_ref[rows, :], before(index)
        )
        into = b_ref[rows, :].astype(low)
        outof = c_ref[rows, :].astype(low)
        step = step_ref[rows, :]
        scores = dot_nt(outof, into)
        left = iota((chunk, lanes), 1) < MP
        grad_scores = jnp.zeros((chunk, chunk), jnp.float32)
        grad_into = jnp.zeros((chunk, b_ref.shape[1]), jnp.float32)
        grad_outof = jnp.zeros((chunk, b_ref.shape[1]), jnp.float32)
        grad_cum = jnp.zeros((chunk, lanes), jnp.float32)
        grad_step = jnp.zeros((chunk, lanes), jnp.float32)
        for pair in range(pairs):
            cols = slice(pair * lanes, (pair + 1) * lanes)
            x = x_ref[rows, cols]
            step_pair = spread(step, pair)
            taken = x * step_pair
            taken_low = taken.astype(low)
            dy = dy_ref[rows, cols]
            dy_low = dy.astype(low)
            parts = []
            for half, head in enumerate((2 * pair, 2 * pair + 1)):
                decays = decays_of(cumulative, transposed, related, head)
                parts.append(dot_tn((decays * scores).astype(low), dy_low))
                own = jnp.where(left if half == 0 else ~left, dy_low, jnp.zeros_like(dy_low))
                grad_scores = grad_scores + decays * dot_nt(own, taken_low)
            later = grads[cols, :]
            later_low = later.astype(low)
            ending_pair = spread(ending, pair)
            grad_taken = jnp.where(left, parts[0], parts[1]) + ending_pair * dot_nt(
                into, later_low
            )
            grad_into = grad_into + dot_nn((taken * ending_pair).astype(low), later_low)
            dy_enter = (dy * spread(entering, pair)).astype(low)
            grad_outof = grad_outof + dot_nn(dy_enter, states[index, cols, :].astype(low))
            grads[cols, :] = row_factor(whole, pair, later.shape[1]) * later + dot_tn(
                dy_enter, outof
            )
            grad_cum = grad_cum + head_sums(dy * ssd_ref[rows, cols] - taken * grad_taken, pair)
            grad_step = grad_step + head_sums(x * grad_taken, pair)
            dx_ref[rows, cols] = step_pair * grad_taken + skip_ref[:, cols] * dy
        grad_scores_low = grad_scores.astype(low)
        db_ref[rows, :] = grad_into + dot_tn(grad_scores_low, outof)
        dc_ref[rows, :] = grad_outof + dot_nn(grad_scores_low, into)
        dstep_ref[rows, :] = grad_step
        upper = (iota((chunk, chunk), 0) <= iota((chunk, chunk), 1)).astype(jnp.float32)
        ddecay_ref[rows, :] = dot_nn(upper, grad_cum, exact) + carry
        return carry + jnp.sum(grad_cum, axis=0, keepdims=True)

    lax.fori_loop(0, chunks, backward, last[:1, :] + zero_row)


def needed_and_plain(place_ref, block, span):
    mine, earliest, latest = place_ref[0], place_ref[1], place_ref[2]
    needed = (block <= mine) & ((block + 1) * span > earliest)
    return needed, (block < mine) & (block * span >= latest)


def visible_keys(place_ref, first_ref, block, span):
    key_pos = block * span + iota((span, span), 1)
    query_pos = place_ref[0] * span + iota((span, span), 0)
    return (key_pos <= query_pos) & (key_pos >= first_ref[:, :1])


def attend(place_ref, q_ref, first_ref, k_ref, v_ref, out_ref, lse_ref, top, total, summed):
    block = pl.program_id(0)
    span = q_ref.shape[0]
    heads = q_ref.shape[1] // HD

    @pl.when(block == 0)
    def _():
        top[...] = jnp.full_like(top, masked_score)
        total[...] = jnp.zeros_like(total)
        summed[...] = jnp.zeros_like(summed)

    def one(masked):
        keys = k_ref[0]
        values = v_ref[0]
        if masked:
            visible = visible_keys(place_ref, first_ref, block, span)
        for head in range(heads):
            cols = slice(head * HD, (head + 1) * HD)
            scores = dot_nt(q_ref[:, cols], keys) * HD**-0.5
            if masked:
                scores = jnp.where(visible, scores, masked_score)
            old_top = top[head][:, :1]
            new_top = jnp.maximum(old_top, jnp.max(scores, axis=1, keepdims=True))
            weights = jnp.exp(scores - new_top)
            if masked:
                weights = jnp.where(visible, weights, 0.0)
            scale = jnp.exp(old_top - new_top)
            total[head] = total[head] * scale + jnp.sum(weights, axis=1, keepdims=True)
            top[head] = jnp.broadcast_to(new_top, (span, lanes))
            summed[head] = summed[head] * scale + dot_nn(weights.astype(low), values)

    needed, plain = needed_and_plain(place_ref, block, span)
    pl.when(needed & plain)(lambda: one(False))
    pl.when(needed & jnp.logical_not(plain))(lambda: one(True))

    @pl.when(block == pl.num_programs(0) - 1)
    def _():
        for head in range(heads):
            cols = slice(head * HD, (head + 1) * HD)
            out_ref[:, cols] = summed[head] / total[head]
            lse_ref[head] = top[head] + jnp.log(total[head])


def attend_back(
    place_ref, q_ref, first_ref, k_ref, v_ref, grad_ref, out_ref, lse_ref, dq_ref, dk_ref, dv_ref
):
    block = pl.program_id(0)
    span = q_ref.shape[0]
    heads = q_ref.shape[1] // HD

    @pl.when(block == 0)
    def _():
        dq_ref[...] = jnp.zeros_like(dq_ref)

    def one(masked):
        keys = k_ref[0]
        values = v_ref[0]
        if masked:
            visible = visible_keys(place_ref, first_ref, block, span)
        grad_keys = jnp.zeros(keys.shape, jnp.float32)
        grad_values = jnp.zeros(keys.shape, jnp.float32)
        for head in range(heads):
            cols = slice(head * HD, (head + 1) * HD)
            query = q_ref[:, cols]
            grad = grad_ref[:, cols]
            delta = jnp.sum(
                grad.astype(jnp.float32) * out_ref[:, cols], axis=1, keepdims=True
            )
            scores = dot_nt(query, keys) * HD**-0.5
            if masked:
                scores = jnp.where(visible, scores, masked_score)
            weights = jnp.exp(scores - lse_ref[head][:, :1])
            changes = weights * (dot_nt(grad, values) - delta)
            weights_low = weights.astype(low)
            changes_low = (changes * HD**-0.5).astype(low)
            grad_values = grad_values + dot_tn(weights_low, grad)
            grad_keys = grad_keys + dot_tn(changes_low, query)
            dq_ref[:, cols] += dot_nn(changes_low, keys)
        dk_ref[0] = grad_keys.astype(low)
        dv_ref[0] = grad_values.astype(low)

    needed, plain = needed_and_plain(place_ref, block, span)
    pl.when(needed & plain)(lambda: one(False))
    pl.when(needed & jnp.logical_not(plain))(lambda: one(True))

    @pl.when(jnp.logical_not(needed))
    def _():
        dk_ref[...] = jnp.zeros_like(dk_ref)
        dv_ref[...] = jnp.zeros_like(dv_ref)


def shaped(shape, kind):
    return jax.ShapeDtypeStruct(shape, kind)


def call(kernel, outputs, place, operands, after=(), scratch=(), flops=10**6):
    count, skipped = len(operands), len(operands) + len(after)
    sizes = sum(math.prod(a.shape) * a.dtype.itemsize for a in (*operands, *outputs))

    def body(place_ref, *refs):
        kernel(place_ref, *refs[:count], *refs[skipped:])

    return pl.pallas_call(
        body,
        out_shape=outputs,
        in_specs=[pl.BlockSpec(memory_space=pltpu.SMEM)]
        + [pl.BlockSpec(memory_space=pltpu.VMEM)] * count
        + [pl.BlockSpec(memory_space=pl.ANY)] * len(after),
        out_specs=[pl.BlockSpec(memory_space=pltpu.VMEM)] * len(outputs),
        scratch_shapes=list(scratch),
        compiler_params=pltpu.CompilerParams(vmem_limit_bytes=kernel_memory),
        cost_estimate=pl.CostEstimate(flops=flops, bytes_accessed=sizes, transcendentals=0),
    )(place, *operands, *after)


kernel_memory = 44 * 1024 * 1024


def attention(place, query, first_visible, keys, values, after):
    away, span = keys.shape[0], query.shape[0]
    heads = query.shape[1] // HD
    same = lambda d, place: (0, 0)
    block = lambda d, place: (d, 0, 0)
    def body(*refs):
        attend(*refs[:5], *refs[5 + len(after) :])

    return pl.pallas_call(
        body,
        grid_spec=pltpu.PrefetchScalarGridSpec(
            num_scalar_prefetch=1,
            grid=(away,),
            in_specs=[
                pl.BlockSpec(query.shape, same),
                pl.BlockSpec(first_visible.shape, same),
                pl.BlockSpec((1, span, HD), block),
                pl.BlockSpec((1, span, HD), block),
            ]
            + [pl.BlockSpec(memory_space=pl.ANY)] * len(after),
            out_specs=[
                pl.BlockSpec(query.shape, same),
                pl.BlockSpec((heads, span, lanes), lambda d, place: (0, 0, 0)),
            ],
            scratch_shapes=[
                pltpu.VMEM((heads, span, lanes), jnp.float32),
                pltpu.VMEM((heads, span, lanes), jnp.float32),
                pltpu.VMEM((heads, span, HD), jnp.float32),
            ],
        ),
        out_shape=[
            shaped(query.shape, jnp.float32),
            shaped((heads, span, lanes), jnp.float32),
        ],
        compiler_params=pltpu.CompilerParams(vmem_limit_bytes=kernel_memory),
        cost_estimate=pl.CostEstimate(
            flops=20 * 10**9, bytes_accessed=4 * 10**6, transcendentals=0
        ),
    )(place, query, first_visible, keys, values, *after)


def attention_back(place, query, first_visible, keys, values, grad, out, lse, after):
    away, span = keys.shape[0], query.shape[0]
    same = lambda d, place: (0, 0)
    block = lambda d, place: (d, 0, 0)
    def body(*refs):
        attend_back(*refs[:8], *refs[8 + len(after) :])

    return pl.pallas_call(
        body,
        grid_spec=pltpu.PrefetchScalarGridSpec(
            num_scalar_prefetch=1,
            grid=(away,),
            in_specs=[
                pl.BlockSpec(query.shape, same),
                pl.BlockSpec(first_visible.shape, same),
                pl.BlockSpec((1, span, HD), block),
                pl.BlockSpec((1, span, HD), block),
                pl.BlockSpec(query.shape, same),
                pl.BlockSpec(query.shape, same),
                pl.BlockSpec(lse.shape, lambda d, place: (0, 0, 0)),
            ]
            + [pl.BlockSpec(memory_space=pl.ANY)] * len(after),
            out_specs=[
                pl.BlockSpec(query.shape, same),
                pl.BlockSpec((1, span, HD), block),
                pl.BlockSpec((1, span, HD), block),
            ],
        ),
        out_shape=[
            shaped(query.shape, jnp.float32),
            shaped(keys.shape, low),
            shaped(keys.shape, low),
        ],
        compiler_params=pltpu.CompilerParams(vmem_limit_bytes=kernel_memory),
        cost_estimate=pl.CostEstimate(
            flops=30 * 10**9, bytes_accessed=4 * 10**6, transcendentals=0
        ),
    )(place, query, first_visible, keys, values, grad, out, lse, *after)


def conv_act(extended, conv_taps, conv_shift, keep_masks):
    length = keep_masks[0].shape[0]
    result = conv_shift + conv_taps[0] * extended[KW - 1 :]
    for lag_index in range(1, KW):
        begin = KW - 1 - lag_index
        result = (
            result
            + conv_taps[lag_index]
            * keep_masks[lag_index][:, None]
            * extended[begin : begin + length]
        )
    return jax.nn.silu(result)


def step_and_decay(step_raw, step_shift, decay_rate):
    step_size = jax.nn.softplus(step_raw + step_shift)
    return step_size, -step_size * jnp.exp(decay_rate)


def in_lanes(per_head):
    return jnp.pad(per_head, ((0, 0), (0, lanes - per_head.shape[1])))


def summed_over(values_in, axis):
    peers = lax.axis_size(axis)
    by = 1
    while by < peers:
        values_in = values_in + lax.ppermute(values_in, axis, [(i, i ^ by) for i in range(peers)])
        by *= 2
    return values_in


def per_device(
    block_input,
    out_cotangent,
    start_flags,
    in_weight,
    out_weight,
    gate_up_weight,
    down_weight,
    first_gain,
    second_gain,
    conv_weight,
    conv_bias,
    step_bias,
    decay_log,
    skip_gain,
):
    head_count = lax.axis_size("head")
    blocks = lax.axis_size("blk")
    head_index = lax.axis_index("head")
    block_index = lax.axis_index("blk")
    ring = ring_of("blk")
    tokens = block_input[0]
    cotangent = out_cotangent[0]
    row_count = tokens.shape[0]
    span_rows = row_count * head_count
    mamba_width = MH * MP
    even = head_index % 2 == 0
    out_pairs = mixer_place()
    place = jnp.stack(
        [head_index, head_index % 2, 0, 0, block_index, 0, 0, 0]
    ).astype(jnp.int32)

    rows_in = in_weight.shape[0]
    flags_all = summed_over(
        lax.dynamic_update_slice_in_dim(
            jnp.zeros((blocks * span_rows,), jnp.int32),
            start_flags[0],
            block_index * span_rows,
            0,
        ),
        "blk",
    )
    packed_conv, packed_rest = call(
        pack_in,
        [
            shaped((4, rows_in, conv_columns), low),
            shaped((4, rows_in, rest_columns), low),
        ],
        place,
        [in_weight],
        scratch=[pltpu.VMEM((rows_in, lanes), jnp.float32)],
    )
    conv_rows = swap_heads(packed_conv).reshape(-1, conv_columns)
    weights_conv = gather_blocks(conv_rows)
    rest_rows = swap_heads(after(packed_rest, conv_rows)).reshape(-1, rest_columns)
    weights_rest = gather_blocks(rest_rows)
    gathered_tokens = gather_heads(after(tokens, conv_rows))
    out_rows = lax.ppermute(after(out_weight.astype(low), rest_rows), ("head", "blk"), out_pairs)
    weights_out = gather_blocks(out_rows)
    rows_ffn = gate_up_weight.shape[0]
    units = FF // 4
    packed_ffn = call(
        partial(pack_ffn, ring=ring),
        [shaped((4, rows_ffn, 2 * units), low)],
        place,
        [after(gate_up_weight, rest_rows)],
    )[0]
    ffn_rows = swap_heads(packed_ffn).reshape(-1, 2 * units)
    weights_ffn = gather_blocks(after(ffn_rows, out_rows))
    weights_down = gather_blocks(after(down_weight.astype(low), ffn_rows))
    model_cotangent = jnp.concatenate(gather_heads(after(cotangent, ffn_rows)))

    positions = block_index * span_rows + jnp.arange(span_rows, dtype=jnp.int32)
    all_positions = jnp.arange(blocks * span_rows, dtype=jnp.int32)
    starts_all = lax.cummax(jnp.where(flags_all > 0, all_positions, 0), axis=0)
    first_visible = lax.dynamic_slice_in_dim(starts_all, block_index * span_rows, span_rows, 0)
    flags_before = jnp.concatenate([jnp.zeros((KW - 2,), jnp.int32), flags_all])
    flag_ext = lax.dynamic_slice_in_dim(
        flags_before, block_index * span_rows, span_rows + KW - 2, 0
    ).astype(jnp.float32)
    segment = jnp.broadcast_to(
        jnp.cumsum(start_flags[0]).astype(jnp.float32)[:, None], (span_rows, lanes)
    )
    view = jnp.stack([block_index, jnp.min(first_visible), jnp.max(first_visible)])
    first_wide = jnp.broadcast_to(first_visible[:, None], (span_rows, lanes))
    keep_masks = [jnp.ones((span_rows,), jnp.float32)]
    for lag_index in range(1, KW):
        begin = KW - 1 - lag_index
        keep_masks.append(keep_masks[-1] * (1.0 - flag_ext[begin : begin + span_rows]))
    frequencies = rope_base ** (-jnp.arange(HD // 2, dtype=jnp.float32) * 2.0 / HD)
    angles = positions.astype(jnp.float32)[:, None] * frequencies[None, :]
    cosine = jnp.cos(angles)
    sine = jnp.sin(angles)
    cosine_wide = jnp.concatenate([cosine, cosine], axis=1)
    sine_wide = jnp.concatenate([-sine, sine], axis=1)
    conv_taps = jnp.concatenate(
        [
            lax.dynamic_slice_in_dim(conv_weight, head_index * inner_columns, inner_columns, 1),
            conv_weight[:, mamba_width:],
        ],
        axis=1,
    )
    conv_shift = jnp.concatenate(
        [
            lax.dynamic_slice_in_dim(conv_bias, head_index * inner_columns, inner_columns, 0),
            conv_bias[mamba_width:],
        ]
    )
    step_shift = lax.dynamic_slice_in_dim(step_bias, head_index * step_heads, step_heads, 0)
    decay_rate = lax.dynamic_slice_in_dim(decay_log, head_index * step_heads, step_heads, 0)
    skip_local = lax.dynamic_slice_in_dim(skip_gain, head_index * step_heads, step_heads, 0)
    skip_wide = jnp.repeat(skip_local, MP)[None, :]

    normed_one = call(
        partial(norm_one, ring=ring),
        [shaped((span_rows, D), low)],
        place,
        [*gathered_tokens, first_gain[None, :]],
        scratch=[pltpu.VMEM((row_count, D), low)],
    )[0]

    projected = jnp.dot(normed_one, weights_conv, preferred_element_type=jnp.float32)
    kv_mine = call(
        rope_kv,
        [shaped((blocks, span_rows, HD), low)],
        place,
        [projected[:, kv_at:], cosine_wide, sine_wide],
    )[0]
    pair_bc = projected[:, inner_columns:step_at].astype(low)
    conv_local = call(
        join_conv,
        [shaped((span_rows, inner_columns + 2 * NS), low)],
        place,
        [projected[:, :inner_columns], *gather_heads(pair_bc)],
    )[0]
    step_local = projected[:, step_at : step_at + step_heads].astype(low).astype(jnp.float32)
    rim_rows = passed_along(conv_local[span_rows - (KW - 1) :], "blk", 1)
    extended = jnp.concatenate([rim_rows, conv_local], axis=0).astype(jnp.float32)
    active, conv_back = jax.vjp(
        partial(conv_act, keep_masks=keep_masks), extended, conv_taps, conv_shift
    )
    (step_size, log_decay), step_back = jax.vjp(
        step_and_decay, step_local, step_shift, decay_rate
    )
    inner_act = active[:, :inner_columns]
    into_act = active[:, inner_columns : inner_columns + NS]
    outof_act = active[:, inner_columns + NS :]
    step_wide = in_lanes(step_size)
    decay_wide = in_lanes(log_decay)
    tall = shaped((span_rows, inner_columns), jnp.float32)
    tall_low = shaped((span_rows, inner_columns), low)
    narrow = shaped((span_rows, lanes), jnp.float32)
    share = inner_columns // blocks
    sent = shaped((blocks, extra_rows + share, NS), low)
    state_scratch = pltpu.VMEM((inner_columns, NS), jnp.float32)

    def chained(payload, backwards, after=()):
        got = lax.all_to_all(payload, "blk", split_axis=0, concat_axis=0, tiled=True)
        states = call(
            partial(chain, backwards=backwards),
            [shaped((blocks, share, NS), low)],
            place,
            [got],
            after=after,
        )[0]
        moved = lax.all_to_all(states, "blk", split_axis=0, concat_axis=0, tiled=True)
        return moved.reshape(inner_columns, NS), states

    within, state_sent, entering, factor = call(
        ssd_local,
        [tall, sent, narrow, shaped((8, lanes), jnp.float32)],
        place,
        [inner_act, into_act, outof_act, step_wide, decay_wide, segment],
        after=[ffn_rows],
        scratch=[state_scratch],
        flops=6 * 10**9,
    )
    state_in, states_mine = chained(state_sent, False)

    normed_after = after(normed_one, states_mine)
    projected_rest = jnp.dot(normed_after, weights_rest, preferred_element_type=jnp.float32)
    query_local, gate_act = call(
        rope_query,
        [shaped((span_rows, query_columns), low), tall_low],
        place,
        [projected_rest, cosine_wide, sine_wide],
    )
    kv_blocks = lax.all_to_all(
        kv_mine, "blk", split_axis=0, concat_axis=0, tiled=True
    )
    kv_beside = from_head(kv_blocks, 1)
    keys = jnp.where(even, kv_blocks, kv_beside)
    values = jnp.where(even, kv_beside, kv_blocks)
    attended, lse = attention(
        view, query_local, first_wide, keys, values, [states_mine, model_cotangent]
    )

    ssd, mixer = call(
        ssd_finish,
        [tall, shaped((span_rows, query_columns + inner_columns), low)],
        place,
        [within, entering, outof_act, state_in, inner_act, gate_act, skip_wide, attended],
        flops=2 * 10**9,
    )
    pair_rows = 2 * row_count
    mixed_other = jnp.dot(mixer[pair_rows:], weights_out, preferred_element_type=jnp.float32)
    mixed_own = jnp.dot(mixer[:pair_rows], weights_out, preferred_element_type=jnp.float32)
    mixed = scatter_pairs(mixed_own, mixed_other)
    hidden_one, normed_two = call(
        partial(norm_two, ring=ring),
        [shaped((row_count, D), jnp.float32), shaped((row_count, D), low)],
        place,
        [mixed, tokens, second_gain[None, :]],
        scratch=[pltpu.VMEM((row_count, D), low)],
    )
    model_normed = jnp.concatenate(gather_heads(normed_two))
    gate_up = jnp.dot(model_normed, weights_ffn, preferred_element_type=jnp.float32)
    gate_part, up_part = gate_up[:, :units], gate_up[:, units:]
    activated = (jax.nn.silu(gate_part) * up_part).astype(low)
    grad_down_low = outer_grad(activated, model_cotangent).astype(low)
    grad_activated = times_transposed(model_cotangent, after(weights_down, grad_down_low))
    sigmoid_gate = jax.nn.sigmoid(gate_part)
    grad_gate_up = jnp.concatenate(
        [
            grad_activated * up_part * sigmoid_gate * (1.0 + gate_part * (1.0 - sigmoid_gate)),
            grad_activated * jax.nn.silu(gate_part),
        ],
        axis=1,
    ).astype(low)
    grad_down = scatter_blocks(after(grad_down_low, weights_down))
    gate_up_late = after(grad_gate_up, grad_down_low)
    grad_norm_other = times_transposed(gate_up_late[pair_rows:], weights_ffn).astype(low)
    grad_norm_own = times_transposed(gate_up_late[:pair_rows], weights_ffn)
    grad_normed_two = scatter_pairs(grad_norm_own, grad_norm_other, low)
    grad_ffn_low = outer_grad(model_normed, after(grad_gate_up, grad_norm_own)).astype(low)

    grad_hidden, grad_hidden_low, grad_second = call(
        partial(back_two, ring=ring),
        [
            shaped((row_count, D), jnp.float32),
            shaped((row_count, D), low),
            shaped((8, D), jnp.float32),
        ],
        place,
        [
            grad_normed_two,
            hidden_one,
            cotangent,
            second_gain[None, :],
        ],
        after=[grad_down_low, grad_ffn_low],
        scratch=[pltpu.VMEM((row_count, D), jnp.float32)],
    )
    grad_ffn = scatter_blocks(after(grad_ffn_low, grad_down, grad_hidden_low))
    span_grad_hidden = jnp.concatenate(gather_heads(after(grad_hidden_low, grad_down)))
    grad_heads = times_transposed(span_grad_hidden, weights_out).astype(low)
    grad_ssd, grad_gate, grad_sent, grad_skip_wide, grad_attended = call(
        ssd_gate_back,
        [
            tall,
            tall_low,
            sent,
            shaped((8, inner_columns), jnp.float32),
            shaped((span_rows, query_columns), low),
        ],
        place,
        [grad_heads, gate_act, ssd, inner_act, skip_wide, entering, outof_act, factor],
        scratch=[state_scratch],
        flops=2 * 10**9,
    )
    grad_ffn_weight = call(
        partial(unpack_ffn, ring=ring),
        [shaped(gate_up_weight.shape, jnp.float32)],
        place,
        [swap_heads(grad_ffn.reshape(4, rows_ffn, 2 * units))],
    )[0]
    activated_late = after(activated, span_grad_hidden)
    downed_other = jnp.dot(
        activated_late[pair_rows:], weights_down, preferred_element_type=jnp.float32
    )
    downed_own = jnp.dot(
        activated_late[:pair_rows], weights_down, preferred_element_type=jnp.float32
    )
    block_output = (hidden_one + scatter_pairs(downed_own, downed_other, low)).astype(low)

    grad_skip = grad_skip_wide[0].reshape(step_heads, MP).sum(axis=1)
    grad_out_low = outer_grad(mixer, span_grad_hidden).astype(low)
    later_grad, later_mine = chained(grad_sent, True)

    grad_query, grad_keys, grad_values = attention_back(
        view,
        query_local,
        first_wide,
        keys,
        values,
        grad_attended,
        attended,
        lse,
        [grad_out_low],
    )
    kept_kv = jnp.where(even, grad_keys, grad_values)
    given_kv = jnp.where(even, grad_values, grad_keys)
    kv_sums = (kept_kv.astype(jnp.float32) + from_head(given_kv, 1).astype(jnp.float32)).astype(
        low
    )
    grad_rest = call(
        query_back,
        [shaped((span_rows, rest_columns), low)],
        place,
        [grad_query, grad_gate, cosine_wide, sine_wide],
        after=[later_mine],
    )[0]
    grad_rest_low = outer_grad(normed_one, grad_rest).astype(low)
    grad_kv_parts = lax.all_to_all(kv_sums, "blk", split_axis=0, concat_axis=0, tiled=True)

    grad_out_sum = scatter_blocks(after(grad_out_low, grad_ffn, grad_rest_low, kv_sums))
    grad_mix_weight = lax.ppermute(
        grad_out_sum, ("head", "blk"), [(there, here) for here, there in out_pairs]
    ).astype(jnp.float32)
    grad_inner, grad_into, grad_outof, grad_step, grad_decay_line = call(
        ssd_back,
        [
            tall,
            shaped((span_rows, NS), jnp.float32),
            shaped((span_rows, NS), jnp.float32),
            narrow,
            narrow,
        ],
        place,
        [
            inner_act,
            into_act,
            outof_act,
            step_wide,
            decay_wide,
            segment,
            grad_ssd,
            ssd,
            skip_wide,
            state_in,
            later_grad,
        ],
        after=[kv_sums, grad_rest_low, block_output],
        scratch=[
            pltpu.VMEM((span_rows // chunk + 1, inner_columns, NS), jnp.float32),
            state_scratch,
        ],
        flops=10 * 10**9,
    )
    grad_raw, grad_step_shift, grad_rate = step_back(
        (grad_step[:, :step_heads], grad_decay_line[:, :step_heads])
    )
    grad_inner = after(grad_inner, grad_kv_parts)
    grad_extended, grad_taps, grad_shift = conv_back(
        jnp.concatenate([grad_inner, grad_into, grad_outof], axis=1)
    )
    rim_back = passed_along(grad_extended[: KW - 1], "blk", -1)
    conv_grad = grad_extended[KW - 1 :] + jnp.pad(rim_back, ((span_rows - (KW - 1), 0), (0, 0)))
    grad_bc = conv_grad[:, inner_columns:].astype(low).astype(jnp.float32)

    def tile_at(distance):
        at = jnp.bitwise_xor(head_index, distance) * lanes
        return lax.dynamic_slice_in_dim(grad_bc, at, lanes, 1)

    bc_beside = from_head(jnp.stack([tile_at(1), tile_at(3)]).astype(low), 1).astype(jnp.float32)
    bc_far = from_head((tile_at(2) + bc_beside[1]).astype(low), 2)
    bc_near = tile_at(0) + bc_beside[0]
    grad_conv = call(
        conv_joined,
        [shaped((span_rows, conv_columns), low)],
        place,
        [
            conv_grad[:, :inner_columns],
            bc_near,
            bc_far,
            in_lanes(grad_raw),
            cosine_wide,
            sine_wide,
            grad_kv_parts,
        ],
    )[0]
    grad_conv_low = outer_grad(normed_one, grad_conv).astype(low)
    grad_rest_in = scatter_blocks(after(grad_rest_low, grad_out_sum, grad_taps))
    conv_moved, rest_moved = call(
        relative_order,
        [shaped((span_rows, conv_columns), low), shaped((span_rows, rest_columns), low)],
        place,
        [grad_conv, grad_rest],
        after=[grad_conv_low],
    )

    def back_in(part):
        return times_transposed(rest_moved[part], weights_rest) + times_transposed(
            conv_moved[part], weights_conv
        )

    grad_normed_other = back_in(slice(pair_rows, span_rows)).astype(low)
    grad_normed_own = back_in(slice(0, pair_rows))
    rest_swapped = swap_heads(grad_rest_in.reshape(4, rows_in, -1))
    grad_input = call(
        partial(back_one, ring=ring),
        [shaped((row_count, D), low)],
        place,
        [
            scatter_pairs(grad_normed_own, grad_normed_other, low),
            tokens,
            grad_hidden,
            first_gain[None, :],
        ],
        after=[rest_swapped, grad_ffn_weight],
        scratch=[pltpu.VMEM((row_count, D), jnp.float32)],
    )[0]
    first_line = jnp.sum(
        weights_conv.astype(jnp.float32) * grad_conv_low.astype(jnp.float32), axis=1
    ) + jnp.sum(weights_rest.astype(jnp.float32) * after(grad_rest_low, grad_conv_low).astype(jnp.float32), axis=1)
    first_line = first_line.reshape(blocks, 4, -1)
    first_line = jnp.stack([first_line[ring.index(k)] for k in range(blocks)], axis=1).reshape(D)

    def own_part(values_in, total):
        return lax.dynamic_update_slice_in_dim(
            jnp.zeros(values_in.shape[:-1] + (total,), jnp.float32),
            values_in,
            head_index * values_in.shape[-1],
            values_in.ndim - 1,
        )

    small = [
        first_line / first_gain,
        grad_second[0],
        jnp.concatenate(
            [own_part(grad_taps[:, :inner_columns], mamba_width), grad_taps[:, inner_columns:]],
            axis=1,
        ),
        jnp.concatenate(
            [own_part(grad_shift[:inner_columns], mamba_width), grad_shift[inner_columns:]]
        ),
        own_part(grad_step_shift, MH),
        own_part(grad_rate, MH),
        own_part(grad_skip, MH),
    ]
    line = jnp.concatenate([part.reshape(-1) for part in small])
    line = jnp.pad(line, (0, -line.shape[0] % 1024)).reshape(-1, 128)
    line = summed_over(summed_over(line, "head"), "blk").reshape(-1)
    grad_conv_in = scatter_blocks(after(grad_conv_low, grad_rest_in, grad_normed_own))
    grad_proj_weight = call(
        unpack_in,
        [shaped(in_weight.shape, jnp.float32)],
        place,
        [swap_heads(grad_conv_in.reshape(4, rows_in, -1)), rest_swapped],
    )[0]
    summed_small = []
    at = 0
    for part in small:
        summed_small.append(line[at : at + part.size].reshape(part.shape))
        at += part.size
    return (
        block_output[None],
        grad_input[None],
        grad_proj_weight,
        grad_mix_weight,
        grad_ffn_weight,
        grad_down.astype(jnp.float32),
        *summed_small,
    )


def own_first(chunks, mine, order=(0, 1, 2, 3)):
    return [lax.dynamic_index_in_dim(chunks, jnp.bitwise_xor(mine, d), 0, False) for d in order]


def solution(mesh):
    placed = (
        P("blk", "head", None),
        P("blk", "head", None),
        P("blk", None),
        P(("head", "blk"), None),
        P(("head", "blk"), None),
        P(("head", "blk"), None),
        P(("head", "blk"), None),
        P(),
        P(),
        P(),
        P(),
        P(),
        P(),
        P(),
    )
    return jax.shard_map(
        per_device,
        mesh=mesh,
        in_specs=placed,
        out_specs=(
            P("blk", "head", None),
            P("blk", "head", None),
            P(("head", "blk"), None),
            P(("head", "blk"), None),
            P(("head", "blk"), None),
            P(("head", "blk"), None),
            P(),
            P(),
            P(),
            P(),
            P(),
            P(),
            P(),
        ),
        check_vma=False,
    )
```

```python
import math
from functools import partial

import jax
import jax.numpy as jnp
from jax import lax
from jax.experimental import pallas as pl
from jax.experimental.pallas import tpu as pltpu
from jax.sharding import PartitionSpec as P

D = 2048
QH = 8
KVH = 2
HD = 128
MH = 48
MP = 64
NS = 256
FF = 4096
KW = 4


epsilon = 1e-05
rope_base = 100000000000.0
masked_score = -1e30


def after(value, *others):
    return lax.optimization_barrier((value, *others))[0]


def passed_along(shard, axis, by):
    peers = lax.axis_size(axis)
    pairs = [(i, i + by) for i in range(peers) if 0 <= i + by < peers]
    return lax.ppermute(shard, axis, pairs)


def ring_of(axis):
    peers = lax.axis_size(axis)
    if peers != 8:
        return list(range(peers))
    return [0, 2, 4, 6, 7, 5, 3, 1]


def gather_blocks(shard):
    return lax.all_gather(shard, "blk", axis=0, tiled=True, axis_index_groups=[ring_of("blk")])


def scatter_blocks(partial_sums):
    return lax.psum_scatter(
        partial_sums,
        "blk",
        scatter_dimension=0,
        tiled=True,
        axis_index_groups=[ring_of("blk")],
    )


def from_head(shard, distance):
    peers = lax.axis_size("head")
    return lax.ppermute(shard, "head", [(i, i ^ distance) for i in range(peers)])


def gather_heads(shard):
    across = from_head(shard, 2)
    return [shard, across, from_head(shard, 1), from_head(across, 1)]


def in_head_order(parts):
    mine = lax.axis_index("head")
    stacked = jnp.stack([parts[0], parts[2], parts[1], parts[3]])
    return [
        lax.dynamic_index_in_dim(stacked, jnp.bitwise_xor(mine, j), 0, False) for j in range(4)
    ]


def scatter_pairs(own, other, middle=jnp.float32):
    rows = own.shape[0] // 2
    got = from_head(other.astype(middle), 1).astype(jnp.float32)
    far = from_head((own[rows:] + got[rows:]).astype(low), 2)
    return own[:rows] + got[:rows] + far.astype(jnp.float32)


def swap_heads(pieces):
    return lax.all_to_all(pieces, "head", split_axis=0, concat_axis=0, tiled=True)


def mixer_place():
    heads, ring = lax.axis_size("head"), ring_of("blk")
    peers = heads * len(ring)
    rows = (QH * HD + MH * MP) // peers
    query_blocks, mamba_blocks = QH * HD // rows // heads, MH * MP // rows // heads
    pairs = []
    for r in range(peers):
        if r < query_blocks * heads:
            group, slot = divmod(r, query_blocks)
        else:
            group, slot = divmod(r - query_blocks * heads, mamba_blocks)
            slot += query_blocks
        pairs.append((r, group * len(ring) + ring[slot]))
    return pairs


kv_begin = QH * HD
z_begin = kv_begin + 2 * KVH * HD
x_begin = z_begin + MH * MP
b_begin = x_begin + MH * MP
dt_begin = b_begin + 2 * NS
query_columns = QH * HD // 4
inner_columns = MH * MP // 4
bc_columns = 2 * NS // 4
step_heads = MH // 4
step_at = inner_columns + bc_columns
kv_at = step_at + 128
conv_columns = kv_at + HD
rest_columns = query_columns + inner_columns


def column_parts(head):
    conv = [
        (x_begin + head * inner_columns, 0, inner_columns),
        (b_begin + head * bc_columns, inner_columns, bc_columns),
        (kv_begin + (head % 2) * KVH * HD + (head // 2) * HD, kv_at, HD),
    ]
    rest = [
        (head * query_columns, 0, query_columns),
        (z_begin + head * inner_columns, query_columns, inner_columns),
    ]
    return conv, rest


def pack_in(place_ref, weight_ref, conv_ref, rest_ref, tail_ref):
    tail_ref[...] = jnp.zeros_like(tail_ref)
    tail_ref[:, :MH] = weight_ref[:, dt_begin : dt_begin + MH]
    last = tail_ref[...]
    lane = iota(last.shape, 1)
    for head in range(4):
        for parts, ref in zip(column_parts(head), (conv_ref, rest_ref)):
            for begin, at, size in parts:
                ref[head, :, at : at + size] = weight_ref[:, begin : begin + size].astype(low)
        steps = pltpu.roll(last, lanes - step_heads * head, 1) if head else last
        conv_ref[head, :, step_at:kv_at] = jnp.where(lane < step_heads, steps, 0.0).astype(low)


def unpack_in(place_ref, conv_ref, rest_ref, out_ref):
    total = jnp.zeros((out_ref.shape[0], lanes), jnp.float32)
    lane = iota(total.shape, 1)
    for head in range(4):
        for parts, ref in zip(column_parts(head), (conv_ref, rest_ref)):
            for begin, at, size in parts:
                out_ref[:, begin : begin + size] = ref[head, :, at : at + size].astype(jnp.float32)
        steps = conv_ref[head, :, step_at:kv_at].astype(jnp.float32)
        steps = jnp.where(lane < step_heads, steps, 0.0)
        total = total + (pltpu.roll(steps, step_heads * head, 1) if head else steps)
    out_ref[:, dt_begin : dt_begin + MH] = total[:, :MH]


def ffn_moves(ring):
    unit = FF // (4 * len(ring))
    return unit, [
        (
            head,
            half * FF + (head * len(ring) + k) * unit,
            half * (FF // 4) + i * unit,
        )
        for half in range(2)
        for head in range(4)
        for i, k in enumerate(ring)
    ]


def pack_ffn(place_ref, weight_ref, out_ref, *, ring):
    unit, moves = ffn_moves(ring)
    for head, begin, at in moves:
        out_ref[head, :, at : at + unit] = weight_ref[:, begin : begin + unit].astype(low)


def unpack_ffn(place_ref, in_ref, out_ref, *, ring):
    unit, moves = ffn_moves(ring)
    for head, begin, at in moves:
        out_ref[:, begin : begin + unit] = in_ref[head, :, at : at + unit].astype(jnp.float32)


def inverse_rms(values_in):
    return lax.rsqrt(jnp.mean(values_in * values_in, axis=1, keepdims=True) + epsilon)


def feature_moves(ring):
    piece = D // 4 // len(ring)
    return piece, [
        ((e * len(ring) + k) * piece, (4 * i + e) * piece)
        for e in range(4)
        for i, k in enumerate(ring)
    ]


def whole_lanes(begin, size):
    return pl.ds(pl.multiple_of(begin, 128), size)


def norm_one(place_ref, own, across, beside, both, gain_ref, out_ref, line_ref, *, ring):
    rows = own.shape[0]
    piece, moves = feature_moves(ring)
    for distance, ref in ((0, own), (2, across), (1, beside), (3, both)):
        x = ref[...].astype(jnp.float32)
        line_ref[...] = (x * inverse_rms(x) * gain_ref[...]).astype(low)
        there = jnp.bitwise_xor(place_ref[0], distance) * rows
        there = pl.ds(pl.multiple_of(there, rows), rows)
        for source, at in moves:
            out_ref[there, at : at + piece] = line_ref[:, source : source + piece]


def norm_two(place_ref, mixed_ref, tokens_ref, gain_ref, hidden_ref, out_ref, line_ref, *, ring):
    hidden = tokens_ref[...].astype(jnp.float32) + mixed_ref[...]
    hidden_ref[...] = hidden
    line_ref[...] = (hidden * inverse_rms(hidden) * gain_ref[...]).astype(low)
    piece, moves = feature_moves(ring)
    for source, at in moves:
        out_ref[:, at : at + piece] = line_ref[:, source : source + piece]


def back_two(
    place_ref, grad_ref, hidden_ref, cotangent_ref, gain_ref, out_ref, low_ref, sum_ref, plain_ref,
    *, ring,
):
    piece, moves = feature_moves(ring)
    for source, at in moves:
        plain_ref[:, source : source + piece] = grad_ref[:, at : at + piece]
    grad = plain_ref[...]
    hidden = hidden_ref[...]
    inverse = inverse_rms(hidden)
    scaled = grad * gain_ref[...]
    total = (
        cotangent_ref[...].astype(jnp.float32)
        + inverse * scaled
        - hidden * (inverse * inverse * inverse * jnp.mean(scaled * hidden, axis=1, keepdims=True))
    )
    out_ref[...] = total
    low_ref[...] = total.astype(low)
    sum_ref[...] = jnp.broadcast_to(
        jnp.sum(grad * hidden * inverse, axis=0, keepdims=True), sum_ref.shape
    )


def back_one(
    place_ref, grad_ref, tokens_ref, hidden_ref, gain_ref, out_ref, plain_ref, *, ring
):
    piece, moves = feature_moves(ring)
    for source, at in moves:
        plain_ref[:, source : source + piece] = grad_ref[:, at : at + piece]
    grad = plain_ref[...]
    x = tokens_ref[...].astype(jnp.float32)
    inverse = inverse_rms(x)
    scaled = grad * gain_ref[...]
    out_ref[...] = (
        hidden_ref[...]
        + inverse * scaled
        - x * (inverse * inverse * inverse * jnp.mean(scaled * x, axis=1, keepdims=True))
    ).astype(low)


def turned(values_in, cosine, sine):
    return values_in * cosine + pltpu.roll(values_in, HD // 2, 1) * sine


def rope_kv(place_ref, in_ref, cosine_ref, sine_ref, out_ref):
    kv = in_ref[...]
    out_ref[...] = jnp.where(
        place_ref[1] == 0, turned(kv, cosine_ref[...], sine_ref[...]), kv
    ).astype(low)


def kv_moves(span):
    height = span * HD // D
    return height, [(j * height, j * HD) for j in range(D // HD)]


def pack_out(place_ref, out_rows_ref, kv_ref, packed_ref):
    rows = out_rows_ref.shape[0]
    packed_ref[:rows, :] = out_rows_ref[...]
    height, moves = kv_moves(kv_ref.shape[0])
    for begin, at in moves:
        packed_ref[rows:, at : at + HD] = kv_ref[begin : begin + height, :]


def unpack_out(place_ref, packed_ref, out_ref, kv_ref, *, ring):
    rows = out_ref.shape[1]
    height, moves = kv_moves(kv_ref.shape[1])
    for i, k in enumerate(ring):
        out_ref[i] = packed_ref[i, :rows, :]
        for begin, at in moves:
            kv_ref[k, begin : begin + height, :] = packed_ref[i, rows:, at : at + HD]


def pack_out_grads(place_ref, out_ref, kv_ref, packed_ref, *, ring):
    rows = out_ref.shape[1]
    height, moves = kv_moves(kv_ref.shape[1])
    for i, k in enumerate(ring):
        packed_ref[i, :rows, :] = out_ref[i]
        for begin, at in moves:
            packed_ref[i, rows:, at : at + HD] = kv_ref[k, begin : begin + height, :]


def rope_query(place_ref, in_ref, cosine_ref, sine_ref, query_ref, gate_ref):
    cosine, sine = cosine_ref[...], sine_ref[...]
    for begin in range(0, query_columns, HD):
        query_ref[:, begin : begin + HD] = turned(
            in_ref[:, begin : begin + HD], cosine, sine
        ).astype(low)
    gate_ref[...] = in_ref[:, query_columns:].astype(low)


def query_back(place_ref, query_ref, gate_ref, cosine_ref, sine_ref, out_ref):
    cosine, sine = cosine_ref[...], -sine_ref[...]
    for begin in range(0, query_columns, HD):
        rounded = query_ref[:, begin : begin + HD].astype(low).astype(jnp.float32)
        out_ref[:, begin : begin + HD] = turned(rounded, cosine, sine).astype(low)
    out_ref[:, query_columns:] = gate_ref[...]


def join_conv(place_ref, inner_ref, own, across, beside, both, out_ref):
    out_ref[:, :inner_columns] = inner_ref[...].astype(low)
    for distance, ref in ((0, own), (2, across), (1, beside), (3, both)):
        at = inner_columns + jnp.bitwise_xor(place_ref[0], distance) * lanes
        out_ref[:, whole_lanes(at, lanes)] = ref[...]


def conv_joined(
    place_ref, inner_ref, near_ref, far_ref, step_ref, cosine_ref, sine_ref, kv_ref, out_ref
):
    out_ref[:, :inner_columns] = inner_ref[...].astype(low)
    out_ref[:, inner_columns:step_at] = (near_ref[...] + far_ref[...].astype(jnp.float32)).astype(low)
    out_ref[:, step_at:kv_at] = step_ref[...].astype(low)
    height, moves = kv_moves(out_ref.shape[0])
    for begin, at in moves:
        rows = slice(begin, begin + height)
        kv = kv_ref[:, at : at + HD].astype(jnp.float32)
        out_ref[rows, kv_at:] = jnp.where(
            place_ref[1] == 0, turned(kv, cosine_ref[rows, :], -sine_ref[rows, :]), kv
        ).astype(low)


def relative_order(place_ref, first_ref, second_ref, first_out, second_out):
    for at, distance in enumerate((0, 2, 1, 3)):
        there = jnp.bitwise_xor(place_ref[0], distance) * chunk
        there = pl.ds(pl.multiple_of(there, chunk), chunk)
        rows = slice(at * chunk, (at + 1) * chunk)
        first_out[rows, :] = first_ref[there, :]
        second_out[rows, :] = second_ref[there, :]


def outer_grad(left_side, grad_side):
    return lax.dot_general(
        left_side, grad_side, (((0,), (0,)), ((), ())), preferred_element_type=jnp.float32
    )


def times_transposed(grad_side, weight):
    return lax.dot_general(
        grad_side, weight, (((1,), (1,)), ((), ())), preferred_element_type=jnp.float32
    )


chunk = 128
lanes = 128
low = jnp.bfloat16
exact = lax.Precision.HIGHEST


def dot_nn(a, b, precision=None):
    return lax.dot_general(
        a, b, (((1,), (0,)), ((), ())), precision=precision, preferred_element_type=jnp.float32
    )


def dot_nt(a, b):
    return lax.dot_general(a, b, (((1,), (1,)), ((), ())), preferred_element_type=jnp.float32)


def dot_tn(a, b):
    return lax.dot_general(a, b, (((0,), (0,)), ((), ())), preferred_element_type=jnp.float32)


def iota(shape, dim):
    return lax.broadcasted_iota(jnp.int32, shape, dim)


def spread(per_head, pair):
    rows = per_head.shape[0]
    first = per_head[:, 2 * pair : 2 * pair + 1]
    second = per_head[:, 2 * pair + 1 : 2 * pair + 2]
    return jnp.where(iota((rows, lanes), 1) < MP, first, second)


def head_sums(products, pair):
    mine = 2 * pair + (iota((lanes, lanes), 0) >= MP).astype(jnp.int32)
    ones = (mine == iota((lanes, lanes), 1)).astype(jnp.float32)
    return dot_nn(products, ones, exact)


def chunk_terms(decay, segment, segment_before):
    lower = iota((chunk, chunk), 0) >= iota((chunk, chunk), 1)
    cumulative = dot_nn(lower.astype(jnp.float32), decay, exact)
    total = cumulative[chunk - 1 :, :]
    segment_end = segment[chunk - 1 :, :]
    related = lower & (segment == segment.T)
    entering = jnp.where(segment == segment_before, jnp.exp(cumulative), 0.0)
    ending = jnp.where(segment == segment_end, jnp.exp(total - cumulative), 0.0)
    whole = jnp.where(segment_end == segment_before, jnp.exp(total), 0.0)
    return cumulative, cumulative.T, related, entering, ending, whole, total, segment_end


def decays_of(cumulative, transposed, related, head):
    apart = cumulative[:, head : head + 1] - transposed[head : head + 1, :]
    return jnp.exp(jnp.where(related, apart, masked_score))


def row_factor(whole, pair, width):
    first = whole[:, 2 * pair : 2 * pair + 1]
    second = whole[:, 2 * pair + 1 : 2 * pair + 2]
    return jnp.where(iota((lanes, width), 0) < MP, first, second)


def chunk_rows(index):
    return pl.ds(pl.multiple_of(index * chunk, chunk), chunk)


def pack_states(state_ref, factor, out_ref):
    blocks, rows, width = out_ref.shape
    share = rows - extra_rows
    row = iota((extra_rows, width), 0)
    for k in range(blocks):
        extra = jnp.zeros((extra_rows, width), jnp.float32)
        for e in range(4):
            head = k * share // MP + e
            if head * MP < state_ref.shape[0]:
                whole = factor[:, head : head + 1]
                rough = whole.astype(low).astype(jnp.float32)
                extra = jnp.where(row == e, rough, extra)
                extra = jnp.where(row == 4 + e, whole - rough, extra)
        out_ref[k, :extra_rows, :] = extra.astype(low)
        out_ref[k, extra_rows:, :] = state_ref[k * share : (k + 1) * share, :].astype(low)


extra_rows = 16


def chain(place_ref, got_ref, out_ref, backwards):
    blocks, rows, width = got_ref.shape
    share = rows - extra_rows
    row = iota((share, width), 0) + lax.rem(place_ref[4] * share, MP)
    state = jnp.zeros((share, width), jnp.float32)
    for k in range(blocks - 1, -1, -1) if backwards else range(blocks):
        out_ref[k] = state.astype(low)
        extra = got_ref[k, :extra_rows, :].astype(jnp.float32)
        factor = extra[0:1, :] + extra[4:5, :]
        for e in range(1, 4):
            factor = jnp.where(row >= e * MP, extra[e : e + 1, :] + extra[4 + e : 5 + e, :], factor)
        state = factor * state + got_ref[k, extra_rows:, :].astype(jnp.float32)


def ssd_local(
    place_ref, x_ref, b_ref, c_ref, step_ref, decay_ref, seg_ref,
    y_ref, sent_ref, enter_ref, fac_ref, state_ref,
):
    pairs = x_ref.shape[1] // lanes
    state_ref[...] = jnp.zeros_like(state_ref)

    def body(index, carry):
        segment_before, base = carry
        rows = chunk_rows(index)
        segment = seg_ref[rows, :]
        cumulative, transposed, related, entering, ending, whole, total, segment_end = chunk_terms(
            decay_ref[rows, :], segment, segment_before
        )
        enter_ref[rows, :] = jnp.where(segment == 0.0, jnp.exp(base + cumulative), 0.0)
        into = b_ref[rows, :].astype(low)
        outof = c_ref[rows, :].astype(low)
        step = step_ref[rows, :]
        scores = dot_nt(outof, into)
        left = iota((chunk, lanes), 1) < MP
        for pair in range(pairs):
            cols = slice(pair * lanes, (pair + 1) * lanes)
            taken = x_ref[rows, cols] * spread(step, pair)
            taken_low = taken.astype(low)
            parts = []
            for head in (2 * pair, 2 * pair + 1):
                weights = decays_of(cumulative, transposed, related, head) * scores
                parts.append(dot_nn(weights.astype(low), taken_low))
            state = state_ref[cols, :]
            y_ref[rows, cols] = jnp.where(left, parts[0], parts[1]) + spread(
                entering, pair
            ) * dot_nt(outof, state.astype(low))
            kept = (taken * spread(ending, pair)).astype(low)
            state_ref[cols, :] = row_factor(whole, pair, state.shape[1]) * state + dot_tn(
                kept, into
            )
        return segment_end, base + total

    start = jnp.zeros((1, lanes), jnp.float32)
    segment_end, base = lax.fori_loop(0, x_ref.shape[0] // chunk, body, (start, start))
    factor = jnp.where(segment_end == 0.0, jnp.exp(base), 0.0)
    fac_ref[...] = jnp.broadcast_to(factor, fac_ref.shape)
    pack_states(state_ref, factor, sent_ref)


def relative_rows(place_ref, index):
    distance = jnp.bitwise_xor(place_ref[0], index)
    at = (distance % 2) * 2 + distance // 2
    return pl.ds(pl.multiple_of(at * chunk, chunk), chunk)


def ssd_finish(
    place_ref, y_ref, enter_ref, c_ref, state_ref, x_ref, z_ref, skip_ref, attended_ref,
    ssd_ref, mixer_ref,
):
    pairs = x_ref.shape[1] // lanes
    width = attended_ref.shape[1]

    def body(index, carry):
        rows = chunk_rows(index)
        there = relative_rows(place_ref, index)
        outof = c_ref[rows, :].astype(low)
        entering = enter_ref[rows, :]
        mixer_ref[there, :width] = attended_ref[rows, :].astype(low)
        for pair in range(pairs):
            cols = slice(pair * lanes, (pair + 1) * lanes)
            ssd = y_ref[rows, cols] + spread(entering, pair) * dot_nt(outof, state_ref[cols, :])
            ssd_ref[rows, cols] = ssd
            gate = z_ref[rows, cols].astype(jnp.float32)
            total = ssd + skip_ref[:, cols] * x_ref[rows, cols]
            mixer_ref[there, width + pair * lanes : width + (pair + 1) * lanes] = (
                total * gate / (1.0 + jnp.exp(-gate))
            ).astype(low)
        return carry

    lax.fori_loop(0, x_ref.shape[0] // chunk, body, 0)


def ssd_gate_back(
    place_ref, grad_ref, z_ref, ssd_ref, x_ref, skip_ref, enter_ref, c_ref, fac_ref,
    dy_ref, dz_ref, sent_ref, dskip_ref, datt_ref, dstate_ref,
):
    pairs = x_ref.shape[1] // lanes
    width = datt_ref.shape[1]
    dstate_ref[...] = jnp.zeros_like(dstate_ref)
    dskip_ref[...] = jnp.zeros_like(dskip_ref)

    def body(index, carry):
        rows = chunk_rows(index)
        there = relative_rows(place_ref, index)
        outof = c_ref[rows, :].astype(low)
        entering = enter_ref[rows, :]
        datt_ref[rows, :] = grad_ref[there, :width]
        for pair in range(pairs):
            cols = slice(pair * lanes, (pair + 1) * lanes)
            gate = z_ref[rows, cols].astype(jnp.float32)
            sigmoid = 1.0 / (1.0 + jnp.exp(-gate))
            grad = grad_ref[
                there, width + pair * lanes : width + (pair + 1) * lanes
            ].astype(jnp.float32)
            x = x_ref[rows, cols]
            total = ssd_ref[rows, cols] + skip_ref[:, cols] * x
            dz_ref[rows, cols] = (
                grad * total * sigmoid * (1.0 + gate * (1.0 - sigmoid))
            ).astype(low)
            dy = grad * gate * sigmoid
            dy_ref[rows, cols] = dy
            dskip_ref[:, cols] += jnp.broadcast_to(
                jnp.sum(dy * x, axis=0, keepdims=True), (dskip_ref.shape[0], lanes)
            )
            dstate_ref[cols, :] += dot_tn((dy * spread(entering, pair)).astype(low), outof)
        return carry

    lax.fori_loop(0, x_ref.shape[0] // chunk, body, 0)
    pack_states(dstate_ref, fac_ref[:1, :], sent_ref)


def ssd_back(
    place_ref, x_ref, b_ref, c_ref, step_ref, decay_ref, seg_ref, dy_ref, ssd_ref, skip_ref, state_ref, later_ref,
    dx_ref, db_ref, dc_ref, dstep_ref, ddecay_ref, states, grads,
):
    pairs = x_ref.shape[1] // lanes
    chunks = x_ref.shape[0] // chunk
    zero_row = jnp.zeros((1, lanes), jnp.float32)

    def before(index):
        rows = pl.ds(pl.multiple_of(jnp.maximum(index - 1, 0) * chunk, chunk), chunk)
        return jnp.where(index == 0, 0.0, seg_ref[rows, :][chunk - 1 :, :])

    states[0] = state_ref[...].astype(jnp.float32)

    def forward(index, carry):
        rows = chunk_rows(index)
        _, _, _, _, ending, whole, _, _ = chunk_terms(
            decay_ref[rows, :], seg_ref[rows, :], before(index)
        )
        into = b_ref[rows, :].astype(low)
        step = step_ref[rows, :]
        for pair in range(pairs):
            cols = slice(pair * lanes, (pair + 1) * lanes)
            kept = (x_ref[rows, cols] * spread(step, pair) * spread(ending, pair)).astype(low)
            state = states[index, cols, :]
            states[index + 1, cols, :] = row_factor(
                whole, pair, state.shape[1]
            ) * state + dot_tn(kept, into)
        return carry

    lax.fori_loop(0, chunks, forward, 0)
    grads[...] = later_ref[...].astype(jnp.float32)
    last = jnp.zeros((8, lanes), jnp.float32)
    for pair in range(pairs):
        cols = slice(pair * lanes, (pair + 1) * lanes)
        product = grads[cols, :] * states[chunks, cols, :]
        along = lax.dot_general(
            jnp.ones((8, product.shape[1]), jnp.float32),
            product,
            (((1,), (1,)), ((), ())),
            precision=exact,
            preferred_element_type=jnp.float32,
        )
        last = last + head_sums(along, pair)

    def backward(at, carry):
        index = chunks - 1 - at
        rows = chunk_rows(index)
        cumulative, transposed, related, entering, ending, whole, _, _ = chunk_terms(
            decay_ref[rows, :], seg_ref[rows, :], before(index)
        )
        into = b_ref[rows, :].astype(low)
        outof = c_ref[rows, :].astype(low)
        step = step_ref[rows, :]
        scores = dot_nt(outof, into)
        left = iota((chunk, lanes), 1) < MP
        grad_scores = jnp.zeros((chunk, chunk), jnp.float32)
        grad_into = jnp.zeros((chunk, b_ref.shape[1]), jnp.float32)
        grad_outof = jnp.zeros((chunk, b_ref.shape[1]), jnp.float32)
        grad_cum = jnp.zeros((chunk, lanes), jnp.float32)
        grad_step = jnp.zeros((chunk, lanes), jnp.float32)
        for pair in range(pairs):
            cols = slice(pair * lanes, (pair + 1) * lanes)
            x = x_ref[rows, cols]
            step_pair = spread(step, pair)
            taken = x * step_pair
            taken_low = taken.astype(low)
            dy = dy_ref[rows, cols]
            dy_low = dy.astype(low)
            parts = []
            for half, head in enumerate((2 * pair, 2 * pair + 1)):
                decays = decays_of(cumulative, transposed, related, head)
                parts.append(dot_tn((decays * scores).astype(low), dy_low))
                own = jnp.where(left if half == 0 else ~left, dy_low, jnp.zeros_like(dy_low))
                grad_scores = grad_scores + decays * dot_nt(own, taken_low)
            later = grads[cols, :]
            later_low = later.astype(low)
            ending_pair = spread(ending, pair)
            grad_taken = jnp.where(left, parts[0], parts[1]) + ending_pair * dot_nt(
                into, later_low
            )
            grad_into = grad_into + dot_nn((taken * ending_pair).astype(low), later_low)
            dy_enter = (dy * spread(entering, pair)).astype(low)
            grad_outof = grad_outof + dot_nn(dy_enter, states[index, cols, :].astype(low))
            grads[cols, :] = row_factor(whole, pair, later.shape[1]) * later + dot_tn(
                dy_enter, outof
            )
            grad_cum = grad_cum + head_sums(dy * ssd_ref[rows, cols] - taken * grad_taken, pair)
            grad_step = grad_step + head_sums(x * grad_taken, pair)
            dx_ref[rows, cols] = step_pair * grad_taken + skip_ref[:, cols] * dy
        grad_scores_low = grad_scores.astype(low)
        db_ref[rows, :] = grad_into + dot_tn(grad_scores_low, outof)
        dc_ref[rows, :] = grad_outof + dot_nn(grad_scores_low, into)
        dstep_ref[rows, :] = grad_step
        upper = (iota((chunk, chunk), 0) <= iota((chunk, chunk), 1)).astype(jnp.float32)
        ddecay_ref[rows, :] = dot_nn(upper, grad_cum, exact) + carry
        return carry + jnp.sum(grad_cum, axis=0, keepdims=True)

    lax.fori_loop(0, chunks, backward, last[:1, :] + zero_row)


def needed_and_plain(place_ref, block, span):
    mine, earliest, latest = place_ref[0], place_ref[1], place_ref[2]
    needed = (block <= mine) & ((block + 1) * span > earliest)
    return needed, (block < mine) & (block * span >= latest)


def visible_keys(place_ref, first_ref, block, span):
    key_pos = block * span + iota((span, span), 1)
    query_pos = place_ref[0] * span + iota((span, span), 0)
    return (key_pos <= query_pos) & (key_pos >= first_ref[:, :1])


def attend(place_ref, q_ref, first_ref, k_ref, v_ref, out_ref, lse_ref, top, total, summed):
    block = pl.program_id(0)
    span = q_ref.shape[0]
    heads = q_ref.shape[1] // HD

    @pl.when(block == 0)
    def _():
        top[...] = jnp.full_like(top, masked_score)
        total[...] = jnp.zeros_like(total)
        summed[...] = jnp.zeros_like(summed)

    def one(masked):
        keys = k_ref[0]
        values = v_ref[0]
        if masked:
            visible = visible_keys(place_ref, first_ref, block, span)
        for head in range(heads):
            cols = slice(head * HD, (head + 1) * HD)
            scores = dot_nt(q_ref[:, cols], keys) * HD**-0.5
            if masked:
                scores = jnp.where(visible, scores, masked_score)
            old_top = top[head][:, :1]
            new_top = jnp.maximum(old_top, jnp.max(scores, axis=1, keepdims=True))
            weights = jnp.exp(scores - new_top)
            if masked:
                weights = jnp.where(visible, weights, 0.0)
            scale = jnp.exp(old_top - new_top)
            total[head] = total[head] * scale + jnp.sum(weights, axis=1, keepdims=True)
            top[head] = jnp.broadcast_to(new_top, (span, lanes))
            summed[head] = summed[head] * scale + dot_nn(weights.astype(low), values)

    needed, plain = needed_and_plain(place_ref, block, span)
    pl.when(needed & plain)(lambda: one(False))
    pl.when(needed & jnp.logical_not(plain))(lambda: one(True))

    @pl.when(block == pl.num_programs(0) - 1)
    def _():
        for head in range(heads):
            cols = slice(head * HD, (head + 1) * HD)
            out_ref[:, cols] = summed[head] / total[head]
            lse_ref[head] = top[head] + jnp.log(total[head])


def attend_back(
    place_ref, q_ref, first_ref, k_ref, v_ref, grad_ref, out_ref, lse_ref, dq_ref, dk_ref, dv_ref
):
    block = pl.program_id(0)
    span = q_ref.shape[0]
    heads = q_ref.shape[1] // HD

    @pl.when(block == 0)
    def _():
        dq_ref[...] = jnp.zeros_like(dq_ref)

    def one(masked):
        keys = k_ref[0]
        values = v_ref[0]
        if masked:
            visible = visible_keys(place_ref, first_ref, block, span)
        grad_keys = jnp.zeros(keys.shape, jnp.float32)
        grad_values = jnp.zeros(keys.shape, jnp.float32)
        for head in range(heads):
            cols = slice(head * HD, (head + 1) * HD)
            query = q_ref[:, cols]
            grad = grad_ref[:, cols]
            delta = jnp.sum(
                grad.astype(jnp.float32) * out_ref[:, cols], axis=1, keepdims=True
            )
            scores = dot_nt(query, keys) * HD**-0.5
            if masked:
                scores = jnp.where(visible, scores, masked_score)
            weights = jnp.exp(scores - lse_ref[head][:, :1])
            changes = weights * (dot_nt(grad, values) - delta)
            weights_low = weights.astype(low)
            changes_low = (changes * HD**-0.5).astype(low)
            grad_values = grad_values + dot_tn(weights_low, grad)
            grad_keys = grad_keys + dot_tn(changes_low, query)
            dq_ref[:, cols] += dot_nn(changes_low, keys)
        dk_ref[0] = grad_keys.astype(low)
        dv_ref[0] = grad_values.astype(low)

    needed, plain = needed_and_plain(place_ref, block, span)
    pl.when(needed & plain)(lambda: one(False))
    pl.when(needed & jnp.logical_not(plain))(lambda: one(True))

    @pl.when(jnp.logical_not(needed))
    def _():
        dk_ref[...] = jnp.zeros_like(dk_ref)
        dv_ref[...] = jnp.zeros_like(dv_ref)


def shaped(shape, kind):
    return jax.ShapeDtypeStruct(shape, kind)


def call(kernel, outputs, place, operands, after=(), scratch=(), flops=10**6):
    count, skipped = len(operands), len(operands) + len(after)
    sizes = sum(math.prod(a.shape) * a.dtype.itemsize for a in (*operands, *outputs))

    def body(place_ref, *refs):
        kernel(place_ref, *refs[:count], *refs[skipped:])

    return pl.pallas_call(
        body,
        out_shape=outputs,
        in_specs=[pl.BlockSpec(memory_space=pltpu.SMEM)]
        + [pl.BlockSpec(memory_space=pltpu.VMEM)] * count
        + [pl.BlockSpec(memory_space=pl.ANY)] * len(after),
        out_specs=[pl.BlockSpec(memory_space=pltpu.VMEM)] * len(outputs),
        scratch_shapes=list(scratch),
        compiler_params=pltpu.CompilerParams(vmem_limit_bytes=kernel_memory),
        cost_estimate=pl.CostEstimate(flops=flops, bytes_accessed=sizes, transcendentals=0),
    )(place, *operands, *after)


kernel_memory = 44 * 1024 * 1024


def attention(place, query, first_visible, keys, values, after):
    away, span = keys.shape[0], query.shape[0]
    heads = query.shape[1] // HD
    same = lambda d, place: (0, 0)
    block = lambda d, place: (d, 0, 0)
    def body(*refs):
        attend(*refs[:5], *refs[5 + len(after) :])

    return pl.pallas_call(
        body,
        grid_spec=pltpu.PrefetchScalarGridSpec(
            num_scalar_prefetch=1,
            grid=(away,),
            in_specs=[
                pl.BlockSpec(query.shape, same),
                pl.BlockSpec(first_visible.shape, same),
                pl.BlockSpec((1, span, HD), block),
                pl.BlockSpec((1, span, HD), block),
            ]
            + [pl.BlockSpec(memory_space=pl.ANY)] * len(after),
            out_specs=[
                pl.BlockSpec(query.shape, same),
                pl.BlockSpec((heads, span, lanes), lambda d, place: (0, 0, 0)),
            ],
            scratch_shapes=[
                pltpu.VMEM((heads, span, lanes), jnp.float32),
                pltpu.VMEM((heads, span, lanes), jnp.float32),
                pltpu.VMEM((heads, span, HD), jnp.float32),
            ],
        ),
        out_shape=[
            shaped(query.shape, jnp.float32),
            shaped((heads, span, lanes), jnp.float32),
        ],
        compiler_params=pltpu.CompilerParams(vmem_limit_bytes=kernel_memory),
        cost_estimate=pl.CostEstimate(
            flops=20 * 10**9, bytes_accessed=4 * 10**6, transcendentals=0
        ),
    )(place, query, first_visible, keys, values, *after)


def attention_back(place, query, first_visible, keys, values, grad, out, lse, after):
    away, span = keys.shape[0], query.shape[0]
    same = lambda d, place: (0, 0)
    block = lambda d, place: (d, 0, 0)
    def body(*refs):
        attend_back(*refs[:8], *refs[8 + len(after) :])

    return pl.pallas_call(
        body,
        grid_spec=pltpu.PrefetchScalarGridSpec(
            num_scalar_prefetch=1,
            grid=(away,),
            in_specs=[
                pl.BlockSpec(query.shape, same),
                pl.BlockSpec(first_visible.shape, same),
                pl.BlockSpec((1, span, HD), block),
                pl.BlockSpec((1, span, HD), block),
                pl.BlockSpec(query.shape, same),
                pl.BlockSpec(query.shape, same),
                pl.BlockSpec(lse.shape, lambda d, place: (0, 0, 0)),
            ]
            + [pl.BlockSpec(memory_space=pl.ANY)] * len(after),
            out_specs=[
                pl.BlockSpec(query.shape, same),
                pl.BlockSpec((1, span, HD), block),
                pl.BlockSpec((1, span, HD), block),
            ],
        ),
        out_shape=[
            shaped(query.shape, jnp.float32),
            shaped(keys.shape, low),
            shaped(keys.shape, low),
        ],
        compiler_params=pltpu.CompilerParams(vmem_limit_bytes=kernel_memory),
        cost_estimate=pl.CostEstimate(
            flops=30 * 10**9, bytes_accessed=4 * 10**6, transcendentals=0
        ),
    )(place, query, first_visible, keys, values, grad, out, lse, *after)


def conv_act(extended, conv_taps, conv_shift, keep_masks):
    length = keep_masks[0].shape[0]
    result = conv_shift + conv_taps[0] * extended[KW - 1 :]
    for lag_index in range(1, KW):
        begin = KW - 1 - lag_index
        result = (
            result
            + conv_taps[lag_index]
            * keep_masks[lag_index][:, None]
            * extended[begin : begin + length]
        )
    return jax.nn.silu(result)


def step_and_decay(step_raw, step_shift, decay_rate):
    step_size = jax.nn.softplus(step_raw + step_shift)
    return step_size, -step_size * jnp.exp(decay_rate)


def in_lanes(per_head):
    return jnp.pad(per_head, ((0, 0), (0, lanes - per_head.shape[1])))


def summed_over(values_in, axis):
    peers = lax.axis_size(axis)
    by = 1
    while by < peers:
        values_in = values_in + lax.ppermute(values_in, axis, [(i, i ^ by) for i in range(peers)])
        by *= 2
    return values_in


def per_device(
    block_input,
    out_cotangent,
    start_flags,
    in_weight,
    out_weight,
    gate_up_weight,
    down_weight,
    first_gain,
    second_gain,
    conv_weight,
    conv_bias,
    step_bias,
    decay_log,
    skip_gain,
):
    head_count = lax.axis_size("head")
    blocks = lax.axis_size("blk")
    head_index = lax.axis_index("head")
    block_index = lax.axis_index("blk")
    ring = ring_of("blk")
    tokens = block_input[0]
    cotangent = out_cotangent[0]
    row_count = tokens.shape[0]
    span_rows = row_count * head_count
    mamba_width = MH * MP
    even = head_index % 2 == 0
    out_pairs = mixer_place()
    place = jnp.stack(
        [head_index, head_index % 2, 0, 0, block_index, 0, 0, 0]
    ).astype(jnp.int32)

    rows_in = in_weight.shape[0]
    flags_all = summed_over(
        lax.dynamic_update_slice_in_dim(
            jnp.zeros((blocks * span_rows,), jnp.int32),
            start_flags[0],
            block_index * span_rows,
            0,
        ),
        "blk",
    )
    packed_conv, packed_rest = call(
        pack_in,
        [
            shaped((4, rows_in, conv_columns), low),
            shaped((4, rows_in, rest_columns), low),
        ],
        place,
        [in_weight],
        scratch=[pltpu.VMEM((rows_in, lanes), jnp.float32)],
    )
    conv_rows = swap_heads(packed_conv).reshape(-1, conv_columns)
    weights_conv = gather_blocks(conv_rows)
    rest_rows = swap_heads(after(packed_rest, conv_rows)).reshape(-1, rest_columns)
    weights_rest = gather_blocks(rest_rows)
    gathered_tokens = gather_heads(after(tokens, conv_rows))
    out_rows = lax.ppermute(after(out_weight.astype(low), rest_rows), ("head", "blk"), out_pairs)
    rows_ffn = gate_up_weight.shape[0]
    units = FF // 4
    packed_ffn = call(
        partial(pack_ffn, ring=ring),
        [shaped((4, rows_ffn, 2 * units), low)],
        place,
        [after(gate_up_weight, rest_rows)],
    )[0]
    ffn_rows = swap_heads(packed_ffn).reshape(-1, 2 * units)
    model_cotangent = jnp.concatenate(gather_heads(after(cotangent, ffn_rows)))

    positions = block_index * span_rows + jnp.arange(span_rows, dtype=jnp.int32)
    all_positions = jnp.arange(blocks * span_rows, dtype=jnp.int32)
    starts_all = lax.cummax(jnp.where(flags_all > 0, all_positions, 0), axis=0)
    first_visible = lax.dynamic_slice_in_dim(starts_all, block_index * span_rows, span_rows, 0)
    flags_before = jnp.concatenate([jnp.zeros((KW - 2,), jnp.int32), flags_all])
    flag_ext = lax.dynamic_slice_in_dim(
        flags_before, block_index * span_rows, span_rows + KW - 2, 0
    ).astype(jnp.float32)
    segment = jnp.broadcast_to(
        jnp.cumsum(start_flags[0]).astype(jnp.float32)[:, None], (span_rows, lanes)
    )
    view = jnp.stack([block_index, jnp.min(first_visible), jnp.max(first_visible)])
    first_wide = jnp.broadcast_to(first_visible[:, None], (span_rows, lanes))
    keep_masks = [jnp.ones((span_rows,), jnp.float32)]
    for lag_index in range(1, KW):
        begin = KW - 1 - lag_index
        keep_masks.append(keep_masks[-1] * (1.0 - flag_ext[begin : begin + span_rows]))
    frequencies = rope_base ** (-jnp.arange(HD // 2, dtype=jnp.float32) * 2.0 / HD)
    angles = positions.astype(jnp.float32)[:, None] * frequencies[None, :]
    cosine = jnp.cos(angles)
    sine = jnp.sin(angles)
    cosine_wide = jnp.concatenate([cosine, cosine], axis=1)
    sine_wide = jnp.concatenate([-sine, sine], axis=1)
    conv_taps = jnp.concatenate(
        [
            lax.dynamic_slice_in_dim(conv_weight, head_index * inner_columns, inner_columns, 1),
            conv_weight[:, mamba_width:],
        ],
        axis=1,
    )
    conv_shift = jnp.concatenate(
        [
            lax.dynamic_slice_in_dim(conv_bias, head_index * inner_columns, inner_columns, 0),
            conv_bias[mamba_width:],
        ]
    )
    step_shift = lax.dynamic_slice_in_dim(step_bias, head_index * step_heads, step_heads, 0)
    decay_rate = lax.dynamic_slice_in_dim(decay_log, head_index * step_heads, step_heads, 0)
    skip_local = lax.dynamic_slice_in_dim(skip_gain, head_index * step_heads, step_heads, 0)
    skip_wide = jnp.repeat(skip_local, MP)[None, :]

    normed_one = call(
        partial(norm_one, ring=ring),
        [shaped((span_rows, D), low)],
        place,
        [*gathered_tokens, first_gain[None, :]],
        scratch=[pltpu.VMEM((row_count, D), low)],
    )[0]

    projected = jnp.dot(normed_one, weights_conv, preferred_element_type=jnp.float32)
    kv_mine = call(
        rope_kv,
        [shaped((span_rows, HD), low)],
        place,
        [projected[:, kv_at:], cosine_wide, sine_wide],
    )[0]
    pair_bc = projected[:, inner_columns:step_at].astype(low)
    conv_local = call(
        join_conv,
        [shaped((span_rows, inner_columns + 2 * NS), low)],
        place,
        [projected[:, :inner_columns], *gather_heads(pair_bc)],
    )[0]
    step_local = projected[:, step_at : step_at + step_heads].astype(low).astype(jnp.float32)
    rim_rows = passed_along(conv_local[span_rows - (KW - 1) :], "blk", 1)
    extended = jnp.concatenate([rim_rows, conv_local], axis=0).astype(jnp.float32)
    active, conv_back = jax.vjp(
        partial(conv_act, keep_masks=keep_masks), extended, conv_taps, conv_shift
    )
    (step_size, log_decay), step_back = jax.vjp(
        step_and_decay, step_local, step_shift, decay_rate
    )
    inner_act = active[:, :inner_columns]
    into_act = active[:, inner_columns : inner_columns + NS]
    outof_act = active[:, inner_columns + NS :]
    step_wide = in_lanes(step_size)
    decay_wide = in_lanes(log_decay)
    tall = shaped((span_rows, inner_columns), jnp.float32)
    tall_low = shaped((span_rows, inner_columns), low)
    narrow = shaped((span_rows, lanes), jnp.float32)
    share = inner_columns // blocks
    sent = shaped((blocks, extra_rows + share, NS), low)
    state_scratch = pltpu.VMEM((inner_columns, NS), jnp.float32)

    def chained(payload, backwards, after=()):
        got = lax.all_to_all(payload, "blk", split_axis=0, concat_axis=0, tiled=True)
        states = call(
            partial(chain, backwards=backwards),
            [shaped((blocks, share, NS), low)],
            place,
            [got],
            after=after,
        )[0]
        moved = lax.all_to_all(states, "blk", split_axis=0, concat_axis=0, tiled=True)
        return moved.reshape(inner_columns, NS), states

    within, state_sent, entering, factor = call(
        ssd_local,
        [tall, sent, narrow, shaped((8, lanes), jnp.float32)],
        place,
        [inner_act, into_act, outof_act, step_wide, decay_wide, segment],
        after=[ffn_rows],
        scratch=[state_scratch],
        flops=6 * 10**9,
    )
    state_in, states_mine = chained(state_sent, False)

    normed_after = after(normed_one, states_mine)
    projected_rest = jnp.dot(normed_after, weights_rest, preferred_element_type=jnp.float32)
    query_local, gate_act = call(
        rope_query,
        [shaped((span_rows, query_columns), low), tall_low],
        place,
        [projected_rest, cosine_wide, sine_wide],
    )
    out_height = out_weight.shape[0] + span_rows * HD // D
    out_packed = call(
        pack_out, [shaped((out_height, D), low)], place, [out_rows, kv_mine]
    )[0]
    out_gathered = gather_blocks(after(out_packed, weights_rest, state_sent)).reshape(blocks, out_height, D)
    weights_out, kv_blocks = call(
        partial(unpack_out, ring=ring),
        [
            shaped((blocks, *out_weight.shape), low),
            shaped((blocks, span_rows, HD), low),
        ],
        place,
        [out_gathered],
        after=[query_local, states_mine],
    )
    weights_out = weights_out.reshape(-1, D)
    weights_ffn = gather_blocks(after(ffn_rows, out_gathered, query_local, states_mine))
    weights_down = gather_blocks(after(down_weight.astype(low), weights_ffn))
    kv_beside = from_head(kv_blocks, 1)
    keys = jnp.where(even, kv_blocks, kv_beside)
    values = jnp.where(even, kv_beside, kv_blocks)
    attended, lse = attention(
        view, query_local, first_wide, keys, values, [states_mine, model_cotangent]
    )

    ssd, mixer = call(
        ssd_finish,
        [tall, shaped((span_rows, query_columns + inner_columns), low)],
        place,
        [within, entering, outof_act, state_in, inner_act, gate_act, skip_wide, attended],
        flops=2 * 10**9,
    )
    pair_rows = 2 * row_count
    mixed_other = jnp.dot(mixer[pair_rows:], weights_out, preferred_element_type=jnp.float32)
    mixed_own = jnp.dot(mixer[:pair_rows], weights_out, preferred_element_type=jnp.float32)
    mixed = scatter_pairs(mixed_own, mixed_other)
    hidden_one, normed_two = call(
        partial(norm_two, ring=ring),
        [shaped((row_count, D), jnp.float32), shaped((row_count, D), low)],
        place,
        [mixed, tokens, second_gain[None, :]],
        scratch=[pltpu.VMEM((row_count, D), low)],
    )
    model_normed = jnp.concatenate(gather_heads(normed_two))
    gate_up = jnp.dot(model_normed, weights_ffn, preferred_element_type=jnp.float32)
    gate_part, up_part = gate_up[:, :units], gate_up[:, units:]
    activated = (jax.nn.silu(gate_part) * up_part).astype(low)
    grad_down_low = outer_grad(activated, model_cotangent).astype(low)
    grad_activated = times_transposed(model_cotangent, after(weights_down, grad_down_low))
    sigmoid_gate = jax.nn.sigmoid(gate_part)
    grad_gate_up = jnp.concatenate(
        [
            grad_activated * up_part * sigmoid_gate * (1.0 + gate_part * (1.0 - sigmoid_gate)),
            grad_activated * jax.nn.silu(gate_part),
        ],
        axis=1,
    ).astype(low)
    grad_down = scatter_blocks(after(grad_down_low, weights_down))
    gate_up_late = after(grad_gate_up, grad_down_low)
    grad_norm_other = times_transposed(gate_up_late[pair_rows:], weights_ffn).astype(low)
    grad_norm_own = times_transposed(gate_up_late[:pair_rows], weights_ffn)
    grad_normed_two = scatter_pairs(grad_norm_own, grad_norm_other, low)
    grad_ffn_low = outer_grad(model_normed, after(grad_gate_up, grad_norm_own)).astype(low)

    grad_hidden, grad_hidden_low, grad_second = call(
        partial(back_two, ring=ring),
        [
            shaped((row_count, D), jnp.float32),
            shaped((row_count, D), low),
            shaped((8, D), jnp.float32),
        ],
        place,
        [
            grad_normed_two,
            hidden_one,
            cotangent,
            second_gain[None, :],
        ],
        after=[grad_down_low, grad_ffn_low],
        scratch=[pltpu.VMEM((row_count, D), jnp.float32)],
    )
    grad_ffn = scatter_blocks(after(grad_ffn_low, grad_down, grad_hidden_low))
    span_grad_hidden = jnp.concatenate(gather_heads(after(grad_hidden_low, grad_down)))
    grad_heads = times_transposed(span_grad_hidden, weights_out).astype(low)
    grad_ssd, grad_gate, grad_sent, grad_skip_wide, grad_attended = call(
        ssd_gate_back,
        [
            tall,
            tall_low,
            sent,
            shaped((8, inner_columns), jnp.float32),
            shaped((span_rows, query_columns), low),
        ],
        place,
        [grad_heads, gate_act, ssd, inner_act, skip_wide, entering, outof_act, factor],
        scratch=[state_scratch],
        flops=2 * 10**9,
    )
    ffn_swapped = swap_heads(grad_ffn.reshape(4, rows_ffn, 2 * units))
    grad_ffn_weight = call(
        partial(unpack_ffn, ring=ring),
        [shaped(gate_up_weight.shape, jnp.float32)],
        place,
        [ffn_swapped],
    )[0]
    activated_late = after(activated, span_grad_hidden)
    downed_other = jnp.dot(
        activated_late[pair_rows:], weights_down, preferred_element_type=jnp.float32
    )
    downed_own = jnp.dot(
        activated_late[:pair_rows], weights_down, preferred_element_type=jnp.float32
    )
    block_output = (hidden_one + scatter_pairs(downed_own, downed_other, low)).astype(low)

    grad_skip = grad_skip_wide[0].reshape(step_heads, MP).sum(axis=1)
    grad_out_low = outer_grad(mixer, span_grad_hidden).astype(low)
    later_grad, later_mine = chained(grad_sent, True)

    grad_query, grad_keys, grad_values = attention_back(
        view,
        query_local,
        first_wide,
        keys,
        values,
        grad_attended,
        attended,
        lse,
        [grad_out_low],
    )
    kept_kv = jnp.where(even, grad_keys, grad_values)
    given_kv = jnp.where(even, grad_values, grad_keys)
    kv_sums = (kept_kv.astype(jnp.float32) + from_head(given_kv, 1).astype(jnp.float32)).astype(
        low
    )
    grad_rest = call(
        query_back,
        [shaped((span_rows, rest_columns), low)],
        place,
        [grad_query, grad_gate, cosine_wide, sine_wide],
        after=[later_mine],
    )[0]
    grad_rest_low = outer_grad(normed_one, grad_rest).astype(low)

    grad_out_packed = call(
        partial(pack_out_grads, ring=ring),
        [shaped((blocks, out_height, D), low)],
        place,
        [grad_out_low.reshape(blocks, -1, D), kv_sums],
        after=[grad_rest_low],
    )[0]
    grad_out_sum = scatter_blocks(
        after(grad_out_packed.reshape(-1, D), grad_ffn)
    )
    grad_kv = grad_out_sum[out_weight.shape[0] :]
    grad_inner, grad_into, grad_outof, grad_step, grad_decay_line = call(
        ssd_back,
        [
            tall,
            shaped((span_rows, NS), jnp.float32),
            shaped((span_rows, NS), jnp.float32),
            narrow,
            narrow,
        ],
        place,
        [
            inner_act,
            into_act,
            outof_act,
            step_wide,
            decay_wide,
            segment,
            grad_ssd,
            ssd,
            skip_wide,
            state_in,
            later_grad,
        ],
        after=[grad_out_packed, block_output],
        scratch=[
            pltpu.VMEM((span_rows // chunk + 1, inner_columns, NS), jnp.float32),
            state_scratch,
        ],
        flops=10 * 10**9,
    )
    grad_raw, grad_step_shift, grad_rate = step_back(
        (grad_step[:, :step_heads], grad_decay_line[:, :step_heads])
    )
    grad_extended, grad_taps, grad_shift = conv_back(
        jnp.concatenate([grad_inner, grad_into, grad_outof], axis=1)
    )
    rim_back = passed_along(grad_extended[: KW - 1], "blk", -1)
    conv_grad = grad_extended[KW - 1 :] + jnp.pad(rim_back, ((span_rows - (KW - 1), 0), (0, 0)))
    grad_bc = conv_grad[:, inner_columns:].astype(low).astype(jnp.float32)

    def tile_at(distance):
        at = jnp.bitwise_xor(head_index, distance) * lanes
        return lax.dynamic_slice_in_dim(grad_bc, at, lanes, 1)

    bc_beside = from_head(jnp.stack([tile_at(1), tile_at(3)]).astype(low), 1).astype(jnp.float32)
    bc_far = from_head((tile_at(2) + bc_beside[1]).astype(low), 2)
    bc_near = tile_at(0) + bc_beside[0]
    grad_conv = call(
        conv_joined,
        [shaped((span_rows, conv_columns), low)],
        place,
        [
            conv_grad[:, :inner_columns],
            bc_near,
            bc_far,
            in_lanes(grad_raw),
            cosine_wide,
            sine_wide,
            grad_kv,
        ],
        after=[ffn_swapped],
    )[0]
    grad_conv_low = outer_grad(normed_one, grad_conv).astype(low)
    grad_rest_in = scatter_blocks(after(grad_rest_low, grad_out_sum, grad_inner))
    conv_moved, rest_moved = call(
        relative_order,
        [shaped((span_rows, conv_columns), low), shaped((span_rows, rest_columns), low)],
        place,
        [grad_conv, grad_rest],
        after=[grad_conv_low],
    )

    def back_in(part):
        return times_transposed(rest_moved[part], weights_rest) + times_transposed(
            conv_moved[part], weights_conv
        )

    grad_normed_other = back_in(slice(pair_rows, span_rows)).astype(low)
    grad_normed_own = back_in(slice(0, pair_rows))
    rest_swapped = swap_heads(grad_rest_in.reshape(4, rows_in, -1))
    grad_input = call(
        partial(back_one, ring=ring),
        [shaped((row_count, D), low)],
        place,
        [
            scatter_pairs(grad_normed_own, grad_normed_other, low),
            tokens,
            grad_hidden,
            first_gain[None, :],
        ],
        after=[rest_swapped, grad_ffn_weight],
        scratch=[pltpu.VMEM((row_count, D), jnp.float32)],
    )[0]
    first_line = jnp.sum(
        weights_conv.astype(jnp.float32) * grad_conv_low.astype(jnp.float32), axis=1
    ) + jnp.sum(weights_rest.astype(jnp.float32) * after(grad_rest_low, grad_conv_low).astype(jnp.float32), axis=1)
    first_line = first_line.reshape(blocks, 4, -1)
    first_line = jnp.stack([first_line[ring.index(k)] for k in range(blocks)], axis=1).reshape(D)

    def own_part(values_in, total):
        return lax.dynamic_update_slice_in_dim(
            jnp.zeros(values_in.shape[:-1] + (total,), jnp.float32),
            values_in,
            head_index * values_in.shape[-1],
            values_in.ndim - 1,
        )

    small = [
        first_line / first_gain,
        grad_second[0],
        jnp.concatenate(
            [own_part(grad_taps[:, :inner_columns], mamba_width), grad_taps[:, inner_columns:]],
            axis=1,
        ),
        jnp.concatenate(
            [own_part(grad_shift[:inner_columns], mamba_width), grad_shift[inner_columns:]]
        ),
        own_part(grad_step_shift, MH),
        own_part(grad_rate, MH),
        own_part(grad_skip, MH),
    ]
    line = jnp.concatenate([part.reshape(-1) for part in small])
    line = jnp.pad(line, (0, -line.shape[0] % 1024)).reshape(-1, 128)
    line = summed_over(summed_over(line, "head"), "blk").reshape(-1)
    grad_conv_in = scatter_blocks(after(grad_conv_low, grad_rest_in))
    grad_mix_weight = lax.ppermute(
        after(grad_out_sum[: out_weight.shape[0]], grad_conv_in),
        ("head", "blk"),
        [(there, here) for here, there in out_pairs],
    ).astype(jnp.float32)
    grad_proj_weight = call(
        unpack_in,
        [shaped(in_weight.shape, jnp.float32)],
        place,
        [swap_heads(grad_conv_in.reshape(4, rows_in, -1)), rest_swapped],
    )[0]
    summed_small = []
    at = 0
    for part in small:
        summed_small.append(line[at : at + part.size].reshape(part.shape))
        at += part.size
    return (
        block_output[None],
        grad_input[None],
        grad_proj_weight,
        grad_mix_weight,
        grad_ffn_weight,
        grad_down.astype(jnp.float32),
        *summed_small,
    )


def own_first(chunks, mine, order=(0, 1, 2, 3)):
    return [lax.dynamic_index_in_dim(chunks, jnp.bitwise_xor(mine, d), 0, False) for d in order]


def solution(mesh):
    placed = (
        P("blk", "head", None),
        P("blk", "head", None),
        P("blk", None),
        P(("head", "blk"), None),
        P(("head", "blk"), None),
        P(("head", "blk"), None),
        P(("head", "blk"), None),
        P(),
        P(),
        P(),
        P(),
        P(),
        P(),
        P(),
    )
    return jax.shard_map(
        per_device,
        mesh=mesh,
        in_specs=placed,
        out_specs=(
            P("blk", "head", None),
            P("blk", "head", None),
            P(("head", "blk"), None),
            P(("head", "blk"), None),
            P(("head", "blk"), None),
            P(("head", "blk"), None),
            P(),
            P(),
            P(),
            P(),
            P(),
            P(),
            P(),
        ),
        check_vma=False,
    )
```

```python
import math
from functools import partial

import jax
import jax.numpy as jnp
from jax import lax
from jax.experimental import pallas as pl
from jax.experimental.pallas import tpu as pltpu
from jax.sharding import PartitionSpec as P

D = 2048
QH = 8
KVH = 2
HD = 128
MH = 48
MP = 64
NS = 256
FF = 4096
KW = 4


epsilon = 1e-05
rope_base = 100000000000.0
masked_score = -1e30


def after(value, *others):
    return lax.optimization_barrier((value, *others))[0]


def passed_along(shard, axis, by):
    peers = lax.axis_size(axis)
    pairs = [(i, i + by) for i in range(peers) if 0 <= i + by < peers]
    return lax.ppermute(shard, axis, pairs)


def ring_of(axis):
    peers = lax.axis_size(axis)
    if peers != 8:
        return list(range(peers))
    return [0, 2, 4, 6, 7, 5, 3, 1]


def gather_blocks(shard):
    return lax.all_gather(shard, "blk", axis=0, tiled=True, axis_index_groups=[ring_of("blk")])


def scatter_blocks(partial_sums):
    return lax.psum_scatter(
        partial_sums,
        "blk",
        scatter_dimension=0,
        tiled=True,
        axis_index_groups=[ring_of("blk")],
    )


def from_head(shard, distance):
    peers = lax.axis_size("head")
    return lax.ppermute(shard, "head", [(i, i ^ distance) for i in range(peers)])


def gather_heads(shard):
    across = from_head(shard, 2)
    return [shard, across, from_head(shard, 1), from_head(across, 1)]


def in_head_order(parts):
    mine = lax.axis_index("head")
    stacked = jnp.stack([parts[0], parts[2], parts[1], parts[3]])
    return [
        lax.dynamic_index_in_dim(stacked, jnp.bitwise_xor(mine, j), 0, False) for j in range(4)
    ]


def scatter_pairs(own, other, middle=jnp.float32):
    rows = own.shape[0] // 2
    got = from_head(other.astype(middle), 1).astype(jnp.float32)
    far = from_head((own[rows:] + got[rows:]).astype(low), 2)
    return own[:rows] + got[:rows] + far.astype(jnp.float32)


def swap_heads(pieces):
    return lax.all_to_all(pieces, "head", split_axis=0, concat_axis=0, tiled=True)


def mixer_place():
    heads, ring = lax.axis_size("head"), ring_of("blk")
    peers = heads * len(ring)
    rows = (QH * HD + MH * MP) // peers
    query_blocks, mamba_blocks = QH * HD // rows // heads, MH * MP // rows // heads
    pairs = []
    for r in range(peers):
        if r < query_blocks * heads:
            group, slot = divmod(r, query_blocks)
            turn = slot + mamba_blocks
        else:
            group, turn = divmod(r - query_blocks * heads, mamba_blocks)
            slot = turn + query_blocks
        block = (mamba_blocks * group + turn) % len(ring) if len(ring) == 8 else ring[slot]
        pairs.append((r, group * len(ring) + block))
    return pairs


kv_begin = QH * HD
z_begin = kv_begin + 2 * KVH * HD
x_begin = z_begin + MH * MP
b_begin = x_begin + MH * MP
dt_begin = b_begin + 2 * NS
query_columns = QH * HD // 4
inner_columns = MH * MP // 4
bc_columns = 2 * NS // 4
step_heads = MH // 4
step_at = inner_columns + bc_columns
kv_at = step_at + 128
conv_columns = kv_at + HD
rest_columns = query_columns + inner_columns


def column_parts(head):
    conv = [
        (x_begin + head * inner_columns, 0, inner_columns),
        (b_begin + head * bc_columns, inner_columns, bc_columns),
        (kv_begin + (head % 2) * KVH * HD + (head // 2) * HD, kv_at, HD),
    ]
    rest = [
        (head * query_columns, 0, query_columns),
        (z_begin + head * inner_columns, query_columns, inner_columns),
    ]
    return conv, rest


def pack_in(place_ref, weight_ref, conv_ref, rest_ref, tail_ref):
    tail_ref[...] = jnp.zeros_like(tail_ref)
    tail_ref[:, :MH] = weight_ref[:, dt_begin : dt_begin + MH]
    last = tail_ref[...]
    lane = iota(last.shape, 1)
    for head in range(4):
        for parts, ref in zip(column_parts(head), (conv_ref, rest_ref)):
            for begin, at, size in parts:
                ref[head, :, at : at + size] = weight_ref[:, begin : begin + size].astype(low)
        steps = pltpu.roll(last, lanes - step_heads * head, 1) if head else last
        conv_ref[head, :, step_at:kv_at] = jnp.where(lane < step_heads, steps, 0.0).astype(low)


def unpack_in(place_ref, conv_ref, rest_ref, out_ref):
    total = jnp.zeros((out_ref.shape[0], lanes), jnp.float32)
    lane = iota(total.shape, 1)
    for head in range(4):
        for parts, ref in zip(column_parts(head), (conv_ref, rest_ref)):
            for begin, at, size in parts:
                out_ref[:, begin : begin + size] = ref[head, :, at : at + size].astype(jnp.float32)
        steps = conv_ref[head, :, step_at:kv_at].astype(jnp.float32)
        steps = jnp.where(lane < step_heads, steps, 0.0)
        total = total + (pltpu.roll(steps, step_heads * head, 1) if head else steps)
    out_ref[:, dt_begin : dt_begin + MH] = total[:, :MH]


def ffn_moves(ring):
    unit = FF // (4 * len(ring))
    return unit, [
        (
            head,
            half * FF + (head * len(ring) + k) * unit,
            half * (FF // 4) + i * unit,
        )
        for half in range(2)
        for head in range(4)
        for i, k in enumerate(ring)
    ]


def pack_ffn(place_ref, weight_ref, out_ref, *, ring):
    unit, moves = ffn_moves(ring)
    for head, begin, at in moves:
        out_ref[head, :, at : at + unit] = weight_ref[:, begin : begin + unit].astype(low)


def unpack_ffn(place_ref, in_ref, out_ref, *, ring):
    unit, moves = ffn_moves(ring)
    for head, begin, at in moves:
        out_ref[:, begin : begin + unit] = in_ref[head, :, at : at + unit].astype(jnp.float32)


def inverse_rms(values_in):
    return lax.rsqrt(jnp.mean(values_in * values_in, axis=1, keepdims=True) + epsilon)


def feature_moves(ring):
    piece = D // 4 // len(ring)
    return piece, [
        ((e * len(ring) + k) * piece, (4 * i + e) * piece)
        for e in range(4)
        for i, k in enumerate(ring)
    ]


def whole_lanes(begin, size):
    return pl.ds(pl.multiple_of(begin, 128), size)


def norm_one(place_ref, own, across, beside, both, gain_ref, out_ref, line_ref, *, ring):
    rows = own.shape[0]
    piece, moves = feature_moves(ring)
    for distance, ref in ((0, own), (2, across), (1, beside), (3, both)):
        x = ref[...].astype(jnp.float32)
        line_ref[...] = (x * inverse_rms(x) * gain_ref[...]).astype(low)
        there = jnp.bitwise_xor(place_ref[0], distance) * rows
        there = pl.ds(pl.multiple_of(there, rows), rows)
        for source, at in moves:
            out_ref[there, at : at + piece] = line_ref[:, source : source + piece]


def norm_two(place_ref, mixed_ref, tokens_ref, gain_ref, hidden_ref, out_ref, line_ref, *, ring):
    hidden = tokens_ref[...].astype(jnp.float32) + mixed_ref[...]
    hidden_ref[...] = hidden
    line_ref[...] = (hidden * inverse_rms(hidden) * gain_ref[...]).astype(low)
    piece, moves = feature_moves(ring)
    for source, at in moves:
        out_ref[:, at : at + piece] = line_ref[:, source : source + piece]


def back_two(
    place_ref, grad_ref, hidden_ref, cotangent_ref, gain_ref, out_ref, low_ref, sum_ref, plain_ref,
    *, ring,
):
    piece, moves = feature_moves(ring)
    for source, at in moves:
        plain_ref[:, source : source + piece] = grad_ref[:, at : at + piece]
    grad = plain_ref[...]
    hidden = hidden_ref[...]
    inverse = inverse_rms(hidden)
    scaled = grad * gain_ref[...]
    total = (
        cotangent_ref[...].astype(jnp.float32)
        + inverse * scaled
        - hidden * (inverse * inverse * inverse * jnp.mean(scaled * hidden, axis=1, keepdims=True))
    )
    out_ref[...] = total
    low_ref[...] = total.astype(low)
    sum_ref[...] = jnp.broadcast_to(
        jnp.sum(grad * hidden * inverse, axis=0, keepdims=True), sum_ref.shape
    )


def back_one(
    place_ref, grad_ref, tokens_ref, hidden_ref, gain_ref, out_ref, plain_ref, *, ring
):
    piece, moves = feature_moves(ring)
    for source, at in moves:
        plain_ref[:, source : source + piece] = grad_ref[:, at : at + piece]
    grad = plain_ref[...]
    x = tokens_ref[...].astype(jnp.float32)
    inverse = inverse_rms(x)
    scaled = grad * gain_ref[...]
    out_ref[...] = (
        hidden_ref[...]
        + inverse * scaled
        - x * (inverse * inverse * inverse * jnp.mean(scaled * x, axis=1, keepdims=True))
    ).astype(low)


def turned(values_in, cosine, sine):
    return values_in * cosine + pltpu.roll(values_in, HD // 2, 1) * sine


def rope_kv(place_ref, in_ref, cosine_ref, sine_ref, out_ref):
    kv = in_ref[...]
    out_ref[...] = jnp.where(
        place_ref[1] == 0, turned(kv, cosine_ref[...], sine_ref[...]), kv
    ).astype(low)


def kv_moves(span):
    height = span * HD // D
    return height, [(j * height, j * HD) for j in range(D // HD)]


def pack_out(place_ref, out_rows_ref, kv_ref, packed_ref):
    rows = out_rows_ref.shape[0]
    packed_ref[:rows, :] = out_rows_ref[...]
    height, moves = kv_moves(kv_ref.shape[0])
    for begin, at in moves:
        packed_ref[rows:, at : at + HD] = kv_ref[begin : begin + height, :]


def unpack_out(place_ref, packed_ref, out_ref, kv_ref, *, ring):
    rows = out_ref.shape[1]
    height, moves = kv_moves(kv_ref.shape[1])
    for i, k in enumerate(ring):
        out_ref[i] = packed_ref[i, :rows, :]
        for begin, at in moves:
            kv_ref[k, begin : begin + height, :] = packed_ref[i, rows:, at : at + HD]


def pack_out_grads(place_ref, out_ref, kv_ref, packed_ref, *, ring):
    rows = out_ref.shape[1]
    height, moves = kv_moves(kv_ref.shape[1])
    for i, k in enumerate(ring):
        packed_ref[i, :rows, :] = out_ref[i]
        for begin, at in moves:
            packed_ref[i, rows:, at : at + HD] = kv_ref[k, begin : begin + height, :]


def rope_query(place_ref, in_ref, cosine_ref, sine_ref, query_ref, gate_ref):
    cosine, sine = cosine_ref[...], sine_ref[...]
    for begin in range(0, query_columns, HD):
        query_ref[:, begin : begin + HD] = turned(
            in_ref[:, begin : begin + HD], cosine, sine
        ).astype(low)
    gate_ref[...] = in_ref[:, query_columns:].astype(low)


def query_back(place_ref, query_ref, gate_ref, cosine_ref, sine_ref, out_ref):
    cosine, sine = cosine_ref[...], -sine_ref[...]
    for begin in range(0, query_columns, HD):
        rounded = query_ref[:, begin : begin + HD].astype(low).astype(jnp.float32)
        out_ref[:, begin : begin + HD] = turned(rounded, cosine, sine).astype(low)
    out_ref[:, query_columns:] = gate_ref[...]


def join_conv(place_ref, inner_ref, own, across, beside, both, out_ref):
    out_ref[:, :inner_columns] = inner_ref[...].astype(low)
    for distance, ref in ((0, own), (2, across), (1, beside), (3, both)):
        at = inner_columns + jnp.bitwise_xor(place_ref[0], distance) * lanes
        out_ref[:, whole_lanes(at, lanes)] = ref[...]


def conv_joined(
    place_ref, inner_ref, near_ref, far_ref, step_ref, cosine_ref, sine_ref, kv_ref, out_ref
):
    out_ref[:, :inner_columns] = inner_ref[...].astype(low)
    out_ref[:, inner_columns:step_at] = (near_ref[...] + far_ref[...].astype(jnp.float32)).astype(low)
    out_ref[:, step_at:kv_at] = step_ref[...].astype(low)
    height, moves = kv_moves(out_ref.shape[0])
    for begin, at in moves:
        rows = slice(begin, begin + height)
        kv = kv_ref[:, at : at + HD].astype(jnp.float32)
        out_ref[rows, kv_at:] = jnp.where(
            place_ref[1] == 0, turned(kv, cosine_ref[rows, :], -sine_ref[rows, :]), kv
        ).astype(low)


def relative_order(place_ref, first_ref, second_ref, first_out, second_out):
    for at, distance in enumerate((0, 2, 1, 3)):
        there = jnp.bitwise_xor(place_ref[0], distance) * chunk
        there = pl.ds(pl.multiple_of(there, chunk), chunk)
        rows = slice(at * chunk, (at + 1) * chunk)
        first_out[rows, :] = first_ref[there, :]
        second_out[rows, :] = second_ref[there, :]


def outer_grad(left_side, grad_side):
    return lax.dot_general(
        left_side, grad_side, (((0,), (0,)), ((), ())), preferred_element_type=jnp.float32
    )


def times_transposed(grad_side, weight):
    return lax.dot_general(
        grad_side, weight, (((1,), (1,)), ((), ())), preferred_element_type=jnp.float32
    )


chunk = 128
lanes = 128
low = jnp.bfloat16
exact = lax.Precision.HIGHEST


def dot_nn(a, b, precision=None):
    return lax.dot_general(
        a, b, (((1,), (0,)), ((), ())), precision=precision, preferred_element_type=jnp.float32
    )


def dot_nt(a, b):
    return lax.dot_general(a, b, (((1,), (1,)), ((), ())), preferred_element_type=jnp.float32)


def dot_tn(a, b):
    return lax.dot_general(a, b, (((0,), (0,)), ((), ())), preferred_element_type=jnp.float32)


def iota(shape, dim):
    return lax.broadcasted_iota(jnp.int32, shape, dim)


def spread(per_head, pair):
    rows = per_head.shape[0]
    first = per_head[:, 2 * pair : 2 * pair + 1]
    second = per_head[:, 2 * pair + 1 : 2 * pair + 2]
    return jnp.where(iota((rows, lanes), 1) < MP, first, second)


def head_sums(products, pair):
    mine = 2 * pair + (iota((lanes, lanes), 0) >= MP).astype(jnp.int32)
    ones = (mine == iota((lanes, lanes), 1)).astype(jnp.float32)
    return dot_nn(products, ones, exact)


def chunk_terms(decay, segment, segment_before):
    lower = iota((chunk, chunk), 0) >= iota((chunk, chunk), 1)
    cumulative = dot_nn(lower.astype(jnp.float32), decay, exact)
    total = cumulative[chunk - 1 :, :]
    segment_end = segment[chunk - 1 :, :]
    related = lower & (segment == segment.T)
    entering = jnp.where(segment == segment_before, jnp.exp(cumulative), 0.0)
    ending = jnp.where(segment == segment_end, jnp.exp(total - cumulative), 0.0)
    whole = jnp.where(segment_end == segment_before, jnp.exp(total), 0.0)
    return cumulative, cumulative.T, related, entering, ending, whole, total, segment_end


def decays_of(cumulative, transposed, related, head):
    apart = cumulative[:, head : head + 1] - transposed[head : head + 1, :]
    return jnp.exp(jnp.where(related, apart, masked_score))


def row_factor(whole, pair, width):
    first = whole[:, 2 * pair : 2 * pair + 1]
    second = whole[:, 2 * pair + 1 : 2 * pair + 2]
    return jnp.where(iota((lanes, width), 0) < MP, first, second)


def chunk_rows(index):
    return pl.ds(pl.multiple_of(index * chunk, chunk), chunk)


def pack_states(state_ref, factor, out_ref):
    blocks, rows, width = out_ref.shape
    share = rows - extra_rows
    row = iota((extra_rows, width), 0)
    for k in range(blocks):
        extra = jnp.zeros((extra_rows, width), jnp.float32)
        for e in range(4):
            head = k * share // MP + e
            if head * MP < state_ref.shape[0]:
                whole = factor[:, head : head + 1]
                rough = whole.astype(low).astype(jnp.float32)
                extra = jnp.where(row == e, rough, extra)
                extra = jnp.where(row == 4 + e, whole - rough, extra)
        out_ref[k, :extra_rows, :] = extra.astype(low)
        out_ref[k, extra_rows:, :] = state_ref[k * share : (k + 1) * share, :].astype(low)


extra_rows = 16


def chain(place_ref, got_ref, out_ref, backwards):
    blocks, rows, width = got_ref.shape
    share = rows - extra_rows
    row = iota((share, width), 0) + lax.rem(place_ref[4] * share, MP)
    state = jnp.zeros((share, width), jnp.float32)
    for k in range(blocks - 1, -1, -1) if backwards else range(blocks):
        out_ref[k] = state.astype(low)
        extra = got_ref[k, :extra_rows, :].astype(jnp.float32)
        factor = extra[0:1, :] + extra[4:5, :]
        for e in range(1, 4):
            factor = jnp.where(row >= e * MP, extra[e : e + 1, :] + extra[4 + e : 5 + e, :], factor)
        state = factor * state + got_ref[k, extra_rows:, :].astype(jnp.float32)


def ssd_local(
    place_ref, x_ref, b_ref, c_ref, step_ref, decay_ref, seg_ref,
    y_ref, sent_ref, enter_ref, fac_ref, state_ref,
):
    pairs = x_ref.shape[1] // lanes
    state_ref[...] = jnp.zeros_like(state_ref)

    def body(index, carry):
        segment_before, base = carry
        rows = chunk_rows(index)
        segment = seg_ref[rows, :]
        cumulative, transposed, related, entering, ending, whole, total, segment_end = chunk_terms(
            decay_ref[rows, :], segment, segment_before
        )
        enter_ref[rows, :] = jnp.where(segment == 0.0, jnp.exp(base + cumulative), 0.0)
        into = b_ref[rows, :].astype(low)
        outof = c_ref[rows, :].astype(low)
        step = step_ref[rows, :]
        scores = dot_nt(outof, into)
        left = iota((chunk, lanes), 1) < MP
        for pair in range(pairs):
            cols = slice(pair * lanes, (pair + 1) * lanes)
            taken = x_ref[rows, cols] * spread(step, pair)
            taken_low = taken.astype(low)
            parts = []
            for head in (2 * pair, 2 * pair + 1):
                weights = decays_of(cumulative, transposed, related, head) * scores
                parts.append(dot_nn(weights.astype(low), taken_low))
            state = state_ref[cols, :]
            y_ref[rows, cols] = jnp.where(left, parts[0], parts[1]) + spread(
                entering, pair
            ) * dot_nt(outof, state.astype(low))
            kept = (taken * spread(ending, pair)).astype(low)
            state_ref[cols, :] = row_factor(whole, pair, state.shape[1]) * state + dot_tn(
                kept, into
            )
        return segment_end, base + total

    start = jnp.zeros((1, lanes), jnp.float32)
    segment_end, base = lax.fori_loop(0, x_ref.shape[0] // chunk, body, (start, start))
    factor = jnp.where(segment_end == 0.0, jnp.exp(base), 0.0)
    fac_ref[...] = jnp.broadcast_to(factor, fac_ref.shape)
    pack_states(state_ref, factor, sent_ref)


def relative_rows(place_ref, index):
    distance = jnp.bitwise_xor(place_ref[0], index)
    at = (distance % 2) * 2 + distance // 2
    return pl.ds(pl.multiple_of(at * chunk, chunk), chunk)


def mixer_lanes(place_ref, part, turned_columns):
    if not turned_columns:
        begin = (part + 2) % 8 * lanes
        return slice(begin, begin + lanes)
    block = lax.rem(6 * place_ref[0] + part, 8)
    at = jnp.where(block % 2 == 0, block // 2, 7 - block // 2)
    return pl.ds(pl.multiple_of(at * lanes, lanes), lanes)


def ssd_finish(
    place_ref, y_ref, enter_ref, c_ref, state_ref, x_ref, z_ref, skip_ref, attended_ref,
    ssd_ref, mixer_ref, *, turned_columns,
):
    pairs = x_ref.shape[1] // lanes

    def body(index, carry):
        rows = chunk_rows(index)
        there = relative_rows(place_ref, index)
        outof = c_ref[rows, :].astype(low)
        entering = enter_ref[rows, :]
        for half in range(2):
            mixer_ref[there, mixer_lanes(place_ref, 6 + half, turned_columns)] = attended_ref[
                rows, half * lanes : (half + 1) * lanes
            ].astype(low)
        for pair in range(pairs):
            cols = slice(pair * lanes, (pair + 1) * lanes)
            ssd = y_ref[rows, cols] + spread(entering, pair) * dot_nt(outof, state_ref[cols, :])
            ssd_ref[rows, cols] = ssd
            gate = z_ref[rows, cols].astype(jnp.float32)
            total = ssd + skip_ref[:, cols] * x_ref[rows, cols]
            mixer_ref[there, mixer_lanes(place_ref, pair, turned_columns)] = (
                total * gate / (1.0 + jnp.exp(-gate))
            ).astype(low)
        return carry

    lax.fori_loop(0, x_ref.shape[0] // chunk, body, 0)


def ssd_gate_back(
    place_ref, grad_ref, z_ref, ssd_ref, x_ref, skip_ref, enter_ref, c_ref, fac_ref,
    dy_ref, dz_ref, sent_ref, dskip_ref, datt_ref, dstate_ref, *, turned_columns,
):
    pairs = x_ref.shape[1] // lanes
    dstate_ref[...] = jnp.zeros_like(dstate_ref)
    dskip_ref[...] = jnp.zeros_like(dskip_ref)

    def body(index, carry):
        rows = chunk_rows(index)
        there = relative_rows(place_ref, index)
        outof = c_ref[rows, :].astype(low)
        entering = enter_ref[rows, :]
        for half in range(2):
            datt_ref[rows, half * lanes : (half + 1) * lanes] = grad_ref[
                there, mixer_lanes(place_ref, 6 + half, turned_columns)
            ]
        for pair in range(pairs):
            cols = slice(pair * lanes, (pair + 1) * lanes)
            gate = z_ref[rows, cols].astype(jnp.float32)
            sigmoid = 1.0 / (1.0 + jnp.exp(-gate))
            grad = grad_ref[there, mixer_lanes(place_ref, pair, turned_columns)].astype(
                jnp.float32
            )
            x = x_ref[rows, cols]
            total = ssd_ref[rows, cols] + skip_ref[:, cols] * x
            dz_ref[rows, cols] = (
                grad * total * sigmoid * (1.0 + gate * (1.0 - sigmoid))
            ).astype(low)
            dy = grad * gate * sigmoid
            dy_ref[rows, cols] = dy
            dskip_ref[:, cols] += jnp.broadcast_to(
                jnp.sum(dy * x, axis=0, keepdims=True), (dskip_ref.shape[0], lanes)
            )
            dstate_ref[cols, :] += dot_tn((dy * spread(entering, pair)).astype(low), outof)
        return carry

    lax.fori_loop(0, x_ref.shape[0] // chunk, body, 0)
    pack_states(dstate_ref, fac_ref[:1, :], sent_ref)


def ssd_back(
    place_ref, x_ref, b_ref, c_ref, step_ref, decay_ref, seg_ref, dy_ref, ssd_ref, skip_ref, state_ref, later_ref,
    dx_ref, db_ref, dc_ref, dstep_ref, ddecay_ref, states, grads,
):
    pairs = x_ref.shape[1] // lanes
    chunks = x_ref.shape[0] // chunk
    zero_row = jnp.zeros((1, lanes), jnp.float32)

    def before(index):
        rows = pl.ds(pl.multiple_of(jnp.maximum(index - 1, 0) * chunk, chunk), chunk)
        return jnp.where(index == 0, 0.0, seg_ref[rows, :][chunk - 1 :, :])

    states[0] = state_ref[...].astype(jnp.float32)

    def forward(index, carry):
        rows = chunk_rows(index)
        _, _, _, _, ending, whole, _, _ = chunk_terms(
            decay_ref[rows, :], seg_ref[rows, :], before(index)
        )
        into = b_ref[rows, :].astype(low)
        step = step_ref[rows, :]
        for pair in range(pairs):
            cols = slice(pair * lanes, (pair + 1) * lanes)
            kept = (x_ref[rows, cols] * spread(step, pair) * spread(ending, pair)).astype(low)
            state = states[index, cols, :]
            states[index + 1, cols, :] = row_factor(
                whole, pair, state.shape[1]
            ) * state + dot_tn(kept, into)
        return carry

    lax.fori_loop(0, chunks, forward, 0)
    grads[...] = later_ref[...].astype(jnp.float32)
    last = jnp.zeros((8, lanes), jnp.float32)
    for pair in range(pairs):
        cols = slice(pair * lanes, (pair + 1) * lanes)
        product = grads[cols, :] * states[chunks, cols, :]
        along = lax.dot_general(
            jnp.ones((8, product.shape[1]), jnp.float32),
            product,
            (((1,), (1,)), ((), ())),
            precision=exact,
            preferred_element_type=jnp.float32,
        )
        last = last + head_sums(along, pair)

    def backward(at, carry):
        index = chunks - 1 - at
        rows = chunk_rows(index)
        cumulative, transposed, related, entering, ending, whole, _, _ = chunk_terms(
            decay_ref[rows, :], seg_ref[rows, :], before(index)
        )
        into = b_ref[rows, :].astype(low)
        outof = c_ref[rows, :].astype(low)
        step = step_ref[rows, :]
        scores = dot_nt(outof, into)
        left = iota((chunk, lanes), 1) < MP
        grad_scores = jnp.zeros((chunk, chunk), jnp.float32)
        grad_into = jnp.zeros((chunk, b_ref.shape[1]), jnp.float32)
        grad_outof = jnp.zeros((chunk, b_ref.shape[1]), jnp.float32)
        grad_cum = jnp.zeros((chunk, lanes), jnp.float32)
        grad_step = jnp.zeros((chunk, lanes), jnp.float32)
        for pair in range(pairs):
            cols = slice(pair * lanes, (pair + 1) * lanes)
            x = x_ref[rows, cols]
            step_pair = spread(step, pair)
            taken = x * step_pair
            taken_low = taken.astype(low)
            dy = dy_ref[rows, cols]
            dy_low = dy.astype(low)
            parts = []
            for half, head in enumerate((2 * pair, 2 * pair + 1)):
                decays = decays_of(cumulative, transposed, related, head)
                parts.append(dot_tn((decays * scores).astype(low), dy_low))
                own = jnp.where(left if half == 0 else ~left, dy_low, jnp.zeros_like(dy_low))
                grad_scores = grad_scores + decays * dot_nt(own, taken_low)
            later = grads[cols, :]
            later_low = later.astype(low)
            ending_pair = spread(ending, pair)
            grad_taken = jnp.where(left, parts[0], parts[1]) + ending_pair * dot_nt(
                into, later_low
            )
            grad_into = grad_into + dot_nn((taken * ending_pair).astype(low), later_low)
            dy_enter = (dy * spread(entering, pair)).astype(low)
            grad_outof = grad_outof + dot_nn(dy_enter, states[index, cols, :].astype(low))
            grads[cols, :] = row_factor(whole, pair, later.shape[1]) * later + dot_tn(
                dy_enter, outof
            )
            grad_cum = grad_cum + head_sums(dy * ssd_ref[rows, cols] - taken * grad_taken, pair)
            grad_step = grad_step + head_sums(x * grad_taken, pair)
            dx_ref[rows, cols] = step_pair * grad_taken + skip_ref[:, cols] * dy
        grad_scores_low = grad_scores.astype(low)
        db_ref[rows, :] = grad_into + dot_tn(grad_scores_low, outof)
        dc_ref[rows, :] = grad_outof + dot_nn(grad_scores_low, into)
        dstep_ref[rows, :] = grad_step
        upper = (iota((chunk, chunk), 0) <= iota((chunk, chunk), 1)).astype(jnp.float32)
        ddecay_ref[rows, :] = dot_nn(upper, grad_cum, exact) + carry
        return carry + jnp.sum(grad_cum, axis=0, keepdims=True)

    lax.fori_loop(0, chunks, backward, last[:1, :] + zero_row)


def needed_and_plain(place_ref, block, span):
    mine, earliest, latest = place_ref[0], place_ref[1], place_ref[2]
    needed = (block <= mine) & ((block + 1) * span > earliest)
    return needed, (block < mine) & (block * span >= latest)


def visible_keys(place_ref, first_ref, block, span):
    key_pos = block * span + iota((span, span), 1)
    query_pos = place_ref[0] * span + iota((span, span), 0)
    return (key_pos <= query_pos) & (key_pos >= first_ref[:, :1])


def attend(place_ref, q_ref, first_ref, k_ref, v_ref, out_ref, lse_ref, top, total, summed):
    block = pl.program_id(0)
    span = q_ref.shape[0]
    heads = q_ref.shape[1] // HD

    @pl.when(block == 0)
    def _():
        top[...] = jnp.full_like(top, masked_score)
        total[...] = jnp.zeros_like(total)
        summed[...] = jnp.zeros_like(summed)

    def one(masked):
        keys = k_ref[0]
        values = v_ref[0]
        if masked:
            visible = visible_keys(place_ref, first_ref, block, span)
        for head in range(heads):
            cols = slice(head * HD, (head + 1) * HD)
            scores = dot_nt(q_ref[:, cols], keys) * HD**-0.5
            if masked:
                scores = jnp.where(visible, scores, masked_score)
            old_top = top[head][:, :1]
            new_top = jnp.maximum(old_top, jnp.max(scores, axis=1, keepdims=True))
            weights = jnp.exp(scores - new_top)
            if masked:
                weights = jnp.where(visible, weights, 0.0)
            scale = jnp.exp(old_top - new_top)
            total[head] = total[head] * scale + jnp.sum(weights, axis=1, keepdims=True)
            top[head] = jnp.broadcast_to(new_top, (span, lanes))
            summed[head] = summed[head] * scale + dot_nn(weights.astype(low), values)

    needed, plain = needed_and_plain(place_ref, block, span)
    pl.when(needed & plain)(lambda: one(False))
    pl.when(needed & jnp.logical_not(plain))(lambda: one(True))

    @pl.when(block == pl.num_programs(0) - 1)
    def _():
        for head in range(heads):
            cols = slice(head * HD, (head + 1) * HD)
            out_ref[:, cols] = summed[head] / total[head]
            lse_ref[head] = top[head] + jnp.log(total[head])


def attend_back(
    place_ref, q_ref, first_ref, k_ref, v_ref, grad_ref, out_ref, lse_ref, dq_ref, dk_ref, dv_ref
):
    block = pl.program_id(0)
    span = q_ref.shape[0]
    heads = q_ref.shape[1] // HD

    @pl.when(block == 0)
    def _():
        dq_ref[...] = jnp.zeros_like(dq_ref)

    def one(masked):
        keys = k_ref[0]
        values = v_ref[0]
        if masked:
            visible = visible_keys(place_ref, first_ref, block, span)
        grad_keys = jnp.zeros(keys.shape, jnp.float32)
        grad_values = jnp.zeros(keys.shape, jnp.float32)
        for head in range(heads):
            cols = slice(head * HD, (head + 1) * HD)
            query = q_ref[:, cols]
            grad = grad_ref[:, cols]
            delta = jnp.sum(
                grad.astype(jnp.float32) * out_ref[:, cols], axis=1, keepdims=True
            )
            scores = dot_nt(query, keys) * HD**-0.5
            if masked:
                scores = jnp.where(visible, scores, masked_score)
            weights = jnp.exp(scores - lse_ref[head][:, :1])
            changes = weights * (dot_nt(grad, values) - delta)
            weights_low = weights.astype(low)
            changes_low = (changes * HD**-0.5).astype(low)
            grad_values = grad_values + dot_tn(weights_low, grad)
            grad_keys = grad_keys + dot_tn(changes_low, query)
            dq_ref[:, cols] += dot_nn(changes_low, keys)
        dk_ref[0] = grad_keys.astype(low)
        dv_ref[0] = grad_values.astype(low)

    needed, plain = needed_and_plain(place_ref, block, span)
    pl.when(needed & plain)(lambda: one(False))
    pl.when(needed & jnp.logical_not(plain))(lambda: one(True))

    @pl.when(jnp.logical_not(needed))
    def _():
        dk_ref[...] = jnp.zeros_like(dk_ref)
        dv_ref[...] = jnp.zeros_like(dv_ref)


def shaped(shape, kind):
    return jax.ShapeDtypeStruct(shape, kind)


def call(kernel, outputs, place, operands, after=(), scratch=(), flops=10**6):
    count, skipped = len(operands), len(operands) + len(after)
    sizes = sum(math.prod(a.shape) * a.dtype.itemsize for a in (*operands, *outputs))

    def body(place_ref, *refs):
        kernel(place_ref, *refs[:count], *refs[skipped:])

    return pl.pallas_call(
        body,
        out_shape=outputs,
        in_specs=[pl.BlockSpec(memory_space=pltpu.SMEM)]
        + [pl.BlockSpec(memory_space=pltpu.VMEM)] * count
        + [pl.BlockSpec(memory_space=pl.ANY)] * len(after),
        out_specs=[pl.BlockSpec(memory_space=pltpu.VMEM)] * len(outputs),
        scratch_shapes=list(scratch),
        compiler_params=pltpu.CompilerParams(vmem_limit_bytes=kernel_memory),
        cost_estimate=pl.CostEstimate(flops=flops, bytes_accessed=sizes, transcendentals=0),
    )(place, *operands, *after)


kernel_memory = 44 * 1024 * 1024


def attention(place, query, first_visible, keys, values, after):
    away, span = keys.shape[0], query.shape[0]
    heads = query.shape[1] // HD
    same = lambda d, place: (0, 0)
    block = lambda d, place: (d, 0, 0)
    def body(*refs):
        attend(*refs[:5], *refs[5 + len(after) :])

    return pl.pallas_call(
        body,
        grid_spec=pltpu.PrefetchScalarGridSpec(
            num_scalar_prefetch=1,
            grid=(away,),
            in_specs=[
                pl.BlockSpec(query.shape, same),
                pl.BlockSpec(first_visible.shape, same),
                pl.BlockSpec((1, span, HD), block),
                pl.BlockSpec((1, span, HD), block),
            ]
            + [pl.BlockSpec(memory_space=pl.ANY)] * len(after),
            out_specs=[
                pl.BlockSpec(query.shape, same),
                pl.BlockSpec((heads, span, lanes), lambda d, place: (0, 0, 0)),
            ],
            scratch_shapes=[
                pltpu.VMEM((heads, span, lanes), jnp.float32),
                pltpu.VMEM((heads, span, lanes), jnp.float32),
                pltpu.VMEM((heads, span, HD), jnp.float32),
            ],
        ),
        out_shape=[
            shaped(query.shape, jnp.float32),
            shaped((heads, span, lanes), jnp.float32),
        ],
        compiler_params=pltpu.CompilerParams(vmem_limit_bytes=kernel_memory),
        cost_estimate=pl.CostEstimate(
            flops=20 * 10**9, bytes_accessed=4 * 10**6, transcendentals=0
        ),
    )(place, query, first_visible, keys, values, *after)


def attention_back(place, query, first_visible, keys, values, grad, out, lse, after):
    away, span = keys.shape[0], query.shape[0]
    same = lambda d, place: (0, 0)
    block = lambda d, place: (d, 0, 0)
    def body(*refs):
        attend_back(*refs[:8], *refs[8 + len(after) :])

    return pl.pallas_call(
        body,
        grid_spec=pltpu.PrefetchScalarGridSpec(
            num_scalar_prefetch=1,
            grid=(away,),
            in_specs=[
                pl.BlockSpec(query.shape, same),
                pl.BlockSpec(first_visible.shape, same),
                pl.BlockSpec((1, span, HD), block),
                pl.BlockSpec((1, span, HD), block),
                pl.BlockSpec(query.shape, same),
                pl.BlockSpec(query.shape, same),
                pl.BlockSpec(lse.shape, lambda d, place: (0, 0, 0)),
            ]
            + [pl.BlockSpec(memory_space=pl.ANY)] * len(after),
            out_specs=[
                pl.BlockSpec(query.shape, same),
                pl.BlockSpec((1, span, HD), block),
                pl.BlockSpec((1, span, HD), block),
            ],
        ),
        out_shape=[
            shaped(query.shape, jnp.float32),
            shaped(keys.shape, low),
            shaped(keys.shape, low),
        ],
        compiler_params=pltpu.CompilerParams(vmem_limit_bytes=kernel_memory),
        cost_estimate=pl.CostEstimate(
            flops=30 * 10**9, bytes_accessed=4 * 10**6, transcendentals=0
        ),
    )(place, query, first_visible, keys, values, grad, out, lse, *after)


def conv_act(extended, conv_taps, conv_shift, keep_masks):
    length = keep_masks[0].shape[0]
    result = conv_shift + conv_taps[0] * extended[KW - 1 :]
    for lag_index in range(1, KW):
        begin = KW - 1 - lag_index
        result = (
            result
            + conv_taps[lag_index]
            * keep_masks[lag_index][:, None]
            * extended[begin : begin + length]
        )
    return jax.nn.silu(result)


def step_and_decay(step_raw, step_shift, decay_rate):
    step_size = jax.nn.softplus(step_raw + step_shift)
    return step_size, -step_size * jnp.exp(decay_rate)


def in_lanes(per_head):
    return jnp.pad(per_head, ((0, 0), (0, lanes - per_head.shape[1])))


def summed_over(values_in, axis):
    peers = lax.axis_size(axis)
    by = 1
    while by < peers:
        values_in = values_in + lax.ppermute(values_in, axis, [(i, i ^ by) for i in range(peers)])
        by *= 2
    return values_in


def per_device(
    block_input,
    out_cotangent,
    start_flags,
    in_weight,
    out_weight,
    gate_up_weight,
    down_weight,
    first_gain,
    second_gain,
    conv_weight,
    conv_bias,
    step_bias,
    decay_log,
    skip_gain,
):
    head_count = lax.axis_size("head")
    blocks = lax.axis_size("blk")
    head_index = lax.axis_index("head")
    block_index = lax.axis_index("blk")
    ring = ring_of("blk")
    tokens = block_input[0]
    cotangent = out_cotangent[0]
    row_count = tokens.shape[0]
    span_rows = row_count * head_count
    mamba_width = MH * MP
    even = head_index % 2 == 0
    out_pairs = mixer_place()
    place = jnp.stack(
        [head_index, head_index % 2, 0, 0, block_index, 0, 0, 0]
    ).astype(jnp.int32)

    rows_in = in_weight.shape[0]
    flags_all = summed_over(
        lax.dynamic_update_slice_in_dim(
            jnp.zeros((blocks * span_rows,), jnp.int32),
            start_flags[0],
            block_index * span_rows,
            0,
        ),
        "blk",
    )
    packed_conv, packed_rest = call(
        pack_in,
        [
            shaped((4, rows_in, conv_columns), low),
            shaped((4, rows_in, rest_columns), low),
        ],
        place,
        [in_weight],
        scratch=[pltpu.VMEM((rows_in, lanes), jnp.float32)],
    )
    conv_rows = swap_heads(packed_conv).reshape(-1, conv_columns)
    weights_conv = gather_blocks(conv_rows)
    rest_rows = swap_heads(after(packed_rest, conv_rows)).reshape(-1, rest_columns)
    weights_rest = gather_blocks(rest_rows)
    gathered_tokens = gather_heads(after(tokens, conv_rows))
    out_rows = lax.ppermute(after(out_weight.astype(low), rest_rows), ("head", "blk"), out_pairs)
    rows_ffn = gate_up_weight.shape[0]
    units = FF // 4
    packed_ffn = call(
        partial(pack_ffn, ring=ring),
        [shaped((4, rows_ffn, 2 * units), low)],
        place,
        [after(gate_up_weight, rest_rows)],
    )[0]
    ffn_rows = swap_heads(packed_ffn).reshape(-1, 2 * units)
    model_cotangent = jnp.concatenate(gather_heads(after(cotangent, ffn_rows)))

    positions = block_index * span_rows + jnp.arange(span_rows, dtype=jnp.int32)
    all_positions = jnp.arange(blocks * span_rows, dtype=jnp.int32)
    starts_all = lax.cummax(jnp.where(flags_all > 0, all_positions, 0), axis=0)
    first_visible = lax.dynamic_slice_in_dim(starts_all, block_index * span_rows, span_rows, 0)
    flags_before = jnp.concatenate([jnp.zeros((KW - 2,), jnp.int32), flags_all])
    flag_ext = lax.dynamic_slice_in_dim(
        flags_before, block_index * span_rows, span_rows + KW - 2, 0
    ).astype(jnp.float32)
    segment = jnp.broadcast_to(
        jnp.cumsum(start_flags[0]).astype(jnp.float32)[:, None], (span_rows, lanes)
    )
    view = jnp.stack([block_index, jnp.min(first_visible), jnp.max(first_visible)])
    first_wide = jnp.broadcast_to(first_visible[:, None], (span_rows, lanes))
    keep_masks = [jnp.ones((span_rows,), jnp.float32)]
    for lag_index in range(1, KW):
        begin = KW - 1 - lag_index
        keep_masks.append(keep_masks[-1] * (1.0 - flag_ext[begin : begin + span_rows]))
    frequencies = rope_base ** (-jnp.arange(HD // 2, dtype=jnp.float32) * 2.0 / HD)
    angles = positions.astype(jnp.float32)[:, None] * frequencies[None, :]
    cosine = jnp.cos(angles)
    sine = jnp.sin(angles)
    cosine_wide = jnp.concatenate([cosine, cosine], axis=1)
    sine_wide = jnp.concatenate([-sine, sine], axis=1)
    conv_taps = jnp.concatenate(
        [
            lax.dynamic_slice_in_dim(conv_weight, head_index * inner_columns, inner_columns, 1),
            conv_weight[:, mamba_width:],
        ],
        axis=1,
    )
    conv_shift = jnp.concatenate(
        [
            lax.dynamic_slice_in_dim(conv_bias, head_index * inner_columns, inner_columns, 0),
            conv_bias[mamba_width:],
        ]
    )
    step_shift = lax.dynamic_slice_in_dim(step_bias, head_index * step_heads, step_heads, 0)
    decay_rate = lax.dynamic_slice_in_dim(decay_log, head_index * step_heads, step_heads, 0)
    skip_local = lax.dynamic_slice_in_dim(skip_gain, head_index * step_heads, step_heads, 0)
    skip_wide = jnp.repeat(skip_local, MP)[None, :]

    normed_one = call(
        partial(norm_one, ring=ring),
        [shaped((span_rows, D), low)],
        place,
        [*gathered_tokens, first_gain[None, :]],
        scratch=[pltpu.VMEM((row_count, D), low)],
    )[0]

    projected = jnp.dot(normed_one, weights_conv, preferred_element_type=jnp.float32)
    kv_mine = call(
        rope_kv,
        [shaped((span_rows, HD), low)],
        place,
        [projected[:, kv_at:], cosine_wide, sine_wide],
    )[0]
    pair_bc = projected[:, inner_columns:step_at].astype(low)
    conv_local = call(
        join_conv,
        [shaped((span_rows, inner_columns + 2 * NS), low)],
        place,
        [projected[:, :inner_columns], *gather_heads(pair_bc)],
    )[0]
    step_local = projected[:, step_at : step_at + step_heads].astype(low).astype(jnp.float32)
    rim_rows = passed_along(conv_local[span_rows - (KW - 1) :], "blk", 1)
    extended = jnp.concatenate([rim_rows, conv_local], axis=0).astype(jnp.float32)
    active, conv_back = jax.vjp(
        partial(conv_act, keep_masks=keep_masks), extended, conv_taps, conv_shift
    )
    (step_size, log_decay), step_back = jax.vjp(
        step_and_decay, step_local, step_shift, decay_rate
    )
    inner_act = active[:, :inner_columns]
    into_act = active[:, inner_columns : inner_columns + NS]
    outof_act = active[:, inner_columns + NS :]
    step_wide = in_lanes(step_size)
    decay_wide = in_lanes(log_decay)
    tall = shaped((span_rows, inner_columns), jnp.float32)
    tall_low = shaped((span_rows, inner_columns), low)
    narrow = shaped((span_rows, lanes), jnp.float32)
    share = inner_columns // blocks
    sent = shaped((blocks, extra_rows + share, NS), low)
    state_scratch = pltpu.VMEM((inner_columns, NS), jnp.float32)

    def chained(payload, backwards, after=()):
        got = lax.all_to_all(payload, "blk", split_axis=0, concat_axis=0, tiled=True)
        states = call(
            partial(chain, backwards=backwards),
            [shaped((blocks, share, NS), low)],
            place,
            [got],
            after=after,
        )[0]
        moved = lax.all_to_all(states, "blk", split_axis=0, concat_axis=0, tiled=True)
        return moved.reshape(inner_columns, NS), states

    within, state_sent, entering, factor = call(
        ssd_local,
        [tall, sent, narrow, shaped((8, lanes), jnp.float32)],
        place,
        [inner_act, into_act, outof_act, step_wide, decay_wide, segment],
        after=[ffn_rows],
        scratch=[state_scratch],
        flops=6 * 10**9,
    )
    state_in, states_mine = chained(state_sent, False)

    normed_after = after(normed_one, states_mine)
    projected_rest = jnp.dot(normed_after, weights_rest, preferred_element_type=jnp.float32)
    query_local, gate_act = call(
        rope_query,
        [shaped((span_rows, query_columns), low), tall_low],
        place,
        [projected_rest, cosine_wide, sine_wide],
    )
    out_height = out_weight.shape[0] + span_rows * HD // D
    out_packed = call(
        pack_out, [shaped((out_height, D), low)], place, [out_rows, kv_mine]
    )[0]
    out_gathered = gather_blocks(after(out_packed, weights_rest, state_sent)).reshape(blocks, out_height, D)
    weights_out, kv_blocks = call(
        partial(unpack_out, ring=ring),
        [
            shaped((blocks, *out_weight.shape), low),
            shaped((blocks, span_rows, HD), low),
        ],
        place,
        [out_gathered],
        after=[query_local, states_mine],
    )
    weights_out = weights_out.reshape(-1, D)
    weights_ffn = gather_blocks(after(ffn_rows, out_gathered, query_local, states_mine))
    weights_down = gather_blocks(after(down_weight.astype(low), weights_ffn))
    kv_beside = from_head(kv_blocks, 1)
    keys = jnp.where(even, kv_blocks, kv_beside)
    values = jnp.where(even, kv_beside, kv_blocks)
    attended, lse = attention(
        view, query_local, first_wide, keys, values, [states_mine, model_cotangent]
    )

    ssd, mixer = call(
        partial(ssd_finish, turned_columns=blocks == 8),
        [tall, shaped((span_rows, query_columns + inner_columns), low)],
        place,
        [within, entering, outof_act, state_in, inner_act, gate_act, skip_wide, attended],
        flops=2 * 10**9,
    )
    pair_rows = 2 * row_count
    mixed_other = jnp.dot(mixer[pair_rows:], weights_out, preferred_element_type=jnp.float32)
    mixed_own = jnp.dot(mixer[:pair_rows], weights_out, preferred_element_type=jnp.float32)
    mixed = scatter_pairs(mixed_own, mixed_other)
    hidden_one, normed_two = call(
        partial(norm_two, ring=ring),
        [shaped((row_count, D), jnp.float32), shaped((row_count, D), low)],
        place,
        [mixed, tokens, second_gain[None, :]],
        scratch=[pltpu.VMEM((row_count, D), low)],
    )
    model_normed = jnp.concatenate(gather_heads(normed_two))
    gate_up = jnp.dot(model_normed, weights_ffn, preferred_element_type=jnp.float32)
    gate_part, up_part = gate_up[:, :units], gate_up[:, units:]
    activated = (jax.nn.silu(gate_part) * up_part).astype(low)
    grad_down_low = outer_grad(activated, model_cotangent).astype(low)
    grad_activated = times_transposed(model_cotangent, after(weights_down, grad_down_low))
    sigmoid_gate = jax.nn.sigmoid(gate_part)
    grad_gate_up = jnp.concatenate(
        [
            grad_activated * up_part * sigmoid_gate * (1.0 + gate_part * (1.0 - sigmoid_gate)),
            grad_activated * jax.nn.silu(gate_part),
        ],
        axis=1,
    ).astype(low)
    grad_down = scatter_blocks(after(grad_down_low, weights_down))
    gate_up_late = after(grad_gate_up, grad_down_low)
    grad_norm_other = times_transposed(gate_up_late[pair_rows:], weights_ffn).astype(low)
    grad_norm_own = times_transposed(gate_up_late[:pair_rows], weights_ffn)
    grad_normed_two = scatter_pairs(grad_norm_own, grad_norm_other, low)
    grad_ffn_low = outer_grad(model_normed, after(grad_gate_up, grad_norm_own)).astype(low)

    grad_hidden, grad_hidden_low, grad_second = call(
        partial(back_two, ring=ring),
        [
            shaped((row_count, D), jnp.float32),
            shaped((row_count, D), low),
            shaped((8, D), jnp.float32),
        ],
        place,
        [
            grad_normed_two,
            hidden_one,
            cotangent,
            second_gain[None, :],
        ],
        after=[grad_down_low, grad_ffn_low],
        scratch=[pltpu.VMEM((row_count, D), jnp.float32)],
    )
    grad_ffn = scatter_blocks(after(grad_ffn_low, grad_down, grad_hidden_low))
    span_grad_hidden = jnp.concatenate(gather_heads(after(grad_hidden_low, grad_down)))
    grad_heads = times_transposed(span_grad_hidden, weights_out).astype(low)
    grad_ssd, grad_gate, grad_sent, grad_skip_wide, grad_attended = call(
        partial(ssd_gate_back, turned_columns=blocks == 8),
        [
            tall,
            tall_low,
            sent,
            shaped((8, inner_columns), jnp.float32),
            shaped((span_rows, query_columns), low),
        ],
        place,
        [grad_heads, gate_act, ssd, inner_act, skip_wide, entering, outof_act, factor],
        scratch=[state_scratch],
        flops=2 * 10**9,
    )
    ffn_swapped = swap_heads(grad_ffn.reshape(4, rows_ffn, 2 * units))
    grad_ffn_weight = call(
        partial(unpack_ffn, ring=ring),
        [shaped(gate_up_weight.shape, jnp.float32)],
        place,
        [ffn_swapped],
    )[0]
    activated_late = after(activated, span_grad_hidden)
    downed_other = jnp.dot(
        activated_late[pair_rows:], weights_down, preferred_element_type=jnp.float32
    )
    downed_own = jnp.dot(
        activated_late[:pair_rows], weights_down, preferred_element_type=jnp.float32
    )
    block_output = (hidden_one + scatter_pairs(downed_own, downed_other, low)).astype(low)

    grad_skip = grad_skip_wide[0].reshape(step_heads, MP).sum(axis=1)
    grad_out_low = outer_grad(mixer, span_grad_hidden).astype(low)
    later_grad, later_mine = chained(grad_sent, True)

    grad_query, grad_keys, grad_values = attention_back(
        view,
        query_local,
        first_wide,
        keys,
        values,
        grad_attended,
        attended,
        lse,
        [grad_out_low],
    )
    kept_kv = jnp.where(even, grad_keys, grad_values)
    given_kv = jnp.where(even, grad_values, grad_keys)
    kv_sums = (kept_kv.astype(jnp.float32) + from_head(given_kv, 1).astype(jnp.float32)).astype(
        low
    )
    grad_rest = call(
        query_back,
        [shaped((span_rows, rest_columns), low)],
        place,
        [grad_query, grad_gate, cosine_wide, sine_wide],
        after=[later_mine],
    )[0]
    grad_rest_low = outer_grad(normed_one, grad_rest).astype(low)

    grad_out_packed = call(
        partial(pack_out_grads, ring=ring),
        [shaped((blocks, out_height, D), low)],
        place,
        [grad_out_low.reshape(blocks, -1, D), kv_sums],
        after=[grad_rest_low],
    )[0]
    grad_out_sum = scatter_blocks(
        after(grad_out_packed.reshape(-1, D), grad_ffn)
    )
    grad_kv = grad_out_sum[out_weight.shape[0] :]
    grad_inner, grad_into, grad_outof, grad_step, grad_decay_line = call(
        ssd_back,
        [
            tall,
            shaped((span_rows, NS), jnp.float32),
            shaped((span_rows, NS), jnp.float32),
            narrow,
            narrow,
        ],
        place,
        [
            inner_act,
            into_act,
            outof_act,
            step_wide,
            decay_wide,
            segment,
            grad_ssd,
            ssd,
            skip_wide,
            state_in,
            later_grad,
        ],
        after=[grad_out_packed, block_output],
        scratch=[
            pltpu.VMEM((span_rows // chunk + 1, inner_columns, NS), jnp.float32),
            state_scratch,
        ],
        flops=10 * 10**9,
    )
    grad_raw, grad_step_shift, grad_rate = step_back(
        (grad_step[:, :step_heads], grad_decay_line[:, :step_heads])
    )
    grad_extended, grad_taps, grad_shift = conv_back(
        jnp.concatenate([grad_inner, grad_into, grad_outof], axis=1)
    )
    rim_back = passed_along(grad_extended[: KW - 1], "blk", -1)
    conv_grad = grad_extended[KW - 1 :] + jnp.pad(rim_back, ((span_rows - (KW - 1), 0), (0, 0)))
    grad_bc = conv_grad[:, inner_columns:].astype(low).astype(jnp.float32)

    def tile_at(distance):
        at = jnp.bitwise_xor(head_index, distance) * lanes
        return lax.dynamic_slice_in_dim(grad_bc, at, lanes, 1)

    bc_beside = from_head(jnp.stack([tile_at(1), tile_at(3)]).astype(low), 1).astype(jnp.float32)
    bc_far = from_head((tile_at(2) + bc_beside[1]).astype(low), 2)
    bc_near = tile_at(0) + bc_beside[0]
    grad_conv = call(
        conv_joined,
        [shaped((span_rows, conv_columns), low)],
        place,
        [
            conv_grad[:, :inner_columns],
            bc_near,
            bc_far,
            in_lanes(grad_raw),
            cosine_wide,
            sine_wide,
            grad_kv,
        ],
        after=[ffn_swapped],
    )[0]
    grad_conv_low = outer_grad(normed_one, grad_conv).astype(low)
    grad_rest_in = scatter_blocks(after(grad_rest_low, grad_out_sum, grad_inner))
    conv_moved, rest_moved = call(
        relative_order,
        [shaped((span_rows, conv_columns), low), shaped((span_rows, rest_columns), low)],
        place,
        [grad_conv, grad_rest],
        after=[grad_conv_low],
    )

    def back_in(part):
        return times_transposed(rest_moved[part], weights_rest) + times_transposed(
            conv_moved[part], weights_conv
        )

    grad_normed_other = back_in(slice(pair_rows, span_rows)).astype(low)
    grad_normed_own = back_in(slice(0, pair_rows))
    rest_swapped = swap_heads(grad_rest_in.reshape(4, rows_in, -1))
    grad_input = call(
        partial(back_one, ring=ring),
        [shaped((row_count, D), low)],
        place,
        [
            scatter_pairs(grad_normed_own, grad_normed_other, low),
            tokens,
            grad_hidden,
            first_gain[None, :],
        ],
        after=[rest_swapped, grad_ffn_weight],
        scratch=[pltpu.VMEM((row_count, D), jnp.float32)],
    )[0]
    first_line = jnp.sum(
        weights_conv.astype(jnp.float32) * grad_conv_low.astype(jnp.float32), axis=1
    ) + jnp.sum(weights_rest.astype(jnp.float32) * after(grad_rest_low, grad_conv_low).astype(jnp.float32), axis=1)
    first_line = first_line.reshape(blocks, 4, -1)
    first_line = jnp.stack([first_line[ring.index(k)] for k in range(blocks)], axis=1).reshape(D)

    def own_part(values_in, total):
        return lax.dynamic_update_slice_in_dim(
            jnp.zeros(values_in.shape[:-1] + (total,), jnp.float32),
            values_in,
            head_index * values_in.shape[-1],
            values_in.ndim - 1,
        )

    small = [
        first_line / first_gain,
        grad_second[0],
        jnp.concatenate(
            [own_part(grad_taps[:, :inner_columns], mamba_width), grad_taps[:, inner_columns:]],
            axis=1,
        ),
        jnp.concatenate(
            [own_part(grad_shift[:inner_columns], mamba_width), grad_shift[inner_columns:]]
        ),
        own_part(grad_step_shift, MH),
        own_part(grad_rate, MH),
        own_part(grad_skip, MH),
    ]
    line = jnp.concatenate([part.reshape(-1) for part in small])
    line = jnp.pad(line, (0, -line.shape[0] % 1024)).reshape(-1, 128)
    line = summed_over(summed_over(line, "head"), "blk").reshape(-1)
    grad_conv_in = scatter_blocks(after(grad_conv_low, grad_rest_in))
    grad_mix_weight = lax.ppermute(
        after(grad_out_sum[: out_weight.shape[0]], grad_conv_in),
        ("head", "blk"),
        [(there, here) for here, there in out_pairs],
    ).astype(jnp.float32)
    grad_proj_weight = call(
        unpack_in,
        [shaped(in_weight.shape, jnp.float32)],
        place,
        [swap_heads(grad_conv_in.reshape(4, rows_in, -1)), rest_swapped],
    )[0]
    summed_small = []
    at = 0
    for part in small:
        summed_small.append(line[at : at + part.size].reshape(part.shape))
        at += part.size
    return (
        block_output[None],
        grad_input[None],
        grad_proj_weight,
        grad_mix_weight,
        grad_ffn_weight,
        grad_down.astype(jnp.float32),
        *summed_small,
    )


def own_first(chunks, mine, order=(0, 1, 2, 3)):
    return [lax.dynamic_index_in_dim(chunks, jnp.bitwise_xor(mine, d), 0, False) for d in order]


def solution(mesh):
    placed = (
        P("blk", "head", None),
        P("blk", "head", None),
        P("blk", None),
        P(("head", "blk"), None),
        P(("head", "blk"), None),
        P(("head", "blk"), None),
        P(("head", "blk"), None),
        P(),
        P(),
        P(),
        P(),
        P(),
        P(),
        P(),
    )
    return jax.shard_map(
        per_device,
        mesh=mesh,
        in_specs=placed,
        out_specs=(
            P("blk", "head", None),
            P("blk", "head", None),
            P(("head", "blk"), None),
            P(("head", "blk"), None),
            P(("head", "blk"), None),
            P(("head", "blk"), None),
            P(),
            P(),
            P(),
            P(),
            P(),
            P(),
            P(),
        ),
        check_vma=False,
    )
```

```python
import math
from functools import partial

import jax
import jax.numpy as jnp
from jax import lax
from jax.experimental import pallas as pl
from jax.experimental.pallas import tpu as pltpu
from jax.sharding import PartitionSpec as P

D = 2048
QH = 8
KVH = 2
HD = 128
MH = 48
MP = 64
NS = 256
FF = 4096
KW = 4


epsilon = 1e-05
rope_base = 100000000000.0
masked_score = -1e30


def after(value, *others):
    return lax.optimization_barrier((value, *others))[0]


def passed_along(shard, axis, by):
    peers = lax.axis_size(axis)
    pairs = [(i, i + by) for i in range(peers) if 0 <= i + by < peers]
    return lax.ppermute(shard, axis, pairs)


def ring_of(axis):
    peers = lax.axis_size(axis)
    if peers != 8:
        return list(range(peers))
    return [0, 2, 4, 6, 7, 5, 3, 1]


def gather_blocks(shard):
    return lax.all_gather(shard, "blk", axis=0, tiled=True, axis_index_groups=[ring_of("blk")])


def scatter_blocks(partial_sums):
    return lax.psum_scatter(
        partial_sums,
        "blk",
        scatter_dimension=0,
        tiled=True,
        axis_index_groups=[ring_of("blk")],
    )


def from_head(shard, distance):
    peers = lax.axis_size("head")
    return lax.ppermute(shard, "head", [(i, i ^ distance) for i in range(peers)])


def gather_heads(shard):
    across = from_head(shard, 2)
    return [shard, across, from_head(shard, 1), from_head(across, 1)]


def in_head_order(parts):
    mine = lax.axis_index("head")
    stacked = jnp.stack([parts[0], parts[2], parts[1], parts[3]])
    return [
        lax.dynamic_index_in_dim(stacked, jnp.bitwise_xor(mine, j), 0, False) for j in range(4)
    ]


def scatter_pairs(own, other, middle=jnp.float32):
    rows = own.shape[0] // 2
    got = from_head(other.astype(middle), 1).astype(jnp.float32)
    far = from_head((own[rows:] + got[rows:]).astype(low), 2)
    return own[:rows] + got[:rows] + far.astype(jnp.float32)


def swap_heads(pieces):
    return lax.all_to_all(pieces, "head", split_axis=0, concat_axis=0, tiled=True)


def mixer_place():
    heads, ring = lax.axis_size("head"), ring_of("blk")
    peers = heads * len(ring)
    rows = (QH * HD + MH * MP) // peers
    query_blocks, mamba_blocks = QH * HD // rows // heads, MH * MP // rows // heads
    pairs = []
    for r in range(peers):
        if r < query_blocks * heads:
            group, slot = divmod(r, query_blocks)
            turn = slot + mamba_blocks
        else:
            group, turn = divmod(r - query_blocks * heads, mamba_blocks)
            slot = turn + query_blocks
        block = (mamba_blocks * group + turn) % len(ring) if len(ring) == 8 else ring[slot]
        pairs.append((r, group * len(ring) + block))
    return pairs


kv_begin = QH * HD
z_begin = kv_begin + 2 * KVH * HD
x_begin = z_begin + MH * MP
b_begin = x_begin + MH * MP
dt_begin = b_begin + 2 * NS
query_columns = QH * HD // 4
inner_columns = MH * MP // 4
bc_columns = 2 * NS // 4
step_heads = MH // 4
step_at = inner_columns + bc_columns
kv_at = step_at + 128
conv_columns = kv_at + HD
rest_columns = query_columns + inner_columns


def column_parts(head):
    conv = [
        (x_begin + head * inner_columns, 0, inner_columns),
        (b_begin + head * bc_columns, inner_columns, bc_columns),
        (kv_begin + (head % 2) * KVH * HD + (head // 2) * HD, kv_at, HD),
    ]
    rest = [
        (head * query_columns, 0, query_columns),
        (z_begin + head * inner_columns, query_columns, inner_columns),
    ]
    return conv, rest


def pack_in(place_ref, weight_ref, conv_ref, rest_ref, tail_ref):
    tail_ref[...] = jnp.zeros_like(tail_ref)
    tail_ref[:, :MH] = weight_ref[:, dt_begin : dt_begin + MH]
    last = tail_ref[...]
    lane = iota(last.shape, 1)
    for head in range(4):
        for parts, ref in zip(column_parts(head), (conv_ref, rest_ref)):
            for begin, at, size in parts:
                ref[head, :, at : at + size] = weight_ref[:, begin : begin + size].astype(low)
        steps = pltpu.roll(last, lanes - step_heads * head, 1) if head else last
        conv_ref[head, :, step_at:kv_at] = jnp.where(lane < step_heads, steps, 0.0).astype(low)


def unpack_in(place_ref, conv_ref, rest_ref, out_ref):
    total = jnp.zeros((out_ref.shape[0], lanes), jnp.float32)
    lane = iota(total.shape, 1)
    for head in range(4):
        for parts, ref in zip(column_parts(head), (conv_ref, rest_ref)):
            for begin, at, size in parts:
                out_ref[:, begin : begin + size] = ref[head, :, at : at + size].astype(jnp.float32)
        steps = conv_ref[head, :, step_at:kv_at].astype(jnp.float32)
        steps = jnp.where(lane < step_heads, steps, 0.0)
        total = total + (pltpu.roll(steps, step_heads * head, 1) if head else steps)
    out_ref[:, dt_begin : dt_begin + MH] = total[:, :MH]


def ffn_moves(ring):
    unit = FF // (4 * len(ring))
    return unit, [
        (
            head,
            half * FF + (head * len(ring) + k) * unit,
            half * (FF // 4) + i * unit,
        )
        for half in range(2)
        for head in range(4)
        for i, k in enumerate(ring)
    ]


def pack_ffn(place_ref, weight_ref, out_ref, *, ring):
    unit, moves = ffn_moves(ring)
    for head, begin, at in moves:
        out_ref[head, :, at : at + unit] = weight_ref[:, begin : begin + unit].astype(low)


def unpack_ffn(place_ref, in_ref, out_ref, *, ring):
    unit, moves = ffn_moves(ring)
    for head, begin, at in moves:
        out_ref[:, begin : begin + unit] = in_ref[head, :, at : at + unit].astype(jnp.float32)


def inverse_rms(values_in):
    return lax.rsqrt(jnp.mean(values_in * values_in, axis=1, keepdims=True) + epsilon)


def feature_moves(ring):
    piece = D // 4 // len(ring)
    return piece, [
        ((e * len(ring) + k) * piece, (4 * i + e) * piece)
        for e in range(4)
        for i, k in enumerate(ring)
    ]


def whole_lanes(begin, size):
    return pl.ds(pl.multiple_of(begin, 128), size)


def norm_one(place_ref, own, across, beside, both, gain_ref, out_ref, line_ref, *, ring):
    rows = own.shape[0]
    piece, moves = feature_moves(ring)
    for distance, ref in ((0, own), (2, across), (1, beside), (3, both)):
        x = ref[...].astype(jnp.float32)
        line_ref[...] = (x * inverse_rms(x) * gain_ref[...]).astype(low)
        there = jnp.bitwise_xor(place_ref[0], distance) * rows
        there = pl.ds(pl.multiple_of(there, rows), rows)
        for source, at in moves:
            out_ref[there, at : at + piece] = line_ref[:, source : source + piece]


def norm_two(place_ref, mixed_ref, tokens_ref, gain_ref, hidden_ref, out_ref, line_ref, *, ring):
    hidden = tokens_ref[...].astype(jnp.float32) + mixed_ref[...]
    hidden_ref[...] = hidden
    line_ref[...] = (hidden * inverse_rms(hidden) * gain_ref[...]).astype(low)
    piece, moves = feature_moves(ring)
    for source, at in moves:
        out_ref[:, at : at + piece] = line_ref[:, source : source + piece]


def back_two(
    place_ref, grad_ref, hidden_ref, cotangent_ref, gain_ref, out_ref, low_ref, sum_ref, plain_ref,
    *, ring,
):
    piece, moves = feature_moves(ring)
    for source, at in moves:
        plain_ref[:, source : source + piece] = grad_ref[:, at : at + piece]
    grad = plain_ref[...]
    hidden = hidden_ref[...]
    inverse = inverse_rms(hidden)
    scaled = grad * gain_ref[...]
    total = (
        cotangent_ref[...].astype(jnp.float32)
        + inverse * scaled
        - hidden * (inverse * inverse * inverse * jnp.mean(scaled * hidden, axis=1, keepdims=True))
    )
    out_ref[...] = total
    low_ref[...] = total.astype(low)
    sum_ref[...] = jnp.broadcast_to(
        jnp.sum(grad * hidden * inverse, axis=0, keepdims=True), sum_ref.shape
    )


def back_one(
    place_ref, grad_ref, tokens_ref, hidden_ref, gain_ref, out_ref, plain_ref, *, ring
):
    piece, moves = feature_moves(ring)
    for source, at in moves:
        plain_ref[:, source : source + piece] = grad_ref[:, at : at + piece]
    grad = plain_ref[...]
    x = tokens_ref[...].astype(jnp.float32)
    inverse = inverse_rms(x)
    scaled = grad * gain_ref[...]
    out_ref[...] = (
        hidden_ref[...]
        + inverse * scaled
        - x * (inverse * inverse * inverse * jnp.mean(scaled * x, axis=1, keepdims=True))
    ).astype(low)


def turned(values_in, cosine, sine):
    return values_in * cosine + pltpu.roll(values_in, HD // 2, 1) * sine


def rope_kv(place_ref, in_ref, cosine_ref, sine_ref, out_ref):
    kv = in_ref[...]
    out_ref[...] = jnp.where(
        place_ref[1] == 0, turned(kv, cosine_ref[...], sine_ref[...]), kv
    ).astype(low)


def kv_moves(span):
    height = span * HD // D
    return height, [(j * height, j * HD) for j in range(D // HD)]


def pack_out(place_ref, out_rows_ref, kv_ref, packed_ref):
    rows = out_rows_ref.shape[0]
    packed_ref[:rows, :] = out_rows_ref[...]
    height, moves = kv_moves(kv_ref.shape[0])
    for begin, at in moves:
        packed_ref[rows:, at : at + HD] = kv_ref[begin : begin + height, :]


def unpack_out(place_ref, packed_ref, out_ref, kv_ref, *, ring):
    rows = out_ref.shape[1]
    height, moves = kv_moves(kv_ref.shape[1])
    for i, k in enumerate(ring):
        out_ref[i] = packed_ref[i, :rows, :]
        for begin, at in moves:
            kv_ref[k, begin : begin + height, :] = packed_ref[i, rows:, at : at + HD]


def pack_out_grads(place_ref, out_ref, kv_ref, packed_ref, *, ring):
    rows = out_ref.shape[1]
    height, moves = kv_moves(kv_ref.shape[1])
    for i, k in enumerate(ring):
        packed_ref[i, :rows, :] = out_ref[i]
        for begin, at in moves:
            packed_ref[i, rows:, at : at + HD] = kv_ref[k, begin : begin + height, :]


def rope_query(place_ref, in_ref, cosine_ref, sine_ref, query_ref, gate_ref):
    cosine, sine = cosine_ref[...], sine_ref[...]
    for begin in range(0, query_columns, HD):
        query_ref[:, begin : begin + HD] = turned(
            in_ref[:, begin : begin + HD], cosine, sine
        ).astype(low)
    gate_ref[...] = in_ref[:, query_columns:].astype(low)


def query_back(place_ref, query_ref, gate_ref, cosine_ref, sine_ref, out_ref):
    cosine, sine = cosine_ref[...], -sine_ref[...]
    for begin in range(0, query_columns, HD):
        rounded = query_ref[:, begin : begin + HD].astype(low).astype(jnp.float32)
        out_ref[:, begin : begin + HD] = turned(rounded, cosine, sine).astype(low)
    out_ref[:, query_columns:] = gate_ref[...]


def join_conv(place_ref, inner_ref, own, across, beside, both, out_ref):
    out_ref[:, :inner_columns] = inner_ref[...].astype(low)
    for distance, ref in ((0, own), (2, across), (1, beside), (3, both)):
        at = inner_columns + jnp.bitwise_xor(place_ref[0], distance) * lanes
        out_ref[:, whole_lanes(at, lanes)] = ref[...]


def conv_joined(
    place_ref, inner_ref, near_ref, far_ref, step_ref, cosine_ref, sine_ref, kv_ref, out_ref
):
    out_ref[:, :inner_columns] = inner_ref[...].astype(low)
    out_ref[:, inner_columns:step_at] = (near_ref[...] + far_ref[...].astype(jnp.float32)).astype(low)
    out_ref[:, step_at:kv_at] = step_ref[...].astype(low)
    height, moves = kv_moves(out_ref.shape[0])
    for begin, at in moves:
        rows = slice(begin, begin + height)
        kv = kv_ref[:, at : at + HD].astype(jnp.float32)
        out_ref[rows, kv_at:] = jnp.where(
            place_ref[1] == 0, turned(kv, cosine_ref[rows, :], -sine_ref[rows, :]), kv
        ).astype(low)


def relative_order(place_ref, first_ref, second_ref, first_out, second_out):
    for at, distance in enumerate((0, 2, 1, 3)):
        there = jnp.bitwise_xor(place_ref[0], distance) * chunk
        there = pl.ds(pl.multiple_of(there, chunk), chunk)
        rows = slice(at * chunk, (at + 1) * chunk)
        first_out[rows, :] = first_ref[there, :]
        second_out[rows, :] = second_ref[there, :]


def outer_grad(left_side, grad_side):
    return lax.dot_general(
        left_side, grad_side, (((0,), (0,)), ((), ())), preferred_element_type=jnp.float32
    )


def times_transposed(grad_side, weight):
    return lax.dot_general(
        grad_side, weight, (((1,), (1,)), ((), ())), preferred_element_type=jnp.float32
    )


chunk = 128
lanes = 128
low = jnp.bfloat16
exact = lax.Precision.HIGHEST


def dot_nn(a, b, precision=None):
    return lax.dot_general(
        a, b, (((1,), (0,)), ((), ())), precision=precision, preferred_element_type=jnp.float32
    )


def dot_nt(a, b):
    return lax.dot_general(a, b, (((1,), (1,)), ((), ())), preferred_element_type=jnp.float32)


def dot_tn(a, b):
    return lax.dot_general(a, b, (((0,), (0,)), ((), ())), preferred_element_type=jnp.float32)


def iota(shape, dim):
    return lax.broadcasted_iota(jnp.int32, shape, dim)


def spread(per_head, pair):
    rows = per_head.shape[0]
    first = per_head[:, 2 * pair : 2 * pair + 1]
    second = per_head[:, 2 * pair + 1 : 2 * pair + 2]
    return jnp.where(iota((rows, lanes), 1) < MP, first, second)


def head_sums(products, pair):
    mine = 2 * pair + (iota((lanes, lanes), 0) >= MP).astype(jnp.int32)
    ones = (mine == iota((lanes, lanes), 1)).astype(jnp.float32)
    return dot_nn(products, ones, exact)


def chunk_terms(decay, segment, segment_before):
    lower = iota((chunk, chunk), 0) >= iota((chunk, chunk), 1)
    cumulative = dot_nn(lower.astype(jnp.float32), decay, exact)
    total = cumulative[chunk - 1 :, :]
    segment_end = segment[chunk - 1 :, :]
    related = lower & (segment == segment.T)
    entering = jnp.where(segment == segment_before, jnp.exp(cumulative), 0.0)
    ending = jnp.where(segment == segment_end, jnp.exp(total - cumulative), 0.0)
    whole = jnp.where(segment_end == segment_before, jnp.exp(total), 0.0)
    return cumulative, cumulative.T, related, entering, ending, whole, total, segment_end


def decays_of(cumulative, transposed, related, head):
    apart = cumulative[:, head : head + 1] - transposed[head : head + 1, :]
    return jnp.exp(jnp.where(related, apart, masked_score))


def row_factor(whole, pair, width):
    first = whole[:, 2 * pair : 2 * pair + 1]
    second = whole[:, 2 * pair + 1 : 2 * pair + 2]
    return jnp.where(iota((lanes, width), 0) < MP, first, second)


def chunk_rows(index):
    return pl.ds(pl.multiple_of(index * chunk, chunk), chunk)


def pack_states(state_ref, factor, out_ref):
    blocks, rows, width = out_ref.shape
    share = rows - extra_rows
    row = iota((extra_rows, width), 0)
    for k in range(blocks):
        extra = jnp.zeros((extra_rows, width), jnp.float32)
        for e in range(4):
            head = k * share // MP + e
            if head * MP < state_ref.shape[0]:
                whole = factor[:, head : head + 1]
                rough = whole.astype(low).astype(jnp.float32)
                extra = jnp.where(row == e, rough, extra)
                extra = jnp.where(row == 4 + e, whole - rough, extra)
        out_ref[k, :extra_rows, :] = extra.astype(low)
        out_ref[k, extra_rows:, :] = state_ref[k * share : (k + 1) * share, :].astype(low)


extra_rows = 16


def chain(place_ref, got_ref, out_ref, backwards):
    blocks, rows, width = got_ref.shape
    share = rows - extra_rows
    row = iota((share, width), 0) + lax.rem(place_ref[4] * share, MP)
    state = jnp.zeros((share, width), jnp.float32)
    for k in range(blocks - 1, -1, -1) if backwards else range(blocks):
        out_ref[k] = state.astype(low)
        extra = got_ref[k, :extra_rows, :].astype(jnp.float32)
        factor = extra[0:1, :] + extra[4:5, :]
        for e in range(1, 4):
            factor = jnp.where(row >= e * MP, extra[e : e + 1, :] + extra[4 + e : 5 + e, :], factor)
        state = factor * state + got_ref[k, extra_rows:, :].astype(jnp.float32)


def ssd_local(
    place_ref, x_ref, b_ref, c_ref, step_ref, decay_ref, seg_ref,
    y_ref, sent_ref, enter_ref, fac_ref, state_ref,
):
    pairs = x_ref.shape[1] // lanes
    state_ref[...] = jnp.zeros_like(state_ref)

    def body(index, carry):
        segment_before, base = carry
        rows = chunk_rows(index)
        segment = seg_ref[rows, :]
        cumulative, transposed, related, entering, ending, whole, total, segment_end = chunk_terms(
            decay_ref[rows, :], segment, segment_before
        )
        enter_ref[rows, :] = jnp.where(segment == 0.0, jnp.exp(base + cumulative), 0.0)
        into = b_ref[rows, :].astype(low)
        outof = c_ref[rows, :].astype(low)
        step = step_ref[rows, :]
        scores = dot_nt(outof, into)
        left = iota((chunk, lanes), 1) < MP
        for pair in range(pairs):
            cols = slice(pair * lanes, (pair + 1) * lanes)
            taken = x_ref[rows, cols] * spread(step, pair)
            taken_low = taken.astype(low)
            parts = []
            for head in (2 * pair, 2 * pair + 1):
                weights = decays_of(cumulative, transposed, related, head) * scores
                parts.append(dot_nn(weights.astype(low), taken_low))
            state = state_ref[cols, :]
            y_ref[rows, cols] = jnp.where(left, parts[0], parts[1]) + spread(
                entering, pair
            ) * dot_nt(outof, state.astype(low))
            kept = (taken * spread(ending, pair)).astype(low)
            state_ref[cols, :] = row_factor(whole, pair, state.shape[1]) * state + dot_tn(
                kept, into
            )
        return segment_end, base + total

    start = jnp.zeros((1, lanes), jnp.float32)
    segment_end, base = lax.fori_loop(0, x_ref.shape[0] // chunk, body, (start, start))
    factor = jnp.where(segment_end == 0.0, jnp.exp(base), 0.0)
    fac_ref[...] = jnp.broadcast_to(factor, fac_ref.shape)
    pack_states(state_ref, factor, sent_ref)


def relative_rows(place_ref, index):
    distance = jnp.bitwise_xor(place_ref[0], index)
    at = (distance % 2) * 2 + distance // 2
    return pl.ds(pl.multiple_of(at * chunk, chunk), chunk)


def mixer_lanes(place_ref, part, turned_columns):
    if not turned_columns:
        begin = (part + 2) % 8 * lanes
        return slice(begin, begin + lanes)
    block = lax.rem(6 * place_ref[0] + part, 8)
    at = jnp.where(block % 2 == 0, block // 2, 7 - block // 2)
    return pl.ds(pl.multiple_of(at * lanes, lanes), lanes)


def ssd_finish(
    place_ref, y_ref, enter_ref, c_ref, state_ref, x_ref, z_ref, skip_ref, attended_ref,
    ssd_ref, mixer_ref, *, turned_columns,
):
    pairs = x_ref.shape[1] // lanes

    def body(index, carry):
        rows = chunk_rows(index)
        there = relative_rows(place_ref, index)
        outof = c_ref[rows, :].astype(low)
        entering = enter_ref[rows, :]
        for half in range(2):
            mixer_ref[there, mixer_lanes(place_ref, 6 + half, turned_columns)] = attended_ref[
                rows, half * lanes : (half + 1) * lanes
            ].astype(low)
        for pair in range(pairs):
            cols = slice(pair * lanes, (pair + 1) * lanes)
            ssd = y_ref[rows, cols] + spread(entering, pair) * dot_nt(outof, state_ref[cols, :])
            ssd_ref[rows, cols] = ssd
            gate = z_ref[rows, cols].astype(jnp.float32)
            total = ssd + skip_ref[:, cols] * x_ref[rows, cols]
            mixer_ref[there, mixer_lanes(place_ref, pair, turned_columns)] = (
                total * gate / (1.0 + jnp.exp(-gate))
            ).astype(low)
        return carry

    lax.fori_loop(0, x_ref.shape[0] // chunk, body, 0)


def ssd_gate_back(
    place_ref, grad_ref, z_ref, ssd_ref, x_ref, skip_ref, enter_ref, c_ref, fac_ref,
    dy_ref, dz_ref, sent_ref, dskip_ref, datt_ref, dstate_ref, *, turned_columns,
):
    pairs = x_ref.shape[1] // lanes
    dstate_ref[...] = jnp.zeros_like(dstate_ref)
    dskip_ref[...] = jnp.zeros_like(dskip_ref)

    def body(index, carry):
        rows = chunk_rows(index)
        there = relative_rows(place_ref, index)
        outof = c_ref[rows, :].astype(low)
        entering = enter_ref[rows, :]
        for half in range(2):
            datt_ref[rows, half * lanes : (half + 1) * lanes] = grad_ref[
                there, mixer_lanes(place_ref, 6 + half, turned_columns)
            ]
        for pair in range(pairs):
            cols = slice(pair * lanes, (pair + 1) * lanes)
            gate = z_ref[rows, cols].astype(jnp.float32)
            sigmoid = 1.0 / (1.0 + jnp.exp(-gate))
            grad = grad_ref[there, mixer_lanes(place_ref, pair, turned_columns)].astype(
                jnp.float32
            )
            x = x_ref[rows, cols]
            total = ssd_ref[rows, cols] + skip_ref[:, cols] * x
            dz_ref[rows, cols] = (
                grad * total * sigmoid * (1.0 + gate * (1.0 - sigmoid))
            ).astype(low)
            dy = grad * gate * sigmoid
            dy_ref[rows, cols] = dy
            dskip_ref[:, cols] += jnp.broadcast_to(
                jnp.sum(dy * x, axis=0, keepdims=True), (dskip_ref.shape[0], lanes)
            )
            dstate_ref[cols, :] += dot_tn((dy * spread(entering, pair)).astype(low), outof)
        return carry

    lax.fori_loop(0, x_ref.shape[0] // chunk, body, 0)
    pack_states(dstate_ref, fac_ref[:1, :], sent_ref)


def ssd_back(
    place_ref, x_ref, b_ref, c_ref, step_ref, decay_ref, seg_ref, dy_ref, ssd_ref, skip_ref, state_ref, later_ref,
    dx_ref, db_ref, dc_ref, dstep_ref, ddecay_ref, states, grads,
):
    pairs = x_ref.shape[1] // lanes
    chunks = x_ref.shape[0] // chunk
    zero_row = jnp.zeros((1, lanes), jnp.float32)

    def before(index):
        rows = pl.ds(pl.multiple_of(jnp.maximum(index - 1, 0) * chunk, chunk), chunk)
        return jnp.where(index == 0, 0.0, seg_ref[rows, :][chunk - 1 :, :])

    states[0] = state_ref[...].astype(jnp.float32)

    def forward(index, carry):
        rows = chunk_rows(index)
        _, _, _, _, ending, whole, _, _ = chunk_terms(
            decay_ref[rows, :], seg_ref[rows, :], before(index)
        )
        into = b_ref[rows, :].astype(low)
        step = step_ref[rows, :]
        for pair in range(pairs):
            cols = slice(pair * lanes, (pair + 1) * lanes)
            kept = (x_ref[rows, cols] * spread(step, pair) * spread(ending, pair)).astype(low)
            state = states[index, cols, :]
            states[index + 1, cols, :] = row_factor(
                whole, pair, state.shape[1]
            ) * state + dot_tn(kept, into)
        return carry

    lax.fori_loop(0, chunks, forward, 0)
    grads[...] = later_ref[...].astype(jnp.float32)
    last = jnp.zeros((8, lanes), jnp.float32)
    for pair in range(pairs):
        cols = slice(pair * lanes, (pair + 1) * lanes)
        product = grads[cols, :] * states[chunks, cols, :]
        along = lax.dot_general(
            jnp.ones((8, product.shape[1]), jnp.float32),
            product,
            (((1,), (1,)), ((), ())),
            precision=exact,
            preferred_element_type=jnp.float32,
        )
        last = last + head_sums(along, pair)

    def backward(at, carry):
        index = chunks - 1 - at
        rows = chunk_rows(index)
        cumulative, transposed, related, entering, ending, whole, _, _ = chunk_terms(
            decay_ref[rows, :], seg_ref[rows, :], before(index)
        )
        into = b_ref[rows, :].astype(low)
        outof = c_ref[rows, :].astype(low)
        step = step_ref[rows, :]
        scores = dot_nt(outof, into)
        left = iota((chunk, lanes), 1) < MP
        grad_scores = jnp.zeros((chunk, chunk), jnp.float32)
        grad_into = jnp.zeros((chunk, b_ref.shape[1]), jnp.float32)
        grad_outof = jnp.zeros((chunk, b_ref.shape[1]), jnp.float32)
        grad_cum = jnp.zeros((chunk, lanes), jnp.float32)
        grad_step = jnp.zeros((chunk, lanes), jnp.float32)
        for pair in range(pairs):
            cols = slice(pair * lanes, (pair + 1) * lanes)
            x = x_ref[rows, cols]
            step_pair = spread(step, pair)
            taken = x * step_pair
            taken_low = taken.astype(low)
            dy = dy_ref[rows, cols]
            dy_low = dy.astype(low)
            parts = []
            for half, head in enumerate((2 * pair, 2 * pair + 1)):
                decays = decays_of(cumulative, transposed, related, head)
                parts.append(dot_tn((decays * scores).astype(low), dy_low))
                own = jnp.where(left if half == 0 else ~left, dy_low, jnp.zeros_like(dy_low))
                grad_scores = grad_scores + decays * dot_nt(own, taken_low)
            later = grads[cols, :]
            later_low = later.astype(low)
            ending_pair = spread(ending, pair)
            grad_taken = jnp.where(left, parts[0], parts[1]) + ending_pair * dot_nt(
                into, later_low
            )
            grad_into = grad_into + dot_nn((taken * ending_pair).astype(low), later_low)
            dy_enter = (dy * spread(entering, pair)).astype(low)
            grad_outof = grad_outof + dot_nn(dy_enter, states[index, cols, :].astype(low))
            grads[cols, :] = row_factor(whole, pair, later.shape[1]) * later + dot_tn(
                dy_enter, outof
            )
            grad_cum = grad_cum + head_sums(dy * ssd_ref[rows, cols] - taken * grad_taken, pair)
            grad_step = grad_step + head_sums(x * grad_taken, pair)
            dx_ref[rows, cols] = step_pair * grad_taken + skip_ref[:, cols] * dy
        grad_scores_low = grad_scores.astype(low)
        db_ref[rows, :] = grad_into + dot_tn(grad_scores_low, outof)
        dc_ref[rows, :] = grad_outof + dot_nn(grad_scores_low, into)
        dstep_ref[rows, :] = grad_step
        upper = (iota((chunk, chunk), 0) <= iota((chunk, chunk), 1)).astype(jnp.float32)
        ddecay_ref[rows, :] = dot_nn(upper, grad_cum, exact) + carry
        return carry + jnp.sum(grad_cum, axis=0, keepdims=True)

    lax.fori_loop(0, chunks, backward, last[:1, :] + zero_row)


def needed_and_plain(place_ref, block, span):
    mine, earliest, latest = place_ref[0], place_ref[1], place_ref[2]
    needed = (block <= mine) & ((block + 1) * span > earliest)
    return needed, (block < mine) & (block * span >= latest)


def visible_keys(place_ref, first_ref, block, span):
    key_pos = block * span + iota((span, span), 1)
    query_pos = place_ref[0] * span + iota((span, span), 0)
    return (key_pos <= query_pos) & (key_pos >= first_ref[:, :1])


def attend(place_ref, q_ref, first_ref, k_ref, v_ref, out_ref, lse_ref, top, total, summed):
    block = pl.program_id(0)
    span = q_ref.shape[0]
    heads = q_ref.shape[1] // HD

    @pl.when(block == 0)
    def _():
        top[...] = jnp.full_like(top, masked_score)
        total[...] = jnp.zeros_like(total)
        summed[...] = jnp.zeros_like(summed)

    def one(masked):
        keys = k_ref[0]
        values = v_ref[0]
        if masked:
            visible = visible_keys(place_ref, first_ref, block, span)
        for head in range(heads):
            cols = slice(head * HD, (head + 1) * HD)
            scores = dot_nt(q_ref[:, cols], keys) * HD**-0.5
            if masked:
                scores = jnp.where(visible, scores, masked_score)
            old_top = top[head][:, :1]
            new_top = jnp.maximum(old_top, jnp.max(scores, axis=1, keepdims=True))
            weights = jnp.exp(scores - new_top)
            if masked:
                weights = jnp.where(visible, weights, 0.0)
            scale = jnp.exp(old_top - new_top)
            total[head] = total[head] * scale + jnp.sum(weights, axis=1, keepdims=True)
            top[head] = jnp.broadcast_to(new_top, (span, lanes))
            summed[head] = summed[head] * scale + dot_nn(weights.astype(low), values)

    needed, plain = needed_and_plain(place_ref, block, span)
    pl.when(needed & plain)(lambda: one(False))
    pl.when(needed & jnp.logical_not(plain))(lambda: one(True))

    @pl.when(block == pl.num_programs(0) - 1)
    def _():
        for head in range(heads):
            cols = slice(head * HD, (head + 1) * HD)
            out_ref[:, cols] = summed[head] / total[head]
            lse_ref[head] = top[head] + jnp.log(total[head])


def attend_back(
    place_ref, q_ref, first_ref, k_ref, v_ref, grad_ref, out_ref, lse_ref, dq_ref, dk_ref, dv_ref
):
    block = pl.program_id(0)
    span = q_ref.shape[0]
    heads = q_ref.shape[1] // HD

    @pl.when(block == 0)
    def _():
        dq_ref[...] = jnp.zeros_like(dq_ref)

    def one(masked):
        keys = k_ref[0]
        values = v_ref[0]
        if masked:
            visible = visible_keys(place_ref, first_ref, block, span)
        grad_keys = jnp.zeros(keys.shape, jnp.float32)
        grad_values = jnp.zeros(keys.shape, jnp.float32)
        for head in range(heads):
            cols = slice(head * HD, (head + 1) * HD)
            query = q_ref[:, cols]
            grad = grad_ref[:, cols]
            delta = jnp.sum(
                grad.astype(jnp.float32) * out_ref[:, cols], axis=1, keepdims=True
            )
            scores = dot_nt(query, keys) * HD**-0.5
            if masked:
                scores = jnp.where(visible, scores, masked_score)
            weights = jnp.exp(scores - lse_ref[head][:, :1])
            changes = weights * (dot_nt(grad, values) - delta)
            weights_low = weights.astype(low)
            changes_low = (changes * HD**-0.5).astype(low)
            grad_values = grad_values + dot_tn(weights_low, grad)
            grad_keys = grad_keys + dot_tn(changes_low, query)
            dq_ref[:, cols] += dot_nn(changes_low, keys)
        dk_ref[0] = grad_keys.astype(low)
        dv_ref[0] = grad_values.astype(low)

    needed, plain = needed_and_plain(place_ref, block, span)
    pl.when(needed & plain)(lambda: one(False))
    pl.when(needed & jnp.logical_not(plain))(lambda: one(True))

    @pl.when(jnp.logical_not(needed))
    def _():
        dk_ref[...] = jnp.zeros_like(dk_ref)
        dv_ref[...] = jnp.zeros_like(dv_ref)


def shaped(shape, kind):
    return jax.ShapeDtypeStruct(shape, kind)


def call(kernel, outputs, place, operands, after=(), scratch=(), flops=10**6):
    count, skipped = len(operands), len(operands) + len(after)
    sizes = sum(math.prod(a.shape) * a.dtype.itemsize for a in (*operands, *outputs))

    def body(place_ref, *refs):
        kernel(place_ref, *refs[:count], *refs[skipped:])

    return pl.pallas_call(
        body,
        out_shape=outputs,
        in_specs=[pl.BlockSpec(memory_space=pltpu.SMEM)]
        + [pl.BlockSpec(memory_space=pltpu.VMEM)] * count
        + [pl.BlockSpec(memory_space=pl.ANY)] * len(after),
        out_specs=[pl.BlockSpec(memory_space=pltpu.VMEM)] * len(outputs),
        scratch_shapes=list(scratch),
        compiler_params=pltpu.CompilerParams(vmem_limit_bytes=kernel_memory),
        cost_estimate=pl.CostEstimate(flops=flops, bytes_accessed=sizes, transcendentals=0),
    )(place, *operands, *after)


kernel_memory = 44 * 1024 * 1024


def attention(place, query, first_visible, keys, values, after):
    away, span = keys.shape[0], query.shape[0]
    heads = query.shape[1] // HD
    same = lambda d, place: (0, 0)
    block = lambda d, place: (d, 0, 0)
    def body(*refs):
        attend(*refs[:5], *refs[5 + len(after) :])

    return pl.pallas_call(
        body,
        grid_spec=pltpu.PrefetchScalarGridSpec(
            num_scalar_prefetch=1,
            grid=(away,),
            in_specs=[
                pl.BlockSpec(query.shape, same),
                pl.BlockSpec(first_visible.shape, same),
                pl.BlockSpec((1, span, HD), block),
                pl.BlockSpec((1, span, HD), block),
            ]
            + [pl.BlockSpec(memory_space=pl.ANY)] * len(after),
            out_specs=[
                pl.BlockSpec(query.shape, same),
                pl.BlockSpec((heads, span, lanes), lambda d, place: (0, 0, 0)),
            ],
            scratch_shapes=[
                pltpu.VMEM((heads, span, lanes), jnp.float32),
                pltpu.VMEM((heads, span, lanes), jnp.float32),
                pltpu.VMEM((heads, span, HD), jnp.float32),
            ],
        ),
        out_shape=[
            shaped(query.shape, jnp.float32),
            shaped((heads, span, lanes), jnp.float32),
        ],
        compiler_params=pltpu.CompilerParams(vmem_limit_bytes=kernel_memory),
        cost_estimate=pl.CostEstimate(
            flops=20 * 10**9, bytes_accessed=4 * 10**6, transcendentals=0
        ),
    )(place, query, first_visible, keys, values, *after)


def attention_back(place, query, first_visible, keys, values, grad, out, lse, after):
    away, span = keys.shape[0], query.shape[0]
    same = lambda d, place: (0, 0)
    block = lambda d, place: (d, 0, 0)
    def body(*refs):
        attend_back(*refs[:8], *refs[8 + len(after) :])

    return pl.pallas_call(
        body,
        grid_spec=pltpu.PrefetchScalarGridSpec(
            num_scalar_prefetch=1,
            grid=(away,),
            in_specs=[
                pl.BlockSpec(query.shape, same),
                pl.BlockSpec(first_visible.shape, same),
                pl.BlockSpec((1, span, HD), block),
                pl.BlockSpec((1, span, HD), block),
                pl.BlockSpec(query.shape, same),
                pl.BlockSpec(query.shape, same),
                pl.BlockSpec(lse.shape, lambda d, place: (0, 0, 0)),
            ]
            + [pl.BlockSpec(memory_space=pl.ANY)] * len(after),
            out_specs=[
                pl.BlockSpec(query.shape, same),
                pl.BlockSpec((1, span, HD), block),
                pl.BlockSpec((1, span, HD), block),
            ],
        ),
        out_shape=[
            shaped(query.shape, jnp.float32),
            shaped(keys.shape, low),
            shaped(keys.shape, low),
        ],
        compiler_params=pltpu.CompilerParams(vmem_limit_bytes=kernel_memory),
        cost_estimate=pl.CostEstimate(
            flops=30 * 10**9, bytes_accessed=4 * 10**6, transcendentals=0
        ),
    )(place, query, first_visible, keys, values, grad, out, lse, *after)


def conv_act(extended, conv_taps, conv_shift, keep_masks):
    length = keep_masks[0].shape[0]
    result = conv_shift + conv_taps[0] * extended[KW - 1 :]
    for lag_index in range(1, KW):
        begin = KW - 1 - lag_index
        result = (
            result
            + conv_taps[lag_index]
            * keep_masks[lag_index][:, None]
            * extended[begin : begin + length]
        )
    return jax.nn.silu(result)


def step_and_decay(step_raw, step_shift, decay_rate):
    step_size = jax.nn.softplus(step_raw + step_shift)
    return step_size, -step_size * jnp.exp(decay_rate)


def in_lanes(per_head):
    return jnp.pad(per_head, ((0, 0), (0, lanes - per_head.shape[1])))


def summed_over(values_in, axis):
    peers = lax.axis_size(axis)
    by = 1
    while by < peers:
        values_in = values_in + lax.ppermute(values_in, axis, [(i, i ^ by) for i in range(peers)])
        by *= 2
    return values_in


def per_device(
    block_input,
    out_cotangent,
    start_flags,
    in_weight,
    out_weight,
    gate_up_weight,
    down_weight,
    first_gain,
    second_gain,
    conv_weight,
    conv_bias,
    step_bias,
    decay_log,
    skip_gain,
):
    head_count = lax.axis_size("head")
    blocks = lax.axis_size("blk")
    head_index = lax.axis_index("head")
    block_index = lax.axis_index("blk")
    ring = ring_of("blk")
    tokens = block_input[0]
    cotangent = out_cotangent[0]
    row_count = tokens.shape[0]
    span_rows = row_count * head_count
    mamba_width = MH * MP
    even = head_index % 2 == 0
    out_pairs = mixer_place()
    place = jnp.stack(
        [head_index, head_index % 2, 0, 0, block_index, 0, 0, 0]
    ).astype(jnp.int32)

    rows_in = in_weight.shape[0]
    flags_all = summed_over(
        lax.dynamic_update_slice_in_dim(
            jnp.zeros((blocks * span_rows,), jnp.int32),
            start_flags[0],
            block_index * span_rows,
            0,
        ),
        "blk",
    )
    packed_conv, packed_rest = call(
        pack_in,
        [
            shaped((4, rows_in, conv_columns), low),
            shaped((4, rows_in, rest_columns), low),
        ],
        place,
        [in_weight],
        scratch=[pltpu.VMEM((rows_in, lanes), jnp.float32)],
    )
    conv_rows = swap_heads(packed_conv).reshape(-1, conv_columns)
    weights_conv = gather_blocks(conv_rows)
    rest_rows = swap_heads(after(packed_rest, conv_rows)).reshape(-1, rest_columns)
    weights_rest = gather_blocks(rest_rows)
    gathered_tokens = gather_heads(after(tokens, conv_rows))
    out_rows = lax.ppermute(after(out_weight.astype(low), rest_rows), ("head", "blk"), out_pairs)
    rows_ffn = gate_up_weight.shape[0]
    units = FF // 4
    packed_ffn = call(
        partial(pack_ffn, ring=ring),
        [shaped((4, rows_ffn, 2 * units), low)],
        place,
        [after(gate_up_weight, rest_rows)],
    )[0]
    ffn_rows = swap_heads(packed_ffn).reshape(-1, 2 * units)
    model_cotangent = jnp.concatenate(gather_heads(after(cotangent, ffn_rows)))

    positions = block_index * span_rows + jnp.arange(span_rows, dtype=jnp.int32)
    all_positions = jnp.arange(blocks * span_rows, dtype=jnp.int32)
    starts_all = lax.cummax(jnp.where(flags_all > 0, all_positions, 0), axis=0)
    first_visible = lax.dynamic_slice_in_dim(starts_all, block_index * span_rows, span_rows, 0)
    flags_before = jnp.concatenate([jnp.zeros((KW - 2,), jnp.int32), flags_all])
    flag_ext = lax.dynamic_slice_in_dim(
        flags_before, block_index * span_rows, span_rows + KW - 2, 0
    ).astype(jnp.float32)
    segment = jnp.broadcast_to(
        jnp.cumsum(start_flags[0]).astype(jnp.float32)[:, None], (span_rows, lanes)
    )
    view = jnp.stack([block_index, jnp.min(first_visible), jnp.max(first_visible)])
    first_wide = jnp.broadcast_to(first_visible[:, None], (span_rows, lanes))
    keep_masks = [jnp.ones((span_rows,), jnp.float32)]
    for lag_index in range(1, KW):
        begin = KW - 1 - lag_index
        keep_masks.append(keep_masks[-1] * (1.0 - flag_ext[begin : begin + span_rows]))
    frequencies = rope_base ** (-jnp.arange(HD // 2, dtype=jnp.float32) * 2.0 / HD)
    angles = positions.astype(jnp.float32)[:, None] * frequencies[None, :]
    cosine = jnp.cos(angles)
    sine = jnp.sin(angles)
    cosine_wide = jnp.concatenate([cosine, cosine], axis=1)
    sine_wide = jnp.concatenate([-sine, sine], axis=1)
    conv_taps = jnp.concatenate(
        [
            lax.dynamic_slice_in_dim(conv_weight, head_index * inner_columns, inner_columns, 1),
            conv_weight[:, mamba_width:],
        ],
        axis=1,
    )
    conv_shift = jnp.concatenate(
        [
            lax.dynamic_slice_in_dim(conv_bias, head_index * inner_columns, inner_columns, 0),
            conv_bias[mamba_width:],
        ]
    )
    step_shift = lax.dynamic_slice_in_dim(step_bias, head_index * step_heads, step_heads, 0)
    decay_rate = lax.dynamic_slice_in_dim(decay_log, head_index * step_heads, step_heads, 0)
    skip_local = lax.dynamic_slice_in_dim(skip_gain, head_index * step_heads, step_heads, 0)
    skip_wide = jnp.repeat(skip_local, MP)[None, :]

    normed_one = call(
        partial(norm_one, ring=ring),
        [shaped((span_rows, D), low)],
        place,
        [*gathered_tokens, first_gain[None, :]],
        scratch=[pltpu.VMEM((row_count, D), low)],
    )[0]

    projected = jnp.dot(normed_one, weights_conv, preferred_element_type=jnp.float32)
    kv_mine = call(
        rope_kv,
        [shaped((span_rows, HD), low)],
        place,
        [projected[:, kv_at:], cosine_wide, sine_wide],
    )[0]
    pair_bc = projected[:, inner_columns:step_at].astype(low)
    conv_local = call(
        join_conv,
        [shaped((span_rows, inner_columns + 2 * NS), low)],
        place,
        [projected[:, :inner_columns], *gather_heads(pair_bc)],
    )[0]
    step_local = projected[:, step_at : step_at + step_heads].astype(low).astype(jnp.float32)
    rim_rows = passed_along(conv_local[span_rows - (KW - 1) :], "blk", 1)
    extended = jnp.concatenate([rim_rows, conv_local], axis=0).astype(jnp.float32)
    active, conv_back = jax.vjp(
        partial(conv_act, keep_masks=keep_masks), extended, conv_taps, conv_shift
    )
    (step_size, log_decay), step_back = jax.vjp(
        step_and_decay, step_local, step_shift, decay_rate
    )
    inner_act = active[:, :inner_columns]
    into_act = active[:, inner_columns : inner_columns + NS]
    outof_act = active[:, inner_columns + NS :]
    step_wide = in_lanes(step_size)
    decay_wide = in_lanes(log_decay)
    tall = shaped((span_rows, inner_columns), jnp.float32)
    tall_low = shaped((span_rows, inner_columns), low)
    narrow = shaped((span_rows, lanes), jnp.float32)
    share = inner_columns // blocks
    sent = shaped((blocks, extra_rows + share, NS), low)
    state_scratch = pltpu.VMEM((inner_columns, NS), jnp.float32)

    def chained(payload, backwards, after=()):
        got = lax.all_to_all(payload, "blk", split_axis=0, concat_axis=0, tiled=True)
        states = call(
            partial(chain, backwards=backwards),
            [shaped((blocks, share, NS), low)],
            place,
            [got],
            after=after,
        )[0]
        moved = lax.all_to_all(states, "blk", split_axis=0, concat_axis=0, tiled=True)
        return moved.reshape(inner_columns, NS), states

    within, state_sent, entering, factor = call(
        ssd_local,
        [tall, sent, narrow, shaped((8, lanes), jnp.float32)],
        place,
        [inner_act, into_act, outof_act, step_wide, decay_wide, segment],
        after=[ffn_rows],
        scratch=[state_scratch],
        flops=6 * 10**9,
    )
    state_in, states_mine = chained(state_sent, False)

    normed_after = after(normed_one, states_mine)
    projected_rest = jnp.dot(normed_after, weights_rest, preferred_element_type=jnp.float32)
    query_local, gate_act = call(
        rope_query,
        [shaped((span_rows, query_columns), low), tall_low],
        place,
        [projected_rest, cosine_wide, sine_wide],
    )
    out_height = out_weight.shape[0] + span_rows * HD // D
    out_packed = call(
        pack_out, [shaped((out_height, D), low)], place, [out_rows, kv_mine]
    )[0]
    out_gathered = gather_blocks(after(out_packed, weights_rest, state_sent)).reshape(blocks, out_height, D)
    weights_out, kv_blocks = call(
        partial(unpack_out, ring=ring),
        [
            shaped((blocks, *out_weight.shape), low),
            shaped((blocks, span_rows, HD), low),
        ],
        place,
        [out_gathered],
        after=[query_local, states_mine],
    )
    weights_out = weights_out.reshape(-1, D)
    weights_ffn = gather_blocks(after(ffn_rows, out_gathered, query_local, states_mine))
    weights_down = gather_blocks(after(down_weight.astype(low), weights_ffn))
    kv_beside = from_head(kv_blocks, 1)
    keys = jnp.where(even, kv_blocks, kv_beside)
    values = jnp.where(even, kv_beside, kv_blocks)
    attended, lse = attention(
        view, query_local, first_wide, keys, values, [states_mine, model_cotangent]
    )

    ssd, mixer = call(
        partial(ssd_finish, turned_columns=blocks == 8),
        [tall, shaped((span_rows, query_columns + inner_columns), low)],
        place,
        [within, entering, outof_act, state_in, inner_act, gate_act, skip_wide, attended],
        flops=2 * 10**9,
    )
    pair_rows = 2 * row_count
    mixed_other = jnp.dot(mixer[pair_rows:], weights_out, preferred_element_type=jnp.float32)
    mixed_own = jnp.dot(mixer[:pair_rows], weights_out, preferred_element_type=jnp.float32)
    mixed = scatter_pairs(mixed_own, mixed_other)
    hidden_one, normed_two = call(
        partial(norm_two, ring=ring),
        [shaped((row_count, D), jnp.float32), shaped((row_count, D), low)],
        place,
        [mixed, tokens, second_gain[None, :]],
        scratch=[pltpu.VMEM((row_count, D), low)],
    )
    model_normed = jnp.concatenate(gather_heads(normed_two))
    gate_up = jnp.dot(model_normed, weights_ffn, preferred_element_type=jnp.float32)
    gate_part, up_part = gate_up[:, :units], gate_up[:, units:]
    activated = (jax.nn.silu(gate_part) * up_part).astype(low)
    grad_down_low = outer_grad(activated, model_cotangent).astype(low)
    grad_activated = times_transposed(model_cotangent, after(weights_down, grad_down_low))
    sigmoid_gate = jax.nn.sigmoid(gate_part)
    grad_gate_up = jnp.concatenate(
        [
            grad_activated * up_part * sigmoid_gate * (1.0 + gate_part * (1.0 - sigmoid_gate)),
            grad_activated * jax.nn.silu(gate_part),
        ],
        axis=1,
    ).astype(low)
    grad_down = scatter_blocks(after(grad_down_low, weights_down))
    gate_up_late = after(grad_gate_up, grad_down_low)
    grad_norm_other = times_transposed(gate_up_late[pair_rows:], weights_ffn).astype(low)
    grad_norm_own = times_transposed(gate_up_late[:pair_rows], weights_ffn)
    grad_normed_two = scatter_pairs(grad_norm_own, grad_norm_other, low)
    grad_ffn_low = outer_grad(model_normed, after(grad_gate_up, grad_norm_own)).astype(low)

    grad_hidden, grad_hidden_low, grad_second = call(
        partial(back_two, ring=ring),
        [
            shaped((row_count, D), jnp.float32),
            shaped((row_count, D), low),
            shaped((8, D), jnp.float32),
        ],
        place,
        [
            grad_normed_two,
            hidden_one,
            cotangent,
            second_gain[None, :],
        ],
        after=[grad_down_low, grad_ffn_low],
        scratch=[pltpu.VMEM((row_count, D), jnp.float32)],
    )
    grad_ffn = scatter_blocks(after(grad_ffn_low, grad_down, grad_hidden_low))
    span_grad_hidden = jnp.concatenate(gather_heads(after(grad_hidden_low, grad_down)))
    grad_heads = times_transposed(span_grad_hidden, weights_out).astype(low)
    grad_ssd, grad_gate, grad_sent, grad_skip_wide, grad_attended = call(
        partial(ssd_gate_back, turned_columns=blocks == 8),
        [
            tall,
            tall_low,
            sent,
            shaped((8, inner_columns), jnp.float32),
            shaped((span_rows, query_columns), low),
        ],
        place,
        [grad_heads, gate_act, ssd, inner_act, skip_wide, entering, outof_act, factor],
        scratch=[state_scratch],
        flops=2 * 10**9,
    )
    ffn_swapped = swap_heads(grad_ffn.reshape(4, rows_ffn, 2 * units))
    grad_ffn_weight = call(
        partial(unpack_ffn, ring=ring),
        [shaped(gate_up_weight.shape, jnp.float32)],
        place,
        [ffn_swapped],
    )[0]
    activated_late = after(activated, span_grad_hidden)
    downed_other = jnp.dot(
        activated_late[pair_rows:], weights_down, preferred_element_type=jnp.float32
    )
    downed_own = jnp.dot(
        activated_late[:pair_rows], weights_down, preferred_element_type=jnp.float32
    )
    block_output = (hidden_one + scatter_pairs(downed_own, downed_other, low)).astype(low)

    grad_skip = grad_skip_wide[0].reshape(step_heads, MP).sum(axis=1)
    grad_out_low = outer_grad(mixer, span_grad_hidden).astype(low)
    later_grad, later_mine = chained(grad_sent, True)

    grad_query, grad_keys, grad_values = attention_back(
        view,
        query_local,
        first_wide,
        keys,
        values,
        grad_attended,
        attended,
        lse,
        [grad_out_low],
    )
    kept_kv = jnp.where(even, grad_keys, grad_values)
    given_kv = jnp.where(even, grad_values, grad_keys)
    kv_sums = (kept_kv.astype(jnp.float32) + from_head(given_kv, 1).astype(jnp.float32)).astype(
        low
    )
    grad_rest = call(
        query_back,
        [shaped((span_rows, rest_columns), low)],
        place,
        [grad_query, grad_gate, cosine_wide, sine_wide],
        after=[later_mine],
    )[0]
    grad_rest_low = outer_grad(normed_one, grad_rest).astype(low)

    grad_out_packed = call(
        partial(pack_out_grads, ring=ring),
        [shaped((blocks, out_height, D), low)],
        place,
        [grad_out_low.reshape(blocks, -1, D), kv_sums],
        after=[grad_rest_low],
    )[0]
    grad_out_sum = scatter_blocks(
        after(grad_out_packed.reshape(-1, D), grad_ffn)
    )
    grad_kv = grad_out_sum[out_weight.shape[0] :]
    grad_inner, grad_into, grad_outof, grad_step, grad_decay_line = call(
        ssd_back,
        [
            tall,
            shaped((span_rows, NS), jnp.float32),
            shaped((span_rows, NS), jnp.float32),
            narrow,
            narrow,
        ],
        place,
        [
            inner_act,
            into_act,
            outof_act,
            step_wide,
            decay_wide,
            segment,
            grad_ssd,
            ssd,
            skip_wide,
            state_in,
            later_grad,
        ],
        after=[grad_out_packed, block_output],
        scratch=[
            pltpu.VMEM((span_rows // chunk + 1, inner_columns, NS), jnp.float32),
            state_scratch,
        ],
        flops=10 * 10**9,
    )
    grad_raw, grad_step_shift, grad_rate = step_back(
        (grad_step[:, :step_heads], grad_decay_line[:, :step_heads])
    )
    grad_extended, grad_taps, grad_shift = conv_back(
        jnp.concatenate([grad_inner, grad_into, grad_outof], axis=1)
    )
    rim_back = passed_along(grad_extended[: KW - 1], "blk", -1)
    conv_grad = grad_extended[KW - 1 :] + jnp.pad(rim_back, ((span_rows - (KW - 1), 0), (0, 0)))
    grad_bc = conv_grad[:, inner_columns:].astype(low).astype(jnp.float32)

    def tile_at(distance):
        at = jnp.bitwise_xor(head_index, distance) * lanes
        return lax.dynamic_slice_in_dim(grad_bc, at, lanes, 1)

    bc_beside = from_head(jnp.stack([tile_at(1), tile_at(3)]).astype(low), 1).astype(jnp.float32)
    bc_far = from_head((tile_at(2) + bc_beside[1]).astype(low), 2)
    bc_near = tile_at(0) + bc_beside[0]
    grad_conv = call(
        conv_joined,
        [shaped((span_rows, conv_columns), low)],
        place,
        [
            conv_grad[:, :inner_columns],
            bc_near,
            bc_far,
            in_lanes(grad_raw),
            cosine_wide,
            sine_wide,
            grad_kv,
        ],
        after=[ffn_swapped],
    )[0]
    grad_conv_low = outer_grad(normed_one, grad_conv).astype(low)
    grad_rest_in = scatter_blocks(after(grad_rest_low, grad_out_sum, grad_inner))
    conv_moved, rest_moved = call(
        relative_order,
        [shaped((span_rows, conv_columns), low), shaped((span_rows, rest_columns), low)],
        place,
        [grad_conv, grad_rest],
        after=[grad_conv_low],
    )

    def back_in(part):
        return times_transposed(rest_moved[part], weights_rest) + times_transposed(
            conv_moved[part], weights_conv
        )

    grad_normed_other = back_in(slice(pair_rows, span_rows)).astype(low)
    grad_normed_own = back_in(slice(0, pair_rows))
    rest_swapped = swap_heads(grad_rest_in.reshape(4, rows_in, -1))
    grad_out_rows = grad_out_sum[: out_weight.shape[0]]

    def to_owners(rows, along_heads):
        pairs = [
            (there, here)
            for here, there in out_pairs
            if (here % blocks == there % blocks) == along_heads
        ]
        return lax.ppermute(rows, ("head", "blk"), pairs)

    grad_mix_early = to_owners(after(grad_out_rows, grad_rest_in), True)
    grad_normed_own = after(grad_normed_own, rest_swapped, grad_mix_early)
    grad_input = call(
        partial(back_one, ring=ring),
        [shaped((row_count, D), low)],
        place,
        [
            scatter_pairs(grad_normed_own, grad_normed_other, low),
            tokens,
            grad_hidden,
            first_gain[None, :],
        ],
        after=[grad_ffn_weight],
        scratch=[pltpu.VMEM((row_count, D), jnp.float32)],
    )[0]
    first_line = jnp.sum(
        weights_conv.astype(jnp.float32) * grad_conv_low.astype(jnp.float32), axis=1
    ) + jnp.sum(weights_rest.astype(jnp.float32) * after(grad_rest_low, grad_conv_low).astype(jnp.float32), axis=1)
    first_line = first_line.reshape(blocks, 4, -1)
    first_line = jnp.stack([first_line[ring.index(k)] for k in range(blocks)], axis=1).reshape(D)

    def own_part(values_in, total):
        return lax.dynamic_update_slice_in_dim(
            jnp.zeros(values_in.shape[:-1] + (total,), jnp.float32),
            values_in,
            head_index * values_in.shape[-1],
            values_in.ndim - 1,
        )

    small = [
        first_line / first_gain,
        grad_second[0],
        jnp.concatenate(
            [own_part(grad_taps[:, :inner_columns], mamba_width), grad_taps[:, inner_columns:]],
            axis=1,
        ),
        jnp.concatenate(
            [own_part(grad_shift[:inner_columns], mamba_width), grad_shift[inner_columns:]]
        ),
        own_part(grad_step_shift, MH),
        own_part(grad_rate, MH),
        own_part(grad_skip, MH),
    ]
    line = jnp.concatenate([part.reshape(-1) for part in small])
    line = jnp.pad(line, (0, -line.shape[0] % 1024)).reshape(-1, 128)
    line = summed_over(summed_over(line, "head"), "blk").reshape(-1)
    grad_conv_in = scatter_blocks(after(grad_conv_low, grad_rest_in))
    grad_mix_late = to_owners(after(grad_out_rows, grad_conv_in), False)
    grad_mix_weight = grad_mix_early.astype(jnp.float32) + grad_mix_late.astype(jnp.float32)
    grad_proj_weight = call(
        unpack_in,
        [shaped(in_weight.shape, jnp.float32)],
        place,
        [swap_heads(grad_conv_in.reshape(4, rows_in, -1)), rest_swapped],
    )[0]
    summed_small = []
    at = 0
    for part in small:
        summed_small.append(line[at : at + part.size].reshape(part.shape))
        at += part.size
    return (
        block_output[None],
        grad_input[None],
        grad_proj_weight,
        grad_mix_weight,
        grad_ffn_weight,
        grad_down.astype(jnp.float32),
        *summed_small,
    )


def own_first(chunks, mine, order=(0, 1, 2, 3)):
    return [lax.dynamic_index_in_dim(chunks, jnp.bitwise_xor(mine, d), 0, False) for d in order]


def solution(mesh):
    placed = (
        P("blk", "head", None),
        P("blk", "head", None),
        P("blk", None),
        P(("head", "blk"), None),
        P(("head", "blk"), None),
        P(("head", "blk"), None),
        P(("head", "blk"), None),
        P(),
        P(),
        P(),
        P(),
        P(),
        P(),
        P(),
    )
    return jax.shard_map(
        per_device,
        mesh=mesh,
        in_specs=placed,
        out_specs=(
            P("blk", "head", None),
            P("blk", "head", None),
            P(("head", "blk"), None),
            P(("head", "blk"), None),
            P(("head", "blk"), None),
            P(("head", "blk"), None),
            P(),
            P(),
            P(),
            P(),
            P(),
            P(),
            P(),
        ),
        check_vma=False,
    )
```

```python
import math
from functools import partial

import jax
import jax.numpy as jnp
from jax import lax
from jax.experimental import pallas as pl
from jax.experimental.pallas import tpu as pltpu
from jax.sharding import PartitionSpec as P

D = 2048
QH = 8
KVH = 2
HD = 128
MH = 48
MP = 64
NS = 256
FF = 4096
KW = 4


epsilon = 1e-05
rope_base = 100000000000.0
masked_score = -1e30


def after(value, *others):
    return lax.optimization_barrier((value, *others))[0]


def passed_along(shard, axis, by):
    peers = lax.axis_size(axis)
    pairs = [(i, i + by) for i in range(peers) if 0 <= i + by < peers]
    return lax.ppermute(shard, axis, pairs)


def ring_of(axis):
    peers = lax.axis_size(axis)
    if peers != 8:
        return list(range(peers))
    return [0, 2, 4, 6, 7, 5, 3, 1]


def gather_blocks(shard):
    return lax.all_gather(shard, "blk", axis=0, tiled=True, axis_index_groups=[ring_of("blk")])


def scatter_blocks(partial_sums):
    return lax.psum_scatter(
        partial_sums,
        "blk",
        scatter_dimension=0,
        tiled=True,
        axis_index_groups=[ring_of("blk")],
    )


def from_head(shard, distance):
    peers = lax.axis_size("head")
    return lax.ppermute(shard, "head", [(i, i ^ distance) for i in range(peers)])


def gather_heads(shard):
    across = from_head(shard, 2)
    return [shard, across, from_head(shard, 1), from_head(across, 1)]


def in_head_order(parts):
    mine = lax.axis_index("head")
    stacked = jnp.stack([parts[0], parts[2], parts[1], parts[3]])
    return [
        lax.dynamic_index_in_dim(stacked, jnp.bitwise_xor(mine, j), 0, False) for j in range(4)
    ]


def scatter_pairs(own, other, middle=jnp.float32):
    rows = own.shape[0] // 2
    got = from_head(other.astype(middle), 1).astype(jnp.float32)
    far = from_head((own[rows:] + got[rows:]).astype(low), 2)
    return own[:rows] + got[:rows] + far.astype(jnp.float32)


def swap_heads(pieces):
    return lax.all_to_all(pieces, "head", split_axis=0, concat_axis=0, tiled=True)


def mixer_place():
    heads, ring = lax.axis_size("head"), ring_of("blk")
    peers = heads * len(ring)
    rows = (QH * HD + MH * MP) // peers
    query_blocks, mamba_blocks = QH * HD // rows // heads, MH * MP // rows // heads
    pairs = []
    for r in range(peers):
        if r < query_blocks * heads:
            group, slot = divmod(r, query_blocks)
            turn = slot + mamba_blocks
        else:
            group, turn = divmod(r - query_blocks * heads, mamba_blocks)
            slot = turn + query_blocks
        block = (mamba_blocks * group + turn) % len(ring) if len(ring) == 8 else ring[slot]
        pairs.append((r, group * len(ring) + block))
    return pairs


kv_begin = QH * HD
z_begin = kv_begin + 2 * KVH * HD
x_begin = z_begin + MH * MP
b_begin = x_begin + MH * MP
dt_begin = b_begin + 2 * NS
query_columns = QH * HD // 4
inner_columns = MH * MP // 4
bc_columns = 2 * NS // 4
step_heads = MH // 4
step_at = inner_columns + bc_columns
kv_at = step_at + 128
conv_columns = kv_at + HD
rest_columns = query_columns + inner_columns


def column_parts(head):
    conv = [
        (x_begin + head * inner_columns, 0, inner_columns),
        (b_begin + head * bc_columns, inner_columns, bc_columns),
        (kv_begin + (head % 2) * KVH * HD + (head // 2) * HD, kv_at, HD),
    ]
    rest = [
        (head * query_columns, 0, query_columns),
        (z_begin + head * inner_columns, query_columns, inner_columns),
    ]
    return conv, rest


def pack_in(place_ref, weight_ref, conv_ref, rest_ref, tail_ref):
    tail_ref[...] = jnp.zeros_like(tail_ref)
    tail_ref[:, :MH] = weight_ref[:, dt_begin : dt_begin + MH]
    last = tail_ref[...]
    lane = iota(last.shape, 1)
    for head in range(4):
        for parts, ref in zip(column_parts(head), (conv_ref, rest_ref)):
            for begin, at, size in parts:
                ref[head, :, at : at + size] = weight_ref[:, begin : begin + size].astype(low)
        steps = pltpu.roll(last, lanes - step_heads * head, 1) if head else last
        conv_ref[head, :, step_at:kv_at] = jnp.where(lane < step_heads, steps, 0.0).astype(low)


def unpack_in(place_ref, conv_ref, rest_ref, out_ref):
    total = jnp.zeros((out_ref.shape[0], lanes), jnp.float32)
    lane = iota(total.shape, 1)
    for head in range(4):
        for parts, ref in zip(column_parts(head), (conv_ref, rest_ref)):
            for begin, at, size in parts:
                out_ref[:, begin : begin + size] = ref[head, :, at : at + size].astype(jnp.float32)
        steps = conv_ref[head, :, step_at:kv_at].astype(jnp.float32)
        steps = jnp.where(lane < step_heads, steps, 0.0)
        total = total + (pltpu.roll(steps, step_heads * head, 1) if head else steps)
    out_ref[:, dt_begin : dt_begin + MH] = total[:, :MH]


def ffn_moves(ring):
    unit = FF // (4 * len(ring))
    return unit, [
        (
            head,
            half * FF + (head * len(ring) + k) * unit,
            half * (FF // 4) + i * unit,
        )
        for half in range(2)
        for head in range(4)
        for i, k in enumerate(ring)
    ]


def pack_ffn(place_ref, weight_ref, out_ref, *, ring):
    unit, moves = ffn_moves(ring)
    for head, begin, at in moves:
        out_ref[head, :, at : at + unit] = weight_ref[:, begin : begin + unit].astype(low)


def unpack_ffn(place_ref, in_ref, out_ref, *, ring):
    unit, moves = ffn_moves(ring)
    for head, begin, at in moves:
        out_ref[:, begin : begin + unit] = in_ref[head, :, at : at + unit].astype(jnp.float32)


def inverse_rms(values_in):
    return lax.rsqrt(jnp.mean(values_in * values_in, axis=1, keepdims=True) + epsilon)


def feature_moves(ring):
    piece = D // 4 // len(ring)
    return piece, [
        ((e * len(ring) + k) * piece, (4 * i + e) * piece)
        for e in range(4)
        for i, k in enumerate(ring)
    ]


def whole_lanes(begin, size):
    return pl.ds(pl.multiple_of(begin, 128), size)


def norm_one(place_ref, own, across, beside, both, gain_ref, out_ref, line_ref, *, ring):
    rows = own.shape[0]
    piece, moves = feature_moves(ring)
    for distance, ref in ((0, own), (2, across), (1, beside), (3, both)):
        x = ref[...].astype(jnp.float32)
        line_ref[...] = (x * inverse_rms(x) * gain_ref[...]).astype(low)
        there = jnp.bitwise_xor(place_ref[0], distance) * rows
        there = pl.ds(pl.multiple_of(there, rows), rows)
        for source, at in moves:
            out_ref[there, at : at + piece] = line_ref[:, source : source + piece]


def norm_two(place_ref, mixed_ref, tokens_ref, gain_ref, hidden_ref, out_ref, line_ref, *, ring):
    hidden = tokens_ref[...].astype(jnp.float32) + mixed_ref[...]
    hidden_ref[...] = hidden
    line_ref[...] = (hidden * inverse_rms(hidden) * gain_ref[...]).astype(low)
    piece, moves = feature_moves(ring)
    for source, at in moves:
        out_ref[:, at : at + piece] = line_ref[:, source : source + piece]


def back_two(
    place_ref, grad_ref, hidden_ref, cotangent_ref, gain_ref, out_ref, low_ref, sum_ref, plain_ref,
    *, ring,
):
    piece, moves = feature_moves(ring)
    for source, at in moves:
        plain_ref[:, source : source + piece] = grad_ref[:, at : at + piece]
    grad = plain_ref[...]
    hidden = hidden_ref[...]
    inverse = inverse_rms(hidden)
    scaled = grad * gain_ref[...]
    total = (
        cotangent_ref[...].astype(jnp.float32)
        + inverse * scaled
        - hidden * (inverse * inverse * inverse * jnp.mean(scaled * hidden, axis=1, keepdims=True))
    )
    out_ref[...] = total
    low_ref[...] = total.astype(low)
    sum_ref[...] = jnp.broadcast_to(
        jnp.sum(grad * hidden * inverse, axis=0, keepdims=True), sum_ref.shape
    )


def back_one(
    place_ref, grad_ref, tokens_ref, hidden_ref, gain_ref, out_ref, plain_ref, *, ring
):
    piece, moves = feature_moves(ring)
    for source, at in moves:
        plain_ref[:, source : source + piece] = grad_ref[:, at : at + piece]
    grad = plain_ref[...]
    x = tokens_ref[...].astype(jnp.float32)
    inverse = inverse_rms(x)
    scaled = grad * gain_ref[...]
    out_ref[...] = (
        hidden_ref[...]
        + inverse * scaled
        - x * (inverse * inverse * inverse * jnp.mean(scaled * x, axis=1, keepdims=True))
    ).astype(low)


def turned(values_in, cosine, sine):
    return values_in * cosine + pltpu.roll(values_in, HD // 2, 1) * sine


def rope_kv(place_ref, in_ref, cosine_ref, sine_ref, out_ref):
    kv = in_ref[...]
    out_ref[...] = jnp.where(
        place_ref[1] == 0, turned(kv, cosine_ref[...], sine_ref[...]), kv
    ).astype(low)


def kv_moves(span):
    height = span * HD // D
    return height, [(j * height, j * HD) for j in range(D // HD)]


def pack_out(place_ref, out_rows_ref, kv_ref, packed_ref):
    rows = out_rows_ref.shape[0]
    packed_ref[:rows, :] = out_rows_ref[...]
    height, moves = kv_moves(kv_ref.shape[0])
    for begin, at in moves:
        packed_ref[rows:, at : at + HD] = kv_ref[begin : begin + height, :]


def unpack_out(place_ref, packed_ref, out_ref, kv_ref, *, ring):
    rows = out_ref.shape[1]
    height, moves = kv_moves(kv_ref.shape[1])
    for i, k in enumerate(ring):
        out_ref[i] = packed_ref[i, :rows, :]
        for begin, at in moves:
            kv_ref[k, begin : begin + height, :] = packed_ref[i, rows:, at : at + HD]


def pack_out_grads(place_ref, out_ref, kv_ref, packed_ref, *, ring):
    rows = out_ref.shape[1]
    height, moves = kv_moves(kv_ref.shape[1])
    for i, k in enumerate(ring):
        packed_ref[i, :rows, :] = out_ref[i]
        for begin, at in moves:
            packed_ref[i, rows:, at : at + HD] = kv_ref[k, begin : begin + height, :]


def rope_query(place_ref, in_ref, cosine_ref, sine_ref, query_ref, gate_ref):
    cosine, sine = cosine_ref[...], sine_ref[...]
    for begin in range(0, query_columns, HD):
        query_ref[:, begin : begin + HD] = turned(
            in_ref[:, begin : begin + HD], cosine, sine
        ).astype(low)
    gate_ref[...] = in_ref[:, query_columns:].astype(low)


def query_back(place_ref, query_ref, gate_ref, cosine_ref, sine_ref, out_ref):
    cosine, sine = cosine_ref[...], -sine_ref[...]
    for begin in range(0, query_columns, HD):
        rounded = query_ref[:, begin : begin + HD].astype(low).astype(jnp.float32)
        out_ref[:, begin : begin + HD] = turned(rounded, cosine, sine).astype(low)
    out_ref[:, query_columns:] = gate_ref[...]


def join_conv(place_ref, inner_ref, own, across, beside, both, out_ref):
    out_ref[:, :inner_columns] = inner_ref[...].astype(low)
    for distance, ref in ((0, own), (2, across), (1, beside), (3, both)):
        at = inner_columns + jnp.bitwise_xor(place_ref[0], distance) * lanes
        out_ref[:, whole_lanes(at, lanes)] = ref[...]


def conv_joined(
    place_ref, inner_ref, near_ref, far_ref, step_ref, cosine_ref, sine_ref, kv_ref, out_ref
):
    out_ref[:, :inner_columns] = inner_ref[...].astype(low)
    out_ref[:, inner_columns:step_at] = (near_ref[...] + far_ref[...].astype(jnp.float32)).astype(low)
    out_ref[:, step_at:kv_at] = step_ref[...].astype(low)
    height, moves = kv_moves(out_ref.shape[0])
    for begin, at in moves:
        rows = slice(begin, begin + height)
        kv = kv_ref[:, at : at + HD].astype(jnp.float32)
        out_ref[rows, kv_at:] = jnp.where(
            place_ref[1] == 0, turned(kv, cosine_ref[rows, :], -sine_ref[rows, :]), kv
        ).astype(low)


def relative_order(place_ref, first_ref, second_ref, first_out, second_out):
    for at, distance in enumerate((0, 2, 1, 3)):
        there = jnp.bitwise_xor(place_ref[0], distance) * chunk
        there = pl.ds(pl.multiple_of(there, chunk), chunk)
        rows = slice(at * chunk, (at + 1) * chunk)
        first_out[rows, :] = first_ref[there, :]
        second_out[rows, :] = second_ref[there, :]


def outer_grad(left_side, grad_side):
    return lax.dot_general(
        left_side, grad_side, (((0,), (0,)), ((), ())), preferred_element_type=jnp.float32
    )


def times_transposed(grad_side, weight):
    return lax.dot_general(
        grad_side, weight, (((1,), (1,)), ((), ())), preferred_element_type=jnp.float32
    )


chunk = 128
lanes = 128
low = jnp.bfloat16
exact = lax.Precision.HIGHEST


def dot_nn(a, b, precision=None):
    return lax.dot_general(
        a, b, (((1,), (0,)), ((), ())), precision=precision, preferred_element_type=jnp.float32
    )


def dot_nt(a, b):
    return lax.dot_general(a, b, (((1,), (1,)), ((), ())), preferred_element_type=jnp.float32)


def dot_tn(a, b):
    return lax.dot_general(a, b, (((0,), (0,)), ((), ())), preferred_element_type=jnp.float32)


def iota(shape, dim):
    return lax.broadcasted_iota(jnp.int32, shape, dim)


def spread(per_head, pair):
    rows = per_head.shape[0]
    first = per_head[:, 2 * pair : 2 * pair + 1]
    second = per_head[:, 2 * pair + 1 : 2 * pair + 2]
    return jnp.where(iota((rows, lanes), 1) < MP, first, second)


def head_sums(products, pair):
    mine = 2 * pair + (iota((lanes, lanes), 0) >= MP).astype(jnp.int32)
    ones = (mine == iota((lanes, lanes), 1)).astype(jnp.float32)
    return dot_nn(products, ones, exact)


def chunk_terms(decay, segment, segment_before):
    lower = iota((chunk, chunk), 0) >= iota((chunk, chunk), 1)
    cumulative = dot_nn(lower.astype(jnp.float32), decay, exact)
    total = cumulative[chunk - 1 :, :]
    segment_end = segment[chunk - 1 :, :]
    related = lower & (segment == segment.T)
    entering = jnp.where(segment == segment_before, jnp.exp(cumulative), 0.0)
    ending = jnp.where(segment == segment_end, jnp.exp(total - cumulative), 0.0)
    whole = jnp.where(segment_end == segment_before, jnp.exp(total), 0.0)
    return cumulative, cumulative.T, related, entering, ending, whole, total, segment_end


def decays_of(cumulative, transposed, related, head):
    apart = cumulative[:, head : head + 1] - transposed[head : head + 1, :]
    return jnp.exp(jnp.where(related, apart, masked_score))


def row_factor(whole, pair, width):
    first = whole[:, 2 * pair : 2 * pair + 1]
    second = whole[:, 2 * pair + 1 : 2 * pair + 2]
    return jnp.where(iota((lanes, width), 0) < MP, first, second)


def chunk_rows(index):
    return pl.ds(pl.multiple_of(index * chunk, chunk), chunk)


def pack_states(state_ref, factor, out_ref):
    blocks, rows, width = out_ref.shape
    share = rows - extra_rows
    row = iota((extra_rows, width), 0)
    for k in range(blocks):
        extra = jnp.zeros((extra_rows, width), jnp.float32)
        for e in range(4):
            head = k * share // MP + e
            if head * MP < state_ref.shape[0]:
                whole = factor[:, head : head + 1]
                rough = whole.astype(low).astype(jnp.float32)
                extra = jnp.where(row == e, rough, extra)
                extra = jnp.where(row == 4 + e, whole - rough, extra)
        out_ref[k, :extra_rows, :] = extra.astype(low)
        out_ref[k, extra_rows:, :] = state_ref[k * share : (k + 1) * share, :].astype(low)


extra_rows = 16


def chain(place_ref, got_ref, out_ref, backwards):
    blocks, rows, width = got_ref.shape
    share = rows - extra_rows
    row = iota((share, width), 0) + lax.rem(place_ref[4] * share, MP)
    state = jnp.zeros((share, width), jnp.float32)
    for k in range(blocks - 1, -1, -1) if backwards else range(blocks):
        out_ref[k] = state.astype(low)
        extra = got_ref[k, :extra_rows, :].astype(jnp.float32)
        factor = extra[0:1, :] + extra[4:5, :]
        for e in range(1, 4):
            factor = jnp.where(row >= e * MP, extra[e : e + 1, :] + extra[4 + e : 5 + e, :], factor)
        state = factor * state + got_ref[k, extra_rows:, :].astype(jnp.float32)


def ssd_local(
    place_ref, x_ref, b_ref, c_ref, step_ref, decay_ref, seg_ref,
    y_ref, sent_ref, enter_ref, fac_ref, state_ref,
):
    pairs = x_ref.shape[1] // lanes
    state_ref[...] = jnp.zeros_like(state_ref)

    def body(index, carry):
        segment_before, base = carry
        rows = chunk_rows(index)
        segment = seg_ref[rows, :]
        cumulative, transposed, related, entering, ending, whole, total, segment_end = chunk_terms(
            decay_ref[rows, :], segment, segment_before
        )
        enter_ref[rows, :] = jnp.where(segment == 0.0, jnp.exp(base + cumulative), 0.0)
        into = b_ref[rows, :].astype(low)
        outof = c_ref[rows, :].astype(low)
        step = step_ref[rows, :]
        scores = dot_nt(outof, into)
        left = iota((chunk, lanes), 1) < MP
        for pair in range(pairs):
            cols = slice(pair * lanes, (pair + 1) * lanes)
            taken = x_ref[rows, cols] * spread(step, pair)
            taken_low = taken.astype(low)
            parts = []
            for head in (2 * pair, 2 * pair + 1):
                weights = decays_of(cumulative, transposed, related, head) * scores
                parts.append(dot_nn(weights.astype(low), taken_low))
            state = state_ref[cols, :]
            y_ref[rows, cols] = jnp.where(left, parts[0], parts[1]) + spread(
                entering, pair
            ) * dot_nt(outof, state.astype(low))
            kept = (taken * spread(ending, pair)).astype(low)
            state_ref[cols, :] = row_factor(whole, pair, state.shape[1]) * state + dot_tn(
                kept, into
            )
        return segment_end, base + total

    start = jnp.zeros((1, lanes), jnp.float32)
    segment_end, base = lax.fori_loop(0, x_ref.shape[0] // chunk, body, (start, start))
    factor = jnp.where(segment_end == 0.0, jnp.exp(base), 0.0)
    fac_ref[...] = jnp.broadcast_to(factor, fac_ref.shape)
    pack_states(state_ref, factor, sent_ref)


def relative_rows(place_ref, index):
    distance = jnp.bitwise_xor(place_ref[0], index)
    at = (distance % 2) * 2 + distance // 2
    return pl.ds(pl.multiple_of(at * chunk, chunk), chunk)


def mixer_lanes(place_ref, part, turned_columns):
    if not turned_columns:
        begin = (part + 2) % 8 * lanes
        return slice(begin, begin + lanes)
    block = lax.rem(6 * place_ref[0] + part, 8)
    at = jnp.where(block % 2 == 0, block // 2, 7 - block // 2)
    return pl.ds(pl.multiple_of(at * lanes, lanes), lanes)


def ssd_finish(
    place_ref, y_ref, enter_ref, c_ref, state_ref, x_ref, z_ref, skip_ref, attended_ref,
    ssd_ref, mixer_ref, *, turned_columns,
):
    pairs = x_ref.shape[1] // lanes

    def body(index, carry):
        rows = chunk_rows(index)
        there = relative_rows(place_ref, index)
        outof = c_ref[rows, :].astype(low)
        entering = enter_ref[rows, :]
        for half in range(2):
            mixer_ref[there, mixer_lanes(place_ref, 6 + half, turned_columns)] = attended_ref[
                rows, half * lanes : (half + 1) * lanes
            ].astype(low)
        for pair in range(pairs):
            cols = slice(pair * lanes, (pair + 1) * lanes)
            ssd = y_ref[rows, cols] + spread(entering, pair) * dot_nt(outof, state_ref[cols, :])
            ssd_ref[rows, cols] = ssd
            gate = z_ref[rows, cols].astype(jnp.float32)
            total = ssd + skip_ref[:, cols] * x_ref[rows, cols]
            mixer_ref[there, mixer_lanes(place_ref, pair, turned_columns)] = (
                total * gate / (1.0 + jnp.exp(-gate))
            ).astype(low)
        return carry

    lax.fori_loop(0, x_ref.shape[0] // chunk, body, 0)


def ssd_gate_back(
    place_ref, grad_ref, z_ref, ssd_ref, x_ref, skip_ref, enter_ref, c_ref, fac_ref,
    dy_ref, dz_ref, sent_ref, dskip_ref, datt_ref, dstate_ref, *, turned_columns,
):
    pairs = x_ref.shape[1] // lanes
    dstate_ref[...] = jnp.zeros_like(dstate_ref)
    dskip_ref[...] = jnp.zeros_like(dskip_ref)

    def body(index, carry):
        rows = chunk_rows(index)
        there = relative_rows(place_ref, index)
        outof = c_ref[rows, :].astype(low)
        entering = enter_ref[rows, :]
        for half in range(2):
            datt_ref[rows, half * lanes : (half + 1) * lanes] = grad_ref[
                there, mixer_lanes(place_ref, 6 + half, turned_columns)
            ]
        for pair in range(pairs):
            cols = slice(pair * lanes, (pair + 1) * lanes)
            gate = z_ref[rows, cols].astype(jnp.float32)
            sigmoid = 1.0 / (1.0 + jnp.exp(-gate))
            grad = grad_ref[there, mixer_lanes(place_ref, pair, turned_columns)].astype(
                jnp.float32
            )
            x = x_ref[rows, cols]
            total = ssd_ref[rows, cols] + skip_ref[:, cols] * x
            dz_ref[rows, cols] = (
                grad * total * sigmoid * (1.0 + gate * (1.0 - sigmoid))
            ).astype(low)
            dy = grad * gate * sigmoid
            dy_ref[rows, cols] = dy
            dskip_ref[:, cols] += jnp.broadcast_to(
                jnp.sum(dy * x, axis=0, keepdims=True), (dskip_ref.shape[0], lanes)
            )
            dstate_ref[cols, :] += dot_tn((dy * spread(entering, pair)).astype(low), outof)
        return carry

    lax.fori_loop(0, x_ref.shape[0] // chunk, body, 0)
    pack_states(dstate_ref, fac_ref[:1, :], sent_ref)


def ssd_back(
    place_ref, x_ref, b_ref, c_ref, step_ref, decay_ref, seg_ref, dy_ref, ssd_ref, skip_ref, state_ref, later_ref,
    dx_ref, db_ref, dc_ref, dstep_ref, ddecay_ref, states, grads,
):
    pairs = x_ref.shape[1] // lanes
    chunks = x_ref.shape[0] // chunk
    zero_row = jnp.zeros((1, lanes), jnp.float32)

    def before(index):
        rows = pl.ds(pl.multiple_of(jnp.maximum(index - 1, 0) * chunk, chunk), chunk)
        return jnp.where(index == 0, 0.0, seg_ref[rows, :][chunk - 1 :, :])

    states[0] = state_ref[...].astype(jnp.float32)

    def forward(index, carry):
        rows = chunk_rows(index)
        _, _, _, _, ending, whole, _, _ = chunk_terms(
            decay_ref[rows, :], seg_ref[rows, :], before(index)
        )
        into = b_ref[rows, :].astype(low)
        step = step_ref[rows, :]
        for pair in range(pairs):
            cols = slice(pair * lanes, (pair + 1) * lanes)
            kept = (x_ref[rows, cols] * spread(step, pair) * spread(ending, pair)).astype(low)
            state = states[index, cols, :]
            states[index + 1, cols, :] = row_factor(
                whole, pair, state.shape[1]
            ) * state + dot_tn(kept, into)
        return carry

    lax.fori_loop(0, chunks, forward, 0)
    grads[...] = later_ref[...].astype(jnp.float32)
    last = jnp.zeros((8, lanes), jnp.float32)
    for pair in range(pairs):
        cols = slice(pair * lanes, (pair + 1) * lanes)
        product = grads[cols, :] * states[chunks, cols, :]
        along = lax.dot_general(
            jnp.ones((8, product.shape[1]), jnp.float32),
            product,
            (((1,), (1,)), ((), ())),
            precision=exact,
            preferred_element_type=jnp.float32,
        )
        last = last + head_sums(along, pair)

    def backward(at, carry):
        index = chunks - 1 - at
        rows = chunk_rows(index)
        cumulative, transposed, related, entering, ending, whole, _, _ = chunk_terms(
            decay_ref[rows, :], seg_ref[rows, :], before(index)
        )
        into = b_ref[rows, :].astype(low)
        outof = c_ref[rows, :].astype(low)
        step = step_ref[rows, :]
        scores = dot_nt(outof, into)
        left = iota((chunk, lanes), 1) < MP
        grad_scores = jnp.zeros((chunk, chunk), jnp.float32)
        grad_into = jnp.zeros((chunk, b_ref.shape[1]), jnp.float32)
        grad_outof = jnp.zeros((chunk, b_ref.shape[1]), jnp.float32)
        grad_cum = jnp.zeros((chunk, lanes), jnp.float32)
        grad_step = jnp.zeros((chunk, lanes), jnp.float32)
        for pair in range(pairs):
            cols = slice(pair * lanes, (pair + 1) * lanes)
            x = x_ref[rows, cols]
            step_pair = spread(step, pair)
            taken = x * step_pair
            taken_low = taken.astype(low)
            dy = dy_ref[rows, cols]
            dy_low = dy.astype(low)
            parts = []
            for half, head in enumerate((2 * pair, 2 * pair + 1)):
                decays = decays_of(cumulative, transposed, related, head)
                parts.append(dot_tn((decays * scores).astype(low), dy_low))
                own = jnp.where(left if half == 0 else ~left, dy_low, jnp.zeros_like(dy_low))
                grad_scores = grad_scores + decays * dot_nt(own, taken_low)
            later = grads[cols, :]
            later_low = later.astype(low)
            ending_pair = spread(ending, pair)
            grad_taken = jnp.where(left, parts[0], parts[1]) + ending_pair * dot_nt(
                into, later_low
            )
            grad_into = grad_into + dot_nn((taken * ending_pair).astype(low), later_low)
            dy_enter = (dy * spread(entering, pair)).astype(low)
            grad_outof = grad_outof + dot_nn(dy_enter, states[index, cols, :].astype(low))
            grads[cols, :] = row_factor(whole, pair, later.shape[1]) * later + dot_tn(
                dy_enter, outof
            )
            grad_cum = grad_cum + head_sums(dy * ssd_ref[rows, cols] - taken * grad_taken, pair)
            grad_step = grad_step + head_sums(x * grad_taken, pair)
            dx_ref[rows, cols] = step_pair * grad_taken + skip_ref[:, cols] * dy
        grad_scores_low = grad_scores.astype(low)
        db_ref[rows, :] = grad_into + dot_tn(grad_scores_low, outof)
        dc_ref[rows, :] = grad_outof + dot_nn(grad_scores_low, into)
        dstep_ref[rows, :] = grad_step
        upper = (iota((chunk, chunk), 0) <= iota((chunk, chunk), 1)).astype(jnp.float32)
        ddecay_ref[rows, :] = dot_nn(upper, grad_cum, exact) + carry
        return carry + jnp.sum(grad_cum, axis=0, keepdims=True)

    lax.fori_loop(0, chunks, backward, last[:1, :] + zero_row)


def needed_and_plain(place_ref, block, span):
    mine, earliest, latest = place_ref[0], place_ref[1], place_ref[2]
    needed = (block <= mine) & ((block + 1) * span > earliest)
    return needed, (block < mine) & (block * span >= latest)


def visible_keys(place_ref, first_ref, block, span):
    key_pos = block * span + iota((span, span), 1)
    query_pos = place_ref[0] * span + iota((span, span), 0)
    return (key_pos <= query_pos) & (key_pos >= first_ref[:, :1])


def attend(place_ref, q_ref, first_ref, k_ref, v_ref, out_ref, lse_ref, top, total, summed):
    block = pl.program_id(0)
    span = q_ref.shape[0]
    heads = q_ref.shape[1] // HD

    @pl.when(block == 0)
    def _():
        top[...] = jnp.full_like(top, masked_score)
        total[...] = jnp.zeros_like(total)
        summed[...] = jnp.zeros_like(summed)

    def one(masked):
        keys = k_ref[0]
        values = v_ref[0]
        if masked:
            visible = visible_keys(place_ref, first_ref, block, span)
        for head in range(heads):
            cols = slice(head * HD, (head + 1) * HD)
            scores = dot_nt(q_ref[:, cols], keys) * HD**-0.5
            if masked:
                scores = jnp.where(visible, scores, masked_score)
            old_top = top[head][:, :1]
            new_top = jnp.maximum(old_top, jnp.max(scores, axis=1, keepdims=True))
            weights = jnp.exp(scores - new_top)
            if masked:
                weights = jnp.where(visible, weights, 0.0)
            scale = jnp.exp(old_top - new_top)
            total[head] = total[head] * scale + jnp.sum(weights, axis=1, keepdims=True)
            top[head] = jnp.broadcast_to(new_top, (span, lanes))
            summed[head] = summed[head] * scale + dot_nn(weights.astype(low), values)

    needed, plain = needed_and_plain(place_ref, block, span)
    pl.when(needed & plain)(lambda: one(False))
    pl.when(needed & jnp.logical_not(plain))(lambda: one(True))

    @pl.when(block == pl.num_programs(0) - 1)
    def _():
        for head in range(heads):
            cols = slice(head * HD, (head + 1) * HD)
            out_ref[:, cols] = summed[head] / total[head]
            lse_ref[head] = top[head] + jnp.log(total[head])


def attend_back(
    place_ref, q_ref, first_ref, k_ref, v_ref, grad_ref, out_ref, lse_ref, dq_ref, dk_ref, dv_ref
):
    block = pl.program_id(0)
    span = q_ref.shape[0]
    heads = q_ref.shape[1] // HD

    @pl.when(block == 0)
    def _():
        dq_ref[...] = jnp.zeros_like(dq_ref)

    def one(masked):
        keys = k_ref[0]
        values = v_ref[0]
        if masked:
            visible = visible_keys(place_ref, first_ref, block, span)
        grad_keys = jnp.zeros(keys.shape, jnp.float32)
        grad_values = jnp.zeros(keys.shape, jnp.float32)
        for head in range(heads):
            cols = slice(head * HD, (head + 1) * HD)
            query = q_ref[:, cols]
            grad = grad_ref[:, cols]
            delta = jnp.sum(
                grad.astype(jnp.float32) * out_ref[:, cols], axis=1, keepdims=True
            )
            scores = dot_nt(query, keys) * HD**-0.5
            if masked:
                scores = jnp.where(visible, scores, masked_score)
            weights = jnp.exp(scores - lse_ref[head][:, :1])
            changes = weights * (dot_nt(grad, values) - delta)
            weights_low = weights.astype(low)
            changes_low = (changes * HD**-0.5).astype(low)
            grad_values = grad_values + dot_tn(weights_low, grad)
            grad_keys = grad_keys + dot_tn(changes_low, query)
            dq_ref[:, cols] += dot_nn(changes_low, keys)
        dk_ref[0] = grad_keys.astype(low)
        dv_ref[0] = grad_values.astype(low)

    needed, plain = needed_and_plain(place_ref, block, span)
    pl.when(needed & plain)(lambda: one(False))
    pl.when(needed & jnp.logical_not(plain))(lambda: one(True))

    @pl.when(jnp.logical_not(needed))
    def _():
        dk_ref[...] = jnp.zeros_like(dk_ref)
        dv_ref[...] = jnp.zeros_like(dv_ref)


def shaped(shape, kind):
    return jax.ShapeDtypeStruct(shape, kind)


def call(kernel, outputs, place, operands, after=(), scratch=(), flops=10**6):
    count, skipped = len(operands), len(operands) + len(after)
    sizes = sum(math.prod(a.shape) * a.dtype.itemsize for a in (*operands, *outputs))

    def body(place_ref, *refs):
        kernel(place_ref, *refs[:count], *refs[skipped:])

    return pl.pallas_call(
        body,
        out_shape=outputs,
        in_specs=[pl.BlockSpec(memory_space=pltpu.SMEM)]
        + [pl.BlockSpec(memory_space=pltpu.VMEM)] * count
        + [pl.BlockSpec(memory_space=pl.ANY)] * len(after),
        out_specs=[pl.BlockSpec(memory_space=pltpu.VMEM)] * len(outputs),
        scratch_shapes=list(scratch),
        compiler_params=pltpu.CompilerParams(vmem_limit_bytes=kernel_memory),
        cost_estimate=pl.CostEstimate(flops=flops, bytes_accessed=sizes, transcendentals=0),
    )(place, *operands, *after)


kernel_memory = 44 * 1024 * 1024


def attention(place, query, first_visible, keys, values, after):
    away, span = keys.shape[0], query.shape[0]
    heads = query.shape[1] // HD
    same = lambda d, place: (0, 0)
    block = lambda d, place: (d, 0, 0)
    def body(*refs):
        attend(*refs[:5], *refs[5 + len(after) :])

    return pl.pallas_call(
        body,
        grid_spec=pltpu.PrefetchScalarGridSpec(
            num_scalar_prefetch=1,
            grid=(away,),
            in_specs=[
                pl.BlockSpec(query.shape, same),
                pl.BlockSpec(first_visible.shape, same),
                pl.BlockSpec((1, span, HD), block),
                pl.BlockSpec((1, span, HD), block),
            ]
            + [pl.BlockSpec(memory_space=pl.ANY)] * len(after),
            out_specs=[
                pl.BlockSpec(query.shape, same),
                pl.BlockSpec((heads, span, lanes), lambda d, place: (0, 0, 0)),
            ],
            scratch_shapes=[
                pltpu.VMEM((heads, span, lanes), jnp.float32),
                pltpu.VMEM((heads, span, lanes), jnp.float32),
                pltpu.VMEM((heads, span, HD), jnp.float32),
            ],
        ),
        out_shape=[
            shaped(query.shape, jnp.float32),
            shaped((heads, span, lanes), jnp.float32),
        ],
        compiler_params=pltpu.CompilerParams(vmem_limit_bytes=kernel_memory),
        cost_estimate=pl.CostEstimate(
            flops=20 * 10**9, bytes_accessed=4 * 10**6, transcendentals=0
        ),
    )(place, query, first_visible, keys, values, *after)


def attention_back(place, query, first_visible, keys, values, grad, out, lse, after):
    away, span = keys.shape[0], query.shape[0]
    same = lambda d, place: (0, 0)
    block = lambda d, place: (d, 0, 0)
    def body(*refs):
        attend_back(*refs[:8], *refs[8 + len(after) :])

    return pl.pallas_call(
        body,
        grid_spec=pltpu.PrefetchScalarGridSpec(
            num_scalar_prefetch=1,
            grid=(away,),
            in_specs=[
                pl.BlockSpec(query.shape, same),
                pl.BlockSpec(first_visible.shape, same),
                pl.BlockSpec((1, span, HD), block),
                pl.BlockSpec((1, span, HD), block),
                pl.BlockSpec(query.shape, same),
                pl.BlockSpec(query.shape, same),
                pl.BlockSpec(lse.shape, lambda d, place: (0, 0, 0)),
            ]
            + [pl.BlockSpec(memory_space=pl.ANY)] * len(after),
            out_specs=[
                pl.BlockSpec(query.shape, same),
                pl.BlockSpec((1, span, HD), block),
                pl.BlockSpec((1, span, HD), block),
            ],
        ),
        out_shape=[
            shaped(query.shape, jnp.float32),
            shaped(keys.shape, low),
            shaped(keys.shape, low),
        ],
        compiler_params=pltpu.CompilerParams(vmem_limit_bytes=kernel_memory),
        cost_estimate=pl.CostEstimate(
            flops=30 * 10**9, bytes_accessed=4 * 10**6, transcendentals=0
        ),
    )(place, query, first_visible, keys, values, grad, out, lse, *after)


def conv_act(extended, conv_taps, conv_shift, keep_masks):
    length = keep_masks[0].shape[0]
    result = conv_shift + conv_taps[0] * extended[KW - 1 :]
    for lag_index in range(1, KW):
        begin = KW - 1 - lag_index
        result = (
            result
            + conv_taps[lag_index]
            * keep_masks[lag_index][:, None]
            * extended[begin : begin + length]
        )
    return jax.nn.silu(result)


def step_and_decay(step_raw, step_shift, decay_rate):
    step_size = jax.nn.softplus(step_raw + step_shift)
    return step_size, -step_size * jnp.exp(decay_rate)


def in_lanes(per_head):
    return jnp.pad(per_head, ((0, 0), (0, lanes - per_head.shape[1])))


def summed_over(values_in, axis):
    peers = lax.axis_size(axis)
    by = 1
    while by < peers:
        values_in = values_in + lax.ppermute(values_in, axis, [(i, i ^ by) for i in range(peers)])
        by *= 2
    return values_in


def per_device(
    block_input,
    out_cotangent,
    start_flags,
    in_weight,
    out_weight,
    gate_up_weight,
    down_weight,
    first_gain,
    second_gain,
    conv_weight,
    conv_bias,
    step_bias,
    decay_log,
    skip_gain,
):
    head_count = lax.axis_size("head")
    blocks = lax.axis_size("blk")
    head_index = lax.axis_index("head")
    block_index = lax.axis_index("blk")
    ring = ring_of("blk")
    tokens = block_input[0]
    cotangent = out_cotangent[0]
    row_count = tokens.shape[0]
    span_rows = row_count * head_count
    mamba_width = MH * MP
    even = head_index % 2 == 0
    out_pairs = mixer_place()
    place = jnp.stack(
        [head_index, head_index % 2, 0, 0, block_index, 0, 0, 0]
    ).astype(jnp.int32)

    rows_in = in_weight.shape[0]
    flags_all = summed_over(
        lax.dynamic_update_slice_in_dim(
            jnp.zeros((blocks * span_rows,), jnp.int32),
            start_flags[0],
            block_index * span_rows,
            0,
        ),
        "blk",
    )
    packed_conv, packed_rest = call(
        pack_in,
        [
            shaped((4, rows_in, conv_columns), low),
            shaped((4, rows_in, rest_columns), low),
        ],
        place,
        [in_weight],
        scratch=[pltpu.VMEM((rows_in, lanes), jnp.float32)],
    )
    conv_rows = swap_heads(packed_conv).reshape(-1, conv_columns)
    weights_conv = gather_blocks(conv_rows)
    rest_rows = swap_heads(after(packed_rest, conv_rows)).reshape(-1, rest_columns)
    weights_rest = gather_blocks(rest_rows)
    gathered_tokens = gather_heads(after(tokens, conv_rows))
    out_rows = lax.ppermute(after(out_weight.astype(low), rest_rows), ("head", "blk"), out_pairs)
    rows_ffn = gate_up_weight.shape[0]
    units = FF // 4
    packed_ffn = call(
        partial(pack_ffn, ring=ring),
        [shaped((4, rows_ffn, 2 * units), low)],
        place,
        [after(gate_up_weight, rest_rows)],
    )[0]
    ffn_rows = swap_heads(packed_ffn).reshape(-1, 2 * units)
    model_cotangent = jnp.concatenate(gather_heads(after(cotangent, ffn_rows)))

    positions = block_index * span_rows + jnp.arange(span_rows, dtype=jnp.int32)
    all_positions = jnp.arange(blocks * span_rows, dtype=jnp.int32)
    starts_all = lax.cummax(jnp.where(flags_all > 0, all_positions, 0), axis=0)
    first_visible = lax.dynamic_slice_in_dim(starts_all, block_index * span_rows, span_rows, 0)
    flags_before = jnp.concatenate([jnp.zeros((KW - 2,), jnp.int32), flags_all])
    flag_ext = lax.dynamic_slice_in_dim(
        flags_before, block_index * span_rows, span_rows + KW - 2, 0
    ).astype(jnp.float32)
    segment = jnp.broadcast_to(
        jnp.cumsum(start_flags[0]).astype(jnp.float32)[:, None], (span_rows, lanes)
    )
    view = jnp.stack([block_index, jnp.min(first_visible), jnp.max(first_visible)])
    first_wide = jnp.broadcast_to(first_visible[:, None], (span_rows, lanes))
    keep_masks = [jnp.ones((span_rows,), jnp.float32)]
    for lag_index in range(1, KW):
        begin = KW - 1 - lag_index
        keep_masks.append(keep_masks[-1] * (1.0 - flag_ext[begin : begin + span_rows]))
    frequencies = rope_base ** (-jnp.arange(HD // 2, dtype=jnp.float32) * 2.0 / HD)
    angles = positions.astype(jnp.float32)[:, None] * frequencies[None, :]
    cosine = jnp.cos(angles)
    sine = jnp.sin(angles)
    cosine_wide = jnp.concatenate([cosine, cosine], axis=1)
    sine_wide = jnp.concatenate([-sine, sine], axis=1)
    conv_taps = jnp.concatenate(
        [
            lax.dynamic_slice_in_dim(conv_weight, head_index * inner_columns, inner_columns, 1),
            conv_weight[:, mamba_width:],
        ],
        axis=1,
    )
    conv_shift = jnp.concatenate(
        [
            lax.dynamic_slice_in_dim(conv_bias, head_index * inner_columns, inner_columns, 0),
            conv_bias[mamba_width:],
        ]
    )
    step_shift = lax.dynamic_slice_in_dim(step_bias, head_index * step_heads, step_heads, 0)
    decay_rate = lax.dynamic_slice_in_dim(decay_log, head_index * step_heads, step_heads, 0)
    skip_local = lax.dynamic_slice_in_dim(skip_gain, head_index * step_heads, step_heads, 0)
    skip_wide = jnp.repeat(skip_local, MP)[None, :]

    normed_one = call(
        partial(norm_one, ring=ring),
        [shaped((span_rows, D), low)],
        place,
        [*gathered_tokens, first_gain[None, :]],
        scratch=[pltpu.VMEM((row_count, D), low)],
    )[0]

    projected = jnp.dot(normed_one, weights_conv, preferred_element_type=jnp.float32)
    kv_mine = call(
        rope_kv,
        [shaped((span_rows, HD), low)],
        place,
        [projected[:, kv_at:], cosine_wide, sine_wide],
    )[0]
    pair_bc = projected[:, inner_columns:step_at].astype(low)
    conv_local = call(
        join_conv,
        [shaped((span_rows, inner_columns + 2 * NS), low)],
        place,
        [projected[:, :inner_columns], *gather_heads(pair_bc)],
    )[0]
    step_local = projected[:, step_at : step_at + step_heads].astype(low).astype(jnp.float32)
    rim_rows = passed_along(conv_local[span_rows - (KW - 1) :], "blk", 1)
    extended = jnp.concatenate([rim_rows, conv_local], axis=0).astype(jnp.float32)
    active, conv_back = jax.vjp(
        partial(conv_act, keep_masks=keep_masks), extended, conv_taps, conv_shift
    )
    (step_size, log_decay), step_back = jax.vjp(
        step_and_decay, step_local, step_shift, decay_rate
    )
    inner_act = active[:, :inner_columns]
    into_act = active[:, inner_columns : inner_columns + NS]
    outof_act = active[:, inner_columns + NS :]
    step_wide = in_lanes(step_size)
    decay_wide = in_lanes(log_decay)
    tall = shaped((span_rows, inner_columns), jnp.float32)
    tall_low = shaped((span_rows, inner_columns), low)
    narrow = shaped((span_rows, lanes), jnp.float32)
    share = inner_columns // blocks
    sent = shaped((blocks, extra_rows + share, NS), low)
    state_scratch = pltpu.VMEM((inner_columns, NS), jnp.float32)

    def chained(payload, backwards, after=()):
        got = lax.all_to_all(payload, "blk", split_axis=0, concat_axis=0, tiled=True)
        states = call(
            partial(chain, backwards=backwards),
            [shaped((blocks, share, NS), low)],
            place,
            [got],
            after=after,
        )[0]
        moved = lax.all_to_all(states, "blk", split_axis=0, concat_axis=0, tiled=True)
        return moved.reshape(inner_columns, NS), states

    within, state_sent, entering, factor = call(
        ssd_local,
        [tall, sent, narrow, shaped((8, lanes), jnp.float32)],
        place,
        [inner_act, into_act, outof_act, step_wide, decay_wide, segment],
        after=[ffn_rows],
        scratch=[state_scratch],
        flops=6 * 10**9,
    )
    state_in, states_mine = chained(state_sent, False)

    normed_after = after(normed_one, states_mine)
    projected_rest = jnp.dot(normed_after, weights_rest, preferred_element_type=jnp.float32)
    query_local, gate_act = call(
        rope_query,
        [shaped((span_rows, query_columns), low), tall_low],
        place,
        [projected_rest, cosine_wide, sine_wide],
    )
    out_height = out_weight.shape[0] + span_rows * HD // D
    out_packed = call(
        pack_out, [shaped((out_height, D), low)], place, [out_rows, kv_mine]
    )[0]
    out_gathered = gather_blocks(after(out_packed, weights_rest, state_sent)).reshape(blocks, out_height, D)
    weights_out, kv_blocks = call(
        partial(unpack_out, ring=ring),
        [
            shaped((blocks, *out_weight.shape), low),
            shaped((blocks, span_rows, HD), low),
        ],
        place,
        [out_gathered],
        after=[query_local, states_mine],
    )
    weights_out = weights_out.reshape(-1, D)
    weights_ffn = gather_blocks(after(ffn_rows, out_gathered, query_local, states_mine))
    weights_down = gather_blocks(after(down_weight.astype(low), weights_ffn))
    kv_beside = from_head(kv_blocks, 1)
    keys = jnp.where(even, kv_blocks, kv_beside)
    values = jnp.where(even, kv_beside, kv_blocks)
    attended, lse = attention(
        view, query_local, first_wide, keys, values, [states_mine, model_cotangent]
    )

    ssd, mixer = call(
        partial(ssd_finish, turned_columns=blocks == 8),
        [tall, shaped((span_rows, query_columns + inner_columns), low)],
        place,
        [within, entering, outof_act, state_in, inner_act, gate_act, skip_wide, attended],
        flops=2 * 10**9,
    )
    pair_rows = 2 * row_count
    mixed_other = jnp.dot(mixer[pair_rows:], weights_out, preferred_element_type=jnp.float32)
    mixed_own = jnp.dot(mixer[:pair_rows], weights_out, preferred_element_type=jnp.float32)
    mixed = scatter_pairs(mixed_own, mixed_other)
    hidden_one, normed_two = call(
        partial(norm_two, ring=ring),
        [shaped((row_count, D), jnp.float32), shaped((row_count, D), low)],
        place,
        [mixed, tokens, second_gain[None, :]],
        scratch=[pltpu.VMEM((row_count, D), low)],
    )
    model_normed = jnp.concatenate(gather_heads(normed_two))
    gate_up = jnp.dot(model_normed, weights_ffn, preferred_element_type=jnp.float32)
    gate_part, up_part = gate_up[:, :units], gate_up[:, units:]
    activated = (jax.nn.silu(gate_part) * up_part).astype(low)
    grad_down_low = outer_grad(activated, model_cotangent).astype(low)
    grad_activated = times_transposed(model_cotangent, after(weights_down, grad_down_low))
    sigmoid_gate = jax.nn.sigmoid(gate_part)
    grad_gate_up = jnp.concatenate(
        [
            grad_activated * up_part * sigmoid_gate * (1.0 + gate_part * (1.0 - sigmoid_gate)),
            grad_activated * jax.nn.silu(gate_part),
        ],
        axis=1,
    ).astype(low)
    grad_down = scatter_blocks(after(grad_down_low, weights_down))
    gate_up_late = after(grad_gate_up, grad_down_low)
    grad_norm_other = times_transposed(gate_up_late[pair_rows:], weights_ffn).astype(low)
    grad_norm_own = times_transposed(gate_up_late[:pair_rows], weights_ffn)
    grad_normed_two = scatter_pairs(grad_norm_own, grad_norm_other, low)
    grad_ffn_low = outer_grad(model_normed, after(grad_gate_up, grad_norm_own)).astype(low)

    grad_hidden, grad_hidden_low, grad_second = call(
        partial(back_two, ring=ring),
        [
            shaped((row_count, D), jnp.float32),
            shaped((row_count, D), low),
            shaped((8, D), jnp.float32),
        ],
        place,
        [
            grad_normed_two,
            hidden_one,
            cotangent,
            second_gain[None, :],
        ],
        after=[grad_down_low, grad_ffn_low],
        scratch=[pltpu.VMEM((row_count, D), jnp.float32)],
    )
    grad_ffn = scatter_blocks(after(grad_ffn_low, grad_down, grad_hidden_low))
    span_grad_hidden = jnp.concatenate(gather_heads(after(grad_hidden_low, grad_down)))
    grad_heads = times_transposed(span_grad_hidden, weights_out).astype(low)
    grad_ssd, grad_gate, grad_sent, grad_skip_wide, grad_attended = call(
        partial(ssd_gate_back, turned_columns=blocks == 8),
        [
            tall,
            tall_low,
            sent,
            shaped((8, inner_columns), jnp.float32),
            shaped((span_rows, query_columns), low),
        ],
        place,
        [grad_heads, gate_act, ssd, inner_act, skip_wide, entering, outof_act, factor],
        scratch=[state_scratch],
        flops=2 * 10**9,
    )
    ffn_swapped = swap_heads(grad_ffn.reshape(4, rows_ffn, 2 * units))
    grad_ffn_weight = call(
        partial(unpack_ffn, ring=ring),
        [shaped(gate_up_weight.shape, jnp.float32)],
        place,
        [ffn_swapped],
    )[0]
    activated_late = after(activated, span_grad_hidden)
    downed_other = jnp.dot(
        activated_late[pair_rows:], weights_down, preferred_element_type=jnp.float32
    )
    downed_own = jnp.dot(
        activated_late[:pair_rows], weights_down, preferred_element_type=jnp.float32
    )
    block_output = (hidden_one + scatter_pairs(downed_own, downed_other, low)).astype(low)

    grad_skip = grad_skip_wide[0].reshape(step_heads, MP).sum(axis=1)
    grad_out_low = outer_grad(mixer, span_grad_hidden).astype(low)
    later_grad, later_mine = chained(grad_sent, True)

    grad_query, grad_keys, grad_values = attention_back(
        view,
        query_local,
        first_wide,
        keys,
        values,
        grad_attended,
        attended,
        lse,
        [grad_out_low],
    )
    kept_kv = jnp.where(even, grad_keys, grad_values)
    given_kv = jnp.where(even, grad_values, grad_keys)
    kv_sums = (kept_kv.astype(jnp.float32) + from_head(given_kv, 1).astype(jnp.float32)).astype(
        low
    )
    grad_rest = call(
        query_back,
        [shaped((span_rows, rest_columns), low)],
        place,
        [grad_query, grad_gate, cosine_wide, sine_wide],
        after=[later_mine],
    )[0]
    grad_rest_low = outer_grad(normed_one, grad_rest).astype(low)

    grad_out_packed = call(
        partial(pack_out_grads, ring=ring),
        [shaped((blocks, out_height, D), low)],
        place,
        [grad_out_low.reshape(blocks, -1, D), kv_sums],
        after=[grad_rest_low],
    )[0]
    grad_out_sum = scatter_blocks(
        after(grad_out_packed.reshape(-1, D), grad_ffn)
    )
    grad_kv = grad_out_sum[out_weight.shape[0] :]
    grad_inner, grad_into, grad_outof, grad_step, grad_decay_line = call(
        ssd_back,
        [
            tall,
            shaped((span_rows, NS), jnp.float32),
            shaped((span_rows, NS), jnp.float32),
            narrow,
            narrow,
        ],
        place,
        [
            inner_act,
            into_act,
            outof_act,
            step_wide,
            decay_wide,
            segment,
            grad_ssd,
            ssd,
            skip_wide,
            state_in,
            later_grad,
        ],
        after=[grad_out_packed, block_output],
        scratch=[
            pltpu.VMEM((span_rows // chunk + 1, inner_columns, NS), jnp.float32),
            state_scratch,
        ],
        flops=10 * 10**9,
    )
    grad_raw, grad_step_shift, grad_rate = step_back(
        (grad_step[:, :step_heads], grad_decay_line[:, :step_heads])
    )
    grad_extended, grad_taps, grad_shift = conv_back(
        jnp.concatenate([grad_inner, grad_into, grad_outof], axis=1)
    )
    rim_back = passed_along(grad_extended[: KW - 1], "blk", -1)
    conv_grad = grad_extended[KW - 1 :] + jnp.pad(rim_back, ((span_rows - (KW - 1), 0), (0, 0)))
    grad_bc = conv_grad[:, inner_columns:].astype(low).astype(jnp.float32)

    def tile_at(distance):
        at = jnp.bitwise_xor(head_index, distance) * lanes
        return lax.dynamic_slice_in_dim(grad_bc, at, lanes, 1)

    bc_beside = from_head(jnp.stack([tile_at(1), tile_at(3)]).astype(low), 1).astype(jnp.float32)
    bc_far = from_head((tile_at(2) + bc_beside[1]).astype(low), 2)
    bc_near = tile_at(0) + bc_beside[0]
    grad_conv = call(
        conv_joined,
        [shaped((span_rows, conv_columns), low)],
        place,
        [
            conv_grad[:, :inner_columns],
            bc_near,
            bc_far,
            in_lanes(grad_raw),
            cosine_wide,
            sine_wide,
            grad_kv,
        ],
        after=[ffn_swapped],
    )[0]
    grad_conv_low = outer_grad(normed_one, grad_conv).astype(low)
    grad_rest_in = scatter_blocks(after(grad_rest_low, grad_out_sum, grad_inner))
    conv_moved, rest_moved = call(
        relative_order,
        [shaped((span_rows, conv_columns), low), shaped((span_rows, rest_columns), low)],
        place,
        [grad_conv, grad_rest],
        after=[grad_conv_low],
    )

    def back_in(part):
        return times_transposed(rest_moved[part], weights_rest) + times_transposed(
            conv_moved[part], weights_conv
        )

    grad_normed_other = back_in(slice(pair_rows, span_rows)).astype(low)
    grad_normed_own = back_in(slice(0, pair_rows))
    rest_swapped = swap_heads(grad_rest_in.reshape(4, rows_in, -1))
    grad_out_rows = grad_out_sum[: out_weight.shape[0]]

    def to_owners(rows, along_heads):
        pairs = [
            (there, here)
            for here, there in out_pairs
            if (here % blocks == there % blocks) == along_heads
        ]
        return lax.ppermute(rows, ("head", "blk"), pairs)

    grad_mix_early = to_owners(after(grad_out_rows, grad_rest_in), True)
    grad_normed_own = after(grad_normed_own, rest_swapped, grad_mix_early)
    grad_input = call(
        partial(back_one, ring=ring),
        [shaped((row_count, D), low)],
        place,
        [
            scatter_pairs(grad_normed_own, grad_normed_other, low),
            tokens,
            grad_hidden,
            first_gain[None, :],
        ],
        after=[grad_ffn_weight],
        scratch=[pltpu.VMEM((row_count, D), jnp.float32)],
    )[0]
    first_line = jnp.sum(
        weights_conv.astype(jnp.float32) * grad_conv_low.astype(jnp.float32), axis=1
    ) + jnp.sum(weights_rest.astype(jnp.float32) * after(grad_rest_low, grad_conv_low).astype(jnp.float32), axis=1)
    first_line = first_line.reshape(blocks, 4, -1)
    first_line = jnp.stack([first_line[ring.index(k)] for k in range(blocks)], axis=1).reshape(D)

    def own_part(values_in, total):
        return lax.dynamic_update_slice_in_dim(
            jnp.zeros(values_in.shape[:-1] + (total,), jnp.float32),
            values_in,
            head_index * values_in.shape[-1],
            values_in.ndim - 1,
        )

    small = [
        first_line / first_gain,
        grad_second[0],
        jnp.concatenate(
            [own_part(grad_taps[:, :inner_columns], mamba_width), grad_taps[:, inner_columns:]],
            axis=1,
        ),
        jnp.concatenate(
            [own_part(grad_shift[:inner_columns], mamba_width), grad_shift[inner_columns:]]
        ),
        own_part(grad_step_shift, MH),
        own_part(grad_rate, MH),
        own_part(grad_skip, MH),
    ]
    line = jnp.concatenate([part.reshape(-1) for part in small])
    line = jnp.pad(line, (0, -line.shape[0] % 1024)).reshape(-1, 128)
    line = summed_over(summed_over(line, "head"), "blk").reshape(-1)
    grad_conv_in = scatter_blocks(after(grad_conv_low, grad_rest_in))
    grad_mix_late = to_owners(after(grad_out_rows, grad_conv_in), False)
    grad_mix_weight = grad_mix_early.astype(jnp.float32) + grad_mix_late.astype(jnp.float32)
    grad_proj_weight = call(
        unpack_in,
        [shaped(in_weight.shape, jnp.float32)],
        place,
        [swap_heads(grad_conv_in.reshape(4, rows_in, -1)), rest_swapped],
        after=[grad_mix_weight],
    )[0]
    summed_small = []
    at = 0
    for part in small:
        summed_small.append(line[at : at + part.size].reshape(part.shape))
        at += part.size
    return (
        block_output[None],
        grad_input[None],
        grad_proj_weight,
        grad_mix_weight,
        grad_ffn_weight,
        grad_down.astype(jnp.float32),
        *summed_small,
    )


def own_first(chunks, mine, order=(0, 1, 2, 3)):
    return [lax.dynamic_index_in_dim(chunks, jnp.bitwise_xor(mine, d), 0, False) for d in order]


def solution(mesh):
    placed = (
        P("blk", "head", None),
        P("blk", "head", None),
        P("blk", None),
        P(("head", "blk"), None),
        P(("head", "blk"), None),
        P(("head", "blk"), None),
        P(("head", "blk"), None),
        P(),
        P(),
        P(),
        P(),
        P(),
        P(),
        P(),
    )
    return jax.shard_map(
        per_device,
        mesh=mesh,
        in_specs=placed,
        out_specs=(
            P("blk", "head", None),
            P("blk", "head", None),
            P(("head", "blk"), None),
            P(("head", "blk"), None),
            P(("head", "blk"), None),
            P(("head", "blk"), None),
            P(),
            P(),
            P(),
            P(),
            P(),
            P(),
            P(),
        ),
        check_vma=False,
    )
```
